32 devices in a mesh: ctx: 8 (over y, x, core), wa: 4 (over z).
Axes of the slice: x: 2, y: 2, z: 4, core: 2. Of those that a mesh axis runs over, the one named last changes fastest.
Arguments:
- hidden: bfloat16 [4, 2048, 512], P('wa', 'ctx'), may hold values from -6 to 6
- stream: bfloat16 [4, 2048, 512], P('wa', 'ctx'), may hold values from -6 to 6
- encoder: bfloat16 [4, 2048, 512], P('wa', 'ctx'), may hold values from -6 to 6
- lengths: int32 [4, 4], P('wa'), may hold values from 1 to 1024, 2048 in all within a row
- order: int32 [4, 2048], P('wa'), may hold values from 0 to 2047, each once within a row
- ranks: int32 [4, 2048], P('wa'), may hold values from 0 to 1023
- thresholds: int32 [4, 2048], P('wa'), may hold values from 1 to 1024
- self_query: bfloat16 [512, 512], P('wa'), may hold values from -0.25 to 0.25
- self_key_value: bfloat16 [512, 1024], P('wa'), may hold values from -0.25 to 0.25
- self_output: bfloat16 [512, 512], P('wa'), may hold values from -1 to 1
- cross_query: bfloat16 [512, 512], P('wa'), may hold values from -0.25 to 0.25
- cross_key_value: bfloat16 [512, 1024], P('wa'), may hold values from -0.25 to 0.25
- cross_output: bfloat16 [512, 512], P('wa'), may hold values from -1 to 1
- ffn_in: bfloat16 [512, 2048], P('wa'), may hold values from -0.25 to 0.25
- ffn_out: bfloat16 [2048, 512], P('wa'), may hold values from -0.1875 to 0.1875
- norm_gain: bfloat16 [3, 512], P(None, 'wa'), may hold values from 0.5 to 1.5
- norm_shift: bfloat16 [3, 512], P(None, 'wa'), may hold values from -2 to 2
- cotangent: bfloat16 [4, 2048, 512], P('wa', 'ctx'), may hold values from -6 to 6
Outputs:
- layer_out: bfloat16 [4, 2048, 512], P('wa', 'ctx')
- hidden_grad: float32 [4, 2048, 512], P('wa', 'ctx')
- stream_grad: float32 [4, 2048, 512], P('wa', 'ctx')
- encoder_grad: float32 [4, 2048, 512], P('wa', 'ctx')
- self_query_grad: float32 [512, 512], P('wa')
- self_key_value_grad: float32 [512, 1024], P('wa')
- self_output_grad: float32 [512, 512], P('wa')
- cross_query_grad: float32 [512, 512], P('wa')
- cross_key_value_grad: float32 [512, 1024], P('wa')
- cross_output_grad: float32 [512, 512], P('wa')
- ffn_in_grad: float32 [512, 2048], P('wa')
- ffn_out_grad: float32 [2048, 512], P('wa')
- norm_gain_grad: float32 [3, 512], P(None, 'wa')
- norm_shift_grad: float32 [3, 512], P(None, 'wa')
The draws below stay inside these ranges and needn't reach their ends.
All inputs are finite; a program needn't handle non-finite values.
Results may differ from the reference program's by a relative error of at most 0.022.
Values may be sent and summed in bfloat16 or wider, within the bound.
No kernel may reach another device: no remote copies, remote signals or barrier semaphores. Data moves between devices by JAX's collectives and lax.ppermute only.
A program may use at most 384 MiB of HBM per device.

```python
import math
import jax
import jax.numpy as jnp
import numpy as np
from jax import lax

D = 512
HEADS = 8
FF = 2048
HEAD = 64
TOK_DEV = 256
SEQS = 4
RANKS = 1024
GROUPS = 4
GTOK = 2048
MOST = 1024


def plant(entries, rng, smallest, largest):
    shape = entries.shape
    spot = [jax.random.randint(jax.random.fold_in(rng, axis), (), 0, shape[axis]) for axis in range(len(shape))]
    entries = entries.at[tuple(spot)].set(smallest)
    longest = shape.index(max(shape))
    spot[longest] = (spot[longest] + 1) % shape[longest]
    return entries.at[tuple(spot)].set(largest)


def levels(rng, extent, cuts, smallest, top_value):
    level = 1.0
    for axis_at, blocks in cuts:
        steps = jax.random.uniform(jax.random.fold_in(jax.random.fold_in(rng, 6), axis_at), (blocks,), jnp.float32, smallest / len(cuts), top_value / len(cuts))
        level = level * jnp.repeat(jnp.exp(steps), extent[axis_at] // blocks).reshape((-1,) + (1,) * (len(extent) - 1 - axis_at))
    return level


def profile(number_of, total, limit, skew):
    weights = [(1 << 20) // math.isqrt(rank ** skew) + 1 for rank in range(2, number_of + 1)]
    spare, given = total - limit - (number_of - 1), [1] * (number_of - 1)
    while spare > 0:
        movable = [i for i in range(number_of - 1) if given[i] < limit]
        pool, budget = sum([weights[i] for i in movable]), spare
        for i in movable:
            addition = min(limit - given[i], max(1, budget * weights[i] // pool), spare)
            given[i] = given[i] + addition
            spare = spare - addition
    return np.array([limit] + given)


def ragged(stream_key, count, total, reach, skew):
    if count == 2:
        one = jax.random.randint(stream_key, (), max(1, total - reach), min(reach, total - 1) + 1)
        return jnp.stack([one, total - one])
    tallies = jnp.asarray(profile(count, total, reach, skew), jnp.int32)
    twos = (count - 1) // 2
    source_of, taker = tallies[1:1 + 2 * twos:2], tallies[2:2 + 2 * twos:2]
    slack = jnp.minimum(source_of - 1, reach - taker)
    passed = jax.random.randint(jax.random.fold_in(stream_key, 1), (twos,), 0, 1 << 20) % (slack + 1)
    tallies = tallies.at[1:1 + 2 * twos:2].set(source_of - passed).at[2:2 + 2 * twos:2].set(taker + passed)
    return tallies[jax.random.permutation(jax.random.fold_in(stream_key, 2), count)]


def normal_values(rng, extent, width, limit, cuts=(), kind=jnp.bfloat16):
    values = width * jax.random.normal(rng, extent, jnp.float32)
    if cuts:
        values = values * levels(rng, extent, cuts, -0.22, 0.18)
    return jnp.clip(values, -limit, limit).astype(kind)


def setup_inputs(seed: int = 0) -> dict:
    key_of = jax.random.split(jax.random.key(seed), 19)
    hidden = normal_values(key_of[0], (GROUPS, GTOK, D), 1.0, 6.0, ((0, 4), (1, 8)))
    stream = normal_values(key_of[1], (GROUPS, GTOK, D), 1.0, 6.0, ((0, 4), (1, 8)))
    encoder = normal_values(key_of[2], (GROUPS, GTOK, D), 1.0, 6.0, ((0, 4), (1, 8)))
    lengths = jax.vmap(lambda own: ragged(own, SEQS, GTOK, MOST, 2))(jax.random.split(key_of[3], GROUPS)).reshape((GROUPS, SEQS)).astype(jnp.int32)
    order = jax.vmap(lambda own: jax.random.permutation(own, GTOK))(jax.random.split(key_of[4], GROUPS)).reshape((GROUPS, GTOK)).astype(jnp.int32)
    ranks = plant(jax.random.randint(key_of[5], (GROUPS, GTOK), 0, RANKS), jax.random.fold_in(key_of[5], 1), 0, RANKS - 1).astype(jnp.int32)
    thresholds = plant(jax.random.randint(key_of[6], (GROUPS, GTOK), 1, RANKS + 1), jax.random.fold_in(key_of[6], 1), 1, RANKS).astype(jnp.int32)
    self_query = normal_values(key_of[7], (D, D), D ** -0.5, 0.25, ((0, 4),))
    self_key_value = normal_values(key_of[8], (D, 2 * D), D ** -0.5, 0.25, ((0, 4),))
    self_output = normal_values(key_of[9], (D, D), (D // 16) ** -0.5, 1.0, ((0, 4),))
    cross_query = normal_values(key_of[10], (D, D), D ** -0.5, 0.25, ((0, 4),))
    cross_key_value = normal_values(key_of[11], (D, 2 * D), D ** -0.5, 0.25, ((0, 4),))
    cross_output = normal_values(key_of[12], (D, D), (D // 16) ** -0.5, 1.0, ((0, 4),))
    ffn_in = normal_values(key_of[13], (D, FF), D ** -0.5, 0.25, ((0, 4),))
    ffn_out = normal_values(key_of[14], (FF, D), (FF // 2) ** -0.5, 0.1875, ((0, 4),))
    norm_gain = jnp.clip(1.0 + 0.1 * jax.random.normal(key_of[15], (3, D), jnp.float32), 0.5, 1.5).astype(jnp.bfloat16)
    norm_shift = normal_values(key_of[16], (3, D), 0.3, 2.0, ((1, 4),))
    cotangent = normal_values(key_of[17], (GROUPS, GTOK, D), 1.0, 6.0, ((0, 4), (1, 8)))
    return {"hidden": hidden, "stream": stream, "encoder": encoder, "lengths": lengths, "order": order, "ranks": ranks, "thresholds": thresholds, "self_query": self_query, "self_key_value": self_key_value, "self_output": self_output, "cross_query": cross_query, "cross_key_value": cross_key_value, "cross_output": cross_output, "ffn_in": ffn_in, "ffn_out": ffn_out, "norm_gain": norm_gain, "norm_shift": norm_shift, "cotangent": cotangent}


@jax.custom_vjp
def low(v):
    return lax.optimization_barrier(v.astype(jnp.bfloat16)).astype(jnp.float32)

@jax.custom_vjp
def low_back(v):
    return v

def low_keep(v):
    return (low(v), None)

def low_pass(kept, grad):
    return (grad,)

def back_keep(v):
    return (v, None)

def back_low(kept, grad):
    return (low(grad),)
low.defvjp(low_keep, low_pass)
low_back.defvjp(back_keep, back_low)
layer_eps = 1e-05
neg_fill = -1e+30

def matmul(left, right):
    return jnp.dot(left, right, precision=lax.Precision.HIGHEST)

def layer_norm(values, gain_row, shift_row):
    row_mean = lax.optimization_barrier(jnp.mean(values, axis=-1, keepdims=True))
    centred = values - row_mean
    variance = lax.optimization_barrier(jnp.mean(centred * centred, axis=-1, keepdims=True))
    return centred * lax.rsqrt(variance + layer_eps) * gain_row + shift_row

def sequence_ids(positions, seq_ends):
    return lax.optimization_barrier(jnp.sum((positions[:, None] >= seq_ends[None, :]).astype(jnp.int32), axis=1))

def attend(queries, key_values, allowed):
    count_rows = queries.shape[0]
    query_heads = queries.reshape(count_rows, HEADS, HEAD)
    key_heads = key_values[:, :D].reshape(-1, HEADS, HEAD)
    value_heads = key_values[:, D:].reshape(-1, HEADS, HEAD)
    raw_scores = jnp.einsum('lhd,khd->hlk', query_heads, key_heads, precision=lax.Precision.HIGHEST)
    scores = low_back(raw_scores) * float(HEAD) ** (-0.5)
    scores = jnp.where(allowed[None], scores, neg_fill)
    weights = low(jax.nn.softmax(scores, axis=-1))
    mixed = jnp.einsum('hlk,khd->lhd', weights, value_heads, precision=lax.Precision.HIGHEST)
    return mixed.reshape(count_rows, D)

def group_forward(inputs, stream_rows, source_rows, seq_lengths, dealt, key_ranks, limits, params):
    weight_query, weight_pair, weight_output, cross_query_w, cross_pair_w, cross_output_w, weight_in, weight_out, gains, shifts = params
    seq_ends = jnp.cumsum(seq_lengths)
    token_seq = sequence_ids(dealt, seq_ends)
    all_rows = jnp.arange(GTOK, dtype=jnp.int32)
    source_seq = sequence_ids(all_rows, seq_ends)
    blocks = GTOK // TOK_DEV

    def split_rows(array):
        return array.reshape((blocks, TOK_DEV) + array.shape[1:])
    queries = low(low_back(matmul(inputs, weight_query)))
    self_pairs = low(low_back(matmul(stream_rows, weight_pair)))

    def self_block(pieces):
        block_queries, block_seq, block_limit, block_rows = pieces
        allowed = (block_seq[:, None] == token_seq[None, :]) & ((key_ranks[None, :] < block_limit[:, None]) | (block_rows[:, None] == all_rows[None, :]))
        return attend(block_queries, self_pairs, allowed)
    self_mixed = lax.map(jax.checkpoint(self_block), (split_rows(queries), split_rows(token_seq), split_rows(limits), split_rows(all_rows))).reshape(GTOK, D)
    self_low = low(low_back(self_mixed))
    first = layer_norm(inputs + low_back(matmul(self_low, weight_output)), gains[0], shifts[0])
    cross_queries = low(low_back(matmul(low(first), cross_query_w)))
    cross_pairs = low(low_back(matmul(source_rows, cross_pair_w)))

    def cross_block(pieces):
        block_queries, block_seq = pieces
        return attend(block_queries, cross_pairs, block_seq[:, None] == source_seq[None, :])
    cross_mixed = lax.map(jax.checkpoint(cross_block), (split_rows(cross_queries), split_rows(token_seq))).reshape(GTOK, D)
    cross_low = low(low_back(cross_mixed))
    second = layer_norm(first + low_back(matmul(cross_low, cross_output_w)), gains[1], shifts[1])
    hidden_pre = low_back(matmul(low(second), weight_in))
    activated = low(jax.nn.silu(hidden_pre))
    return layer_norm(second + low_back(matmul(activated, weight_out)), gains[2], shifts[2])

def reference(hidden, stream, encoder, lengths, order, ranks, thresholds, self_query, self_key_value, self_output, cross_query, cross_key_value, cross_output, ffn_in, ffn_out, norm_gain, norm_shift, cotangent):
    params = tuple((weight.astype(jnp.float32) for weight in (self_query, self_key_value, self_output, cross_query, cross_key_value, cross_output, ffn_in, ffn_out, norm_gain, norm_shift)))

    def forward(inputs, stream_rows, source_rows, weights):
        outputs = [group_forward(inputs[group_index], stream_rows[group_index], source_rows[group_index], lengths[group_index], order[group_index], ranks[group_index], thresholds[group_index], weights) for group_index in range(GROUPS)]
        return jnp.stack(outputs)
    result, pullback = jax.vjp(forward, hidden.astype(jnp.float32), stream.astype(jnp.float32), encoder.astype(jnp.float32), params)
    grad_inputs, grad_stream, grad_source, grad_params = pullback(cotangent.astype(jnp.float32))
    return (result.astype(jnp.bfloat16), grad_inputs, grad_stream, grad_source, grad_params[0], grad_params[1], grad_params[2], grad_params[3], grad_params[4], grad_params[5], grad_params[6], grad_params[7], grad_params[8], grad_params[9])
```

```python
import functools

import jax
import jax.numpy as jnp
from jax import lax
from jax.experimental import pallas as pl
from jax.experimental.pallas import tpu as pltpu
from jax.sharding import PartitionSpec as P

D = 512
HEADS = 8
HEAD = 64
KEYBLK = 1024


layer_eps = 1e-05
neg_fill = -1e30


def sequence_ids(positions, seq_ends):
    return jnp.sum((positions[:, None] >= seq_ends[None, :]).astype(jnp.int32), axis=1)


def head_split(matrix):
    return matrix.reshape(matrix.shape[0], HEADS, HEAD)


def block_scores(query_heads, key_heads):
    raw_scores = jnp.einsum(
        "lhd,khd->hlk", query_heads, key_heads, preferred_element_type=jnp.float32
    )
    return raw_scores * float(HEAD) ** (-0.5)


def softmax_totals(queries, key_rows, allowed_fn):
    query_heads = head_split(queries)
    count_rows = queries.shape[0]

    def visit(state_pair, block_index):
        running_top, running_sum = state_pair
        block_start = block_index * KEYBLK
        key_piece = lax.dynamic_slice_in_dim(key_rows, block_start, KEYBLK, 0)
        allowed = allowed_fn(block_start)[None]
        scores = jnp.where(
            allowed, block_scores(query_heads, head_split(key_piece[:, :D])), neg_fill
        )
        new_top = jnp.maximum(running_top, jnp.max(scores, axis=2))
        weights = jnp.where(allowed, jnp.exp(scores - new_top[:, :, None]), 0.0)
        running_sum = running_sum * jnp.exp(running_top - new_top) + jnp.sum(weights, axis=2)
        return ((new_top, running_sum), None)

    initial = (
        jnp.full((HEADS, count_rows), neg_fill, jnp.float32),
        jnp.zeros((HEADS, count_rows), jnp.float32),
    )
    (final_top, final_sum), unused = lax.scan(
        visit, initial, jnp.arange(key_rows.shape[0] // KEYBLK)
    )
    return final_top + jnp.log(final_sum)


def attend_values(queries, key_rows, log_totals, allowed_fn):
    query_heads = head_split(queries)

    def visit(running, block_index):
        block_start = block_index * KEYBLK
        key_piece = lax.dynamic_slice_in_dim(key_rows, block_start, KEYBLK, 0)
        allowed = allowed_fn(block_start)[None]
        scores = block_scores(query_heads, head_split(key_piece[:, :D]))
        weights = jnp.where(allowed, jnp.exp(scores - log_totals[:, :, None]), 0.0)
        value_heads = head_split(key_piece[:, D:])
        return (
            running
            + jnp.einsum(
                "hlk,khd->lhd",
                weights.astype(jnp.bfloat16),
                value_heads,
                preferred_element_type=jnp.float32,
            ),
            None,
        )

    mixed, unused = lax.scan(
        visit, jnp.zeros(query_heads.shape, jnp.float32), jnp.arange(key_rows.shape[0] // KEYBLK)
    )
    return mixed.reshape(queries.shape[0], D)


def head_offsets(grad_low, attended):
    return jnp.sum(head_split(grad_low.astype(jnp.float32) * attended), axis=2).T


def attend_back(queries, key_rows, log_totals, attended, grad_low, allowed_fn):
    query_heads = head_split(queries)
    grad_heads = head_split(grad_low)
    offsets = head_offsets(grad_low, attended)
    scale_value = float(HEAD) ** (-0.5)

    def visit(query_grad, block_index):
        block_start = block_index * KEYBLK
        key_piece = lax.dynamic_slice_in_dim(key_rows, block_start, KEYBLK, 0)
        allowed = allowed_fn(block_start)[None]
        key_heads = head_split(key_piece[:, :D])
        value_heads = head_split(key_piece[:, D:])
        weights = jnp.where(
            allowed, jnp.exp(block_scores(query_heads, key_heads) - log_totals[:, :, None]), 0.0
        )
        value_grad = jnp.einsum(
            "hlk,lhd->khd",
            weights.astype(jnp.bfloat16),
            grad_heads,
            preferred_element_type=jnp.float32,
        )
        weight_grad = jnp.einsum(
            "lhd,khd->hlk", grad_heads, value_heads, preferred_element_type=jnp.float32
        )
        score_grad = (weights * (weight_grad - offsets[:, :, None]) * scale_value).astype(
            jnp.bfloat16
        )
        query_grad = query_grad + jnp.einsum(
            "hlk,khd->lhd", score_grad, key_heads, preferred_element_type=jnp.float32
        )
        key_grad = jnp.einsum(
            "hlk,lhd->khd", score_grad, query_heads, preferred_element_type=jnp.float32
        )
        return (
            query_grad,
            jnp.concatenate((key_grad.reshape(KEYBLK, D), value_grad.reshape(KEYBLK, D)), axis=1),
        )

    query_grad, grad_pieces = lax.scan(
        visit, jnp.zeros(query_heads.shape, jnp.float32), jnp.arange(key_rows.shape[0] // KEYBLK)
    )
    return (query_grad.reshape(queries.shape[0], D), grad_pieces.reshape(key_rows.shape[0], 2 * D))


def normalize(values, gain_row, shift_row):
    row_mean = jnp.mean(values, axis=1, keepdims=True)
    centred = values - row_mean
    scale_inv = lax.rsqrt(jnp.mean(centred * centred, axis=1, keepdims=True) + layer_eps)
    normed = centred * scale_inv
    return (normed * gain_row + shift_row, normed, scale_inv)


def normalize_back(grad_out, normed, scale_inv, gain_row):
    gain_term = jnp.sum(grad_out * normed, axis=0)
    shift_term = jnp.sum(grad_out, axis=0)
    scaled = grad_out * gain_row
    grad_in = scale_inv * (
        scaled
        - jnp.mean(scaled, axis=1, keepdims=True)
        - normed * jnp.mean(scaled * normed, axis=1, keepdims=True)
    )
    return (grad_in, gain_term, shift_term)


def matmul(left, right):
    return jnp.dot(left, right, preferred_element_type=jnp.float32)


def general_shards(
    hidden,
    stream,
    encoder,
    lengths,
    order,
    ranks,
    thresholds,
    self_query,
    self_key_value,
    self_output,
    cross_query,
    cross_key_value,
    cross_output,
    ffn_in,
    ffn_out,
    norm_gain,
    norm_shift,
    cotangent,
):
    (
        full_query,
        full_pair,
        full_output,
        full_cross_query,
        full_cross_pair,
        full_cross_output,
        full_in,
        full_out,
        gain_rows,
        shift_rows,
    ) = (
        lax.all_gather(self_query, "wa", axis=0, tiled=True),
        lax.all_gather(self_key_value, "wa", axis=0, tiled=True),
        lax.all_gather(self_output, "wa", axis=0, tiled=True),
        lax.all_gather(cross_query, "wa", axis=0, tiled=True),
        lax.all_gather(cross_key_value, "wa", axis=0, tiled=True),
        lax.all_gather(cross_output, "wa", axis=0, tiled=True),
        lax.all_gather(ffn_in, "wa", axis=0, tiled=True),
        lax.all_gather(ffn_out, "wa", axis=0, tiled=True),
        lax.all_gather(norm_gain, "wa", axis=1, tiled=True),
        lax.all_gather(norm_shift, "wa", axis=1, tiled=True),
    )
    gains = gain_rows.astype(jnp.float32)
    shifts = shift_rows.astype(jnp.float32)
    local_rows = hidden.shape[1]
    total_rows = order.shape[1]
    row_start = lax.axis_index("ctx") * local_rows
    seq_ends = jnp.cumsum(lengths[0])
    token_seq = sequence_ids(order[0], seq_ends)
    source_seq = sequence_ids(jnp.arange(total_rows, dtype=jnp.int32), seq_ends)
    query_seq = lax.dynamic_slice_in_dim(token_seq, row_start, local_rows)
    query_rows = row_start + jnp.arange(local_rows, dtype=jnp.int32)
    all_limits = thresholds[0]
    limits = lax.dynamic_slice_in_dim(all_limits, row_start, local_rows)
    key_ranks = ranks[0]

    def self_allowed(block_start):
        block_seq = lax.dynamic_slice_in_dim(token_seq, block_start, KEYBLK)
        block_rank = lax.dynamic_slice_in_dim(key_ranks, block_start, KEYBLK)
        block_rows = block_start + jnp.arange(KEYBLK, dtype=jnp.int32)
        return (query_seq[:, None] == block_seq[None, :]) & (
            (block_rank[None, :] < limits[:, None]) | (query_rows[:, None] == block_rows[None, :])
        )

    def cross_allowed(block_start):
        return (
            query_seq[:, None] == lax.dynamic_slice_in_dim(source_seq, block_start, KEYBLK)[None, :]
        )

    inputs = hidden[0]
    stream_rows = stream[0]
    source_rows = encoder[0]
    queries = matmul(inputs, full_query).astype(jnp.bfloat16)
    self_local = matmul(stream_rows, full_pair).astype(jnp.bfloat16)
    cross_local = matmul(source_rows, full_cross_pair).astype(jnp.bfloat16)
    self_keys, cross_keys = (
        lax.all_gather(self_local, "ctx", axis=0, tiled=True),
        lax.all_gather(cross_local, "ctx", axis=0, tiled=True),
    )
    self_totals = softmax_totals(queries, self_keys, self_allowed)
    self_mixed = attend_values(queries, self_keys, self_totals, self_allowed)
    self_low = self_mixed.astype(jnp.bfloat16)
    first, first_normed, first_scale = normalize(
        inputs.astype(jnp.float32) + matmul(self_low, full_output), gains[0], shifts[0]
    )
    first_low = first.astype(jnp.bfloat16)
    cross_queries = matmul(first_low, full_cross_query).astype(jnp.bfloat16)
    cross_totals = softmax_totals(cross_queries, cross_keys, cross_allowed)
    cross_mixed = attend_values(cross_queries, cross_keys, cross_totals, cross_allowed)
    cross_low = cross_mixed.astype(jnp.bfloat16)
    second, second_normed, second_scale = normalize(
        first + matmul(cross_low, full_cross_output), gains[1], shifts[1]
    )
    second_low = second.astype(jnp.bfloat16)
    hidden_pre = matmul(second_low, full_in)
    sigmoid_pre = jax.nn.sigmoid(hidden_pre)
    activated = (hidden_pre * sigmoid_pre).astype(jnp.bfloat16)
    result, third_normed, third_scale = normalize(
        second + matmul(activated, full_out), gains[2], shifts[2]
    )
    third_grad, gain_grad_c, shift_grad_c = normalize_back(
        cotangent[0].astype(jnp.float32), third_normed, third_scale, gains[2]
    )
    branch_grad = third_grad.astype(jnp.bfloat16)
    grad_ffn_out = matmul(activated.T, branch_grad)
    slope = sigmoid_pre * (1.0 + hidden_pre * (1.0 - sigmoid_pre))
    pre_grad = (matmul(branch_grad, full_out.T) * slope).astype(jnp.bfloat16)
    grad_ffn_in = matmul(second_low.T, pre_grad)
    second_total = third_grad + matmul(pre_grad, full_in.T)
    second_grad, gain_grad_b, shift_grad_b = normalize_back(
        second_total, second_normed, second_scale, gains[1]
    )
    cross_branch = second_grad.astype(jnp.bfloat16)
    grad_cross_output = matmul(cross_low.T, cross_branch)
    cross_mixed_grad = matmul(cross_branch, full_cross_output.T).astype(jnp.bfloat16)
    cross_query_term, cross_terms = attend_back(
        cross_queries, cross_keys, cross_totals, cross_mixed, cross_mixed_grad, cross_allowed
    )
    cross_query_low = cross_query_term.astype(jnp.bfloat16)
    grad_cross_query = matmul(first_low.T, cross_query_low)
    first_total = second_grad + matmul(cross_query_low, full_cross_query.T)
    first_grad, gain_grad_a, shift_grad_a = normalize_back(
        first_total, first_normed, first_scale, gains[0]
    )
    self_branch = first_grad.astype(jnp.bfloat16)
    grad_self_output = matmul(self_low.T, self_branch)
    self_mixed_grad = matmul(self_branch, full_output.T).astype(jnp.bfloat16)
    self_query_term, self_terms = attend_back(
        queries, self_keys, self_totals, self_mixed, self_mixed_grad, self_allowed
    )
    self_sum, cross_sum = (
        lax.psum_scatter(self_terms, "ctx", scatter_dimension=0, tiled=True),
        lax.psum_scatter(cross_terms, "ctx", scatter_dimension=0, tiled=True),
    )
    self_query_low = self_query_term.astype(jnp.bfloat16)
    grad_self_query = matmul(inputs.T, self_query_low)
    input_grad = first_grad + matmul(self_query_low, full_query.T)
    self_sum_low = self_sum.astype(jnp.bfloat16)
    grad_self_pair = matmul(stream_rows.T, self_sum_low)
    stream_grad = matmul(self_sum_low, full_pair.T)
    cross_sum_low = cross_sum.astype(jnp.bfloat16)
    grad_cross_pair = matmul(source_rows.T, cross_sum_low)
    source_grad = matmul(cross_sum_low, full_cross_pair.T)
    gain_grads = jnp.stack((gain_grad_a, gain_grad_b, gain_grad_c))
    shift_grads = jnp.stack((shift_grad_a, shift_grad_b, shift_grad_c))
    (
        share_query,
        share_pair,
        share_output,
        share_cross_query,
        share_cross_pair,
        share_cross_output,
        share_in,
        share_out,
        share_gain,
        share_shift,
    ) = (
        lax.psum_scatter(
            grad_self_query.astype(jnp.bfloat16), "wa", scatter_dimension=0, tiled=True
        ).astype(jnp.float32),
        lax.psum_scatter(
            grad_self_pair.astype(jnp.bfloat16), "wa", scatter_dimension=0, tiled=True
        ).astype(jnp.float32),
        lax.psum_scatter(
            grad_self_output.astype(jnp.bfloat16), "wa", scatter_dimension=0, tiled=True
        ).astype(jnp.float32),
        lax.psum_scatter(
            grad_cross_query.astype(jnp.bfloat16), "wa", scatter_dimension=0, tiled=True
        ).astype(jnp.float32),
        lax.psum_scatter(
            grad_cross_pair.astype(jnp.bfloat16), "wa", scatter_dimension=0, tiled=True
        ).astype(jnp.float32),
        lax.psum_scatter(
            grad_cross_output.astype(jnp.bfloat16), "wa", scatter_dimension=0, tiled=True
        ).astype(jnp.float32),
        lax.psum_scatter(
            grad_ffn_in.astype(jnp.bfloat16), "wa", scatter_dimension=0, tiled=True
        ).astype(jnp.float32),
        lax.psum_scatter(
            grad_ffn_out.astype(jnp.bfloat16), "wa", scatter_dimension=0, tiled=True
        ).astype(jnp.float32),
        lax.psum_scatter(
            gain_grads.astype(jnp.bfloat16), "wa", scatter_dimension=1, tiled=True
        ).astype(jnp.float32),
        lax.psum_scatter(
            shift_grads.astype(jnp.bfloat16), "wa", scatter_dimension=1, tiled=True
        ).astype(jnp.float32),
    )
    (
        total_query,
        total_pair,
        total_output,
        total_cross_query,
        total_cross_pair,
        total_cross_output,
        total_in,
        total_out,
        total_gain,
        total_shift,
    ) = lax.psum(
        (
            share_query,
            share_pair,
            share_output,
            share_cross_query,
            share_cross_pair,
            share_cross_output,
            share_in,
            share_out,
            share_gain,
            share_shift,
        ),
        "ctx",
    )
    return (
        result.astype(jnp.bfloat16)[None],
        input_grad[None],
        stream_grad[None],
        source_grad[None],
        total_query,
        total_pair,
        total_output,
        total_cross_query,
        total_cross_pair,
        total_cross_output,
        total_in,
        total_out,
        total_gain,
        total_shift,
    )


PAIR = 2 * HEAD
PAIRS = HEADS // 2
FF = 2048
low_t = jnp.bfloat16
wide_t = jnp.float32
vmem_spec = pl.BlockSpec(memory_space=pltpu.VMEM)
smem_spec = pl.BlockSpec(memory_space=pltpu.SMEM)


def run(body, outs, ids, args, scratch=(), flops=0, vmem=56):
    outs = [jax.ShapeDtypeStruct(shape, kind) for shape, kind in outs]
    moved = sum(a.size * a.dtype.itemsize for a in list(args) + outs)
    return pl.pallas_call(
        body,
        out_shape=outs,
        in_specs=[smem_spec] + [vmem_spec] * len(args),
        out_specs=[vmem_spec] * len(outs),
        scratch_shapes=[pltpu.VMEM(shape, kind) for shape, kind in scratch],
        compiler_params=pltpu.CompilerParams(vmem_limit_bytes=vmem * 1024 * 1024),
        cost_estimate=pl.CostEstimate(flops=int(flops), bytes_accessed=moved, transcendentals=0),
    )(ids, *args)


def dot_nn(a, b):
    return lax.dot_general(a, b, (((1,), (0,)), ((), ())), preferred_element_type=wide_t)


def dot_nt(a, b):
    return lax.dot_general(a, b, (((1,), (1,)), ((), ())), preferred_element_type=wide_t)


def dot_tn(a, b):
    return lax.dot_general(a, b, (((0,), (0,)), ((), ())), preferred_element_type=wide_t)


def at16(start, size=16):
    return pl.ds(pl.multiple_of(start, 16), size)


def at128(start, size=128):
    return pl.ds(pl.multiple_of(start, 128), size)


def assemble(ids, parts, whole_ref, columns=None):
    me, mw = ids[0], ids[1]
    for d in range(8):
        own = me ^ d
        for e in range(4):
            row = (mw ^ e) * 128 + own * 16
            piece = parts[d][e * 16 : (e + 1) * 16, :]
            if columns is not None:
                piece = piece[:, columns]
            whole_ref[at16(row), :] = piece


def half_mask(shape, axis, core):
    return (lax.broadcasted_iota(jnp.int32, shape, axis) // HEAD) == core


def attend_rows(q_ref, kv_ref, bias_ref, out_ref):
    rows, keys = bias_ref.shape
    chunk = rows // 2

    def step(i, carry):
        p, r = i // 2, i % 2
        here = pl.ds(pl.multiple_of(r * chunk, chunk), chunk)
        q = q_ref[here, at128(p * PAIR)]
        first = half_mask((chunk, PAIR), 1, 0)
        both = jnp.concatenate(
            (jnp.where(first, q, jnp.zeros_like(q)), jnp.where(first, jnp.zeros_like(q), q)), axis=0
        )
        bias = bias_ref[here, :]
        s = dot_nt(both, kv_ref[:, at128(p * PAIR)]) + jnp.concatenate((bias, bias), axis=0)
        top = jnp.max(s, axis=1, keepdims=True)
        w = jnp.exp(s - top)
        total = jnp.sum(w, axis=1, keepdims=True)
        mixed = dot_nn(w.astype(low_t), kv_ref[:, at128(D + p * PAIR)]) / total
        out_ref[here, at128(p * PAIR)] = jnp.where(first, mixed[:chunk], mixed[chunk:]).astype(low_t)
        return carry

    lax.fori_loop(0, 2 * PAIRS, step, 0)


def project_pairs(parts, weight, kv_ref):
    rows = parts[0].shape[0]
    for d in range(8):
        kv_ref[d * rows : (d + 1) * rows, :] = dot_nn(parts[d][...], weight).astype(low_t)


def self_forward(ids, hidden, *refs):
    stream, slices = refs[:8], refs[8:16]
    code, low_row, high_row, out, w1, q_ref, kv_ref, bias_ref = refs[16:]
    rows = hidden.shape[0]
    assemble(ids, slices, w1)
    q_ref[...] = (dot_nn(hidden[...], w1[:, :D]).astype(low_t) * 0.125).astype(low_t)
    project_pairs(stream, w1[:, D:], kv_ref)
    k = code[...]
    seen = (k >= low_row[...]) & (k < high_row[...])
    bias_ref[...] = jnp.where(seen, 0.0, neg_fill)
    own = lax.broadcasted_iota(jnp.int32, (rows, rows), 0) == lax.broadcasted_iota(
        jnp.int32, (rows, rows), 1
    )
    bias_ref[:, :rows] = jnp.where(own, 0.0, bias_ref[:, :rows])
    attend_rows(q_ref, kv_ref, bias_ref, out)


def layer_norm(values, gain_row, shift_row):
    mean = jnp.mean(values, axis=1, keepdims=True)
    centred = values - mean
    scale = lax.rsqrt(jnp.mean(centred * centred, axis=1, keepdims=True) + layer_eps)
    normed = centred * scale
    return normed * gain_row + shift_row, normed, scale


def layer_norm_back(grad, normed, scale, gain_row):
    gain_term = jnp.sum(grad * normed, axis=0, keepdims=True)
    shift_term = jnp.sum(grad, axis=0, keepdims=True)
    scaled = grad * gain_row
    grad_in = scale * (
        scaled
        - jnp.mean(scaled, axis=1, keepdims=True)
        - normed * jnp.mean(scaled * normed, axis=1, keepdims=True)
    )
    return grad_in, gain_term, shift_term


def deal_pairs(ids, value, out):
    chip = ids[0] // 2
    for p in range(PAIRS):
        out[chip ^ p] = value[:, p * PAIR : (p + 1) * PAIR]


def cross_forward(ids, hidden, self_low, *refs):
    source, slices, norms = refs[:8], refs[8:16], refs[16:20]
    code, seq_col, first, normed, scale_out, first_low, cross_low, dealt, w2, gs = refs[20:30]
    q_ref, kv_ref, bias_ref = refs[30:]
    assemble(ids, slices, w2)
    for e in range(4):
        gs[:, at128((ids[1] ^ e) * 128)] = norms[e][...]
    gain, shift = gs[0:1, :].astype(wide_t), gs[3:4, :].astype(wide_t)
    value, n0, s0 = layer_norm(
        hidden[...].astype(wide_t) + dot_nn(self_low[...], w2[:, :D]), gain, shift
    )
    first[...] = value
    normed[...] = n0
    scale_out[...] = jnp.broadcast_to(s0, scale_out.shape)
    low = value.astype(low_t)
    first_low[...] = low
    q = dot_nn(low, w2[:, D : 2 * D]).astype(low_t)
    deal_pairs(ids, q, dealt)
    q_ref[...] = (q * 0.125).astype(low_t)
    project_pairs(source, w2[:, 2 * D : 4 * D], kv_ref)
    bias_ref[...] = jnp.where(code[...] == seq_col[...], 0.0, neg_fill)
    attend_rows(q_ref, kv_ref, bias_ref, cross_low)


def feed_forward(ids, first, cross_low, w_cross, gs, cotangent, *refs):
    slices = refs[:8]
    (result, dealt, second_grad, second_low, activated, pre_grad, branch, cross_branch, sums) = refs[8:17]
    win, wout, slope = refs[17:]
    rows = first.shape[0]
    me, mw = ids[0], ids[1]
    for d in range(8):
        own = me ^ d
        for e in range(4):
            w = mw ^ e
            here = pl.ds(e * 16, 16)
            win[at16(w * 128 + own * 16), :] = slices[d][here, :FF]
            for g in range(4):
                wout[at16(w * 512 + own * 64 + g * 16), :] = slices[d][
                    here, FF + g * D : FF + (g + 1) * D
                ]
    gains, shifts = gs[0:3, :].astype(wide_t), gs[3:6, :].astype(wide_t)
    second, n1, s1 = layer_norm(
        first[...] + dot_nn(cross_low[...], w_cross[...]), gains[1:2], shifts[1:2]
    )
    low = second.astype(low_t)
    second_low[...] = low
    width = 512
    total = second
    for c in range(FF // width):
        cols = slice(c * width, (c + 1) * width)
        pre = dot_nn(low, win[:, cols])
        sig = 1.0 / (1.0 + jnp.exp(-pre))
        act = (pre * sig).astype(low_t)
        activated[:, cols] = act
        slope[:, cols] = sig * (1.0 + pre * (1.0 - sig))
        total = total + dot_nn(act, wout[cols, :])
    value, n2, s2 = layer_norm(total, gains[2:3], shifts[2:3])
    result[...] = value.astype(low_t)
    third, gain_c, shift_c = layer_norm_back(cotangent[...].astype(wide_t), n2, s2, gains[2:3])
    third_low = third.astype(low_t)
    branch[...] = third_low
    total = third
    for c in range(FF // width):
        cols = slice(c * width, (c + 1) * width)
        back = (dot_nt(third_low, wout[cols, :]) * slope[:, cols]).astype(low_t)
        pre_grad[:, cols] = back
        total = total + dot_nt(back, win[:, cols])
    grad, gain_b, shift_b = layer_norm_back(total, n1, s1, gains[1:2])
    second_grad[...] = grad
    grad_low = grad.astype(low_t)
    cross_branch[...] = grad_low
    deal_pairs(ids, dot_nt(grad_low, w_cross[...]).astype(low_t), dealt)
    zero = jnp.zeros_like(gain_b)
    sums[...] = jnp.concatenate(
        (zero, gain_b, gain_c, zero, shift_b, shift_c, zero, zero), axis=0
    )


def put_pieces(ids, value_ref, depth, keep, send, column):
    me, mw = ids[0], ids[1]
    width = value_ref.shape[1]
    for d in range(8):
        own = me ^ d
        out = send if d % 2 else keep
        for e in range(4):
            w = mw ^ e
            for g in range(depth):
                row = (w * 8 + own) * (16 * depth) + g * 16
                out[d // 2, e * 16 : (e + 1) * 16, column + g * width : column + (g + 1) * width] = (
                    value_ref[at16(row), :]
                )


def weight_grads(depths, ids, *refs):
    n = len(depths)
    lefts, rights = refs[:n], refs[n : 2 * n]
    keep, send = refs[2 * n : 2 * n + 2]
    column = 0
    for left, right, depth, scratch in zip(lefts, rights, depths, refs[2 * n + 2 :]):
        scratch[...] = dot_tn(left[...], right[...]).astype(low_t)
        put_pieces(ids, scratch, depth, keep, send, column)
        column += depth * right.shape[1]


def pair_back(is_self, ids, *refs):
    at = 0

    def take(n):
        nonlocal at
        at += n
        return refs[at - n : at]

    q_parts, do_parts, x_parts = take(8), take(8), take(8)
    if is_self:
        (w_query,) = take(1)
    w_pair, code, low_rows, high_rows = take(4)
    dq_keep, dq_send, dkv_keep, dkv_send, w_keep, w_send = take(6)
    q_all, do_all, k_all, v_all, kt, dq_t, dq_all, dk, dv, s_ref, grads = take(11)
    me, mw = ids[0], ids[1]
    pair, core = me // 2, me % 2
    rows = do_parts[0].shape[0]
    keys = 8 * rows
    mine = half_mask((rows, PAIR), 1, core)
    nothing = jnp.zeros((rows, PAIR), low_t)
    if is_self:
        wq = w_query[:, at128(pair * PAIR)]
    wk, wv = w_pair[:, at128(pair * PAIR)], w_pair[:, at128(D + pair * PAIR)]
    for d in range(8):
        here = slice(d * rows, (d + 1) * rows)
        x = x_parts[d][...]
        k_all[here, :] = dot_nn(x, wk).astype(low_t)
        v_all[here, :] = dot_nn(x, wv).astype(low_t)
        q = dot_nn(q_parts[d][...], wq).astype(low_t) if is_self else q_parts[d][...]
        q_all[d] = (jnp.where(mine, q, nothing) * 0.125).astype(low_t)
        do_all[d] = jnp.where(mine, do_parts[d][...], nothing)
    kt[...] = k_all[...].astype(wide_t).T.astype(low_t)
    dk[...] = jnp.zeros_like(dk)
    dv[...] = jnp.zeros_like(dv)

    def step(b, carry):
        q, do = q_all[b], do_all[b]
        c = jnp.concatenate((code[...],) * (rows // 128), axis=1)
        low_row = low_rows[pl.ds(b, 1), :]
        s = dot_nt(k_all[...], q)
        if is_self:
            s_ref[...] = jnp.where((c >= low_row) & (c < high_rows[pl.ds(b, 1), :]), s, neg_fill)
            block = pl.ds(pl.multiple_of(b * rows, rows), rows)
            own = lax.broadcasted_iota(jnp.int32, (rows, rows), 0) == lax.broadcasted_iota(
                jnp.int32, (rows, rows), 1
            )
            s_ref[block, :] = jnp.where(own, dot_nt(k_all[block, :], q), s_ref[block, :])
        else:
            s_ref[...] = jnp.where(c == low_row, s, neg_fill)
        s = s_ref[...]
        w = jnp.exp(s - jnp.max(s, axis=0, keepdims=True))
        inverse = 1.0 / jnp.sum(w, axis=0, keepdims=True)
        dp = dot_nt(v_all[...], do)
        offset = jnp.sum(w * dp, axis=0, keepdims=True) * inverse
        probs = w * inverse
        dv[...] += dot_nn(probs.astype(low_t), do)
        ds = (probs * (dp - offset)).astype(low_t)
        dk[...] += dot_nn(ds, q)
        dqt = dot_nn(kt[...], ds) * 0.125
        dqt = jnp.where(half_mask((PAIR, rows), 0, core), dqt, 0.0)
        dq_t[b] = dqt.astype(low_t)
        dq_all[b] = dqt.T.astype(low_t)
        return carry

    lax.fori_loop(0, 8, step, 0)
    total_q = jnp.zeros((PAIR, D), wide_t)
    total_k, total_v = total_q, total_q
    for d in range(8):
        here = slice(d * rows, (d + 1) * rows)
        dk_low, dv_low = dk[here, :].astype(low_t), dv[here, :].astype(low_t)
        (dq_send if d % 2 else dq_keep)[d // 2] = dq_all[d]
        out = dkv_send if d % 2 else dkv_keep
        out[d // 2, :, :PAIR] = dk_low
        out[d // 2, :, PAIR:] = dv_low
        x = x_parts[d][...]
        total_k += dot_tn(dk_low, x)
        total_v += dot_tn(dv_low, x)
        if is_self:
            total_q += dot_nn(dq_t[d], q_parts[d][...])
    totals = (total_q, total_k, total_v) if is_self else (total_k, total_v)
    for n, value in enumerate(totals):
        grads[:, n * PAIR : (n + 1) * PAIR] = value.T.astype(low_t)
    for e in range(4):
        row = (mw ^ e) * 128
        w_keep[e * 64 : (e + 1) * 64, :] = grads[at16(row + core * 64, 64), :]
        w_send[e * 64 : (e + 1) * 64, :] = grads[at16(row + (1 - core) * 64, 64), :]


def gather_pairs(ids, parts, column, out):
    chip = ids[0] // 2
    for k in range(PAIRS):
        out[:, at128((chip ^ k) * PAIR)] = parts[k][:, column : column + PAIR]


def first_back(ids, *refs):
    parts = refs[:4]
    second_grad, normed, scale, gs, w_cross_query, w_output, sums_in = refs[4:11]
    first_grad, branch, dealt, dq, sums = refs[11:]
    gather_pairs(ids, parts, 0, dq)
    total = second_grad[...] + dot_nt(dq[...], w_cross_query[...])
    grad, gain_a, shift_a = layer_norm_back(
        total, normed[...], scale[:, 0:1], gs[0:1, :].astype(wide_t)
    )
    first_grad[...] = grad
    low = grad.astype(low_t)
    branch[...] = low
    deal_pairs(ids, dot_nt(low, w_output[...]).astype(low_t), dealt)
    zero = jnp.zeros_like(gain_a)
    sums[...] = sums_in[...] + jnp.concatenate(
        (gain_a, zero, zero, shift_a, zero, zero, zero, zero), axis=0
    )


def source_back(ids, *refs):
    parts, w_pair, out, dkv = refs[:4], refs[4], refs[5], refs[6]
    gather_pairs(ids, parts, 0, dkv.at[:, :D])
    gather_pairs(ids, parts, PAIR, dkv.at[:, D:])
    out[...] = dot_nt(dkv[...], w_pair[...])


def hidden_back(ids, *refs):
    parts, first_grad, w_query, out, dq = refs[:4], refs[4], refs[5], refs[6], refs[7]
    gather_pairs(ids, parts, 0, dq)
    out[...] = first_grad[...] + dot_nt(dq[...], w_query[...])


def add_split(ids, keep, received, *outs):
    for k in range(4):
        outs[k][...] = (keep[k].astype(wide_t) + received[k].astype(wide_t)).astype(low_t)


def add_rows(ids, *refs):
    parts, outs = refs[:-4], refs[-4:]
    size = outs[0].shape[0]
    for e in range(4):
        total = parts[0][e * size : (e + 1) * size, :].astype(wide_t)
        for part in parts[1:]:
            total = total + part[e * size : (e + 1) * size, :].astype(wide_t)
        outs[e][...] = total.astype(low_t)


def add_all(ids, *refs):
    total = refs[0][...].astype(wide_t)
    for part in refs[1:-1]:
        total = total + part[...].astype(wide_t)
    refs[-1][...] = total.astype(low_t)


def place_rows(depths, ids, *refs):
    parts, outs = refs[:8], refs[8:]
    for d in range(8):
        own = ids[0] ^ d
        column = 0
        for depth, out in zip(depths, outs):
            width = out.shape[1]
            for g in range(depth):
                out[at16((own * depth + g) * 16), :] = parts[d][
                    :, column + g * width : column + (g + 1) * width
                ].astype(wide_t)
            column += depth * width


def place_pairs(ids, *refs):
    parts, outs = refs[:8], refs[8:]
    for d in range(8):
        own = ids[0] ^ d
        pair, rows = own // 2, at16((own % 2) * 64, 64)
        column = 0
        for out in outs:
            for start in range(0, out.shape[1], D):
                out[rows, at128(start + pair * PAIR)] = parts[d][:, column : column + PAIR].astype(
                    wide_t
                )
                column += PAIR


def swap(value, axis, bits):
    size = lax.axis_size(axis)
    return lax.ppermute(value, axis, [(i, i ^ bits) for i in range(size)])


def gather_ctx(value):
    parts = [value, None] + [swap(value, "ctx", d) if d % 2 == 0 else None for d in range(2, 8)]
    for d in range(1, 8, 2):
        parts[d] = swap(parts[d - 1], "ctx", 1)
    return parts


def gather_wa(value):
    return [value] + [swap(value, "wa", e) for e in range(1, 4)]


def exchange_pairs(dealt):
    parts = [None] * 8
    for k in range(4):
        parts[2 * k] = dealt[k] if k == 0 else swap(dealt[k], "ctx", 2 * k)
    for k in range(4):
        parts[2 * k + 1] = swap(parts[2 * k], "ctx", 1)
    return parts


def return_pairs(ids, keep, send):
    received = swap(send, "ctx", 1)
    shape = keep.shape[1:]
    sums = run(add_split, [(shape, low_t)] * 4, ids, [keep, received])
    return [sums[0]] + [swap(sums[k], "ctx", 2 * k) for k in range(1, 4)]


def reduce_wa(ids, parts):
    rows, width = parts[0].shape
    size = rows // 4
    split = run(add_rows, [((size, width), low_t)] * 4, ids, parts)
    moved = [split[0]] + [swap(split[e], "wa", e) for e in range(1, 4)]
    (total,) = run(add_all, [((size, width), low_t)], ids, moved)
    return gather_ctx(total)


def reduce_slices(ids, keep, send):
    return reduce_wa(ids, return_pairs(ids, keep, send))


def reduce_halves(ids, keep, send):
    return reduce_wa(ids, [keep, swap(send, "ctx", 1)])


def fast_shards(
    hidden,
    stream,
    encoder,
    lengths,
    order,
    ranks,
    thresholds,
    self_query,
    self_key_value,
    self_output,
    cross_query,
    cross_key_value,
    cross_output,
    ffn_in,
    ffn_out,
    norm_gain,
    norm_shift,
    cotangent,
):
    rows, keys = hidden.shape[1], order.shape[1]
    me, mw = lax.axis_index("ctx"), lax.axis_index("wa")
    ids = jnp.stack((me, mw)).astype(jnp.int32)
    inputs, stream_rows, source_rows = hidden[0], stream[0], encoder[0]

    def row_slice(weight):
        return lax.dynamic_slice_in_dim(weight, me * (weight.shape[0] // 8), weight.shape[0] // 8, 0)

    out_slice = row_slice(ffn_out)
    pack1 = jnp.concatenate((row_slice(self_query), row_slice(self_key_value)), axis=1)
    pack2 = jnp.concatenate(
        [row_slice(w) for w in (self_output, cross_query, cross_key_value, cross_output)], axis=1
    )
    pack3 = jnp.concatenate(
        [row_slice(ffn_in)] + [out_slice[g * 16 : (g + 1) * 16] for g in range(4)], axis=1
    )
    norm_pack = jnp.concatenate(
        (norm_gain, norm_shift, jnp.zeros((10, norm_gain.shape[1]), low_t)), axis=0
    )

    def gather_weights(pack):
        return gather_ctx(jnp.concatenate(gather_wa(pack), axis=0))

    stream_parts = gather_ctx(stream_rows)
    slices1 = gather_weights(pack1)
    norms = gather_wa(norm_pack)
    slices2 = gather_weights(pack2)
    source_parts = gather_ctx(source_rows)
    slices3 = gather_weights(pack3)
    hidden_parts = gather_ctx(inputs)

    seq_ends = jnp.cumsum(lengths[0])
    token_seq = sequence_ids(order[0], seq_ends)
    source_seq = sequence_ids(jnp.arange(keys, dtype=jnp.int32), seq_ends)

    def by_device(vector):
        blocks = vector.reshape(8, rows)
        return jnp.concatenate(
            [lax.dynamic_slice_in_dim(blocks, me ^ d, 1, 0) for d in range(8)], axis=0
        )

    token_rows, source_blocks = by_device(token_seq), by_device(source_seq)
    low_rows = token_rows * 1024
    high_rows = low_rows + by_device(thresholds[0])
    code_rows = low_rows + by_device(ranks[0])
    code_wide = jnp.broadcast_to(code_rows.reshape(keys, 1), (keys, 128))
    source_wide = jnp.broadcast_to(source_blocks.reshape(keys, 1), (keys, 128))

    score_flops = 2 * rows * keys * D
    self_low, w1 = run(
        self_forward,
        [((rows, D), low_t), ((D, 3 * D), low_t)],
        ids,
        [inputs, *stream_parts, *slices1]
        + [code_rows.reshape(1, keys), low_rows[0].reshape(rows, 1), high_rows[0].reshape(rows, 1)],
        [((rows, D), low_t), ((keys, 2 * D), low_t), ((rows, keys), wide_t)],
        flops=8 * score_flops,
    )
    first, normed, scale, first_low, cross_low, cross_dealt, w2, gs = run(
        cross_forward,
        [
            ((rows, D), wide_t),
            ((rows, D), wide_t),
            ((rows, 128), wide_t),
            ((rows, D), low_t),
            ((rows, D), low_t),
            ((PAIRS, rows, PAIR), low_t),
            ((D, 5 * D), low_t),
            ((16, D), low_t),
        ],
        ids,
        [inputs, self_low, *source_parts, *slices2, *norms]
        + [source_blocks.reshape(1, keys), token_rows[0].reshape(rows, 1)],
        [((rows, D), low_t), ((keys, 2 * D), low_t), ((rows, keys), wide_t)],
        flops=8 * score_flops,
    )
    w_output, w_cross_query = w2[:, :D], w2[:, D : 2 * D]
    w_cross_pair, w_cross_output = w2[:, 2 * D : 4 * D], w2[:, 4 * D :]
    w_query, w_pair = w1[:, :D], w1[:, D:]
    cross_q_parts = exchange_pairs(cross_dealt)
    (
        result,
        cross_do_dealt,
        second_grad,
        second_low,
        activated,
        pre_grad,
        branch,
        cross_branch,
        sums,
    ) = run(
        feed_forward,
        [
            ((rows, D), low_t),
            ((PAIRS, rows, PAIR), low_t),
            ((rows, D), wide_t),
            ((rows, D), low_t),
            ((rows, FF), low_t),
            ((rows, FF), low_t),
            ((rows, D), low_t),
            ((rows, D), low_t),
            ((8, D), wide_t),
        ],
        ids,
        [first, cross_low, w_cross_output, gs, cotangent[0], *slices3],
        [((D, FF), low_t), ((FF, D), low_t), ((rows, FF), wide_t)],
        flops=2 * rows * D * (4 * FF + 2 * D),
    )
    cross_do_parts = exchange_pairs(cross_do_dealt)

    def grads_of(depths, lefts, rights):
        width = sum(depth * right.shape[1] for depth, right in zip(depths, rights))
        return run(
            functools.partial(weight_grads, depths),
            [((4, 64, width), low_t)] * 2,
            ids,
            [*lefts, *rights],
            [((left.shape[1], right.shape[1]), low_t) for left, right in zip(lefts, rights)],
            flops=sum(2 * rows * a.shape[1] * b.shape[1] for a, b in zip(lefts, rights)),
        )

    keep_a, send_a = grads_of(
        (1, 4, 1), (second_low, activated, cross_low), (pre_grad, branch, cross_branch)
    )
    parts_a = reduce_slices(ids, keep_a, send_a)

    def back_of(is_self, q_parts, do_parts, x_parts, weights, code, low_limits, high_limits):
        width = (3 if is_self else 2) * PAIR
        return run(
            functools.partial(pair_back, is_self),
            [((4, rows, PAIR), low_t)] * 2
            + [((4, rows, 2 * PAIR), low_t)] * 2
            + [((256, width), low_t)] * 2,
            ids,
            [*q_parts, *do_parts, *x_parts, *weights, code, low_limits, high_limits],
            [((8, rows, PAIR), low_t)] * 2
            + [((keys, PAIR), low_t)] * 2
            + [((PAIR, keys), low_t), ((8, PAIR, rows), low_t), ((8, rows, PAIR), low_t)]
            + [((keys, PAIR), wide_t)] * 2
            + [((keys, rows), wide_t), ((D, width), low_t)],
            flops=16 * score_flops,
        )

    cq_keep, cq_send, ckv_keep, ckv_send, cw_keep, cw_send = back_of(
        False,
        cross_q_parts,
        cross_do_parts,
        source_parts,
        [w_cross_pair],
        source_wide,
        token_rows,
        token_rows,
    )
    cross_dq_parts = return_pairs(ids, cq_keep, cq_send)
    first_grad, self_branch, self_dealt, cross_dq, sums = run(
        first_back,
        [
            ((rows, D), wide_t),
            ((rows, D), low_t),
            ((PAIRS, rows, PAIR), low_t),
            ((rows, D), low_t),
            ((8, D), wide_t),
        ],
        ids,
        [*cross_dq_parts, second_grad, normed, scale, gs, w_cross_query, w_output, sums],
        flops=4 * rows * D * D,
    )
    self_do_parts = exchange_pairs(self_dealt)
    keep_b, send_b = grads_of((1, 1), (first_low, self_low), (cross_dq, self_branch))
    cross_dkv_parts = return_pairs(ids, ckv_keep, ckv_send)
    (source_grad,) = run(
        source_back,
        [((rows, D), wide_t)],
        ids,
        [*cross_dkv_parts, w_cross_pair],
        [((rows, 2 * D), low_t)],
        flops=4 * rows * D * D,
    )
    parts_b = reduce_slices(ids, keep_b, send_b)
    parts_c = reduce_halves(ids, cw_keep, cw_send)
    for bits in (1, 2, 4):
        sums = sums + swap(sums, "ctx", bits)
    for bits in (1, 2):
        sums = sums + swap(sums, "wa", bits)
    norm_sums = lax.dynamic_slice_in_dim(sums, mw * 128, 128, 1)

    q_keep, q_send, kv_keep, kv_send, w_keep, w_send = back_of(
        True,
        hidden_parts,
        self_do_parts,
        stream_parts,
        [w_query, w_pair],
        code_wide,
        low_rows,
        high_rows,
    )
    parts_d = reduce_halves(ids, w_keep, w_send)
    dq_parts = return_pairs(ids, q_keep, q_send)
    (hidden_grad,) = run(
        hidden_back,
        [((rows, D), wide_t)],
        ids,
        [*dq_parts, first_grad, w_query],
        [((rows, D), low_t)],
        flops=2 * rows * D * D,
    )
    dkv_parts = return_pairs(ids, kv_keep, kv_send)
    (stream_grad,) = run(
        source_back,
        [((rows, D), wide_t)],
        ids,
        [*dkv_parts, w_pair],
        [((rows, 2 * D), low_t)],
        flops=4 * rows * D * D,
    )

    grad_in, grad_out, grad_cross_output = run(
        functools.partial(place_rows, (1, 4, 1)),
        [((128, FF), wide_t), ((D, D), wide_t), ((128, D), wide_t)],
        ids,
        parts_a,
    )
    grad_cross_query, grad_output = run(
        functools.partial(place_rows, (1, 1)), [((128, D), wide_t)] * 2, ids, parts_b
    )
    (grad_cross_pair,) = run(place_pairs, [((128, 2 * D), wide_t)], ids, parts_c)
    grad_query, grad_pair = run(
        place_pairs, [((128, D), wide_t), ((128, 2 * D), wide_t)], ids, parts_d
    )
    return (
        result[None],
        hidden_grad[None],
        stream_grad[None],
        source_grad[None],
        grad_query,
        grad_pair,
        grad_output,
        grad_cross_query,
        grad_cross_pair,
        grad_cross_output,
        grad_in,
        grad_out,
        norm_sums[0:3],
        norm_sums[3:6],
    )


def solution(mesh):
    in_specs = (
        P("wa", "ctx", None),
        P("wa", "ctx", None),
        P("wa", "ctx", None),
        P("wa", None),
        P("wa", None),
        P("wa", None),
        P("wa", None),
        P("wa", None),
        P("wa", None),
        P("wa", None),
        P("wa", None),
        P("wa", None),
        P("wa", None),
        P("wa", None),
        P("wa", None),
        P(None, "wa"),
        P(None, "wa"),
        P("wa", "ctx", None),
    )
    out_specs = (
        P("wa", "ctx", None),
        P("wa", "ctx", None),
        P("wa", "ctx", None),
        P("wa", "ctx", None),
        P("wa", None),
        P("wa", None),
        P("wa", None),
        P("wa", None),
        P("wa", None),
        P("wa", None),
        P("wa", None),
        P("wa", None),
        P(None, "wa"),
        P(None, "wa"),
    )
    fast = mesh.shape["ctx"] == HEADS and mesh.shape["wa"] == 4
    body = fast_shards if fast else general_shards
    return jax.shard_map(body, mesh=mesh, in_specs=in_specs, out_specs=out_specs, check_vma=False)
```

```python
import functools

import jax
import jax.numpy as jnp
from jax import lax
from jax.experimental import pallas as pl
from jax.experimental.pallas import tpu as pltpu
from jax.sharding import Mesh
from jax.sharding import PartitionSpec as P

D = 512
HEADS = 8
HEAD = 64
KEYBLK = 1024


layer_eps = 1e-05
neg_fill = -1e30


def sequence_ids(positions, seq_ends):
    return jnp.sum((positions[:, None] >= seq_ends[None, :]).astype(jnp.int32), axis=1)


def head_split(matrix):
    return matrix.reshape(matrix.shape[0], HEADS, HEAD)


def block_scores(query_heads, key_heads):
    raw_scores = jnp.einsum(
        "lhd,khd->hlk", query_heads, key_heads, preferred_element_type=jnp.float32
    )
    return raw_scores * float(HEAD) ** (-0.5)


def softmax_totals(queries, key_rows, allowed_fn):
    query_heads = head_split(queries)
    count_rows = queries.shape[0]

    def visit(state_pair, block_index):
        running_top, running_sum = state_pair
        block_start = block_index * KEYBLK
        key_piece = lax.dynamic_slice_in_dim(key_rows, block_start, KEYBLK, 0)
        allowed = allowed_fn(block_start)[None]
        scores = jnp.where(
            allowed, block_scores(query_heads, head_split(key_piece[:, :D])), neg_fill
        )
        new_top = jnp.maximum(running_top, jnp.max(scores, axis=2))
        weights = jnp.where(allowed, jnp.exp(scores - new_top[:, :, None]), 0.0)
        running_sum = running_sum * jnp.exp(running_top - new_top) + jnp.sum(weights, axis=2)
        return ((new_top, running_sum), None)

    initial = (
        jnp.full((HEADS, count_rows), neg_fill, jnp.float32),
        jnp.zeros((HEADS, count_rows), jnp.float32),
    )
    (final_top, final_sum), unused = lax.scan(
        visit, initial, jnp.arange(key_rows.shape[0] // KEYBLK)
    )
    return final_top + jnp.log(final_sum)


def attend_values(queries, key_rows, log_totals, allowed_fn):
    query_heads = head_split(queries)

    def visit(running, block_index):
        block_start = block_index * KEYBLK
        key_piece = lax.dynamic_slice_in_dim(key_rows, block_start, KEYBLK, 0)
        allowed = allowed_fn(block_start)[None]
        scores = block_scores(query_heads, head_split(key_piece[:, :D]))
        weights = jnp.where(allowed, jnp.exp(scores - log_totals[:, :, None]), 0.0)
        value_heads = head_split(key_piece[:, D:])
        return (
            running
            + jnp.einsum(
                "hlk,khd->lhd",
                weights.astype(jnp.bfloat16),
                value_heads,
                preferred_element_type=jnp.float32,
            ),
            None,
        )

    mixed, unused = lax.scan(
        visit, jnp.zeros(query_heads.shape, jnp.float32), jnp.arange(key_rows.shape[0] // KEYBLK)
    )
    return mixed.reshape(queries.shape[0], D)


def head_offsets(grad_low, attended):
    return jnp.sum(head_split(grad_low.astype(jnp.float32) * attended), axis=2).T


def attend_back(queries, key_rows, log_totals, attended, grad_low, allowed_fn):
    query_heads = head_split(queries)
    grad_heads = head_split(grad_low)
    offsets = head_offsets(grad_low, attended)
    scale_value = float(HEAD) ** (-0.5)

    def visit(query_grad, block_index):
        block_start = block_index * KEYBLK
        key_piece = lax.dynamic_slice_in_dim(key_rows, block_start, KEYBLK, 0)
        allowed = allowed_fn(block_start)[None]
        key_heads = head_split(key_piece[:, :D])
        value_heads = head_split(key_piece[:, D:])
        weights = jnp.where(
            allowed, jnp.exp(block_scores(query_heads, key_heads) - log_totals[:, :, None]), 0.0
        )
        value_grad = jnp.einsum(
            "hlk,lhd->khd",
            weights.astype(jnp.bfloat16),
            grad_heads,
            preferred_element_type=jnp.float32,
        )
        weight_grad = jnp.einsum(
            "lhd,khd->hlk", grad_heads, value_heads, preferred_element_type=jnp.float32
        )
        score_grad = (weights * (weight_grad - offsets[:, :, None]) * scale_value).astype(
            jnp.bfloat16
        )
        query_grad = query_grad + jnp.einsum(
            "hlk,khd->lhd", score_grad, key_heads, preferred_element_type=jnp.float32
        )
        key_grad = jnp.einsum(
            "hlk,lhd->khd", score_grad, query_heads, preferred_element_type=jnp.float32
        )
        return (
            query_grad,
            jnp.concatenate((key_grad.reshape(KEYBLK, D), value_grad.reshape(KEYBLK, D)), axis=1),
        )

    query_grad, grad_pieces = lax.scan(
        visit, jnp.zeros(query_heads.shape, jnp.float32), jnp.arange(key_rows.shape[0] // KEYBLK)
    )
    return (query_grad.reshape(queries.shape[0], D), grad_pieces.reshape(key_rows.shape[0], 2 * D))


def normalize(values, gain_row, shift_row):
    row_mean = jnp.mean(values, axis=1, keepdims=True)
    centred = values - row_mean
    scale_inv = lax.rsqrt(jnp.mean(centred * centred, axis=1, keepdims=True) + layer_eps)
    normed = centred * scale_inv
    return (normed * gain_row + shift_row, normed, scale_inv)


def normalize_back(grad_out, normed, scale_inv, gain_row):
    gain_term = jnp.sum(grad_out * normed, axis=0)
    shift_term = jnp.sum(grad_out, axis=0)
    scaled = grad_out * gain_row
    grad_in = scale_inv * (
        scaled
        - jnp.mean(scaled, axis=1, keepdims=True)
        - normed * jnp.mean(scaled * normed, axis=1, keepdims=True)
    )
    return (grad_in, gain_term, shift_term)


def matmul(left, right):
    return jnp.dot(left, right, preferred_element_type=jnp.float32)


def general_shards(
    hidden,
    stream,
    encoder,
    lengths,
    order,
    ranks,
    thresholds,
    self_query,
    self_key_value,
    self_output,
    cross_query,
    cross_key_value,
    cross_output,
    ffn_in,
    ffn_out,
    norm_gain,
    norm_shift,
    cotangent,
):
    (
        full_query,
        full_pair,
        full_output,
        full_cross_query,
        full_cross_pair,
        full_cross_output,
        full_in,
        full_out,
        gain_rows,
        shift_rows,
    ) = (
        lax.all_gather(self_query, "wa", axis=0, tiled=True),
        lax.all_gather(self_key_value, "wa", axis=0, tiled=True),
        lax.all_gather(self_output, "wa", axis=0, tiled=True),
        lax.all_gather(cross_query, "wa", axis=0, tiled=True),
        lax.all_gather(cross_key_value, "wa", axis=0, tiled=True),
        lax.all_gather(cross_output, "wa", axis=0, tiled=True),
        lax.all_gather(ffn_in, "wa", axis=0, tiled=True),
        lax.all_gather(ffn_out, "wa", axis=0, tiled=True),
        lax.all_gather(norm_gain, "wa", axis=1, tiled=True),
        lax.all_gather(norm_shift, "wa", axis=1, tiled=True),
    )
    gains = gain_rows.astype(jnp.float32)
    shifts = shift_rows.astype(jnp.float32)
    local_rows = hidden.shape[1]
    total_rows = order.shape[1]
    row_start = lax.axis_index("ctx") * local_rows
    seq_ends = jnp.cumsum(lengths[0])
    token_seq = sequence_ids(order[0], seq_ends)
    source_seq = sequence_ids(jnp.arange(total_rows, dtype=jnp.int32), seq_ends)
    query_seq = lax.dynamic_slice_in_dim(token_seq, row_start, local_rows)
    query_rows = row_start + jnp.arange(local_rows, dtype=jnp.int32)
    all_limits = thresholds[0]
    limits = lax.dynamic_slice_in_dim(all_limits, row_start, local_rows)
    key_ranks = ranks[0]

    def self_allowed(block_start):
        block_seq = lax.dynamic_slice_in_dim(token_seq, block_start, KEYBLK)
        block_rank = lax.dynamic_slice_in_dim(key_ranks, block_start, KEYBLK)
        block_rows = block_start + jnp.arange(KEYBLK, dtype=jnp.int32)
        return (query_seq[:, None] == block_seq[None, :]) & (
            (block_rank[None, :] < limits[:, None]) | (query_rows[:, None] == block_rows[None, :])
        )

    def cross_allowed(block_start):
        return (
            query_seq[:, None] == lax.dynamic_slice_in_dim(source_seq, block_start, KEYBLK)[None, :]
        )

    inputs = hidden[0]
    stream_rows = stream[0]
    source_rows = encoder[0]
    queries = matmul(inputs, full_query).astype(jnp.bfloat16)
    self_local = matmul(stream_rows, full_pair).astype(jnp.bfloat16)
    cross_local = matmul(source_rows, full_cross_pair).astype(jnp.bfloat16)
    self_keys, cross_keys = (
        lax.all_gather(self_local, "ctx", axis=0, tiled=True),
        lax.all_gather(cross_local, "ctx", axis=0, tiled=True),
    )
    self_totals = softmax_totals(queries, self_keys, self_allowed)
    self_mixed = attend_values(queries, self_keys, self_totals, self_allowed)
    self_low = self_mixed.astype(jnp.bfloat16)
    first, first_normed, first_scale = normalize(
        inputs.astype(jnp.float32) + matmul(self_low, full_output), gains[0], shifts[0]
    )
    first_low = first.astype(jnp.bfloat16)
    cross_queries = matmul(first_low, full_cross_query).astype(jnp.bfloat16)
    cross_totals = softmax_totals(cross_queries, cross_keys, cross_allowed)
    cross_mixed = attend_values(cross_queries, cross_keys, cross_totals, cross_allowed)
    cross_low = cross_mixed.astype(jnp.bfloat16)
    second, second_normed, second_scale = normalize(
        first + matmul(cross_low, full_cross_output), gains[1], shifts[1]
    )
    second_low = second.astype(jnp.bfloat16)
    hidden_pre = matmul(second_low, full_in)
    sigmoid_pre = jax.nn.sigmoid(hidden_pre)
    activated = (hidden_pre * sigmoid_pre).astype(jnp.bfloat16)
    result, third_normed, third_scale = normalize(
        second + matmul(activated, full_out), gains[2], shifts[2]
    )
    third_grad, gain_grad_c, shift_grad_c = normalize_back(
        cotangent[0].astype(jnp.float32), third_normed, third_scale, gains[2]
    )
    branch_grad = third_grad.astype(jnp.bfloat16)
    grad_ffn_out = matmul(activated.T, branch_grad)
    slope = sigmoid_pre * (1.0 + hidden_pre * (1.0 - sigmoid_pre))
    pre_grad = (matmul(branch_grad, full_out.T) * slope).astype(jnp.bfloat16)
    grad_ffn_in = matmul(second_low.T, pre_grad)
    second_total = third_grad + matmul(pre_grad, full_in.T)
    second_grad, gain_grad_b, shift_grad_b = normalize_back(
        second_total, second_normed, second_scale, gains[1]
    )
    cross_branch = second_grad.astype(jnp.bfloat16)
    grad_cross_output = matmul(cross_low.T, cross_branch)
    cross_mixed_grad = matmul(cross_branch, full_cross_output.T).astype(jnp.bfloat16)
    cross_query_term, cross_terms = attend_back(
        cross_queries, cross_keys, cross_totals, cross_mixed, cross_mixed_grad, cross_allowed
    )
    cross_query_low = cross_query_term.astype(jnp.bfloat16)
    grad_cross_query = matmul(first_low.T, cross_query_low)
    first_total = second_grad + matmul(cross_query_low, full_cross_query.T)
    first_grad, gain_grad_a, shift_grad_a = normalize_back(
        first_total, first_normed, first_scale, gains[0]
    )
    self_branch = first_grad.astype(jnp.bfloat16)
    grad_self_output = matmul(self_low.T, self_branch)
    self_mixed_grad = matmul(self_branch, full_output.T).astype(jnp.bfloat16)
    self_query_term, self_terms = attend_back(
        queries, self_keys, self_totals, self_mixed, self_mixed_grad, self_allowed
    )
    self_sum, cross_sum = (
        lax.psum_scatter(self_terms, "ctx", scatter_dimension=0, tiled=True),
        lax.psum_scatter(cross_terms, "ctx", scatter_dimension=0, tiled=True),
    )
    self_query_low = self_query_term.astype(jnp.bfloat16)
    grad_self_query = matmul(inputs.T, self_query_low)
    input_grad = first_grad + matmul(self_query_low, full_query.T)
    self_sum_low = self_sum.astype(jnp.bfloat16)
    grad_self_pair = matmul(stream_rows.T, self_sum_low)
    stream_grad = matmul(self_sum_low, full_pair.T)
    cross_sum_low = cross_sum.astype(jnp.bfloat16)
    grad_cross_pair = matmul(source_rows.T, cross_sum_low)
    source_grad = matmul(cross_sum_low, full_cross_pair.T)
    gain_grads = jnp.stack((gain_grad_a, gain_grad_b, gain_grad_c))
    shift_grads = jnp.stack((shift_grad_a, shift_grad_b, shift_grad_c))
    (
        share_query,
        share_pair,
        share_output,
        share_cross_query,
        share_cross_pair,
        share_cross_output,
        share_in,
        share_out,
        share_gain,
        share_shift,
    ) = (
        lax.psum_scatter(
            grad_self_query.astype(jnp.bfloat16), "wa", scatter_dimension=0, tiled=True
        ).astype(jnp.float32),
        lax.psum_scatter(
            grad_self_pair.astype(jnp.bfloat16), "wa", scatter_dimension=0, tiled=True
        ).astype(jnp.float32),
        lax.psum_scatter(
            grad_self_output.astype(jnp.bfloat16), "wa", scatter_dimension=0, tiled=True
        ).astype(jnp.float32),
        lax.psum_scatter(
            grad_cross_query.astype(jnp.bfloat16), "wa", scatter_dimension=0, tiled=True
        ).astype(jnp.float32),
        lax.psum_scatter(
            grad_cross_pair.astype(jnp.bfloat16), "wa", scatter_dimension=0, tiled=True
        ).astype(jnp.float32),
        lax.psum_scatter(
            grad_cross_output.astype(jnp.bfloat16), "wa", scatter_dimension=0, tiled=True
        ).astype(jnp.float32),
        lax.psum_scatter(
            grad_ffn_in.astype(jnp.bfloat16), "wa", scatter_dimension=0, tiled=True
        ).astype(jnp.float32),
        lax.psum_scatter(
            grad_ffn_out.astype(jnp.bfloat16), "wa", scatter_dimension=0, tiled=True
        ).astype(jnp.float32),
        lax.psum_scatter(
            gain_grads.astype(jnp.bfloat16), "wa", scatter_dimension=1, tiled=True
        ).astype(jnp.float32),
        lax.psum_scatter(
            shift_grads.astype(jnp.bfloat16), "wa", scatter_dimension=1, tiled=True
        ).astype(jnp.float32),
    )
    (
        total_query,
        total_pair,
        total_output,
        total_cross_query,
        total_cross_pair,
        total_cross_output,
        total_in,
        total_out,
        total_gain,
        total_shift,
    ) = lax.psum(
        (
            share_query,
            share_pair,
            share_output,
            share_cross_query,
            share_cross_pair,
            share_cross_output,
            share_in,
            share_out,
            share_gain,
            share_shift,
        ),
        "ctx",
    )
    return (
        result.astype(jnp.bfloat16)[None],
        input_grad[None],
        stream_grad[None],
        source_grad[None],
        total_query,
        total_pair,
        total_output,
        total_cross_query,
        total_cross_pair,
        total_cross_output,
        total_in,
        total_out,
        total_gain,
        total_shift,
    )


PAIR = 2 * HEAD
PAIRS = HEADS // 2
FF = 2048
low_t = jnp.bfloat16
wide_t = jnp.float32
vmem_spec = pl.BlockSpec(memory_space=pltpu.VMEM)
smem_spec = pl.BlockSpec(memory_space=pltpu.SMEM)


def run(body, outs, ids, args, scratch=(), us=2, vmem=56):
    outs = [jax.ShapeDtypeStruct(shape, kind) for shape, kind in outs]
    moved = sum(a.size * a.dtype.itemsize for a in list(args) + outs)
    return pl.pallas_call(
        body,
        name=getattr(body, "func", body).__name__,
        out_shape=outs,
        in_specs=[smem_spec] + [vmem_spec] * len(args),
        out_specs=[vmem_spec] * len(outs),
        scratch_shapes=[pltpu.VMEM(shape, kind) for shape, kind in scratch],
        compiler_params=pltpu.CompilerParams(vmem_limit_bytes=vmem * 1024 * 1024),
        cost_estimate=pl.CostEstimate(flops=us * 1_000_000_000, bytes_accessed=moved, transcendentals=0),
    )(ids, *args)


def dot_nn(a, b):
    return lax.dot_general(a, b, (((1,), (0,)), ((), ())), preferred_element_type=wide_t)


def dot_nt(a, b):
    return lax.dot_general(a, b, (((1,), (1,)), ((), ())), preferred_element_type=wide_t)


def dot_tn(a, b):
    return lax.dot_general(a, b, (((0,), (0,)), ((), ())), preferred_element_type=wide_t)


def at16(start, size=16):
    return pl.ds(pl.multiple_of(start, 16), size)


def at128(start, size=128):
    return pl.ds(pl.multiple_of(start, 128), size)


def half_mask(shape, axis, core):
    return (lax.broadcasted_iota(jnp.int32, shape, axis) // HEAD) == core


def attend_rows(q_ref, kv_ref, bias_ref, out_ref):
    rows, keys = bias_ref.shape
    chunk = rows // 2

    def step(i, carry):
        p, r = i // 2, i % 2
        here = pl.ds(pl.multiple_of(r * chunk, chunk), chunk)
        q = q_ref[here, at128(p * PAIR)]
        first = half_mask((chunk, PAIR), 1, 0)
        both = jnp.concatenate(
            (jnp.where(first, q, jnp.zeros_like(q)), jnp.where(first, jnp.zeros_like(q), q)), axis=0
        )
        bias = bias_ref[here, :]
        s = dot_nt(both, kv_ref[:, at128(p * PAIR)]) + jnp.concatenate((bias, bias), axis=0)
        top = jnp.max(s, axis=1, keepdims=True)
        w = jnp.exp(s - top)
        total = jnp.sum(w, axis=1, keepdims=True)
        mixed = dot_nn(w.astype(low_t), kv_ref[:, at128(D + p * PAIR)]) / total
        out_ref[here, at128(p * PAIR)] = jnp.where(first, mixed[:chunk], mixed[chunk:]).astype(low_t)
        return carry

    lax.fori_loop(0, 2 * PAIRS, step, 0)


def assemble(ids, parts, column, outs):
    for chip, other, block in parts:
        own = chip * 2 + (ids[1] ^ other)
        for e in range(4):
            rows = at16((ids[2] ^ e) * 128 + own * 16)
            start = column
            for out in outs:
                width = out.shape[1]
                out[rows, :] = block[e * 16 : (e + 1) * 16, start : start + width]
                start += width


def project_pairs(parts, weight, kv_ref):
    for n, part in enumerate(parts):
        for k in range(PAIRS):
            rows = part.shape[1]
            start = (n * 4 + k) * rows
            kv_ref[start : start + rows, :] = dot_nn(part[k], weight[...]).astype(low_t)


def self_forward(ids, hidden, own, other, slices, other_slices, *refs):
    code, low_row, high_row, out, wq, wkv, q_ref, kv_ref, bias_ref = refs
    rows = hidden.shape[0]
    parts = [(k, n, part.at[k]) for n, part in enumerate((slices, other_slices)) for k in range(4)]
    assemble(ids, parts, 0, (wq, wkv))
    q_ref[...] = (dot_nn(hidden[...], wq[...]).astype(low_t) * 0.125).astype(low_t)
    project_pairs((own, other), wkv, kv_ref)
    k = code[...]
    seen = (k >= low_row[...]) & (k < high_row[...])
    bias_ref[...] = jnp.where(seen, 0.0, neg_fill)
    mine = lax.broadcasted_iota(jnp.int32, (rows, rows), 0) == lax.broadcasted_iota(
        jnp.int32, (rows, rows), 1
    )
    block = at128(ids[0] * rows, rows)
    bias_ref[:, block] = jnp.where(mine, 0.0, bias_ref[:, block])
    attend_rows(q_ref, kv_ref, bias_ref, out)


def layer_norm(values, gain_row, shift_row):
    mean = jnp.mean(values, axis=1, keepdims=True)
    centred = values - mean
    scale = lax.rsqrt(jnp.mean(centred * centred, axis=1, keepdims=True) + layer_eps)
    normed = centred * scale
    return normed * gain_row + shift_row, normed, scale


def layer_norm_back(grad, normed, scale, gain_row):
    gain_term = jnp.sum(grad * normed, axis=0, keepdims=True)
    shift_term = jnp.sum(grad, axis=0, keepdims=True)
    scaled = grad * gain_row
    grad_in = scale * (
        scaled
        - jnp.mean(scaled, axis=1, keepdims=True)
        - normed * jnp.mean(scaled * normed, axis=1, keepdims=True)
    )
    return grad_in, gain_term, shift_term


def cross_forward(ids, hidden, self_low, own, other, *refs):
    slices = refs[:2]
    code, seq_col = refs[2:4]
    first, normed, scale_out, first_low, cross_low, cross_q = refs[4:10]
    wo, wcq, wckv, wco, gs, q_ref, kv_ref, bias_ref = refs[10:]
    parts = [(k, n, slices[n].at[k]) for n in range(2) for k in range(4)]
    assemble(ids, parts, 0, (wo, wcq, wckv, wco))
    for e in range(4):
        gs[:, at128((ids[2] ^ e) * 128)] = slices[0][0, e * 16 : (e + 1) * 16, 5 * D :]
    gain, shift = gs[0:1, :].astype(wide_t), gs[3:4, :].astype(wide_t)
    value, n0, s0 = layer_norm(
        hidden[...].astype(wide_t) + dot_nn(self_low[...], wo[...]), gain, shift
    )
    first[...] = value
    normed[...] = n0
    scale_out[...] = jnp.broadcast_to(s0, scale_out.shape)
    low = value.astype(low_t)
    first_low[...] = low
    q = dot_nn(low, wcq[...]).astype(low_t)
    cross_q[...] = q
    q_ref[...] = (q * 0.125).astype(low_t)
    project_pairs((own, other), wckv, kv_ref)
    bias_ref[...] = jnp.where(code[...] == seq_col[...], 0.0, neg_fill)
    attend_rows(q_ref, kv_ref, bias_ref, cross_low)


def feed_forward(ids, first, cross_low, cross_q, wco, gs, cotangent, *refs):
    halves = refs[0:2]
    (result, dealt, second_grad, second_low, activated, pre_grad, branch, cross_branch, sums) = refs[2:11]
    slope, wins, wouts = refs[11:]
    for n, half in enumerate(halves):
        for w in range(4):
            wins[n, w * 128 : (w + 1) * 128, :] = half[w, :128, :]
            for k in range(2):
                start = w * 256 + k * 128
                wouts[n, start : start + 128, :] = half[w, 128:, k * D : (k + 1) * D]
    gains, shifts = gs[0:3, :].astype(wide_t), gs[3:6, :].astype(wide_t)
    second, n1, s1 = layer_norm(
        first[...] + dot_nn(cross_low[...], wco[...]), gains[1:2], shifts[1:2]
    )
    low = second.astype(low_t)
    second_low[...] = low
    width = 512
    chunks = [(n, c) for n in range(2) for c in range(FF // 2 // width)]
    total = second
    for n, c in chunks:
        here = slice(c * width, (c + 1) * width)
        cols = slice(n * (FF // 2) + c * width, n * (FF // 2) + (c + 1) * width)
        pre = dot_nn(low, wins[n, :, here])
        sig = 1.0 / (1.0 + jnp.exp(-pre))
        act = (pre * sig).astype(low_t)
        activated[:, cols] = act
        slope[:, cols] = sig * (1.0 + pre * (1.0 - sig))
        total = total + dot_nn(act, wouts[n, here, :])
    value, n2, s2 = layer_norm(total, gains[2:3], shifts[2:3])
    result[...] = value.astype(low_t)
    third, gain_c, shift_c = layer_norm_back(cotangent[...].astype(wide_t), n2, s2, gains[2:3])
    third_low = third.astype(low_t)
    branch[...] = third_low
    total = third
    for n, c in chunks:
        here = slice(c * width, (c + 1) * width)
        cols = slice(n * (FF // 2) + c * width, n * (FF // 2) + (c + 1) * width)
        back = (dot_nt(third_low, wouts[n, here, :]) * slope[:, cols]).astype(low_t)
        pre_grad[:, cols] = back
        total = total + dot_nt(back, wins[n, :, here])
    grad, gain_b, shift_b = layer_norm_back(total, n1, s1, gains[1:2])
    second_grad[...] = grad
    grad_low = grad.astype(low_t)
    cross_branch[...] = grad_low
    mixed = dot_nt(grad_low, wco[...]).astype(low_t)
    for p in range(PAIRS):
        dealt[p, :, :PAIR] = cross_q[:, p * PAIR : (p + 1) * PAIR]
        dealt[p, :, PAIR:] = mixed[:, p * PAIR : (p + 1) * PAIR]
    zero = jnp.zeros_like(gain_b)
    sums[...] = jnp.concatenate((zero, gain_b, gain_c, zero, shift_b, shift_c, zero, zero), axis=0)


def put_slices(ids, value, keep, send, column):
    width = value.shape[1]
    for other, out in enumerate((keep, send)):
        for chip in range(4):
            own = chip * 2 + (ids[1] ^ other)
            for e in range(4):
                rows = at16((ids[2] ^ e) * 128 + own * 16)
                out[chip, e * 16 : (e + 1) * 16, column : column + width] = value[rows, :]


def grads_a(ids, second_low, pre_grad, activated, branch, cross_low, cross_branch, *refs):
    keep, send, g_in, g_out, g_cross = refs
    core, mw = ids[1], ids[2]
    g_in[...] = dot_tn(second_low[...], pre_grad[...]).astype(low_t)
    g_out[...] = dot_tn(activated[...], branch[...]).astype(low_t)
    g_cross[...] = dot_tn(cross_low[...], cross_branch[...]).astype(low_t)
    put_slices(ids, g_cross, keep, send, 2 * FF)
    half = FF // 2
    for other, out in enumerate((keep, send)):
        for chip in range(4):
            own = chip * 2 + (core ^ other)
            for e in range(4):
                w, here = mw ^ e, slice(e * 16, (e + 1) * 16)
                rows = at16(w * 128 + own * 16)
                for n in range(2):
                    for k in range(4):
                        out[chip, here, at128(k * 512 + (core ^ n) * 256, 256)] = g_in[
                            rows, n * half + k * 256 : n * half + (k + 1) * 256
                        ]
                for g in range(4):
                    row = (core ^ (chip // 2)) * half + w * 256 + (own % 4) * 64 + g * 16
                    out[chip, here, FF + g * D : FF + (g + 1) * D] = g_out[at16(row), :]


def grads_b(ids, first_low, cross_dq, self_low, branch, sums, keep, send, g_query, g_output):
    g_query[...] = dot_tn(first_low[...], cross_dq[...]).astype(low_t)
    g_output[...] = dot_tn(self_low[...], branch[...]).astype(low_t)
    put_slices(ids, g_query, keep, send, 0)
    put_slices(ids, g_output, keep, send, D)
    row = jnp.concatenate((sums[...], jnp.zeros_like(sums[...])), axis=0).astype(low_t)
    for e in range(4):
        w = ids[2] ^ e
        piece = row[:, :128]
        for k in range(1, 4):
            piece = jnp.where(w == k, row[:, k * 128 : (k + 1) * 128], piece)
        for out in (keep, send):
            for chip in range(4):
                out[chip, e * 16 : (e + 1) * 16, 2 * D :] = piece


def pair_back(is_self, ids, *refs):
    at = 0

    def take(n):
        nonlocal at
        at += n
        return refs[at - n : at]

    if is_self:
        hidden_parts, do_parts, x_parts = take(2), take(2), take(2)
        w_query, w_pair, code, low_rows, high_rows = take(5)
        keep, send = take(2)
    else:
        both_parts, x_parts = take(2), take(2)
        w_pair, code, low_rows = take(3)
        dq_keep, dq_send, keep, send = take(4)
    q_all, do_all, k_all, v_all, kt, dq_t, dq_all, dk, dv, s_ref, grads = take(11)
    chip, core, mw = ids[0], ids[1], ids[2]
    rows = q_all.shape[1]
    mine = half_mask((rows, PAIR), 1, core)
    nothing = jnp.zeros((rows, PAIR), low_t)
    pair = at128(chip * PAIR)
    if is_self:
        wq = w_query[:, pair]
    wk, wv = w_pair[:, pair], w_pair[:, at128(D + chip * PAIR)]
    for n in range(2):
        for k in range(4):
            b = n * 4 + k
            here = slice(b * rows, (b + 1) * rows)
            x = x_parts[n][k]
            k_all[here, :] = dot_nn(x, wk).astype(low_t)
            v_all[here, :] = dot_nn(x, wv).astype(low_t)
            if is_self:
                q, do = dot_nn(hidden_parts[n][k], wq).astype(low_t), do_parts[n][k]
            else:
                q, do = both_parts[n][k, :, :PAIR], both_parts[n][k, :, PAIR:]
            q_all[b] = (jnp.where(mine, q, nothing) * 0.125).astype(low_t)
            do_all[b] = jnp.where(mine, do, nothing)
    kt[...] = k_all[...].astype(wide_t).T.astype(low_t)
    dk[...] = jnp.zeros_like(dk)
    dv[...] = jnp.zeros_like(dv)

    def step(b, carry):
        q, do = q_all[b], do_all[b]
        c = jnp.concatenate((code[...],) * (rows // 128), axis=1)
        low_row = low_rows[pl.ds(b, 1), :]
        s = dot_nt(k_all[...], q)
        if is_self:
            s_ref[...] = jnp.where((c >= low_row) & (c < high_rows[pl.ds(b, 1), :]), s, neg_fill)
            block = at128(b * rows, rows)
            own = lax.broadcasted_iota(jnp.int32, (rows, rows), 0) == lax.broadcasted_iota(
                jnp.int32, (rows, rows), 1
            )
            s_ref[block, :] = jnp.where(own, dot_nt(k_all[block, :], q), s_ref[block, :])
        else:
            s_ref[...] = jnp.where(c == low_row, s, neg_fill)
        s = s_ref[...]
        w = jnp.exp(s - jnp.max(s, axis=0, keepdims=True))
        inverse = 1.0 / jnp.sum(w, axis=0, keepdims=True)
        dp = dot_nt(v_all[...], do)
        offset = jnp.sum(w * dp, axis=0, keepdims=True) * inverse
        probs = w * inverse
        dv[...] += dot_nn(probs.astype(low_t), do)
        ds = (probs * (dp - offset)).astype(low_t)
        dk[...] += dot_nn(ds, q)
        dqt = dot_nn(kt[...], ds) * 0.125
        dqt = jnp.where(half_mask((PAIR, rows), 0, core), dqt, 0.0)
        dq_t[b] = dqt.astype(low_t)
        dq_all[b] = dqt.T.astype(low_t)
        return carry

    lax.fori_loop(0, 8, step, 0)
    total_q = jnp.zeros((PAIR, D), wide_t)
    total_k, total_v = total_q, total_q
    at_kv = PAIR if is_self else 0
    for n, out in enumerate((keep, send)):
        for k in range(4):
            b = n * 4 + k
            here = slice(b * rows, (b + 1) * rows)
            dk_low, dv_low = dk[here, :].astype(low_t), dv[here, :].astype(low_t)
            if is_self:
                out[k, :, :PAIR] = dq_all[b]
            else:
                (dq_keep, dq_send)[n][k] = dq_all[b]
            out[k, :, at_kv : at_kv + PAIR] = dk_low
            out[k, :, at_kv + PAIR :] = dv_low
            x = x_parts[n][k]
            total_k += dot_tn(dk_low, x)
            total_v += dot_tn(dv_low, x)
            if is_self:
                total_q += dot_nn(dq_t[b], hidden_parts[n][k])
    totals = (total_q, total_k, total_v) if is_self else (total_k, total_v)
    for n, value in enumerate(totals):
        grads[:, n * PAIR : (n + 1) * PAIR] = value.T.astype(low_t)
    for e in range(4):
        row, here = (mw ^ e) * 128, slice(e * 64, (e + 1) * 64)
        keep[4, here, :] = grads[at16(row + core * 64, 64), :]
        send[4, here, :] = grads[at16(row + (1 - core) * 64, 64), :]


def first_back(ids, back, second_grad, normed, scale, gs, wcq, wo, sums_in, *refs):
    first_grad, branch, dealt, dq, sums = refs
    for p in range(PAIRS):
        dq[:, p * PAIR : (p + 1) * PAIR] = back[p]
    total = second_grad[...] + dot_nt(dq[...], wcq[...])
    grad, gain_a, shift_a = layer_norm_back(
        total, normed[...], scale[:, 0:1], gs[0:1, :].astype(wide_t)
    )
    first_grad[...] = grad
    low = grad.astype(low_t)
    branch[...] = low
    mixed = dot_nt(low, wo[...]).astype(low_t)
    for p in range(PAIRS):
        dealt[p] = mixed[:, p * PAIR : (p + 1) * PAIR]
    zero = jnp.zeros_like(gain_a)
    sums[...] = sums_in[...] + jnp.concatenate(
        (gain_a, zero, zero, shift_a, zero, zero, zero, zero), axis=0
    )


def source_back(ids, parts, wckv, out, dkv):
    base = parts.shape[2] - 8 * PAIR
    for p in range(PAIRS):
        for g in range(4):
            rows = slice(g * 64, (g + 1) * 64)
            start = base + g * 2 * PAIR
            dkv[rows, p * PAIR : (p + 1) * PAIR] = parts[p, :, start : start + PAIR]
            dkv[rows, D + p * PAIR : D + (p + 1) * PAIR] = parts[
                p, :, start + PAIR : start + 2 * PAIR
            ]
    out[...] = dot_nt(dkv[...], wckv[...])


def hidden_back(ids, back, first_grad, wq, wkv, hidden_grad, stream_grad, dq, dkv):
    for p in range(PAIRS):
        dq[:, p * PAIR : (p + 1) * PAIR] = back[p, :, :PAIR]
        dkv[:, p * PAIR : (p + 1) * PAIR] = back[p, :, PAIR : 2 * PAIR]
        dkv[:, D + p * PAIR : D + (p + 1) * PAIR] = back[p, :, 2 * PAIR :]
    hidden_grad[...] = first_grad[...] + dot_nt(dq[...], wq[...])
    stream_grad[...] = dot_nt(dkv[...], wkv[...])


def plus(a, b):
    return (a.astype(wide_t) + b.astype(wide_t)).astype(low_t)


def add_two(ids, keep, received, out):
    for k in range(4):
        out[k] = plus(keep[k], received[k])


def add_mixed(ids, keep, received, cross_keep, cross_received, out):
    width = keep.shape[2]
    for k in range(4):
        out[k, :, :width] = plus(keep[k], received[k])
        for g in range(4):
            rows = slice(g * 64, (g + 1) * 64)
            start = width + g * 2 * PAIR
            out[k, :, start : start + 2 * PAIR] = plus(
                cross_keep[k, rows, :], cross_received[k, rows, :]
            )


def add_chips(ids, parts, *outs):
    for e in range(4):
        here = slice(e * 16, (e + 1) * 16)
        total = parts[0, here, :].astype(wide_t)
        for k in range(1, 4):
            total = total + parts[k, here, :].astype(wide_t)
        outs[e][...] = total.astype(low_t)


def add_four(ids, a, b, c, d, out):
    total = a[...].astype(wide_t) + b[...].astype(wide_t) + c[...].astype(wide_t) + d[...].astype(wide_t)
    for k in range(4):
        out[k] = total.astype(low_t)


def end_sums(ids, keep, received, cross_keep, cross_received, mixed, back, *outs):
    for k in range(4):
        back[k] = plus(keep[k], received[k])
    width = 2 * D + 128
    for e in range(4):
        here = slice(e * 16, (e + 1) * 16)
        total = mixed[0, here, :width].astype(wide_t)
        for k in range(1, 4):
            total = total + mixed[k, here, :width].astype(wide_t)
        outs[e][:, :width] = total.astype(low_t)
        start = width
        for one, two in ((cross_keep, cross_received), (keep, received)):
            for g in range(4):
                rows = slice(e * 64 + g * 16, e * 64 + (g + 1) * 16)
                outs[e][:, start : start + one.shape[2]] = plus(one[4, rows, :], two[4, rows, :])
                start += one.shape[2]


def place_a(ids, own, other, g_in, g_out, g_cross):
    for n, part in enumerate((own, other)):
        for chip in range(4):
            c = chip * 2 + (ids[1] ^ n)
            rows = at16(c * 16)
            g_in[rows, :] = part[chip, :, :FF].astype(wide_t)
            for g in range(4):
                g_out[at16(c * 64 + g * 16), :] = part[
                    chip, :, FF + g * D : FF + (g + 1) * D
                ].astype(wide_t)
            g_cross[rows, :] = part[chip, :, 2 * FF :].astype(wide_t)


def place_end(ids, own, other, g_cross_query, g_output, norms, g_cross_pair, g_query, g_pair):
    norms[...] = own[0, :, 2 * D : 2 * D + 128].astype(wide_t)
    for n, part in enumerate((own, other)):
        for chip in range(4):
            core = ids[1] ^ n
            rows = at16((chip * 2 + core) * 16)
            g_cross_query[rows, :] = part[chip, :, :D].astype(wide_t)
            g_output[rows, :] = part[chip, :, D : 2 * D].astype(wide_t)
            start = 2 * D + 128
            for outs in (((g_cross_pair, 0), (g_cross_pair, D)), ((g_query, 0), (g_pair, 0), (g_pair, D))):
                for g in range(4):
                    here = at16(core * 64 + g * 16)
                    for out, base in outs:
                        column = base + chip * PAIR
                        out[here, column : column + PAIR] = part[
                            chip, :, start : start + PAIR
                        ].astype(wide_t)
                        start += PAIR


def pack_start(ids, stream, *refs):
    weights, (gain, shift), (many, pack) = refs[:6], refs[6:8], refs[8:]
    for k in range(4):
        many[k] = stream[...]
    rows = at16((ids[0] * 2 + ids[1]) * 16)
    start = 0
    for w in weights:
        pack[:, start : start + w.shape[1]] = w[rows, :]
        start += w.shape[1]
    norms = (gain[...].astype(wide_t), shift[...].astype(wide_t), jnp.zeros((10, 128), wide_t))
    pack[:, start:] = jnp.concatenate(norms, axis=0).astype(low_t)


def pack_first(ids, *refs):
    parts, outs = refs[:4], refs[4:]
    for e in range(4):
        start = 0
        for out in outs:
            piece = parts[e][:, start : start + out.shape[2]]
            for k in range(4):
                out[k, e * 16 : (e + 1) * 16, :] = piece
            start += out.shape[2]


def core_swap(value):
    return lax.ppermute(value, "core", [(0, 1), (1, 0)])


def chip_swaps(parts):
    moves = [[(i, i ^ k) for i in range(4)] for k in range(4)]
    return [parts[0]] + [lax.ppermute(parts[k], "chip", moves[k]) for k in range(1, 4)]


def shard_swaps(parts):
    moves = [[(i, i ^ k) for i in range(4)] for k in range(4)]
    return [parts[0]] + [lax.ppermute(parts[k], "wa", moves[k]) for k in range(1, 4)]


def deal(value):
    return lax.all_to_all(value, "chip", 0, 0, tiled=True)


def deal_both(value):
    own = deal(value)
    return own, core_swap(own)


def after(value, *others):
    return lax.optimization_barrier((value,) + others)[0]


def fast_shards(
    hidden,
    stream,
    encoder,
    lengths,
    order,
    ranks,
    thresholds,
    self_query,
    self_key_value,
    self_output,
    cross_query,
    cross_key_value,
    cross_output,
    ffn_in,
    ffn_out,
    norm_gain,
    norm_shift,
    cotangent,
):
    rows, keys = hidden.shape[1], order.shape[1]
    chip, core, mw = lax.axis_index("chip"), lax.axis_index("core"), lax.axis_index("wa")
    ids = jnp.stack((chip, core, mw)).astype(jnp.int32)
    inputs = hidden[0]
    me = chip * 2 + core

    stream_copies, pack = run(
        pack_start,
        [((4, rows, D), low_t), ((16, 8 * D + 128), low_t)],
        ids,
        [stream[0], self_query, self_key_value, self_output, cross_query, cross_key_value, cross_output]
        + [norm_gain, norm_shift],
    )
    stream_own, stream_other = deal_both(stream_copies)
    source_own = lax.all_gather(encoder[0], "chip", axis=0)
    shards = shard_swaps([pack] * 4)
    copies1, copies2 = run(
        pack_first,
        [((4, 64, 3 * D), low_t), ((4, 64, 5 * D + 128), low_t)],
        ids,
        [after(shards[0], stream_own)] + shards[1:],
    )
    slices1, slices1_other = deal_both(copies1)
    slices2 = deal(after(copies2, slices1))
    half_columns = [
        lax.dynamic_slice_in_dim(ffn_in, k * 512 + core * 256, 256, 1) for k in range(4)
    ]
    half_rows = [lax.dynamic_slice_in_dim(ffn_out, core * 256 + n * 128, 128, 0) for n in range(2)]
    half = jnp.concatenate(
        (jnp.concatenate(half_columns, axis=1), jnp.concatenate(half_rows, axis=1)), axis=0
    )
    ffn_own = lax.all_gather(after(half, source_own), "wa", axis=0)
    hidden_own = lax.all_gather(after(inputs, ffn_own), "chip", axis=0)

    seq_ends = jnp.cumsum(lengths[0])
    token_seq = sequence_ids(order[0], seq_ends)
    source_seq = sequence_ids(jnp.arange(keys, dtype=jnp.int32), seq_ends)

    def by_device(vector):
        blocks = vector.reshape(4, 2, rows)
        return jnp.concatenate(
            [lax.dynamic_index_in_dim(blocks, core ^ n, 1, keepdims=False) for n in range(2)], axis=0
        )

    token_rows, source_blocks = by_device(token_seq), by_device(source_seq)
    low_rows = token_rows * 1024
    high_rows = low_rows + by_device(thresholds[0])
    code_rows = low_rows + by_device(ranks[0])
    code_wide = jnp.broadcast_to(code_rows.reshape(keys, 1), (keys, 128))
    source_wide = jnp.broadcast_to(source_blocks.reshape(keys, 1), (keys, 128))

    def own_column(blocks):
        return lax.dynamic_slice_in_dim(blocks, chip, 1, 0).reshape(rows, 1)

    attend_scratch = [((rows, D), low_t), ((keys, 2 * D), low_t), ((rows, keys), wide_t)]
    self_low, wq, wkv = run(
        self_forward,
        [((rows, D), low_t), ((D, D), low_t), ((D, 2 * D), low_t)],
        ids,
        [inputs, stream_own, stream_other, slices1, slices1_other]
        + [code_rows.reshape(1, keys), own_column(low_rows), own_column(high_rows)],
        attend_scratch,
        us=15,
    )
    slices2_other = core_swap(after(slices2, self_low))
    source_other = core_swap(after(source_own, self_low))
    first, normed, scale, first_low, cross_low, cross_q, wo, wcq, wckv, wco, gs = run(
        cross_forward,
        [((rows, D), wide_t)] * 2
        + [((rows, 128), wide_t)]
        + [((rows, D), low_t)] * 3
        + [((D, D), low_t), ((D, D), low_t), ((D, 2 * D), low_t), ((D, D), low_t), ((16, D), low_t)],
        ids,
        [inputs, self_low, source_own, source_other, slices2, slices2_other]
        + [source_blocks.reshape(1, keys), own_column(token_rows)],
        attend_scratch,
        us=15,
    )
    ffn_other = core_swap(after(ffn_own, cross_low))
    (
        result,
        cross_dealt,
        second_grad,
        second_low,
        activated,
        pre_grad,
        branch,
        cross_branch,
        sums,
    ) = run(
        feed_forward,
        [
            ((rows, D), low_t),
            ((PAIRS, rows, 2 * PAIR), low_t),
            ((rows, D), wide_t),
            ((rows, D), low_t),
            ((rows, FF), low_t),
            ((rows, FF), low_t),
            ((rows, D), low_t),
            ((rows, D), low_t),
            ((8, D), wide_t),
        ],
        ids,
        [first, cross_low, cross_q, wco, gs, cotangent[0], ffn_own, ffn_other],
        [((rows, FF), wide_t), ((2, D, FF // 2), low_t), ((2, FF // 2, D), low_t)],
        us=8,
    )
    both_own, both_other = deal_both(cross_dealt)

    width_a = 2 * FF + D
    keep_a, send_a = run(
        grads_a,
        [((4, 64, width_a), low_t)] * 2,
        ids,
        [second_low, pre_grad, activated, branch, cross_low, cross_branch],
        [((D, FF), low_t), ((FF, D), low_t), ((D, D), low_t)],
        us=6,
    )
    (sum_a,) = run(add_two, [((4, 64, width_a), low_t)], ids, [keep_a, core_swap(after(send_a, both_own))])
    rows_a = deal(after(sum_a, both_own))

    def back_scratch(width):
        return (
            [((8, rows, PAIR), low_t)] * 2
            + [((keys, PAIR), low_t)] * 2
            + [((PAIR, keys), low_t), ((8, PAIR, rows), low_t), ((8, rows, PAIR), low_t)]
            + [((keys, PAIR), wide_t)] * 2
            + [((keys, rows), wide_t), ((D, width), low_t)]
        )

    cq_keep, cq_send, ckv_keep, ckv_send = run(
        functools.partial(pair_back, False),
        [((4, rows, PAIR), low_t)] * 2 + [((5, rows, 2 * PAIR), low_t)] * 2,
        ids,
        [after(both_own, sum_a), both_other, source_own, source_other, wckv, source_wide, token_rows],
        back_scratch(2 * PAIR),
        us=25,
    )
    (cq_sum,) = run(add_two, [((4, rows, PAIR), low_t)], ids, [cq_keep, core_swap(cq_send)])
    cross_back = deal(after(cq_sum, rows_a))
    shards_a = run(add_chips, [((16, width_a), low_t)] * 4, ids, [after(rows_a, cq_sum)])
    moved_a = shard_swaps([after(part, cross_back) for part in shards_a])
    ckv_received = core_swap(after(ckv_send, cross_back))
    first_grad, self_branch, self_dealt, cross_dq, sums = run(
        first_back,
        [
            ((rows, D), wide_t),
            ((rows, D), low_t),
            ((PAIRS, rows, PAIR), low_t),
            ((rows, D), low_t),
            ((8, D), wide_t),
        ],
        ids,
        [cross_back, second_grad, normed, scale, gs, wcq, wo, sums],
        us=3,
    )
    do_own, do_other = deal_both(self_dealt)
    width_b = 2 * D + 128
    keep_b, send_b = run(
        grads_b,
        [((4, 64, width_b), low_t)] * 2,
        ids,
        [first_low, cross_dq, self_low, self_branch, sums],
        [((D, D), low_t)] * 2,
        us=3,
    )
    width_m = width_b + 8 * PAIR
    (sum_b,) = run(
        add_mixed,
        [((4, 64, width_m), low_t)],
        ids,
        [keep_b, core_swap(after(send_b, do_own)), ckv_keep, ckv_received],
    )
    mixed_b = deal(after(sum_b, do_own))
    hidden_other = core_swap(after(hidden_own, cross_back))
    keep_s, send_s = run(
        functools.partial(pair_back, True),
        [((5, rows, 3 * PAIR), low_t)] * 2,
        ids,
        [hidden_own, hidden_other, after(do_own, sum_b, *moved_a), do_other, stream_own, stream_other]
        + [wq, wkv, code_wide, low_rows, high_rows],
        back_scratch(3 * PAIR),
        us=25,
    )
    keep_s_received = core_swap(send_s)
    (copies_a,) = run(add_four, [((4, 16, width_a), low_t)], ids, [after(moved_a[0], keep_s)] + moved_a[1:])
    a_own, a_other = deal_both(copies_a)
    end_width = width_b + 8 * PAIR + 12 * PAIR
    back_s, *end_parts = run(
        end_sums,
        [((4, rows, 3 * PAIR), low_t)] + [((16, end_width), low_t)] * 4,
        ids,
        [keep_s, keep_s_received, ckv_keep, ckv_received, mixed_b],
    )
    self_back = deal(after(back_s, a_own))
    (copies_end,) = run(add_four, [((4, 16, end_width), low_t)], ids, shard_swaps(end_parts))
    end_own = deal(after(copies_end, self_back))
    (source_grad,) = run(
        source_back,
        [((rows, D), wide_t)],
        ids,
        [mixed_b, wckv],
        [((rows, 2 * D), low_t)],
        us=3,
    )
    hidden_grad, stream_grad = run(
        hidden_back,
        [((rows, D), wide_t)] * 2,
        ids,
        [self_back, first_grad, wq, wkv],
        [((rows, D), low_t), ((rows, 2 * D), low_t)],
        us=3,
    )
    grad_in, grad_out, grad_cross_output = run(
        place_a,
        [((128, FF), wide_t), ((D, D), wide_t), ((128, D), wide_t)],
        ids,
        [a_own, a_other],
    )
    end_other = core_swap(after(end_own, hidden_grad, source_grad, grad_in))
    grad_cross_query, grad_output, norm_sums, grad_cross_pair, grad_query, grad_pair = run(
        place_end,
        [((128, D), wide_t)] * 2
        + [((16, 128), wide_t), ((128, 2 * D), wide_t), ((128, D), wide_t), ((128, 2 * D), wide_t)],
        ids,
        [end_own, end_other],
    )
    return (
        result[None],
        hidden_grad[None],
        stream_grad[None],
        source_grad[None],
        grad_query,
        grad_pair,
        grad_output,
        grad_cross_query,
        grad_cross_pair,
        grad_cross_output,
        grad_in,
        grad_out,
        norm_sums[0:3],
        norm_sums[3:6],
    )


def solution(mesh):
    in_specs = (
        P("wa", "ctx", None),
        P("wa", "ctx", None),
        P("wa", "ctx", None),
        P("wa", None),
        P("wa", None),
        P("wa", None),
        P("wa", None),
        P("wa", None),
        P("wa", None),
        P("wa", None),
        P("wa", None),
        P("wa", None),
        P("wa", None),
        P("wa", None),
        P("wa", None),
        P(None, "wa"),
        P(None, "wa"),
        P("wa", "ctx", None),
    )
    out_specs = (
        P("wa", "ctx", None),
        P("wa", "ctx", None),
        P("wa", "ctx", None),
        P("wa", "ctx", None),
        P("wa", None),
        P("wa", None),
        P("wa", None),
        P("wa", None),
        P("wa", None),
        P("wa", None),
        P("wa", None),
        P("wa", None),
        P(None, "wa"),
        P(None, "wa"),
    )
    if mesh.axis_names != ("ctx", "wa") or mesh.shape["ctx"] != HEADS or mesh.shape["wa"] != 4:
        return jax.shard_map(
            general_shards, mesh=mesh, in_specs=in_specs, out_specs=out_specs, check_vma=False
        )

    def finer(spec):
        return P(*(("chip", "core") if axis == "ctx" else axis for axis in spec))

    return jax.shard_map(
        fast_shards,
        mesh=Mesh(mesh.devices.reshape(4, 2, 4), ("chip", "core", "wa")),
        in_specs=tuple(finer(spec) for spec in in_specs),
        out_specs=tuple(finer(spec) for spec in out_specs),
        check_vma=False,
    )
```

```python
import functools

import jax
import jax.numpy as jnp
from jax import lax
from jax.experimental import pallas as pl
from jax.experimental.pallas import tpu as pltpu
from jax.sharding import Mesh
from jax.sharding import PartitionSpec as P

D = 512
HEADS = 8
HEAD = 64
KEYBLK = 1024


layer_eps = 1e-05
neg_fill = -1e30


def sequence_ids(positions, seq_ends):
    return jnp.sum((positions[:, None] >= seq_ends[None, :]).astype(jnp.int32), axis=1)


def head_split(matrix):
    return matrix.reshape(matrix.shape[0], HEADS, HEAD)


def block_scores(query_heads, key_heads):
    raw_scores = jnp.einsum(
        "lhd,khd->hlk", query_heads, key_heads, preferred_element_type=jnp.float32
    )
    return raw_scores * float(HEAD) ** (-0.5)


def softmax_totals(queries, key_rows, allowed_fn):
    query_heads = head_split(queries)
    count_rows = queries.shape[0]

    def visit(state_pair, block_index):
        running_top, running_sum = state_pair
        block_start = block_index * KEYBLK
        key_piece = lax.dynamic_slice_in_dim(key_rows, block_start, KEYBLK, 0)
        allowed = allowed_fn(block_start)[None]
        scores = jnp.where(
            allowed, block_scores(query_heads, head_split(key_piece[:, :D])), neg_fill
        )
        new_top = jnp.maximum(running_top, jnp.max(scores, axis=2))
        weights = jnp.where(allowed, jnp.exp(scores - new_top[:, :, None]), 0.0)
        running_sum = running_sum * jnp.exp(running_top - new_top) + jnp.sum(weights, axis=2)
        return ((new_top, running_sum), None)

    initial = (
        jnp.full((HEADS, count_rows), neg_fill, jnp.float32),
        jnp.zeros((HEADS, count_rows), jnp.float32),
    )
    (final_top, final_sum), unused = lax.scan(
        visit, initial, jnp.arange(key_rows.shape[0] // KEYBLK)
    )
    return final_top + jnp.log(final_sum)


def attend_values(queries, key_rows, log_totals, allowed_fn):
    query_heads = head_split(queries)

    def visit(running, block_index):
        block_start = block_index * KEYBLK
        key_piece = lax.dynamic_slice_in_dim(key_rows, block_start, KEYBLK, 0)
        allowed = allowed_fn(block_start)[None]
        scores = block_scores(query_heads, head_split(key_piece[:, :D]))
        weights = jnp.where(allowed, jnp.exp(scores - log_totals[:, :, None]), 0.0)
        value_heads = head_split(key_piece[:, D:])
        return (
            running
            + jnp.einsum(
                "hlk,khd->lhd",
                weights.astype(jnp.bfloat16),
                value_heads,
                preferred_element_type=jnp.float32,
            ),
            None,
        )

    mixed, unused = lax.scan(
        visit, jnp.zeros(query_heads.shape, jnp.float32), jnp.arange(key_rows.shape[0] // KEYBLK)
    )
    return mixed.reshape(queries.shape[0], D)


def head_offsets(grad_low, attended):
    return jnp.sum(head_split(grad_low.astype(jnp.float32) * attended), axis=2).T


def attend_back(queries, key_rows, log_totals, attended, grad_low, allowed_fn):
    query_heads = head_split(queries)
    grad_heads = head_split(grad_low)
    offsets = head_offsets(grad_low, attended)
    scale_value = float(HEAD) ** (-0.5)

    def visit(query_grad, block_index):
        block_start = block_index * KEYBLK
        key_piece = lax.dynamic_slice_in_dim(key_rows, block_start, KEYBLK, 0)
        allowed = allowed_fn(block_start)[None]
        key_heads = head_split(key_piece[:, :D])
        value_heads = head_split(key_piece[:, D:])
        weights = jnp.where(
            allowed, jnp.exp(block_scores(query_heads, key_heads) - log_totals[:, :, None]), 0.0
        )
        value_grad = jnp.einsum(
            "hlk,lhd->khd",
            weights.astype(jnp.bfloat16),
            grad_heads,
            preferred_element_type=jnp.float32,
        )
        weight_grad = jnp.einsum(
            "lhd,khd->hlk", grad_heads, value_heads, preferred_element_type=jnp.float32
        )
        score_grad = (weights * (weight_grad - offsets[:, :, None]) * scale_value).astype(
            jnp.bfloat16
        )
        query_grad = query_grad + jnp.einsum(
            "hlk,khd->lhd", score_grad, key_heads, preferred_element_type=jnp.float32
        )
        key_grad = jnp.einsum(
            "hlk,lhd->khd", score_grad, query_heads, preferred_element_type=jnp.float32
        )
        return (
            query_grad,
            jnp.concatenate((key_grad.reshape(KEYBLK, D), value_grad.reshape(KEYBLK, D)), axis=1),
        )

    query_grad, grad_pieces = lax.scan(
        visit, jnp.zeros(query_heads.shape, jnp.float32), jnp.arange(key_rows.shape[0] // KEYBLK)
    )
    return (query_grad.reshape(queries.shape[0], D), grad_pieces.reshape(key_rows.shape[0], 2 * D))


def normalize(values, gain_row, shift_row):
    row_mean = jnp.mean(values, axis=1, keepdims=True)
    centred = values - row_mean
    scale_inv = lax.rsqrt(jnp.mean(centred * centred, axis=1, keepdims=True) + layer_eps)
    normed = centred * scale_inv
    return (normed * gain_row + shift_row, normed, scale_inv)


def normalize_back(grad_out, normed, scale_inv, gain_row):
    gain_term = jnp.sum(grad_out * normed, axis=0)
    shift_term = jnp.sum(grad_out, axis=0)
    scaled = grad_out * gain_row
    grad_in = scale_inv * (
        scaled
        - jnp.mean(scaled, axis=1, keepdims=True)
        - normed * jnp.mean(scaled * normed, axis=1, keepdims=True)
    )
    return (grad_in, gain_term, shift_term)


def matmul(left, right):
    return jnp.dot(left, right, preferred_element_type=jnp.float32)


def general_shards(
    hidden,
    stream,
    encoder,
    lengths,
    order,
    ranks,
    thresholds,
    self_query,
    self_key_value,
    self_output,
    cross_query,
    cross_key_value,
    cross_output,
    ffn_in,
    ffn_out,
    norm_gain,
    norm_shift,
    cotangent,
):
    (
        full_query,
        full_pair,
        full_output,
        full_cross_query,
        full_cross_pair,
        full_cross_output,
        full_in,
        full_out,
        gain_rows,
        shift_rows,
    ) = (
        lax.all_gather(self_query, "wa", axis=0, tiled=True),
        lax.all_gather(self_key_value, "wa", axis=0, tiled=True),
        lax.all_gather(self_output, "wa", axis=0, tiled=True),
        lax.all_gather(cross_query, "wa", axis=0, tiled=True),
        lax.all_gather(cross_key_value, "wa", axis=0, tiled=True),
        lax.all_gather(cross_output, "wa", axis=0, tiled=True),
        lax.all_gather(ffn_in, "wa", axis=0, tiled=True),
        lax.all_gather(ffn_out, "wa", axis=0, tiled=True),
        lax.all_gather(norm_gain, "wa", axis=1, tiled=True),
        lax.all_gather(norm_shift, "wa", axis=1, tiled=True),
    )
    gains = gain_rows.astype(jnp.float32)
    shifts = shift_rows.astype(jnp.float32)
    local_rows = hidden.shape[1]
    total_rows = order.shape[1]
    row_start = lax.axis_index("ctx") * local_rows
    seq_ends = jnp.cumsum(lengths[0])
    token_seq = sequence_ids(order[0], seq_ends)
    source_seq = sequence_ids(jnp.arange(total_rows, dtype=jnp.int32), seq_ends)
    query_seq = lax.dynamic_slice_in_dim(token_seq, row_start, local_rows)
    query_rows = row_start + jnp.arange(local_rows, dtype=jnp.int32)
    all_limits = thresholds[0]
    limits = lax.dynamic_slice_in_dim(all_limits, row_start, local_rows)
    key_ranks = ranks[0]

    def self_allowed(block_start):
        block_seq = lax.dynamic_slice_in_dim(token_seq, block_start, KEYBLK)
        block_rank = lax.dynamic_slice_in_dim(key_ranks, block_start, KEYBLK)
        block_rows = block_start + jnp.arange(KEYBLK, dtype=jnp.int32)
        return (query_seq[:, None] == block_seq[None, :]) & (
            (block_rank[None, :] < limits[:, None]) | (query_rows[:, None] == block_rows[None, :])
        )

    def cross_allowed(block_start):
        return (
            query_seq[:, None] == lax.dynamic_slice_in_dim(source_seq, block_start, KEYBLK)[None, :]
        )

    inputs = hidden[0]
    stream_rows = stream[0]
    source_rows = encoder[0]
    queries = matmul(inputs, full_query).astype(jnp.bfloat16)
    self_local = matmul(stream_rows, full_pair).astype(jnp.bfloat16)
    cross_local = matmul(source_rows, full_cross_pair).astype(jnp.bfloat16)
    self_keys, cross_keys = (
        lax.all_gather(self_local, "ctx", axis=0, tiled=True),
        lax.all_gather(cross_local, "ctx", axis=0, tiled=True),
    )
    self_totals = softmax_totals(queries, self_keys, self_allowed)
    self_mixed = attend_values(queries, self_keys, self_totals, self_allowed)
    self_low = self_mixed.astype(jnp.bfloat16)
    first, first_normed, first_scale = normalize(
        inputs.astype(jnp.float32) + matmul(self_low, full_output), gains[0], shifts[0]
    )
    first_low = first.astype(jnp.bfloat16)
    cross_queries = matmul(first_low, full_cross_query).astype(jnp.bfloat16)
    cross_totals = softmax_totals(cross_queries, cross_keys, cross_allowed)
    cross_mixed = attend_values(cross_queries, cross_keys, cross_totals, cross_allowed)
    cross_low = cross_mixed.astype(jnp.bfloat16)
    second, second_normed, second_scale = normalize(
        first + matmul(cross_low, full_cross_output), gains[1], shifts[1]
    )
    second_low = second.astype(jnp.bfloat16)
    hidden_pre = matmul(second_low, full_in)
    sigmoid_pre = jax.nn.sigmoid(hidden_pre)
    activated = (hidden_pre * sigmoid_pre).astype(jnp.bfloat16)
    result, third_normed, third_scale = normalize(
        second + matmul(activated, full_out), gains[2], shifts[2]
    )
    third_grad, gain_grad_c, shift_grad_c = normalize_back(
        cotangent[0].astype(jnp.float32), third_normed, third_scale, gains[2]
    )
    branch_grad = third_grad.astype(jnp.bfloat16)
    grad_ffn_out = matmul(activated.T, branch_grad)
    slope = sigmoid_pre * (1.0 + hidden_pre * (1.0 - sigmoid_pre))
    pre_grad = (matmul(branch_grad, full_out.T) * slope).astype(jnp.bfloat16)
    grad_ffn_in = matmul(second_low.T, pre_grad)
    second_total = third_grad + matmul(pre_grad, full_in.T)
    second_grad, gain_grad_b, shift_grad_b = normalize_back(
        second_total, second_normed, second_scale, gains[1]
    )
    cross_branch = second_grad.astype(jnp.bfloat16)
    grad_cross_output = matmul(cross_low.T, cross_branch)
    cross_mixed_grad = matmul(cross_branch, full_cross_output.T).astype(jnp.bfloat16)
    cross_query_term, cross_terms = attend_back(
        cross_queries, cross_keys, cross_totals, cross_mixed, cross_mixed_grad, cross_allowed
    )
    cross_query_low = cross_query_term.astype(jnp.bfloat16)
    grad_cross_query = matmul(first_low.T, cross_query_low)
    first_total = second_grad + matmul(cross_query_low, full_cross_query.T)
    first_grad, gain_grad_a, shift_grad_a = normalize_back(
        first_total, first_normed, first_scale, gains[0]
    )
    self_branch = first_grad.astype(jnp.bfloat16)
    grad_self_output = matmul(self_low.T, self_branch)
    self_mixed_grad = matmul(self_branch, full_output.T).astype(jnp.bfloat16)
    self_query_term, self_terms = attend_back(
        queries, self_keys, self_totals, self_mixed, self_mixed_grad, self_allowed
    )
    self_sum, cross_sum = (
        lax.psum_scatter(self_terms, "ctx", scatter_dimension=0, tiled=True),
        lax.psum_scatter(cross_terms, "ctx", scatter_dimension=0, tiled=True),
    )
    self_query_low = self_query_term.astype(jnp.bfloat16)
    grad_self_query = matmul(inputs.T, self_query_low)
    input_grad = first_grad + matmul(self_query_low, full_query.T)
    self_sum_low = self_sum.astype(jnp.bfloat16)
    grad_self_pair = matmul(stream_rows.T, self_sum_low)
    stream_grad = matmul(self_sum_low, full_pair.T)
    cross_sum_low = cross_sum.astype(jnp.bfloat16)
    grad_cross_pair = matmul(source_rows.T, cross_sum_low)
    source_grad = matmul(cross_sum_low, full_cross_pair.T)
    gain_grads = jnp.stack((gain_grad_a, gain_grad_b, gain_grad_c))
    shift_grads = jnp.stack((shift_grad_a, shift_grad_b, shift_grad_c))
    (
        share_query,
        share_pair,
        share_output,
        share_cross_query,
        share_cross_pair,
        share_cross_output,
        share_in,
        share_out,
        share_gain,
        share_shift,
    ) = (
        lax.psum_scatter(
            grad_self_query.astype(jnp.bfloat16), "wa", scatter_dimension=0, tiled=True
        ).astype(jnp.float32),
        lax.psum_scatter(
            grad_self_pair.astype(jnp.bfloat16), "wa", scatter_dimension=0, tiled=True
        ).astype(jnp.float32),
        lax.psum_scatter(
            grad_self_output.astype(jnp.bfloat16), "wa", scatter_dimension=0, tiled=True
        ).astype(jnp.float32),
        lax.psum_scatter(
            grad_cross_query.astype(jnp.bfloat16), "wa", scatter_dimension=0, tiled=True
        ).astype(jnp.float32),
        lax.psum_scatter(
            grad_cross_pair.astype(jnp.bfloat16), "wa", scatter_dimension=0, tiled=True
        ).astype(jnp.float32),
        lax.psum_scatter(
            grad_cross_output.astype(jnp.bfloat16), "wa", scatter_dimension=0, tiled=True
        ).astype(jnp.float32),
        lax.psum_scatter(
            grad_ffn_in.astype(jnp.bfloat16), "wa", scatter_dimension=0, tiled=True
        ).astype(jnp.float32),
        lax.psum_scatter(
            grad_ffn_out.astype(jnp.bfloat16), "wa", scatter_dimension=0, tiled=True
        ).astype(jnp.float32),
        lax.psum_scatter(
            gain_grads.astype(jnp.bfloat16), "wa", scatter_dimension=1, tiled=True
        ).astype(jnp.float32),
        lax.psum_scatter(
            shift_grads.astype(jnp.bfloat16), "wa", scatter_dimension=1, tiled=True
        ).astype(jnp.float32),
    )
    (
        total_query,
        total_pair,
        total_output,
        total_cross_query,
        total_cross_pair,
        total_cross_output,
        total_in,
        total_out,
        total_gain,
        total_shift,
    ) = lax.psum(
        (
            share_query,
            share_pair,
            share_output,
            share_cross_query,
            share_cross_pair,
            share_cross_output,
            share_in,
            share_out,
            share_gain,
            share_shift,
        ),
        "ctx",
    )
    return (
        result.astype(jnp.bfloat16)[None],
        input_grad[None],
        stream_grad[None],
        source_grad[None],
        total_query,
        total_pair,
        total_output,
        total_cross_query,
        total_cross_pair,
        total_cross_output,
        total_in,
        total_out,
        total_gain,
        total_shift,
    )


PAIR = 2 * HEAD
PAIRS = HEADS // 2
FF = 2048
low_t = jnp.bfloat16
wide_t = jnp.float32
vmem_spec = pl.BlockSpec(memory_space=pltpu.VMEM)
smem_spec = pl.BlockSpec(memory_space=pltpu.SMEM)


def run(body, outs, ids, args, scratch=(), us=2, vmem=56):
    outs = [jax.ShapeDtypeStruct(shape, kind) for shape, kind in outs]
    arrays = [arg[0] if isinstance(arg, tuple) else arg for arg in args]

    def view(arg, ref):
        if not isinstance(arg, tuple):
            return ref
        if len(arg) == 3:
            return ref.at[arg[2]]
        return ref.at[:, :, arg[1] * D : (arg[1] + 1) * D]

    def kernel(ids, *refs):
        views = [view(arg, ref) for arg, ref in zip(args, refs)]
        body(ids, *views, *refs[len(args) :])

    moved = sum(a.size * a.dtype.itemsize for a in arrays + outs)
    return pl.pallas_call(
        kernel,
        name=getattr(body, "func", body).__name__,
        out_shape=outs,
        in_specs=[smem_spec] + [vmem_spec] * len(args),
        out_specs=[vmem_spec] * len(outs),
        scratch_shapes=[pltpu.VMEM(shape, kind) for shape, kind in scratch],
        compiler_params=pltpu.CompilerParams(vmem_limit_bytes=vmem * 1024 * 1024),
        cost_estimate=pl.CostEstimate(flops=us * 1_000_000_000, bytes_accessed=moved, transcendentals=0),
    )(ids, *arrays)


def dot_nn(a, b):
    return lax.dot_general(a, b, (((1,), (0,)), ((), ())), preferred_element_type=wide_t)


def dot_nt(a, b):
    return lax.dot_general(a, b, (((1,), (1,)), ((), ())), preferred_element_type=wide_t)


def dot_tn(a, b):
    return lax.dot_general(a, b, (((0,), (0,)), ((), ())), preferred_element_type=wide_t)


def at16(start, size=16):
    return pl.ds(pl.multiple_of(start, 16), size)


def at128(start, size=128):
    return pl.ds(pl.multiple_of(start, 128), size)


def half_mask(shape, axis, core):
    return (lax.broadcasted_iota(jnp.int32, shape, axis) // HEAD) == core


def attend_rows(q_ref, k_ref, vt_ref, bias_ref, s_ref, ot_ref, lse_ref):
    keys, rows = bias_ref.shape
    tile = min(1024, keys)
    tiles = keys // tile

    def step(p, carry):
        q = q_ref[:, at128(p * PAIR)]
        for h in range(2):
            mine = half_mask((rows, PAIR), 1, h)
            own_q = jnp.where(mine, q, jnp.zeros_like(q))
            top = jnp.full((8, rows), neg_fill, wide_t)
            for t in range(tiles):
                here = slice(t * tile, (t + 1) * tile)
                s = dot_nt(k_ref[here, at128(p * PAIR)], own_q) + bias_ref[here, :]
                s_ref[h, here, :] = s
                top = jnp.maximum(top, jnp.max(s.reshape(tile // 8, 8, rows), axis=0))
            top = jnp.max(top, axis=0, keepdims=True)
            total = jnp.zeros((8, rows), wide_t)
            mixed = jnp.zeros((HEAD, rows), wide_t)
            features = pl.ds(pl.multiple_of(p * PAIR + h * HEAD, HEAD), HEAD)
            for t in range(tiles):
                here = slice(t * tile, (t + 1) * tile)
                w = jnp.exp(s_ref[h, here, :] - top)
                total = total + jnp.sum(w.reshape(tile // 8, 8, rows), axis=0)
                mixed = mixed + dot_nn(vt_ref[features, here], w.astype(low_t))
            total = jnp.sum(total, axis=0, keepdims=True)
            ot_ref[features, :] = mixed / total
            lse_ref[pl.ds(p * 2 + h, 1), :] = top + jnp.log(total)
        return carry

    lax.fori_loop(0, PAIRS, step, 0)


def finish_rows(ot_ref, low_out, mixed_out):
    mixed = ot_ref[...].T
    low_out[...] = mixed.astype(low_t)
    mixed_out[...] = mixed


def three_parts(value):
    high = value.astype(low_t).astype(wide_t)
    rest = value - high
    middle = rest.astype(low_t).astype(wide_t)
    return high, middle, rest - middle


def side_rows(lse, grad_low, mixed, row_data):
    product = grad_low.astype(wide_t) * mixed[...]
    lane = lax.broadcasted_iota(jnp.int32, (grad_low.shape[0], PAIR), 1)
    sums = jnp.zeros((grad_low.shape[0], PAIR), wide_t)
    for p in range(PAIRS):
        piece = product[:, p * PAIR : (p + 1) * PAIR]
        for h in range(2):
            mine = half_mask(piece.shape, 1, h)
            offset = jnp.sum(jnp.where(mine, piece, 0.0), axis=1, keepdims=True)
            sums = jnp.where(lane == p * 2 + h, offset, sums)
    offsets = sums.T
    seq = row_data[16:17, :]
    onehot = [(seq == float(n)).astype(wide_t) for n in range(4)]
    sides = []
    for p in range(PAIRS):
        pieces = []
        for h in range(2):
            head = p * 2 + h
            pieces += three_parts(-lse[head : head + 1, :])
            pieces += three_parts(-offsets[head : head + 1, :])
        sides.append(jnp.concatenate(pieces + onehot, axis=0).astype(low_t))
    return sides


def side_lanes(side, core):
    side = side.astype(wide_t)
    head = jnp.where(core == 0, side[0:6], side[6:12])
    gap = jnp.zeros((5, side.shape[1]), wide_t)
    rest = jnp.zeros((HEAD - 20, side.shape[1]), wide_t)
    half = jnp.concatenate((head[0:3], gap, head[3:6], gap, side[12:16], rest), axis=0)
    return jnp.concatenate((half, half), axis=0).T.astype(low_t)


def assemble(ids, parts, column, outs):
    for chip, other, block in parts:
        own = chip * 2 + (ids[1] ^ other)
        for e in range(4):
            rows = at16((ids[2] ^ e) * 128 + own * 16)
            start = column
            for out in outs:
                width = out.shape[1]
                out[rows, :] = block[e * 16 : (e + 1) * 16, start : start + width]
                start += width


def project_pairs(parts, w_pair, k_ref, vt_ref, wvt_ref):
    wvt_ref[...] = w_pair[:, D:].astype(wide_t).T.astype(low_t)
    for n, part in enumerate(parts):
        for k in range(PAIRS):
            rows = part.shape[1]
            start = (n * 4 + k) * rows
            k_ref[start : start + rows, :] = dot_nn(part[k], w_pair[:, :D]).astype(low_t)
            vt_ref[:, start : start + rows] = dot_nt(wvt_ref[...], part[k]).astype(low_t)


def self_forward(ids, hidden, own, other, *refs):
    slices, (cols, row_data), refs = refs[:8], refs[8:10], refs[10:]
    out, mixed, lse, wq, wkv, q_ref, k_ref, vt_ref, wvt_ref, bias_ref, s_ref, ot_ref = refs
    rows = hidden.shape[0]
    parts = [(ids[0] ^ k, n, slices[n * 4 + k]) for n in range(2) for k in range(4)]
    assemble(ids, parts, 0, (wq, wkv))
    q_ref[...] = (dot_nn(hidden[...], wq[...]).astype(low_t) * 0.125).astype(low_t)
    project_pairs((own, other), wkv, k_ref, vt_ref, wvt_ref)
    seq, limit = row_data[16:17, :], row_data[17:18, :]
    for b in range(8):
        seen = (cols[:, b : b + 1] == seq) & (cols[:, 8 + b : 9 + b] < limit)
        bias_ref[b * rows : (b + 1) * rows, :] = jnp.where(seen, 0.0, neg_fill)
    mine = lax.broadcasted_iota(jnp.int32, (rows, rows), 0) == lax.broadcasted_iota(
        jnp.int32, (rows, rows), 1
    )
    block = at128(ids[0] * rows, rows)
    bias_ref[block, :] = jnp.where(mine, 0.0, bias_ref[block, :])
    attend_rows(q_ref, k_ref, vt_ref, bias_ref, s_ref, ot_ref, lse)
    finish_rows(ot_ref, out, mixed)


def layer_norm(values, gain_row, shift_row):
    mean = jnp.mean(values, axis=1, keepdims=True)
    centred = values - mean
    scale = lax.rsqrt(jnp.mean(centred * centred, axis=1, keepdims=True) + layer_eps)
    normed = centred * scale
    return normed * gain_row + shift_row, normed, scale


def layer_norm_back(grad, normed, scale, gain_row):
    gain_term = jnp.sum(grad * normed, axis=0, keepdims=True)
    shift_term = jnp.sum(grad, axis=0, keepdims=True)
    scaled = grad * gain_row
    grad_in = scale * (
        scaled
        - jnp.mean(scaled, axis=1, keepdims=True)
        - normed * jnp.mean(scaled * normed, axis=1, keepdims=True)
    )
    return grad_in, gain_term, shift_term


def cross_forward(ids, hidden, self_low, own, other, *refs):
    slices, (cols, row_data) = refs[:2], refs[2:4]
    first, normed, scale_out, first_low, cross_low, mixed, lse, cross_q = refs[4:12]
    wo, wcq, wckv, wco, gs, q_ref, k_ref, vt_ref, wvt_ref, bias_ref, s_ref, ot_ref = refs[12:]
    for n in range(2):
        for e in range(4):
            rows = at16(e * 128 + (ids[1] ^ n) * 64, 64)
            start = 0
            for out in (wo, wcq, wckv, wco):
                width = out.shape[1]
                out[rows, :] = slices[n][e, :, start : start + width]
                start += width
    for e in range(4):
        gs[:, e * 128 : (e + 1) * 128] = slices[0][e, :16, 5 * D :]
    gain, shift = gs[0:1, :].astype(wide_t), gs[3:4, :].astype(wide_t)
    value, n0, s0 = layer_norm(
        hidden[...].astype(wide_t) + dot_nn(self_low[...], wo[...]), gain, shift
    )
    first[...] = value
    normed[...] = n0
    scale_out[...] = jnp.broadcast_to(s0, scale_out.shape)
    low = value.astype(low_t)
    first_low[...] = low
    q = dot_nn(low, wcq[...]).astype(low_t)
    cross_q[...] = q
    q_ref[...] = (q * 0.125).astype(low_t)
    rows = hidden.shape[0]
    project_pairs((own, other), wckv, k_ref, vt_ref, wvt_ref)
    for b in range(8):
        seen = cols[:, 16 + b : 17 + b] == row_data[16:17, :]
        bias_ref[b * rows : (b + 1) * rows, :] = jnp.where(seen, 0.0, neg_fill)
    attend_rows(q_ref, k_ref, vt_ref, bias_ref, s_ref, ot_ref, lse)
    finish_rows(ot_ref, cross_low, mixed)


def feed_forward(ids, first, cross_low, cross_mixed, lse, row_data, cross_q, wco, gs, cotangent, *refs):
    slices = refs[0:2]
    result, dealt, second_grad, keep, send, sums, slope, wins, wouts = refs[2:]
    half_ff = FF // 2
    for n, part in enumerate(slices):
        core = ids[1] ^ n
        for chip in range(4):
            for e in range(4):
                w, here = ids[2] ^ e, slice(e * 16, (e + 1) * 16)
                rows = at16(w * 128 + (chip * 2 + core) * 16)
                for g in range(4):
                    row = w * 256 + ((chip % 2) * 2 + core) * 64 + g * 16
                    wouts[(chip // 2) ^ ids[1], at16(row), :] = part[
                        chip, here, FF + g * D : FF + (g + 1) * D
                    ]
                    for h in range(2):
                        column = g * 512 + h * 256
                        wins[h ^ ids[1], rows, g * 256 : (g + 1) * 256] = part[
                            chip, here, column : column + 256
                        ]
    gains, shifts = gs[0:3, :].astype(wide_t), gs[3:6, :].astype(wide_t)
    second, n1, s1 = layer_norm(
        first[...] + dot_nn(cross_low[...], wco[...]), gains[1:2], shifts[1:2]
    )
    low = second.astype(low_t)
    for out in (keep, send):
        out[:, 2 * half_ff : 2 * half_ff + D] = low
        out[:, 2 * half_ff + 2 * D : 2 * half_ff + 3 * D] = cross_low[...]
    width = 512
    chunks = [(n, c) for n in range(2) for c in range(FF // 2 // width)]
    total = second
    for n, c in chunks:
        here = slice(c * width, (c + 1) * width)
        wide = slice(n * half_ff + c * width, n * half_ff + (c + 1) * width)
        pre = dot_nn(low, wins[n, :, here])
        sig = 1.0 / (1.0 + jnp.exp(-pre))
        act = (pre * sig).astype(low_t)
        (keep, send)[n][:, half_ff + c * width : half_ff + (c + 1) * width] = act
        slope[:, wide] = sig * (1.0 + pre * (1.0 - sig))
        total = total + dot_nn(act, wouts[n, here, :])
    value, n2, s2 = layer_norm(total, gains[2:3], shifts[2:3])
    result[...] = value.astype(low_t)
    third, gain_c, shift_c = layer_norm_back(cotangent[...].astype(wide_t), n2, s2, gains[2:3])
    third_low = third.astype(low_t)
    for out in (keep, send):
        out[:, 2 * half_ff + D : 2 * half_ff + 2 * D] = third_low
    total = third
    for n, c in chunks:
        here = slice(c * width, (c + 1) * width)
        wide = slice(n * half_ff + c * width, n * half_ff + (c + 1) * width)
        back = (dot_nt(third_low, wouts[n, here, :]) * slope[:, wide]).astype(low_t)
        (keep, send)[n][:, here] = back
        total = total + dot_nt(back, wins[n, :, here])
    grad, gain_b, shift_b = layer_norm_back(total, n1, s1, gains[1:2])
    second_grad[...] = grad
    grad_low = grad.astype(low_t)
    for out, core in ((keep, ids[1]), (send, 1 - ids[1])):
        half = grad_low[:, : D // 2]
        out[:, 2 * half_ff + 3 * D :] = jnp.where(core == 0, half, grad_low[:, D // 2 :])
    mixed = dot_nt(grad_low, wco[...]).astype(low_t)
    rows = grad_low.shape[0]
    sides = side_rows(lse, mixed, cross_mixed, row_data)
    for p in range(PAIRS):
        dealt[p, :rows, :PAIR] = cross_q[:, p * PAIR : (p + 1) * PAIR]
        dealt[p, :rows, PAIR:] = mixed[:, p * PAIR : (p + 1) * PAIR]
        dealt[p, rows:, :] = sides[p]
    zero = jnp.zeros_like(gain_b)
    sums[...] = jnp.concatenate((zero, gain_b, gain_c, zero, shift_b, shift_c, zero, zero), axis=0)


def grads_a(ids, keep, received, out, g_in, g_out, g_cross):
    half = FF // 2

    def both(left, right):
        return (dot_tn(keep[:, left], keep[:, right]) + dot_tn(received[:, left], received[:, right])).astype(low_t)

    at = [0, half] + [2 * half + n * D for n in range(4)]
    pre, act = slice(at[0], at[1]), slice(at[1], at[2])
    second, branch, low = (slice(at[n], at[n] + D) for n in (2, 3, 4))
    g_in[...] = both(second, pre)
    g_out[...] = both(act, branch)
    g_cross[...] = both(low, slice(at[5], at[5] + D // 2))
    for chip in range(4):
        for e in range(4):
            w, here = ids[2] ^ e, slice(e * 32, (e + 1) * 32)
            rows = at16(w * 128 + chip * 32, 32)
            out[chip, here, :half] = g_in[rows, :]
            for g in range(2):
                out[chip, here, half + g * D : half + (g + 1) * D] = g_out[
                    at16(w * 256 + chip * 64 + g * 32, 32), :
                ]
            out[chip, here, half + 2 * D :] = g_cross[rows, :]


def grads_b(ids, first_low, cross_dq, self_low, branch, sums, dkv, out, g_query, g_output):
    g_query[...] = dot_tn(first_low[...], cross_dq[...]).astype(low_t)
    g_output[...] = dot_tn(self_low[...], branch[...]).astype(low_t)
    row = jnp.concatenate((sums[...], jnp.zeros_like(sums[...])), axis=0).astype(low_t)
    rows = dkv.shape[2]
    for e in range(4):
        w, here = ids[2] ^ e, slice(e * 16, (e + 1) * 16)
        piece = row[:, :128]
        for k in range(1, 4):
            piece = jnp.where(w == k, row[:, k * 128 : (k + 1) * 128], piece)
        for device in range(8):
            own = at16(w * 128 + device * 16)
            out[device, here, :D] = g_query[own, :]
            out[device, here, D : 2 * D] = g_output[own, :]
            out[device, here, 2 * D : 2 * D + 128] = piece
    for device in range(8):
        for n in range(2):
            start = 2 * D + 128 + n * rows
            out[device, :, start : start + rows] = dkv[device, n * HEAD : (n + 1) * HEAD, :]


def pair_setup(is_self, ids, own, other, w_pair, cols, *refs):
    if is_self:
        hidden_own, hidden_other, w_query, q_all, k_all, v_all, kt, turn = refs
    else:
        k_all, v_all, kt, turn = refs
    chip, core = ids[0], ids[1]
    rows = own.shape[1]
    mine = half_mask((rows, PAIR), 1, core)
    features = pl.ds(pl.multiple_of(core * HEAD, HEAD), HEAD)
    lane = lax.broadcasted_iota(jnp.int32, (rows, PAIR), 1) % HEAD
    ones_v = jnp.where((lane >= 8) & (lane < 11), 1.0, 0.0).astype(low_t)
    pair = at128(chip * PAIR)
    wk, wv = w_pair[:, pair], w_pair[:, at128(D + chip * PAIR)]
    if is_self:
        wq = w_query[:, pair]
    for n, part in enumerate((own, other)):
        for k in range(4):
            b = n * 4 + k
            here = slice(b * rows, (b + 1) * rows)
            column = b if is_self else 16 + b
            seq = cols[:, column : column + 1].astype(jnp.int32)
            other_seq = (lane >= 16) & (lane < 20) & (lane != seq + 16)
            ones_k = jnp.where(other_seq, neg_fill, jnp.where(lane < 3, 1.0, 0.0)).astype(low_t)
            key = dot_nn(part[k], wk)
            turn[...] = key.T
            kt[:, here] = turn[features, :].astype(low_t)
            k_all[here, :] = jnp.where(mine, key.astype(low_t), ones_k)
            v_all[here, :] = jnp.where(mine, dot_nn(part[k], wv).astype(low_t), ones_v)
            if is_self:
                q_all[b] = dot_nn((hidden_own, hidden_other)[n][k], wq).astype(low_t)


def pair_back(is_self, ids, *refs):
    if is_self:
        q_parts, do_own, do_other, k_all, v_all, kt, cols, row_data, back = refs[:9]
        do_parts = (do_own, do_other)
    else:
        both_own, both_other, k_all, v_all, kt, back, dkv = refs[:7]
        both_parts = (both_own, both_other)
    q_all, do_all, dq_t, dk, dv, rank, turn = refs[-7:]
    core = ids[1]
    rows = q_all.shape[1]
    keys = 8 * rows
    mine = half_mask((rows, PAIR), 1, core)
    features = pl.ds(pl.multiple_of(core * HEAD, HEAD), HEAD)
    for n in range(2):
        for k in range(4):
            b = n * 4 + k
            if is_self:
                here = slice(b * rows, (b + 1) * rows)
                rank[here, :] = jnp.broadcast_to(cols[:, 8 + b : 9 + b], (rows, 128))
                q, do = q_parts[b], do_parts[n][k, :rows, :]
                side = jnp.concatenate(
                    (do_parts[n][k, rows : rows + 16, :], do_parts[n][k, rows + 16 :, :]), axis=1
                )
            else:
                q, do = both_parts[n][k, :rows, :PAIR], both_parts[n][k, :rows, PAIR:]
                side = both_parts[n][k, rows:, :]
            side = side_lanes(side, core)
            q_all[b] = jnp.where(mine, (q * 0.125).astype(low_t), side)
            do_all[b] = jnp.where(mine, do, side)
    dk[...] = jnp.zeros_like(dk)
    dv[...] = jnp.zeros_like(dv)
    tile = min(1024, keys)

    def step(b, carry):
        q, do = q_all[b], do_all[b]
        dqt = jnp.zeros((HEAD, rows), wide_t)
        for t in range(keys // tile):
            here = slice(t * tile, (t + 1) * tile)
            w = jnp.exp(dot_nt(k_all[here, :], q))
            if is_self:
                ranks = jnp.concatenate((rank[here, :],) * (rows // 128), axis=1)
                index = lax.broadcasted_iota(jnp.int32, (tile, rows), 0)
                own = lax.broadcasted_iota(jnp.int32, (tile, rows), 1) + (b * rows - t * tile)
                w = jnp.where((ranks < row_data[pl.ds(8 + b, 1), :]) | (index == own), w, 0.0)
            ds = (w * dot_nt(v_all[here, :], do)).astype(low_t)
            dv[here, :] += dot_nn(w.astype(low_t), do)
            dk[here, :] += dot_nn(ds, q)
            dqt = dqt + dot_nn(kt[:, here], ds)
        dq_t[b] = (dqt * 0.125).astype(low_t)
        return carry

    lax.fori_loop(0, 8, step, 0)
    for n in range(2):
        for k in range(4):
            b = n * 4 + k
            device = k * 2 + (core ^ n)
            here = slice(b * rows, (b + 1) * rows)
            back[device, :HEAD, :] = dq_t[b]
            out, start = (back, HEAD) if is_self else (dkv, 0)
            for value in (dk, dv):
                turn[...] = value[here, :].T
                out[device, start : start + HEAD, :] = turn[features, :].astype(low_t)
                start += HEAD


def pair_grads(is_self, ids, grads, own, other, *refs):
    dw = refs[-1]
    totals = [jnp.zeros((HEAD, D), wide_t) for n in range(grads.shape[1] // HEAD)]
    for n in range(2):
        for k in range(4):
            device = k * 2 + (ids[1] ^ n)
            for m in range(len(totals)):
                source = refs[:2] if is_self and m == 0 else (own, other)
                totals[m] += dot_nn(grads[device, m * HEAD : (m + 1) * HEAD, :], source[n][k])
    for n, value in enumerate(totals):
        for w in range(4):
            dw[w, n * HEAD : (n + 1) * HEAD, :] = value[:, w * 128 : (w + 1) * 128].astype(low_t)


def turned(value):
    return value.astype(wide_t).T.astype(low_t)


def first_back(ids, back, second_grad, normed, scale, self_mixed, lse, row_data, gs, wcq, wo, sums_in, *refs):
    first_grad, branch, dealt, dq, sums = refs
    dq[...] = turned(back[...].reshape(D, back.shape[2]))
    total = second_grad[...] + dot_nt(dq[...], wcq[...])
    grad, gain_a, shift_a = layer_norm_back(
        total, normed[...], scale[:, 0:1], gs[0:1, :].astype(wide_t)
    )
    first_grad[...] = grad
    low = grad.astype(low_t)
    branch[...] = low
    mixed = dot_nt(low, wo[...]).astype(low_t)
    rows = low.shape[0]
    sides = side_rows(lse, mixed, self_mixed, row_data)
    for p in range(PAIRS):
        dealt[p, :rows, :] = mixed[:, p * PAIR : (p + 1) * PAIR]
        dealt[p, rows : rows + 16, :] = sides[p][:, :PAIR]
        dealt[p, rows + 16 :, :] = sides[p][:, PAIR:]
    zero = jnp.zeros_like(gain_a)
    sums[...] = sums_in[...] + jnp.concatenate(
        (gain_a, zero, zero, shift_a, zero, zero, zero, zero), axis=0
    )


def source_back(ids, parts, wckv, out, dkv):
    rows = out.shape[0]
    for device in range(8):
        for n in range(2):
            start = 2 * D + 128 + n * rows
            dkv[n * D + device * HEAD : n * D + (device + 1) * HEAD, :] = parts[
                device, :, start : start + rows
            ]
    out[...] = dot_nt(turned(dkv[...]), wckv[...])


def hidden_back(ids, back, first_grad, wq, wkv, hidden_grad, stream_grad, all_t):
    for device in range(8):
        for n in range(3):
            all_t[n * D + device * HEAD : n * D + (device + 1) * HEAD, :] = back[
                device, n * HEAD : (n + 1) * HEAD, :
            ]
    hidden_grad[...] = first_grad[...] + dot_nt(turned(all_t[:D, :]), wq[...])
    stream_grad[...] = dot_nt(turned(all_t[D:, :]), wkv[...])


def add_parts(parts, rows, columns):
    total = parts[0, rows, columns].astype(wide_t)
    for n in range(1, parts.shape[0]):
        total = total + parts[n, rows, columns].astype(wide_t)
    return total.astype(low_t)


def add_chips(ids, parts, dw, *outs):
    width = parts.shape[2]
    for e in range(4):
        outs[e][:, :width] = add_parts(parts, slice(e * 32, (e + 1) * 32), slice(None))
        piece = dw[ids[2] ^ e]
        for g in range(4):
            outs[e][:, width + g * 128 : width + (g + 1) * 128] = piece[g * 32 : (g + 1) * 32, :]


def end_sums(ids, parts, dw, *outs):
    width = 2 * D + 128
    for e in range(4):
        outs[e][:, :width] = add_parts(parts, slice(e * 16, (e + 1) * 16), slice(0, width))
        outs[e][:, width : width + 128] = jnp.zeros((16, 128), low_t)
        piece = dw[ids[2] ^ e]
        for g in range(12):
            start = width + 128 + g * 128
            outs[e][:, start : start + 128] = piece[g * 16 : (g + 1) * 16, :]


def add_shards(ids, *refs):
    out = refs[8]

    def total(parts):
        value = parts[0][...].astype(wide_t)
        for part in parts[1:]:
            value = value + part[...].astype(wide_t)
        return value.astype(low_t)

    first, last = total(refs[:4]), total(refs[4:8])
    width, half = first.shape[1], last.shape[1] // 2
    for k in range(4):
        out[k, :, :width] = first
        out[k, :16, width:] = last[:, :half]
        out[k, 16:, width:] = last[:, half:]


def place_all(ids, own, other, *refs):
    g_in, g_out, g_cross, g_cross_pair, g_cross_query, g_output, gains, shifts, g_query, g_pair = refs[:10]
    pair_t, all_t = refs[10:]
    half = FF // 2
    start_cross = half + 2 * D
    start_pair = start_cross + D // 2
    start_end = start_pair + 4 * 128
    half_end = own.shape[2] - start_end
    for n, part in enumerate((own, other)):
        core = ids[1] ^ n
        for chip in range(4):
            rows = slice(chip * 32, (chip + 1) * 32)
            device = chip * 2 + core
            for k in range(4):
                g_in[rows, at128(k * 512 + core * 256, 256)] = part[
                    chip, :, k * 256 : (k + 1) * 256
                ].astype(wide_t)
            for g in range(2):
                g_out[at16(core * 256 + chip * 64 + g * 32, 32), :] = part[
                    chip, :, half + g * D : half + (g + 1) * D
                ].astype(wide_t)
            g_cross[rows, at128(core * 256, 256)] = part[chip, :, start_cross:start_pair].astype(wide_t)
            for g in range(4):
                column = start_pair + g * 128
                row = (g // 2) * D + device * HEAD + (g % 2) * 32
                pair_t[at16(row, 32), :] = part[chip, :, column : column + 128].astype(wide_t)

            def piece(column, width):
                row, at = (0, column) if column < half_end else (16, column - half_end)
                return part[chip, row : row + 16, start_end + at : start_end + at + width].astype(wide_t)

            own_rows = at16(device * 16)
            for column in range(0, D, 128):
                g_cross_query[own_rows, column : column + 128] = piece(column, 128)
                g_output[own_rows, column : column + 128] = piece(D + column, 128)
            if n == 0 and chip == 0:
                norms = piece(2 * D, 128)
                gains[...], shifts[...] = norms[0:3], norms[3:6]
            for g in range(12):
                row = (g // 4) * D + device * HEAD + (g % 4) * 16
                all_t[at16(row), :] = piece(2 * D + 256 + g * 128, 128)
    g_cross_pair[...] = pair_t[...].T
    g_query[...] = all_t[:D, :].T
    g_pair[...] = all_t[D:, :].T


def pack_start(ids, stream, source, wq, wkv, ffn_in, ffn_out, many, pack):
    own = ids[0] * 2 + ids[1]
    for k in range(4):
        many[k, :, :D] = stream[...]
        many[k, :, D:] = source[...]
        start = 3 * D + FF + k * D
        pack[:, start : start + D] = ffn_out[at16(own * 64 + k * 16), :]
    pack[:, :D] = wq[at16(own * 16), :]
    pack[:, D : 3 * D] = wkv[at16(own * 16), :]
    pack[:, 3 * D : 3 * D + FF] = ffn_in[at16(own * 16), :]


def pack_more(ids, *refs):
    weights, gain, shift, rows_in, pack, many = refs[:4], *refs[4:]
    rows = at16(ids[1] * 64, 64)
    norms = (gain[...].astype(wide_t), shift[...].astype(wide_t), jnp.zeros((58, 128), wide_t))
    norms = jnp.concatenate(norms, axis=0).astype(low_t)
    for k in range(4):
        start = 0
        for w in weights:
            pack[k, :, start : start + w.shape[1]] = w[rows, :]
            start += w.shape[1]
        pack[k, :, start:] = norms
        many[k] = rows_in[...]


def mask_data(ids, order, ranks, limits, cols, row_data, all_rows):
    rows = cols.shape[0]
    ends = [ids[3]]
    for n in range(1, 4):
        ends.append(ends[-1] + ids[3 + n])

    def sequence(position):
        return sum((position >= end).astype(wide_t) for end in ends)

    for n in range(2):
        for k in range(4):
            b = n * 4 + k
            device = k * 2 + (ids[1] ^ n)
            here = at128(device * rows, rows)
            index = lax.broadcasted_iota(jnp.int32, (1, rows), 1) + device * rows
            all_rows[b : b + 1, :] = sequence(order[:, here])
            all_rows[8 + b : 9 + b, :] = ranks[:, here].astype(wide_t)
            all_rows[16 + b : 17 + b, :] = sequence(index)
            row_data[8 + b : 9 + b, :] = limits[:, here].astype(wide_t)
    row_data[0:8, :] = all_rows[0:8, :]
    all_rows[24:32, :] = jnp.zeros((8, rows), wide_t)
    all_rows[24:25, :] = all_rows[pl.ds(ids[0], 1), :]
    row_data[16:24, :] = jnp.zeros((8, rows), wide_t)
    row_data[16:17, :] = all_rows[pl.ds(ids[0], 1), :]
    row_data[17:18, :] = row_data[pl.ds(8 + ids[0], 1), :]
    cols[:, :32] = all_rows[...].T


def pack_first(ids, *refs):
    parts, (one, two) = refs[:4], refs[4:]
    width = one.shape[1]
    for e in range(4):
        here = slice(e * 16, (e + 1) * 16)
        one[here, :] = parts[e][:, :width]
        for k in range(4):
            two[k, here, :] = parts[e][:, width:]


def core_swap(value):
    return lax.ppermute(value, "core", [(0, 1), (1, 0)])


def chip_swaps(parts):
    moves = [[(i, i ^ k) for i in range(4)] for k in range(4)]
    return [parts[0]] + [lax.ppermute(parts[k], "chip", moves[k]) for k in range(1, 4)]


def shard_swaps(parts):
    moves = [[(i, i ^ k) for i in range(4)] for k in range(4)]
    return [parts[0]] + [lax.ppermute(parts[k], "wa", moves[k]) for k in range(1, 4)]


def deal(value):
    return lax.all_to_all(value, "chip", 0, 0, tiled=True)


def deal_all(value):
    return lax.all_to_all(value, ("chip", "core"), 0, 0, tiled=True)


def deal_both(value):
    own = deal(value)
    return own, core_swap(own)


def after(value, *others):
    return lax.optimization_barrier((value,) + others)[0]


def fast_shards(
    hidden,
    stream,
    encoder,
    lengths,
    order,
    ranks,
    thresholds,
    self_query,
    self_key_value,
    self_output,
    cross_query,
    cross_key_value,
    cross_output,
    ffn_in,
    ffn_out,
    norm_gain,
    norm_shift,
    cotangent,
):
    rows, keys = hidden.shape[1], order.shape[1]
    chip, core, mw = lax.axis_index("chip"), lax.axis_index("core"), lax.axis_index("wa")
    ids = jnp.concatenate((jnp.stack((chip, core, mw)).astype(jnp.int32), lengths[0]))
    inputs = hidden[0]

    many, pack1 = run(
        pack_start,
        [((4, rows, 2 * D), low_t), ((16, 3 * D + 2 * FF), low_t)],
        ids,
        [stream[0], encoder[0], self_query, self_key_value, ffn_in, ffn_out],
    )
    x_own = deal(many)
    shards1 = shard_swaps([pack1] * 4)
    copies2, hidden_copies = run(
        pack_more,
        [((4, 64, 5 * D + 128), low_t), ((4, rows, D), low_t)],
        ids,
        [after(self_output, pack1), cross_query, cross_key_value, cross_output, norm_gain, norm_shift]
        + [inputs],
    )
    cols, row_data = run(
        mask_data,
        [((rows, 32), wide_t), ((24, rows), wide_t)],
        ids,
        [order, ranks, thresholds],
        [((32, rows), wide_t)],
    )
    part1, copies3 = run(
        pack_first,
        [((64, 3 * D), low_t), ((4, 64, 2 * FF), low_t)],
        ids,
        [after(shards1[0], x_own, cols, copies2)] + shards1[1:],
    )
    slices1 = chip_swaps([part1] * 4)
    slices1 = slices1 + [core_swap(part) for part in slices1]
    shards2 = lax.all_to_all(after(copies2, x_own), "wa", 0, 0, tiled=True)
    x_other = core_swap(after(x_own, part1))
    stream_own, stream_other = (x_own, 0), (x_other, 0)
    source_own, source_other = (x_own, 1), (x_other, 1)

    attend_scratch = [
        ((rows, D), low_t),
        ((keys, D), low_t),
        ((D, keys), low_t),
        ((D, D), low_t),
        ((keys, rows), wide_t),
        ((2, keys, rows), wide_t),
        ((D, rows), wide_t),
    ]
    self_low, self_mixed, self_lse, wq, wkv = run(
        self_forward,
        [((rows, D), low_t), ((rows, D), wide_t), ((HEADS, rows), wide_t)]
        + [((D, D), low_t), ((D, 2 * D), low_t)],
        ids,
        [inputs, stream_own, stream_other, *slices1, cols, row_data],
        attend_scratch,
        us=15,
    )
    shards2_other = core_swap(after(shards2, self_low))
    slices3 = deal(after(copies3, shards2, self_low))
    (
        first,
        normed,
        scale,
        first_low,
        cross_low,
        cross_mixed,
        cross_lse,
        cross_q,
        wo,
        wcq,
        wckv,
        wco,
        gs,
    ) = run(
        cross_forward,
        [((rows, D), wide_t)] * 2
        + [((rows, 128), wide_t)]
        + [((rows, D), low_t)] * 2
        + [((rows, D), wide_t), ((HEADS, rows), wide_t), ((rows, D), low_t)]
        + [((D, D), low_t), ((D, D), low_t), ((D, 2 * D), low_t), ((D, D), low_t), ((16, D), low_t)],
        ids,
        [inputs, self_low, source_own, source_other, shards2, shards2_other, cols, row_data],
        attend_scratch,
        us=15,
    )
    slices3_other = core_swap(after(slices3, cross_low))
    hidden_own = deal(after(hidden_copies, slices3))
    width_s = 2 * FF // 2 + 3 * D + D // 2
    result, cross_dealt, second_grad, keep_a, send_a, sums = run(
        feed_forward,
        [
            ((rows, D), low_t),
            ((PAIRS, rows + 16, 2 * PAIR), low_t),
            ((rows, D), wide_t),
            ((rows, width_s), low_t),
            ((rows, width_s), low_t),
            ((8, D), wide_t),
        ],
        ids,
        [first, cross_low, cross_mixed, cross_lse, row_data, cross_q, wco, gs]
        + [cotangent[0], slices3, slices3_other],
        [((rows, FF), wide_t), ((2, D, FF // 2), low_t), ((2, FF // 2, D), low_t)],
        us=8,
    )
    head_shapes = [((keys, PAIR), low_t)] * 2 + [((HEAD, keys), low_t)]
    cross_head = run(
        functools.partial(pair_setup, False),
        head_shapes,
        ids,
        [source_own, source_other, wckv, after(cols, cross_dealt)],
        [((PAIR, rows), wide_t)],
        us=4,
    )
    both_own = deal(after(cross_dealt, hidden_own))
    both_other = core_swap(after(both_own, cross_head[0]))
    width_a = FF // 2 + 2 * D + D // 2
    (dealt_a,) = run(
        grads_a,
        [((4, 128, width_a), low_t)],
        ids,
        [keep_a, core_swap(after(send_a, hidden_own))],
        [((D, FF // 2), low_t), ((FF // 2, D), low_t), ((D, D // 2), low_t)],
        us=6,
    )
    rows_a = deal(after(dealt_a, both_own))

    back_scratch = (
        [((8, rows, PAIR), low_t)] * 2
        + [((8, HEAD, rows), low_t)]
        + [((keys, PAIR), wide_t)] * 3
        + [((PAIR, rows), wide_t)]
    )
    cross_dq_t, cross_dkv = run(
        functools.partial(pair_back, False),
        [((8, HEAD, rows), low_t), ((8, 2 * HEAD, rows), low_t)],
        ids,
        [after(both_own, dealt_a), both_other, *cross_head],
        back_scratch,
        us=16,
    )
    hidden_other = core_swap(after(hidden_own, both_own))
    self_head = run(
        functools.partial(pair_setup, True),
        [((8, rows, PAIR), low_t)] + head_shapes,
        ids,
        [stream_own, stream_other, wkv, after(cols, cross_dq_t), hidden_own, hidden_other, wq],
        [((PAIR, rows), wide_t)],
        us=4,
    )
    (cross_dw,) = run(
        functools.partial(pair_grads, False),
        [((4, 2 * HEAD, 128), low_t)],
        ids,
        [cross_dkv, source_own, source_other],
    )
    cross_back = deal_all(after(cross_dq_t, rows_a, self_head[0]))
    shards_a = run(
        add_chips,
        [((32, width_a + 512), low_t)] * 4,
        ids,
        [after(rows_a, cross_dq_t), cross_dw],
    )
    first_grad, self_branch, self_dealt, cross_dq, sums = run(
        first_back,
        [
            ((rows, D), wide_t),
            ((rows, D), low_t),
            ((PAIRS, rows + 32, PAIR), low_t),
            ((rows, D), low_t),
            ((8, D), wide_t),
        ],
        ids,
        [after(cross_back, *shards_a), second_grad, normed, scale, self_mixed, self_lse, row_data, gs, wcq, wo, sums],
        us=4,
    )
    do_own = deal(self_dealt)
    moved_a = shard_swaps([after(part, first_grad) for part in shards_a])
    (dealt_b,) = run(
        grads_b,
        [((8, 64, 2 * D + 128 + 2 * rows), low_t)],
        ids,
        [first_low, cross_dq, self_low, self_branch, sums, cross_dkv],
        [((D, D), low_t)] * 2,
        us=3,
    )
    rows_b = deal_all(after(dealt_b, do_own))
    do_other = core_swap(after(do_own, dealt_b))
    (self_back_t,) = run(
        functools.partial(pair_back, True),
        [((8, 3 * HEAD, rows), low_t)],
        ids,
        [self_head[0], after(do_own, dealt_b, *shards_a), do_other, *self_head[1:], cols, row_data],
        back_scratch,
        us=16,
    )
    (self_dw,) = run(
        functools.partial(pair_grads, True),
        [((4, 3 * HEAD, 128), low_t)],
        ids,
        [self_back_t, stream_own, stream_other, hidden_own, hidden_other],
    )
    self_back = deal_all(after(self_back_t, rows_b, *moved_a))
    end_width = 2 * D + 2 * 128 + 12 * 128
    end_parts = run(end_sums, [((16, end_width), low_t)] * 4, ids, [rows_b, self_dw])
    moved_end = shard_swaps(end_parts)
    (source_grad,) = run(
        source_back,
        [((rows, D), wide_t)],
        ids,
        [rows_b, after(wckv, end_parts[0])],
        [((2 * D, rows), low_t)],
        us=3,
    )
    (copies_end,) = run(
        add_shards,
        [((4, 32, width_a + 512 + end_width // 2), low_t)],
        ids,
        [*moved_a, after(moved_end[0], source_grad), *moved_end[1:]],
    )
    all_own = deal(after(copies_end, self_back))
    hidden_grad, stream_grad = run(
        hidden_back,
        [((rows, D), wide_t)] * 2,
        ids,
        [self_back, first_grad, wq, wkv],
        [((3 * D, rows), low_t)],
        us=3,
    )
    all_other = core_swap(after(all_own, hidden_grad))
    (
        grad_in,
        grad_out,
        grad_cross_output,
        grad_cross_pair,
        grad_cross_query,
        grad_output,
        gain_grads,
        shift_grads,
        grad_query,
        grad_pair,
    ) = run(
        place_all,
        [((128, FF), wide_t), ((D, D), wide_t), ((128, D), wide_t), ((128, 2 * D), wide_t)]
        + [((128, D), wide_t)] * 2
        + [((3, 128), wide_t)] * 2
        + [((128, D), wide_t), ((128, 2 * D), wide_t)],
        ids,
        [all_own, all_other],
        [((2 * D, 128), wide_t), ((3 * D, 128), wide_t)],
    )
    return (
        result[None],
        hidden_grad[None],
        stream_grad[None],
        source_grad[None],
        grad_query,
        grad_pair,
        grad_output,
        grad_cross_query,
        grad_cross_pair,
        grad_cross_output,
        grad_in,
        grad_out,
        gain_grads,
        shift_grads,
    )


def solution(mesh):
    in_specs = (
        P("wa", "ctx", None),
        P("wa", "ctx", None),
        P("wa", "ctx", None),
        P("wa", None),
        P("wa", None),
        P("wa", None),
        P("wa", None),
        P("wa", None),
        P("wa", None),
        P("wa", None),
        P("wa", None),
        P("wa", None),
        P("wa", None),
        P("wa", None),
        P("wa", None),
        P(None, "wa"),
        P(None, "wa"),
        P("wa", "ctx", None),
    )
    out_specs = (
        P("wa", "ctx", None),
        P("wa", "ctx", None),
        P("wa", "ctx", None),
        P("wa", "ctx", None),
        P("wa", None),
        P("wa", None),
        P("wa", None),
        P("wa", None),
        P("wa", None),
        P("wa", None),
        P("wa", None),
        P("wa", None),
        P(None, "wa"),
        P(None, "wa"),
    )
    if mesh.axis_names != ("ctx", "wa") or mesh.shape["ctx"] != HEADS or mesh.shape["wa"] != 4:
        return jax.shard_map(
            general_shards, mesh=mesh, in_specs=in_specs, out_specs=out_specs, check_vma=False
        )

    def finer(spec):
        return P(*(("chip", "core") if axis == "ctx" else axis for axis in spec))

    return jax.shard_map(
        fast_shards,
        mesh=Mesh(mesh.devices.reshape(4, 2, 4), ("chip", "core", "wa")),
        in_specs=tuple(finer(spec) for spec in in_specs),
        out_specs=tuple(finer(spec) for spec in out_specs),
        check_vma=False,
    )
```

```python
import functools

import jax
import jax.numpy as jnp
from jax import lax
from jax.experimental import pallas as pl
from jax.experimental.pallas import tpu as pltpu
from jax.sharding import Mesh
from jax.sharding import PartitionSpec as P

D = 512
HEADS = 8
HEAD = 64
KEYBLK = 1024


layer_eps = 1e-05
neg_fill = -1e30


def sequence_ids(positions, seq_ends):
    return jnp.sum((positions[:, None] >= seq_ends[None, :]).astype(jnp.int32), axis=1)


def head_split(matrix):
    return matrix.reshape(matrix.shape[0], HEADS, HEAD)


def block_scores(query_heads, key_heads):
    raw_scores = jnp.einsum(
        "lhd,khd->hlk", query_heads, key_heads, preferred_element_type=jnp.float32
    )
    return raw_scores * float(HEAD) ** (-0.5)


def softmax_totals(queries, key_rows, allowed_fn):
    query_heads = head_split(queries)
    count_rows = queries.shape[0]

    def visit(state_pair, block_index):
        running_top, running_sum = state_pair
        block_start = block_index * KEYBLK
        key_piece = lax.dynamic_slice_in_dim(key_rows, block_start, KEYBLK, 0)
        allowed = allowed_fn(block_start)[None]
        scores = jnp.where(
            allowed, block_scores(query_heads, head_split(key_piece[:, :D])), neg_fill
        )
        new_top = jnp.maximum(running_top, jnp.max(scores, axis=2))
        weights = jnp.where(allowed, jnp.exp(scores - new_top[:, :, None]), 0.0)
        running_sum = running_sum * jnp.exp(running_top - new_top) + jnp.sum(weights, axis=2)
        return ((new_top, running_sum), None)

    initial = (
        jnp.full((HEADS, count_rows), neg_fill, jnp.float32),
        jnp.zeros((HEADS, count_rows), jnp.float32),
    )
    (final_top, final_sum), unused = lax.scan(
        visit, initial, jnp.arange(key_rows.shape[0] // KEYBLK)
    )
    return final_top + jnp.log(final_sum)


def attend_values(queries, key_rows, log_totals, allowed_fn):
    query_heads = head_split(queries)

    def visit(running, block_index):
        block_start = block_index * KEYBLK
        key_piece = lax.dynamic_slice_in_dim(key_rows, block_start, KEYBLK, 0)
        allowed = allowed_fn(block_start)[None]
        scores = block_scores(query_heads, head_split(key_piece[:, :D]))
        weights = jnp.where(allowed, jnp.exp(scores - log_totals[:, :, None]), 0.0)
        value_heads = head_split(key_piece[:, D:])
        return (
            running
            + jnp.einsum(
                "hlk,khd->lhd",
                weights.astype(jnp.bfloat16),
                value_heads,
                preferred_element_type=jnp.float32,
            ),
            None,
        )

    mixed, unused = lax.scan(
        visit, jnp.zeros(query_heads.shape, jnp.float32), jnp.arange(key_rows.shape[0] // KEYBLK)
    )
    return mixed.reshape(queries.shape[0], D)


def head_offsets(grad_low, attended):
    return jnp.sum(head_split(grad_low.astype(jnp.float32) * attended), axis=2).T


def attend_back(queries, key_rows, log_totals, attended, grad_low, allowed_fn):
    query_heads = head_split(queries)
    grad_heads = head_split(grad_low)
    offsets = head_offsets(grad_low, attended)
    scale_value = float(HEAD) ** (-0.5)

    def visit(query_grad, block_index):
        block_start = block_index * KEYBLK
        key_piece = lax.dynamic_slice_in_dim(key_rows, block_start, KEYBLK, 0)
        allowed = allowed_fn(block_start)[None]
        key_heads = head_split(key_piece[:, :D])
        value_heads = head_split(key_piece[:, D:])
        weights = jnp.where(
            allowed, jnp.exp(block_scores(query_heads, key_heads) - log_totals[:, :, None]), 0.0
        )
        value_grad = jnp.einsum(
            "hlk,lhd->khd",
            weights.astype(jnp.bfloat16),
            grad_heads,
            preferred_element_type=jnp.float32,
        )
        weight_grad = jnp.einsum(
            "lhd,khd->hlk", grad_heads, value_heads, preferred_element_type=jnp.float32
        )
        score_grad = (weights * (weight_grad - offsets[:, :, None]) * scale_value).astype(
            jnp.bfloat16
        )
        query_grad = query_grad + jnp.einsum(
            "hlk,khd->lhd", score_grad, key_heads, preferred_element_type=jnp.float32
        )
        key_grad = jnp.einsum(
            "hlk,lhd->khd", score_grad, query_heads, preferred_element_type=jnp.float32
        )
        return (
            query_grad,
            jnp.concatenate((key_grad.reshape(KEYBLK, D), value_grad.reshape(KEYBLK, D)), axis=1),
        )

    query_grad, grad_pieces = lax.scan(
        visit, jnp.zeros(query_heads.shape, jnp.float32), jnp.arange(key_rows.shape[0] // KEYBLK)
    )
    return (query_grad.reshape(queries.shape[0], D), grad_pieces.reshape(key_rows.shape[0], 2 * D))


def normalize(values, gain_row, shift_row):
    row_mean = jnp.mean(values, axis=1, keepdims=True)
    centred = values - row_mean
    scale_inv = lax.rsqrt(jnp.mean(centred * centred, axis=1, keepdims=True) + layer_eps)
    normed = centred * scale_inv
    return (normed * gain_row + shift_row, normed, scale_inv)


def normalize_back(grad_out, normed, scale_inv, gain_row):
    gain_term = jnp.sum(grad_out * normed, axis=0)
    shift_term = jnp.sum(grad_out, axis=0)
    scaled = grad_out * gain_row
    grad_in = scale_inv * (
        scaled
        - jnp.mean(scaled, axis=1, keepdims=True)
        - normed * jnp.mean(scaled * normed, axis=1, keepdims=True)
    )
    return (grad_in, gain_term, shift_term)


def matmul(left, right):
    return jnp.dot(left, right, preferred_element_type=jnp.float32)


def general_shards(
    hidden,
    stream,
    encoder,
    lengths,
    order,
    ranks,
    thresholds,
    self_query,
    self_key_value,
    self_output,
    cross_query,
    cross_key_value,
    cross_output,
    ffn_in,
    ffn_out,
    norm_gain,
    norm_shift,
    cotangent,
):
    (
        full_query,
        full_pair,
        full_output,
        full_cross_query,
        full_cross_pair,
        full_cross_output,
        full_in,
        full_out,
        gain_rows,
        shift_rows,
    ) = (
        lax.all_gather(self_query, "wa", axis=0, tiled=True),
        lax.all_gather(self_key_value, "wa", axis=0, tiled=True),
        lax.all_gather(self_output, "wa", axis=0, tiled=True),
        lax.all_gather(cross_query, "wa", axis=0, tiled=True),
        lax.all_gather(cross_key_value, "wa", axis=0, tiled=True),
        lax.all_gather(cross_output, "wa", axis=0, tiled=True),
        lax.all_gather(ffn_in, "wa", axis=0, tiled=True),
        lax.all_gather(ffn_out, "wa", axis=0, tiled=True),
        lax.all_gather(norm_gain, "wa", axis=1, tiled=True),
        lax.all_gather(norm_shift, "wa", axis=1, tiled=True),
    )
    gains = gain_rows.astype(jnp.float32)
    shifts = shift_rows.astype(jnp.float32)
    local_rows = hidden.shape[1]
    total_rows = order.shape[1]
    row_start = lax.axis_index("ctx") * local_rows
    seq_ends = jnp.cumsum(lengths[0])
    token_seq = sequence_ids(order[0], seq_ends)
    source_seq = sequence_ids(jnp.arange(total_rows, dtype=jnp.int32), seq_ends)
    query_seq = lax.dynamic_slice_in_dim(token_seq, row_start, local_rows)
    query_rows = row_start + jnp.arange(local_rows, dtype=jnp.int32)
    all_limits = thresholds[0]
    limits = lax.dynamic_slice_in_dim(all_limits, row_start, local_rows)
    key_ranks = ranks[0]

    def self_allowed(block_start):
        block_seq = lax.dynamic_slice_in_dim(token_seq, block_start, KEYBLK)
        block_rank = lax.dynamic_slice_in_dim(key_ranks, block_start, KEYBLK)
        block_rows = block_start + jnp.arange(KEYBLK, dtype=jnp.int32)
        return (query_seq[:, None] == block_seq[None, :]) & (
            (block_rank[None, :] < limits[:, None]) | (query_rows[:, None] == block_rows[None, :])
        )

    def cross_allowed(block_start):
        return (
            query_seq[:, None] == lax.dynamic_slice_in_dim(source_seq, block_start, KEYBLK)[None, :]
        )

    inputs = hidden[0]
    stream_rows = stream[0]
    source_rows = encoder[0]
    queries = matmul(inputs, full_query).astype(jnp.bfloat16)
    self_local = matmul(stream_rows, full_pair).astype(jnp.bfloat16)
    cross_local = matmul(source_rows, full_cross_pair).astype(jnp.bfloat16)
    self_keys, cross_keys = (
        lax.all_gather(self_local, "ctx", axis=0, tiled=True),
        lax.all_gather(cross_local, "ctx", axis=0, tiled=True),
    )
    self_totals = softmax_totals(queries, self_keys, self_allowed)
    self_mixed = attend_values(queries, self_keys, self_totals, self_allowed)
    self_low = self_mixed.astype(jnp.bfloat16)
    first, first_normed, first_scale = normalize(
        inputs.astype(jnp.float32) + matmul(self_low, full_output), gains[0], shifts[0]
    )
    first_low = first.astype(jnp.bfloat16)
    cross_queries = matmul(first_low, full_cross_query).astype(jnp.bfloat16)
    cross_totals = softmax_totals(cross_queries, cross_keys, cross_allowed)
    cross_mixed = attend_values(cross_queries, cross_keys, cross_totals, cross_allowed)
    cross_low = cross_mixed.astype(jnp.bfloat16)
    second, second_normed, second_scale = normalize(
        first + matmul(cross_low, full_cross_output), gains[1], shifts[1]
    )
    second_low = second.astype(jnp.bfloat16)
    hidden_pre = matmul(second_low, full_in)
    sigmoid_pre = jax.nn.sigmoid(hidden_pre)
    activated = (hidden_pre * sigmoid_pre).astype(jnp.bfloat16)
    result, third_normed, third_scale = normalize(
        second + matmul(activated, full_out), gains[2], shifts[2]
    )
    third_grad, gain_grad_c, shift_grad_c = normalize_back(
        cotangent[0].astype(jnp.float32), third_normed, third_scale, gains[2]
    )
    branch_grad = third_grad.astype(jnp.bfloat16)
    grad_ffn_out = matmul(activated.T, branch_grad)
    slope = sigmoid_pre * (1.0 + hidden_pre * (1.0 - sigmoid_pre))
    pre_grad = (matmul(branch_grad, full_out.T) * slope).astype(jnp.bfloat16)
    grad_ffn_in = matmul(second_low.T, pre_grad)
    second_total = third_grad + matmul(pre_grad, full_in.T)
    second_grad, gain_grad_b, shift_grad_b = normalize_back(
        second_total, second_normed, second_scale, gains[1]
    )
    cross_branch = second_grad.astype(jnp.bfloat16)
    grad_cross_output = matmul(cross_low.T, cross_branch)
    cross_mixed_grad = matmul(cross_branch, full_cross_output.T).astype(jnp.bfloat16)
    cross_query_term, cross_terms = attend_back(
        cross_queries, cross_keys, cross_totals, cross_mixed, cross_mixed_grad, cross_allowed
    )
    cross_query_low = cross_query_term.astype(jnp.bfloat16)
    grad_cross_query = matmul(first_low.T, cross_query_low)
    first_total = second_grad + matmul(cross_query_low, full_cross_query.T)
    first_grad, gain_grad_a, shift_grad_a = normalize_back(
        first_total, first_normed, first_scale, gains[0]
    )
    self_branch = first_grad.astype(jnp.bfloat16)
    grad_self_output = matmul(self_low.T, self_branch)
    self_mixed_grad = matmul(self_branch, full_output.T).astype(jnp.bfloat16)
    self_query_term, self_terms = attend_back(
        queries, self_keys, self_totals, self_mixed, self_mixed_grad, self_allowed
    )
    self_sum, cross_sum = (
        lax.psum_scatter(self_terms, "ctx", scatter_dimension=0, tiled=True),
        lax.psum_scatter(cross_terms, "ctx", scatter_dimension=0, tiled=True),
    )
    self_query_low = self_query_term.astype(jnp.bfloat16)
    grad_self_query = matmul(inputs.T, self_query_low)
    input_grad = first_grad + matmul(self_query_low, full_query.T)
    self_sum_low = self_sum.astype(jnp.bfloat16)
    grad_self_pair = matmul(stream_rows.T, self_sum_low)
    stream_grad = matmul(self_sum_low, full_pair.T)
    cross_sum_low = cross_sum.astype(jnp.bfloat16)
    grad_cross_pair = matmul(source_rows.T, cross_sum_low)
    source_grad = matmul(cross_sum_low, full_cross_pair.T)
    gain_grads = jnp.stack((gain_grad_a, gain_grad_b, gain_grad_c))
    shift_grads = jnp.stack((shift_grad_a, shift_grad_b, shift_grad_c))
    (
        share_query,
        share_pair,
        share_output,
        share_cross_query,
        share_cross_pair,
        share_cross_output,
        share_in,
        share_out,
        share_gain,
        share_shift,
    ) = (
        lax.psum_scatter(
            grad_self_query.astype(jnp.bfloat16), "wa", scatter_dimension=0, tiled=True
        ).astype(jnp.float32),
        lax.psum_scatter(
            grad_self_pair.astype(jnp.bfloat16), "wa", scatter_dimension=0, tiled=True
        ).astype(jnp.float32),
        lax.psum_scatter(
            grad_self_output.astype(jnp.bfloat16), "wa", scatter_dimension=0, tiled=True
        ).astype(jnp.float32),
        lax.psum_scatter(
            grad_cross_query.astype(jnp.bfloat16), "wa", scatter_dimension=0, tiled=True
        ).astype(jnp.float32),
        lax.psum_scatter(
            grad_cross_pair.astype(jnp.bfloat16), "wa", scatter_dimension=0, tiled=True
        ).astype(jnp.float32),
        lax.psum_scatter(
            grad_cross_output.astype(jnp.bfloat16), "wa", scatter_dimension=0, tiled=True
        ).astype(jnp.float32),
        lax.psum_scatter(
            grad_ffn_in.astype(jnp.bfloat16), "wa", scatter_dimension=0, tiled=True
        ).astype(jnp.float32),
        lax.psum_scatter(
            grad_ffn_out.astype(jnp.bfloat16), "wa", scatter_dimension=0, tiled=True
        ).astype(jnp.float32),
        lax.psum_scatter(
            gain_grads.astype(jnp.bfloat16), "wa", scatter_dimension=1, tiled=True
        ).astype(jnp.float32),
        lax.psum_scatter(
            shift_grads.astype(jnp.bfloat16), "wa", scatter_dimension=1, tiled=True
        ).astype(jnp.float32),
    )
    (
        total_query,
        total_pair,
        total_output,
        total_cross_query,
        total_cross_pair,
        total_cross_output,
        total_in,
        total_out,
        total_gain,
        total_shift,
    ) = lax.psum(
        (
            share_query,
            share_pair,
            share_output,
            share_cross_query,
            share_cross_pair,
            share_cross_output,
            share_in,
            share_out,
            share_gain,
            share_shift,
        ),
        "ctx",
    )
    return (
        result.astype(jnp.bfloat16)[None],
        input_grad[None],
        stream_grad[None],
        source_grad[None],
        total_query,
        total_pair,
        total_output,
        total_cross_query,
        total_cross_pair,
        total_cross_output,
        total_in,
        total_out,
        total_gain,
        total_shift,
    )


PAIR = 2 * HEAD
PAIRS = HEADS // 2
FF = 2048
low_t = jnp.bfloat16
wide_t = jnp.float32
vmem_spec = pl.BlockSpec(memory_space=pltpu.VMEM)
smem_spec = pl.BlockSpec(memory_space=pltpu.SMEM)


def run(body, outs, ids, args, scratch=(), us=2, vmem=56):
    outs = [jax.ShapeDtypeStruct(shape, kind) for shape, kind in outs]
    arrays = [arg[0] if isinstance(arg, tuple) else arg for arg in args]

    def view(arg, ref):
        if not isinstance(arg, tuple):
            return ref
        if len(arg) == 3:
            return ref.at[arg[2]]
        return ref.at[:, :, arg[1] * D : (arg[1] + 1) * D]

    def kernel(ids, *refs):
        views = [view(arg, ref) for arg, ref in zip(args, refs)]
        body(ids, *views, *refs[len(args) :])

    moved = sum(a.size * a.dtype.itemsize for a in arrays + outs)
    return pl.pallas_call(
        kernel,
        name=getattr(body, "func", body).__name__,
        out_shape=outs,
        in_specs=[smem_spec] + [vmem_spec] * len(args),
        out_specs=[vmem_spec] * len(outs),
        scratch_shapes=[pltpu.VMEM(shape, kind) for shape, kind in scratch],
        compiler_params=pltpu.CompilerParams(vmem_limit_bytes=vmem * 1024 * 1024),
        cost_estimate=pl.CostEstimate(flops=us * 1_000_000_000, bytes_accessed=moved, transcendentals=0),
    )(ids, *arrays)


def dot_nn(a, b):
    return lax.dot_general(a, b, (((1,), (0,)), ((), ())), preferred_element_type=wide_t)


def dot_nt(a, b):
    return lax.dot_general(a, b, (((1,), (1,)), ((), ())), preferred_element_type=wide_t)


def dot_tn(a, b):
    return lax.dot_general(a, b, (((0,), (0,)), ((), ())), preferred_element_type=wide_t)


def at16(start, size=16):
    return pl.ds(pl.multiple_of(start, 16), size)


def at128(start, size=128):
    return pl.ds(pl.multiple_of(start, 128), size)


def half_mask(shape, axis, core):
    return (lax.broadcasted_iota(jnp.int32, shape, axis) // HEAD) == core


def attend_rows(q_ref, k_ref, vt_ref, bias_ref, s_ref, ot_ref, lse_ref):
    keys, rows = bias_ref.shape
    tile = min(1024, keys)
    tiles = keys // tile

    def step(p, carry):
        q = q_ref[:, at128(p * PAIR)]
        for h in range(2):
            mine = half_mask((rows, PAIR), 1, h)
            own_q = jnp.where(mine, q, jnp.zeros_like(q))
            top = jnp.full((8, rows), neg_fill, wide_t)
            for t in range(tiles):
                here = slice(t * tile, (t + 1) * tile)
                s = dot_nt(k_ref[here, at128(p * PAIR)], own_q) + bias_ref[here, :]
                s_ref[h, here, :] = s
                top = jnp.maximum(top, jnp.max(s.reshape(tile // 8, 8, rows), axis=0))
            top = jnp.max(top, axis=0, keepdims=True)
            total = jnp.zeros((8, rows), wide_t)
            mixed = jnp.zeros((HEAD, rows), wide_t)
            features = pl.ds(pl.multiple_of(p * PAIR + h * HEAD, HEAD), HEAD)
            for t in range(tiles):
                here = slice(t * tile, (t + 1) * tile)
                w = jnp.exp(s_ref[h, here, :] - top)
                total = total + jnp.sum(w.reshape(tile // 8, 8, rows), axis=0)
                mixed = mixed + dot_nn(vt_ref[features, here], w.astype(low_t))
            total = jnp.sum(total, axis=0, keepdims=True)
            ot_ref[features, :] = mixed / total
            lse_ref[pl.ds(p * 2 + h, 1), :] = top + jnp.log(total)
        return carry

    lax.fori_loop(0, PAIRS, step, 0)


def finish_rows(ot_ref, low_out, mixed_out):
    mixed = ot_ref[...].T
    low_out[...] = mixed.astype(low_t)
    mixed_out[...] = mixed


def three_parts(value):
    high = value.astype(low_t).astype(wide_t)
    rest = value - high
    middle = rest.astype(low_t).astype(wide_t)
    return high, middle, rest - middle


def side_rows(lse, grad_low, mixed, row_data):
    product = grad_low.astype(wide_t) * mixed[...]
    lane = lax.broadcasted_iota(jnp.int32, (grad_low.shape[0], PAIR), 1)
    sums = jnp.zeros((grad_low.shape[0], PAIR), wide_t)
    for p in range(PAIRS):
        piece = product[:, p * PAIR : (p + 1) * PAIR]
        for h in range(2):
            mine = half_mask(piece.shape, 1, h)
            offset = jnp.sum(jnp.where(mine, piece, 0.0), axis=1, keepdims=True)
            sums = jnp.where(lane == p * 2 + h, offset, sums)
    offsets = sums.T
    seq = row_data[16:17, :]
    onehot = [(seq == float(n)).astype(wide_t) for n in range(4)]
    sides = []
    for p in range(PAIRS):
        pieces = []
        for h in range(2):
            head = p * 2 + h
            pieces += three_parts(-lse[head : head + 1, :])
            pieces += three_parts(-offsets[head : head + 1, :])
        sides.append(jnp.concatenate(pieces + onehot, axis=0).astype(low_t))
    return sides


def side_lanes(side, core):
    side = side.astype(wide_t)
    head = jnp.where(core == 0, side[0:6], side[6:12])
    gap = jnp.zeros((5, side.shape[1]), wide_t)
    rest = jnp.zeros((HEAD - 20, side.shape[1]), wide_t)
    half = jnp.concatenate((head[0:3], gap, head[3:6], gap, side[12:16], rest), axis=0)
    return jnp.concatenate((half, half), axis=0).T.astype(low_t)


def assemble(ids, parts, column, outs):
    for chip, other, block in parts:
        own = chip * 2 + (ids[1] ^ other)
        for e in range(4):
            rows = at16((ids[2] ^ e) * 128 + own * 16)
            start = column
            for out in outs:
                width = out.shape[1]
                out[rows, :] = block[e * 16 : (e + 1) * 16, start : start + width]
                start += width


def project_pairs(parts, w_pair, k_ref, vt_ref, wvt_ref):
    wvt_ref[...] = w_pair[:, D:].astype(wide_t).T.astype(low_t)
    for n, part in enumerate(parts):
        for k in range(PAIRS):
            rows = part.shape[1]
            start = (n * 4 + k) * rows
            k_ref[start : start + rows, :] = dot_nn(part[k], w_pair[:, :D]).astype(low_t)
            vt_ref[:, start : start + rows] = dot_nt(wvt_ref[...], part[k]).astype(low_t)


def self_forward(ids, hidden, own, other, *refs):
    slices, (cols, row_data), refs = refs[:8], refs[8:10], refs[10:]
    out, mixed, lse, wq, wkv, q_ref, k_ref, vt_ref, wvt_ref, bias_ref, s_ref, ot_ref = refs
    rows = hidden.shape[0]
    parts = [(ids[0] ^ k, n, slices[n * 4 + k]) for n in range(2) for k in range(4)]
    assemble(ids, parts, 0, (wq, wkv))
    q_ref[...] = (dot_nn(hidden[...], wq[...]).astype(low_t) * 0.125).astype(low_t)
    project_pairs((own, other), wkv, k_ref, vt_ref, wvt_ref)
    seq, limit = row_data[16:17, :], row_data[17:18, :]
    for b in range(8):
        seen = (cols[:, b : b + 1] == seq) & (cols[:, 8 + b : 9 + b] < limit)
        bias_ref[b * rows : (b + 1) * rows, :] = jnp.where(seen, 0.0, neg_fill)
    mine = lax.broadcasted_iota(jnp.int32, (rows, rows), 0) == lax.broadcasted_iota(
        jnp.int32, (rows, rows), 1
    )
    block = at128(ids[0] * rows, rows)
    bias_ref[block, :] = jnp.where(mine, 0.0, bias_ref[block, :])
    attend_rows(q_ref, k_ref, vt_ref, bias_ref, s_ref, ot_ref, lse)
    finish_rows(ot_ref, out, mixed)


def layer_norm(values, gain_row, shift_row):
    mean = jnp.mean(values, axis=1, keepdims=True)
    centred = values - mean
    scale = lax.rsqrt(jnp.mean(centred * centred, axis=1, keepdims=True) + layer_eps)
    normed = centred * scale
    return normed * gain_row + shift_row, normed, scale


def layer_norm_back(grad, normed, scale, gain_row):
    gain_term = jnp.sum(grad * normed, axis=0, keepdims=True)
    shift_term = jnp.sum(grad, axis=0, keepdims=True)
    scaled = grad * gain_row
    grad_in = scale * (
        scaled
        - jnp.mean(scaled, axis=1, keepdims=True)
        - normed * jnp.mean(scaled * normed, axis=1, keepdims=True)
    )
    return grad_in, gain_term, shift_term


def cross_forward(ids, hidden, self_low, own, other, *refs):
    slices, (cols, row_data) = refs[:2], refs[2:4]
    first, normed, scale_out, first_low, cross_low, mixed, lse, cross_q = refs[4:12]
    wo, wcq, wckv, wco, gs, q_ref, k_ref, vt_ref, wvt_ref, bias_ref, s_ref, ot_ref = refs[12:]
    for n in range(2):
        for e in range(4):
            rows = at16(e * 128 + (ids[1] ^ n) * 64, 64)
            start = 0
            for out in (wo, wcq, wckv, wco):
                width = out.shape[1]
                out[rows, :] = slices[n][e, :, start : start + width]
                start += width
    for e in range(4):
        gs[:, e * 128 : (e + 1) * 128] = slices[0][e, :16, 5 * D :]
    gain, shift = gs[0:1, :].astype(wide_t), gs[3:4, :].astype(wide_t)
    value, n0, s0 = layer_norm(
        hidden[...].astype(wide_t) + dot_nn(self_low[...], wo[...]), gain, shift
    )
    first[...] = value
    normed[...] = n0
    scale_out[...] = jnp.broadcast_to(s0, scale_out.shape)
    low = value.astype(low_t)
    first_low[...] = low
    q = dot_nn(low, wcq[...]).astype(low_t)
    cross_q[...] = q
    q_ref[...] = (q * 0.125).astype(low_t)
    rows = hidden.shape[0]
    project_pairs((own, other), wckv, k_ref, vt_ref, wvt_ref)
    for b in range(8):
        seen = cols[:, 16 + b : 17 + b] == row_data[16:17, :]
        bias_ref[b * rows : (b + 1) * rows, :] = jnp.where(seen, 0.0, neg_fill)
    attend_rows(q_ref, k_ref, vt_ref, bias_ref, s_ref, ot_ref, lse)
    finish_rows(ot_ref, cross_low, mixed)


def feed_forward(ids, first, cross_low, cross_mixed, lse, row_data, cross_q, wco, gs, cotangent, *refs):
    slices = refs[0:8]
    result, dealt, second_grad, keep, send, sums, slope, wins, wouts = refs[8:]
    half_ff = FF // 2
    for n in range(2):
        for k in range(4):
            chip, core, part = ids[0] ^ k, ids[1] ^ n, slices[n * 4 + k]
            for e in range(4):
                w, here = ids[2] ^ e, slice(e * 16, (e + 1) * 16)
                rows = at16(w * 128 + (chip * 2 + core) * 16)
                for g in range(4):
                    row = w * 256 + ((chip % 2) * 2 + core) * 64 + g * 16
                    wouts[(chip // 2) ^ ids[1], at16(row), :] = part[here, FF + g * D : FF + (g + 1) * D]
                    for h in range(2):
                        column = g * 512 + h * 256
                        wins[h ^ ids[1], rows, g * 256 : (g + 1) * 256] = part[here, column : column + 256]
    gains, shifts = gs[0:3, :].astype(wide_t), gs[3:6, :].astype(wide_t)
    second, n1, s1 = layer_norm(
        first[...] + dot_nn(cross_low[...], wco[...]), gains[1:2], shifts[1:2]
    )
    low = second.astype(low_t)
    for out in (keep, send):
        out[:, 2 * half_ff : 2 * half_ff + D] = low
        out[:, 2 * half_ff + 2 * D : 2 * half_ff + 3 * D] = cross_low[...]
    width = 512
    chunks = [(n, c) for n in range(2) for c in range(FF // 2 // width)]
    total = second
    for n, c in chunks:
        here = slice(c * width, (c + 1) * width)
        wide = slice(n * half_ff + c * width, n * half_ff + (c + 1) * width)
        pre = dot_nn(low, wins[n, :, here])
        sig = 1.0 / (1.0 + jnp.exp(-pre))
        act = (pre * sig).astype(low_t)
        (keep, send)[n][:, half_ff + c * width : half_ff + (c + 1) * width] = act
        slope[:, wide] = sig * (1.0 + pre * (1.0 - sig))
        total = total + dot_nn(act, wouts[n, here, :])
    value, n2, s2 = layer_norm(total, gains[2:3], shifts[2:3])
    result[...] = value.astype(low_t)
    third, gain_c, shift_c = layer_norm_back(cotangent[...].astype(wide_t), n2, s2, gains[2:3])
    third_low = third.astype(low_t)
    for out in (keep, send):
        out[:, 2 * half_ff + D : 2 * half_ff + 2 * D] = third_low
    total = third
    for n, c in chunks:
        here = slice(c * width, (c + 1) * width)
        wide = slice(n * half_ff + c * width, n * half_ff + (c + 1) * width)
        back = (dot_nt(third_low, wouts[n, here, :]) * slope[:, wide]).astype(low_t)
        (keep, send)[n][:, here] = back
        total = total + dot_nt(back, wins[n, :, here])
    grad, gain_b, shift_b = layer_norm_back(total, n1, s1, gains[1:2])
    second_grad[...] = grad
    grad_low = grad.astype(low_t)
    for out, core in ((keep, ids[1]), (send, 1 - ids[1])):
        half = grad_low[:, : D // 2]
        out[:, 2 * half_ff + 3 * D :] = jnp.where(core == 0, half, grad_low[:, D // 2 :])
    mixed = dot_nt(grad_low, wco[...]).astype(low_t)
    rows = grad_low.shape[0]
    sides = side_rows(lse, mixed, cross_mixed, row_data)
    for p in range(PAIRS):
        dealt[p, :rows, :PAIR] = cross_q[:, p * PAIR : (p + 1) * PAIR]
        dealt[p, :rows, PAIR:] = mixed[:, p * PAIR : (p + 1) * PAIR]
        dealt[p, rows:, :] = sides[p]
    zero = jnp.zeros_like(gain_b)
    sums[...] = jnp.concatenate((zero, gain_b, gain_c, zero, shift_b, shift_c, zero, zero), axis=0)


def grads_a(ids, keep, received, out, g_in, g_out, g_cross):
    half = FF // 2

    def both(left, right):
        return (dot_tn(keep[:, left], keep[:, right]) + dot_tn(received[:, left], received[:, right])).astype(low_t)

    at = [0, half] + [2 * half + n * D for n in range(4)]
    pre, act = slice(at[0], at[1]), slice(at[1], at[2])
    second, branch, low = (slice(at[n], at[n] + D) for n in (2, 3, 4))
    g_in[...] = both(second, pre)
    g_out[...] = both(act, branch)
    g_cross[...] = both(low, slice(at[5], at[5] + D // 2))
    for chip in range(4):
        for e in range(4):
            w, here = ids[2] ^ e, slice(e * 32, (e + 1) * 32)
            rows = at16(w * 128 + chip * 32, 32)
            out[chip, here, :half] = g_in[rows, :]
            for g in range(2):
                out[chip, here, half + g * D : half + (g + 1) * D] = g_out[
                    at16(w * 256 + chip * 64 + g * 32, 32), :
                ]
            out[chip, here, half + 2 * D :] = g_cross[rows, :]


def grads_b(ids, first_low, cross_dq, self_low, branch, sums, dkv, out, g_query, g_output):
    g_query[...] = dot_tn(first_low[...], cross_dq[...]).astype(low_t)
    g_output[...] = dot_tn(self_low[...], branch[...]).astype(low_t)
    row = jnp.concatenate((sums[...], jnp.zeros_like(sums[...])), axis=0).astype(low_t)
    rows = dkv.shape[2]
    for e in range(4):
        w, here = ids[2] ^ e, slice(e * 16, (e + 1) * 16)
        piece = row[:, :128]
        for k in range(1, 4):
            piece = jnp.where(w == k, row[:, k * 128 : (k + 1) * 128], piece)
        for device in range(8):
            own = at16(w * 128 + device * 16)
            out[device, here, :D] = g_query[own, :]
            out[device, here, D : 2 * D] = g_output[own, :]
            out[device, here, 2 * D : 2 * D + 128] = piece
    for device in range(8):
        for n in range(2):
            start = 2 * D + 128 + n * rows
            out[device, :, start : start + rows] = dkv[device, n * HEAD : (n + 1) * HEAD, :]


def pair_setup(is_self, ids, own, other, w_pair, cols, *refs):
    if is_self:
        hidden_own, hidden_other, w_query, q_all, k_all, v_all, kt, turn = refs
    else:
        k_all, v_all, kt, turn = refs
    chip, core = ids[0], ids[1]
    rows = own.shape[1]
    mine = half_mask((rows, PAIR), 1, core)
    features = pl.ds(pl.multiple_of(core * HEAD, HEAD), HEAD)
    lane = lax.broadcasted_iota(jnp.int32, (rows, PAIR), 1) % HEAD
    ones_v = jnp.where((lane >= 8) & (lane < 11), 1.0, 0.0).astype(low_t)
    pair = at128(chip * PAIR)
    wk, wv = w_pair[:, pair], w_pair[:, at128(D + chip * PAIR)]
    if is_self:
        wq = w_query[:, pair]
    for n, part in enumerate((own, other)):
        for k in range(4):
            b = n * 4 + k
            here = slice(b * rows, (b + 1) * rows)
            column = b if is_self else 16 + b
            seq = cols[:, column : column + 1].astype(jnp.int32)
            other_seq = (lane >= 16) & (lane < 20) & (lane != seq + 16)
            ones_k = jnp.where(other_seq, neg_fill, jnp.where(lane < 3, 1.0, 0.0)).astype(low_t)
            key = dot_nn(part[k], wk)
            turn[...] = key.T
            kt[:, here] = turn[features, :].astype(low_t)
            k_all[here, :] = jnp.where(mine, key.astype(low_t), ones_k)
            v_all[here, :] = jnp.where(mine, dot_nn(part[k], wv).astype(low_t), ones_v)
            if is_self:
                q_all[b] = dot_nn((hidden_own, hidden_other)[n][k], wq).astype(low_t)


def pair_back(is_self, ids, *refs):
    if is_self:
        q_parts, do_own, do_other, k_all, v_all, kt, cols, row_data, back = refs[:9]
        do_parts = (do_own, do_other)
    else:
        both_own, both_other, k_all, v_all, kt, back, dkv = refs[:7]
        both_parts = (both_own, both_other)
    q_all, do_all, dq_t, dk, dv, rank, turn = refs[-7:]
    core = ids[1]
    rows = q_all.shape[1]
    keys = 8 * rows
    mine = half_mask((rows, PAIR), 1, core)
    features = pl.ds(pl.multiple_of(core * HEAD, HEAD), HEAD)
    for n in range(2):
        for k in range(4):
            b = n * 4 + k
            if is_self:
                here = slice(b * rows, (b + 1) * rows)
                rank[here, :] = jnp.broadcast_to(cols[:, 8 + b : 9 + b], (rows, 128))
                q, do = q_parts[b], do_parts[n][k, :rows, :]
                side = jnp.concatenate(
                    (do_parts[n][k, rows : rows + 16, :], do_parts[n][k, rows + 16 :, :]), axis=1
                )
            else:
                q, do = both_parts[n][k, :rows, :PAIR], both_parts[n][k, :rows, PAIR:]
                side = both_parts[n][k, rows:, :]
            side = side_lanes(side, core)
            q_all[b] = jnp.where(mine, (q * 0.125).astype(low_t), side)
            do_all[b] = jnp.where(mine, do, side)
    dk[...] = jnp.zeros_like(dk)
    dv[...] = jnp.zeros_like(dv)
    tile = min(1024, keys)

    def step(b, carry):
        q, do = q_all[b], do_all[b]
        dqt = jnp.zeros((HEAD, rows), wide_t)
        for t in range(keys // tile):
            here = slice(t * tile, (t + 1) * tile)
            w = jnp.exp(dot_nt(k_all[here, :], q))
            if is_self:
                ranks = jnp.concatenate((rank[here, :],) * (rows // 128), axis=1)
                index = lax.broadcasted_iota(jnp.int32, (tile, rows), 0)
                own = lax.broadcasted_iota(jnp.int32, (tile, rows), 1) + (b * rows - t * tile)
                w = jnp.where((ranks < row_data[pl.ds(8 + b, 1), :]) | (index == own), w, 0.0)
            ds = (w * dot_nt(v_all[here, :], do)).astype(low_t)
            dv[here, :] += dot_nn(w.astype(low_t), do)
            dk[here, :] += dot_nn(ds, q)
            dqt = dqt + dot_nn(kt[:, here], ds)
        dq_t[b] = (dqt * 0.125).astype(low_t)
        return carry

    lax.fori_loop(0, 8, step, 0)
    for n in range(2):
        for k in range(4):
            b = n * 4 + k
            device = k * 2 + (core ^ n)
            here = slice(b * rows, (b + 1) * rows)
            back[device, :HEAD, :] = dq_t[b]
            out, start = (back, HEAD) if is_self else (dkv, 0)
            for value in (dk, dv):
                turn[...] = value[here, :].T
                out[device, start : start + HEAD, :] = turn[features, :].astype(low_t)
                start += HEAD


def pair_grads(is_self, ids, grads, own, other, *refs):
    dw = refs[-1]
    totals = [jnp.zeros((HEAD, D), wide_t) for n in range(grads.shape[1] // HEAD)]
    for n in range(2):
        for k in range(4):
            device = k * 2 + (ids[1] ^ n)
            for m in range(len(totals)):
                source = refs[:2] if is_self and m == 0 else (own, other)
                totals[m] += dot_nn(grads[device, m * HEAD : (m + 1) * HEAD, :], source[n][k])
    for n, value in enumerate(totals):
        for w in range(4):
            dw[w, n * HEAD : (n + 1) * HEAD, :] = value[:, w * 128 : (w + 1) * 128].astype(low_t)


def turned(value):
    return value.astype(wide_t).T.astype(low_t)


def first_back(ids, back, second_grad, normed, scale, self_mixed, lse, row_data, gs, wcq, wo, sums_in, *refs):
    first_grad, branch, dealt, dq, sums = refs
    dq[...] = turned(back[...].reshape(D, back.shape[2]))
    total = second_grad[...] + dot_nt(dq[...], wcq[...])
    grad, gain_a, shift_a = layer_norm_back(
        total, normed[...], scale[:, 0:1], gs[0:1, :].astype(wide_t)
    )
    first_grad[...] = grad
    low = grad.astype(low_t)
    branch[...] = low
    mixed = dot_nt(low, wo[...]).astype(low_t)
    rows = low.shape[0]
    sides = side_rows(lse, mixed, self_mixed, row_data)
    for p in range(PAIRS):
        dealt[p, :rows, :] = mixed[:, p * PAIR : (p + 1) * PAIR]
        dealt[p, rows : rows + 16, :] = sides[p][:, :PAIR]
        dealt[p, rows + 16 :, :] = sides[p][:, PAIR:]
    zero = jnp.zeros_like(gain_a)
    sums[...] = sums_in[...] + jnp.concatenate(
        (gain_a, zero, zero, shift_a, zero, zero, zero, zero), axis=0
    )


def source_back(ids, parts, wckv, out, dkv):
    rows = out.shape[0]
    for device in range(8):
        for n in range(2):
            start = 2 * D + 128 + n * rows
            dkv[n * D + device * HEAD : n * D + (device + 1) * HEAD, :] = parts[
                device, :, start : start + rows
            ]
    out[...] = dot_nt(turned(dkv[...]), wckv[...])


def hidden_back(ids, back, first_grad, wq, wkv, hidden_grad, stream_grad, all_t):
    for device in range(8):
        for n in range(3):
            all_t[n * D + device * HEAD : n * D + (device + 1) * HEAD, :] = back[
                device, n * HEAD : (n + 1) * HEAD, :
            ]
    hidden_grad[...] = first_grad[...] + dot_nt(turned(all_t[:D, :]), wq[...])
    stream_grad[...] = dot_nt(turned(all_t[D:, :]), wkv[...])


def add_parts(parts, rows, columns):
    total = parts[0, rows, columns].astype(wide_t)
    for n in range(1, parts.shape[0]):
        total = total + parts[n, rows, columns].astype(wide_t)
    return total.astype(low_t)


def add_chips(ids, parts, dw, *outs):
    width = parts.shape[2]
    for e in range(4):
        outs[e][:, :width] = add_parts(parts, slice(e * 32, (e + 1) * 32), slice(None))
        piece = dw[ids[2] ^ e]
        for g in range(4):
            outs[e][:, width + g * 128 : width + (g + 1) * 128] = piece[g * 32 : (g + 1) * 32, :]


def end_sums(ids, parts, dw, *outs):
    width = 2 * D + 128
    for e in range(4):
        outs[e][:, :width] = add_parts(parts, slice(e * 16, (e + 1) * 16), slice(0, width))
        outs[e][:, width : width + 128] = jnp.zeros((16, 128), low_t)
        piece = dw[ids[2] ^ e]
        for g in range(12):
            start = width + 128 + g * 128
            outs[e][:, start : start + 128] = piece[g * 16 : (g + 1) * 16, :]


def add_shards(ids, *refs):
    out = refs[8]

    def total(parts):
        value = parts[0][...].astype(wide_t)
        for part in parts[1:]:
            value = value + part[...].astype(wide_t)
        return value.astype(low_t)

    first, last = total(refs[:4]), total(refs[4:8])
    width, half = first.shape[1], last.shape[1] // 2
    for k in range(4):
        out[k, :, :width] = first
        out[k, :16, width:] = last[:, :half]
        out[k, 16:, width:] = last[:, half:]


def place_all(ids, own, other, *refs):
    g_in, g_out, g_cross, g_cross_pair, g_cross_query, g_output, gains, shifts, g_query, g_pair = refs[:10]
    pair_t, all_t = refs[10:]
    half = FF // 2
    start_cross = half + 2 * D
    start_pair = start_cross + D // 2
    start_end = start_pair + 4 * 128
    half_end = own.shape[2] - start_end
    for n, part in enumerate((own, other)):
        core = ids[1] ^ n
        for chip in range(4):
            rows = slice(chip * 32, (chip + 1) * 32)
            device = chip * 2 + core
            for k in range(4):
                g_in[rows, at128(k * 512 + core * 256, 256)] = part[
                    chip, :, k * 256 : (k + 1) * 256
                ].astype(wide_t)
            for g in range(2):
                g_out[at16(core * 256 + chip * 64 + g * 32, 32), :] = part[
                    chip, :, half + g * D : half + (g + 1) * D
                ].astype(wide_t)
            g_cross[rows, at128(core * 256, 256)] = part[chip, :, start_cross:start_pair].astype(wide_t)
            for g in range(4):
                column = start_pair + g * 128
                row = (g // 2) * D + device * HEAD + (g % 2) * 32
                pair_t[at16(row, 32), :] = part[chip, :, column : column + 128].astype(wide_t)

            def piece(column, width):
                row, at = (0, column) if column < half_end else (16, column - half_end)
                return part[chip, row : row + 16, start_end + at : start_end + at + width].astype(wide_t)

            own_rows = at16(device * 16)
            for column in range(0, D, 128):
                g_cross_query[own_rows, column : column + 128] = piece(column, 128)
                g_output[own_rows, column : column + 128] = piece(D + column, 128)
            if n == 0 and chip == 0:
                norms = piece(2 * D, 128)
                gains[...], shifts[...] = norms[0:3], norms[3:6]
            for g in range(12):
                row = (g // 4) * D + device * HEAD + (g % 4) * 16
                all_t[at16(row), :] = piece(2 * D + 256 + g * 128, 128)
    g_cross_pair[...] = pair_t[...].T
    g_query[...] = all_t[:D, :].T
    g_pair[...] = all_t[D:, :].T


def pack_start(ids, stream, source, wq, wkv, ffn_in, ffn_out, many, pack):
    own = ids[0] * 2 + ids[1]
    for k in range(4):
        many[k, :, :D] = stream[...]
        many[k, :, D:] = source[...]
        start = 3 * D + FF + k * D
        pack[:, start : start + D] = ffn_out[at16(own * 64 + k * 16), :]
    pack[:, :D] = wq[at16(own * 16), :]
    pack[:, D : 3 * D] = wkv[at16(own * 16), :]
    pack[:, 3 * D : 3 * D + FF] = ffn_in[at16(own * 16), :]


def pack_more(ids, *refs):
    weights, gain, shift, rows_in, pack, many = refs[:4], *refs[4:]
    rows = at16(ids[1] * 64, 64)
    norms = (gain[...].astype(wide_t), shift[...].astype(wide_t), jnp.zeros((58, 128), wide_t))
    norms = jnp.concatenate(norms, axis=0).astype(low_t)
    for k in range(4):
        start = 0
        for w in weights:
            pack[k, :, start : start + w.shape[1]] = w[rows, :]
            start += w.shape[1]
        pack[k, :, start:] = norms
        many[k] = rows_in[...]


def mask_data(ids, order, ranks, limits, cols, row_data, all_rows):
    rows = cols.shape[0]
    ends = [ids[3]]
    for n in range(1, 4):
        ends.append(ends[-1] + ids[3 + n])

    def sequence(position):
        return sum((position >= end).astype(wide_t) for end in ends)

    for n in range(2):
        for k in range(4):
            b = n * 4 + k
            device = k * 2 + (ids[1] ^ n)
            here = at128(device * rows, rows)
            index = lax.broadcasted_iota(jnp.int32, (1, rows), 1) + device * rows
            all_rows[b : b + 1, :] = sequence(order[:, here])
            all_rows[8 + b : 9 + b, :] = ranks[:, here].astype(wide_t)
            all_rows[16 + b : 17 + b, :] = sequence(index)
            row_data[8 + b : 9 + b, :] = limits[:, here].astype(wide_t)
    row_data[0:8, :] = all_rows[0:8, :]
    all_rows[24:32, :] = jnp.zeros((8, rows), wide_t)
    all_rows[24:25, :] = all_rows[pl.ds(ids[0], 1), :]
    row_data[16:24, :] = jnp.zeros((8, rows), wide_t)
    row_data[16:17, :] = all_rows[pl.ds(ids[0], 1), :]
    row_data[17:18, :] = row_data[pl.ds(8 + ids[0], 1), :]
    cols[:, :32] = all_rows[...].T


def pack_first(ids, *refs):
    parts, (one, two) = refs[:4], refs[4:]
    width = one.shape[1]
    for e in range(4):
        here = slice(e * 16, (e + 1) * 16)
        one[here, :] = parts[e][:, :width]
        two[here, :] = parts[e][:, width:]


def core_swap(value):
    return lax.ppermute(value, "core", [(0, 1), (1, 0)])


def chip_swaps(parts):
    moves = [[(i, i ^ k) for i in range(4)] for k in range(4)]
    return [parts[0]] + [lax.ppermute(parts[k], "chip", moves[k]) for k in range(1, 4)]


def shard_swaps(parts):
    moves = [[(i, i ^ k) for i in range(4)] for k in range(4)]
    return [parts[0]] + [lax.ppermute(parts[k], "wa", moves[k]) for k in range(1, 4)]


def deal(value):
    return lax.all_to_all(value, "chip", 0, 0, tiled=True)


def deal_all(value):
    return lax.all_to_all(value, ("chip", "core"), 0, 0, tiled=True)


def deal_both(value):
    own = deal(value)
    return own, core_swap(own)


def after(value, *others):
    return lax.optimization_barrier((value,) + others)[0]


def fast_shards(
    hidden,
    stream,
    encoder,
    lengths,
    order,
    ranks,
    thresholds,
    self_query,
    self_key_value,
    self_output,
    cross_query,
    cross_key_value,
    cross_output,
    ffn_in,
    ffn_out,
    norm_gain,
    norm_shift,
    cotangent,
):
    rows, keys = hidden.shape[1], order.shape[1]
    chip, core, mw = lax.axis_index("chip"), lax.axis_index("core"), lax.axis_index("wa")
    ids = jnp.concatenate((jnp.stack((chip, core, mw)).astype(jnp.int32), lengths[0]))
    inputs = hidden[0]

    many, pack1 = run(
        pack_start,
        [((4, rows, 2 * D), low_t), ((16, 3 * D + 2 * FF), low_t)],
        ids,
        [stream[0], encoder[0], self_query, self_key_value, ffn_in, ffn_out],
    )
    x_own = deal(many)
    shards1 = shard_swaps([pack1] * 4)
    copies2, hidden_copies = run(
        pack_more,
        [((4, 64, 5 * D + 128), low_t), ((4, rows, D), low_t)],
        ids,
        [after(self_output, pack1), cross_query, cross_key_value, cross_output, norm_gain, norm_shift]
        + [inputs],
    )
    cols, row_data = run(
        mask_data,
        [((rows, 32), wide_t), ((24, rows), wide_t)],
        ids,
        [order, ranks, thresholds],
        [((32, rows), wide_t)],
    )
    part1, part3 = run(
        pack_first,
        [((64, 3 * D), low_t), ((64, 2 * FF), low_t)],
        ids,
        [after(shards1[0], x_own, cols, copies2)] + shards1[1:],
    )
    slices1 = chip_swaps([part1] * 4)
    slices1 = slices1 + [core_swap(part) for part in slices1]
    shards2 = lax.all_to_all(after(copies2, x_own), "wa", 0, 0, tiled=True)
    x_other = core_swap(after(x_own, part1))
    slices3 = chip_swaps([after(part3, slices1[1])] * 4)
    stream_own, stream_other = (x_own, 0), (x_other, 0)
    source_own, source_other = (x_own, 1), (x_other, 1)

    attend_scratch = [
        ((rows, D), low_t),
        ((keys, D), low_t),
        ((D, keys), low_t),
        ((D, D), low_t),
        ((keys, rows), wide_t),
        ((2, keys, rows), wide_t),
        ((D, rows), wide_t),
    ]
    self_low, self_mixed, self_lse, wq, wkv = run(
        self_forward,
        [((rows, D), low_t), ((rows, D), wide_t), ((HEADS, rows), wide_t)]
        + [((D, D), low_t), ((D, 2 * D), low_t)],
        ids,
        [inputs, stream_own, stream_other, *slices1, cols, row_data],
        attend_scratch,
        us=15,
    )
    shards2_other = core_swap(after(shards2, self_low, *slices3))
    slices3 = slices3 + [core_swap(after(part, self_low)) for part in slices3]
    hidden_own = deal(after(hidden_copies, shards2, self_low, *slices3[:4]))
    (
        first,
        normed,
        scale,
        first_low,
        cross_low,
        cross_mixed,
        cross_lse,
        cross_q,
        wo,
        wcq,
        wckv,
        wco,
        gs,
    ) = run(
        cross_forward,
        [((rows, D), wide_t)] * 2
        + [((rows, 128), wide_t)]
        + [((rows, D), low_t)] * 2
        + [((rows, D), wide_t), ((HEADS, rows), wide_t), ((rows, D), low_t)]
        + [((D, D), low_t), ((D, D), low_t), ((D, 2 * D), low_t), ((D, D), low_t), ((16, D), low_t)],
        ids,
        [inputs, self_low, source_own, source_other, shards2, shards2_other, cols, row_data],
        attend_scratch,
        us=15,
    )
    hidden_other = core_swap(after(hidden_own, cross_low))
    width_s = 2 * FF // 2 + 3 * D + D // 2
    result, cross_dealt, second_grad, keep_a, send_a, sums = run(
        feed_forward,
        [
            ((rows, D), low_t),
            ((PAIRS, rows + 16, 2 * PAIR), low_t),
            ((rows, D), wide_t),
            ((rows, width_s), low_t),
            ((rows, width_s), low_t),
            ((8, D), wide_t),
        ],
        ids,
        [after(first, hidden_own), cross_low, cross_mixed, cross_lse, row_data, cross_q, wco, gs]
        + [cotangent[0], *slices3],
        [((rows, FF), wide_t), ((2, D, FF // 2), low_t), ((2, FF // 2, D), low_t)],
        us=8,
    )
    head_shapes = [((keys, PAIR), low_t)] * 2 + [((HEAD, keys), low_t)]
    cross_head = run(
        functools.partial(pair_setup, False),
        head_shapes,
        ids,
        [source_own, source_other, wckv, after(cols, cross_dealt)],
        [((PAIR, rows), wide_t)],
        us=4,
    )
    both_own = deal(cross_dealt)
    both_other = core_swap(after(both_own, cross_head[0]))
    width_a = FF // 2 + 2 * D + D // 2
    (dealt_a,) = run(
        grads_a,
        [((4, 128, width_a), low_t)],
        ids,
        [keep_a, core_swap(send_a)],
        [((D, FF // 2), low_t), ((FF // 2, D), low_t), ((D, D // 2), low_t)],
        us=6,
    )
    rows_a = deal(after(dealt_a, both_own))

    back_scratch = (
        [((8, rows, PAIR), low_t)] * 2
        + [((8, HEAD, rows), low_t)]
        + [((keys, PAIR), wide_t)] * 3
        + [((PAIR, rows), wide_t)]
    )
    cross_dq_t, cross_dkv = run(
        functools.partial(pair_back, False),
        [((8, HEAD, rows), low_t), ((8, 2 * HEAD, rows), low_t)],
        ids,
        [after(both_own, dealt_a), both_other, *cross_head],
        back_scratch,
        us=16,
    )
    self_head = run(
        functools.partial(pair_setup, True),
        [((8, rows, PAIR), low_t)] + head_shapes,
        ids,
        [stream_own, stream_other, wkv, after(cols, cross_dq_t), hidden_own, hidden_other, wq],
        [((PAIR, rows), wide_t)],
        us=4,
    )
    (cross_dw,) = run(
        functools.partial(pair_grads, False),
        [((4, 2 * HEAD, 128), low_t)],
        ids,
        [cross_dkv, source_own, source_other],
    )
    cross_back = deal_all(after(cross_dq_t, rows_a, self_head[0], cross_dw))
    shards_a = run(
        add_chips,
        [((32, width_a + 512), low_t)] * 4,
        ids,
        [after(rows_a, cross_dq_t), cross_dw],
    )
    first_grad, self_branch, self_dealt, cross_dq, sums = run(
        first_back,
        [
            ((rows, D), wide_t),
            ((rows, D), low_t),
            ((PAIRS, rows + 32, PAIR), low_t),
            ((rows, D), low_t),
            ((8, D), wide_t),
        ],
        ids,
        [after(cross_back, *shards_a), second_grad, normed, scale, self_mixed, self_lse, row_data, gs, wcq, wo, sums],
        us=4,
    )
    do_own = deal(self_dealt)
    moved_a = shard_swaps([after(part, first_grad) for part in shards_a])
    (dealt_b,) = run(
        grads_b,
        [((8, 64, 2 * D + 128 + 2 * rows), low_t)],
        ids,
        [first_low, cross_dq, self_low, self_branch, sums, cross_dkv],
        [((D, D), low_t)] * 2,
        us=3,
    )
    rows_b = deal_all(after(dealt_b, do_own))
    do_other = core_swap(after(do_own, dealt_b))
    (self_back_t,) = run(
        functools.partial(pair_back, True),
        [((8, 3 * HEAD, rows), low_t)],
        ids,
        [self_head[0], after(do_own, dealt_b, *shards_a), do_other, *self_head[1:], cols, row_data],
        back_scratch,
        us=16,
    )
    (self_dw,) = run(
        functools.partial(pair_grads, True),
        [((4, 3 * HEAD, 128), low_t)],
        ids,
        [self_back_t, stream_own, stream_other, hidden_own, hidden_other],
    )
    end_width = 2 * D + 2 * 128 + 12 * 128
    end_parts = run(end_sums, [((16, end_width), low_t)] * 4, ids, [rows_b, self_dw])
    moved_end = shard_swaps(end_parts)
    self_back = deal_all(after(self_back_t, end_parts[0], *moved_a))
    (source_grad,) = run(
        source_back,
        [((rows, D), wide_t)],
        ids,
        [rows_b, after(wckv, end_parts[0])],
        [((2 * D, rows), low_t)],
        us=3,
    )
    (copies_end,) = run(
        add_shards,
        [((4, 32, width_a + 512 + end_width // 2), low_t)],
        ids,
        [*moved_a, after(moved_end[0], source_grad), *moved_end[1:]],
    )
    all_own = deal(after(copies_end, self_back))
    hidden_grad, stream_grad = run(
        hidden_back,
        [((rows, D), wide_t)] * 2,
        ids,
        [self_back, first_grad, wq, wkv],
        [((3 * D, rows), low_t)],
        us=3,
    )
    all_other = core_swap(after(all_own, hidden_grad))
    (
        grad_in,
        grad_out,
        grad_cross_output,
        grad_cross_pair,
        grad_cross_query,
        grad_output,
        gain_grads,
        shift_grads,
        grad_query,
        grad_pair,
    ) = run(
        place_all,
        [((128, FF), wide_t), ((D, D), wide_t), ((128, D), wide_t), ((128, 2 * D), wide_t)]
        + [((128, D), wide_t)] * 2
        + [((3, 128), wide_t)] * 2
        + [((128, D), wide_t), ((128, 2 * D), wide_t)],
        ids,
        [all_own, all_other],
        [((2 * D, 128), wide_t), ((3 * D, 128), wide_t)],
    )
    return (
        result[None],
        hidden_grad[None],
        stream_grad[None],
        source_grad[None],
        grad_query,
        grad_pair,
        grad_output,
        grad_cross_query,
        grad_cross_pair,
        grad_cross_output,
        grad_in,
        grad_out,
        gain_grads,
        shift_grads,
    )


def solution(mesh):
    in_specs = (
        P("wa", "ctx", None),
        P("wa", "ctx", None),
        P("wa", "ctx", None),
        P("wa", None),
        P("wa", None),
        P("wa", None),
        P("wa", None),
        P("wa", None),
        P("wa", None),
        P("wa", None),
        P("wa", None),
        P("wa", None),
        P("wa", None),
        P("wa", None),
        P("wa", None),
        P(None, "wa"),
        P(None, "wa"),
        P("wa", "ctx", None),
    )
    out_specs = (
        P("wa", "ctx", None),
        P("wa", "ctx", None),
        P("wa", "ctx", None),
        P("wa", "ctx", None),
        P("wa", None),
        P("wa", None),
        P("wa", None),
        P("wa", None),
        P("wa", None),
        P("wa", None),
        P("wa", None),
        P("wa", None),
        P(None, "wa"),
        P(None, "wa"),
    )
    if mesh.axis_names != ("ctx", "wa") or mesh.shape["ctx"] != HEADS or mesh.shape["wa"] != 4:
        return jax.shard_map(
            general_shards, mesh=mesh, in_specs=in_specs, out_specs=out_specs, check_vma=False
        )

    def finer(spec):
        return P(*(("chip", "core") if axis == "ctx" else axis for axis in spec))

    return jax.shard_map(
        fast_shards,
        mesh=Mesh(mesh.devices.reshape(4, 2, 4), ("chip", "core", "wa")),
        in_specs=tuple(finer(spec) for spec in in_specs),
        out_specs=tuple(finer(spec) for spec in out_specs),
        check_vma=False,
    )
```

```python
import functools

import jax
import jax.numpy as jnp
from jax import lax
from jax.experimental import pallas as pl
from jax.experimental.pallas import tpu as pltpu
from jax.sharding import Mesh
from jax.sharding import PartitionSpec as P

D = 512
HEADS = 8
HEAD = 64
KEYBLK = 1024


layer_eps = 1e-05
neg_fill = -1e30


def sequence_ids(positions, seq_ends):
    return jnp.sum((positions[:, None] >= seq_ends[None, :]).astype(jnp.int32), axis=1)


def head_split(matrix):
    return matrix.reshape(matrix.shape[0], HEADS, HEAD)


def block_scores(query_heads, key_heads):
    raw_scores = jnp.einsum(
        "lhd,khd->hlk", query_heads, key_heads, preferred_element_type=jnp.float32
    )
    return raw_scores * float(HEAD) ** (-0.5)


def softmax_totals(queries, key_rows, allowed_fn):
    query_heads = head_split(queries)
    count_rows = queries.shape[0]

    def visit(state_pair, block_index):
        running_top, running_sum = state_pair
        block_start = block_index * KEYBLK
        key_piece = lax.dynamic_slice_in_dim(key_rows, block_start, KEYBLK, 0)
        allowed = allowed_fn(block_start)[None]
        scores = jnp.where(
            allowed, block_scores(query_heads, head_split(key_piece[:, :D])), neg_fill
        )
        new_top = jnp.maximum(running_top, jnp.max(scores, axis=2))
        weights = jnp.where(allowed, jnp.exp(scores - new_top[:, :, None]), 0.0)
        running_sum = running_sum * jnp.exp(running_top - new_top) + jnp.sum(weights, axis=2)
        return ((new_top, running_sum), None)

    initial = (
        jnp.full((HEADS, count_rows), neg_fill, jnp.float32),
        jnp.zeros((HEADS, count_rows), jnp.float32),
    )
    (final_top, final_sum), unused = lax.scan(
        visit, initial, jnp.arange(key_rows.shape[0] // KEYBLK)
    )
    return final_top + jnp.log(final_sum)


def attend_values(queries, key_rows, log_totals, allowed_fn):
    query_heads = head_split(queries)

    def visit(running, block_index):
        block_start = block_index * KEYBLK
        key_piece = lax.dynamic_slice_in_dim(key_rows, block_start, KEYBLK, 0)
        allowed = allowed_fn(block_start)[None]
        scores = block_scores(query_heads, head_split(key_piece[:, :D]))
        weights = jnp.where(allowed, jnp.exp(scores - log_totals[:, :, None]), 0.0)
        value_heads = head_split(key_piece[:, D:])
        return (
            running
            + jnp.einsum(
                "hlk,khd->lhd",
                weights.astype(jnp.bfloat16),
                value_heads,
                preferred_element_type=jnp.float32,
            ),
            None,
        )

    mixed, unused = lax.scan(
        visit, jnp.zeros(query_heads.shape, jnp.float32), jnp.arange(key_rows.shape[0] // KEYBLK)
    )
    return mixed.reshape(queries.shape[0], D)


def head_offsets(grad_low, attended):
    return jnp.sum(head_split(grad_low.astype(jnp.float32) * attended), axis=2).T


def attend_back(queries, key_rows, log_totals, attended, grad_low, allowed_fn):
    query_heads = head_split(queries)
    grad_heads = head_split(grad_low)
    offsets = head_offsets(grad_low, attended)
    scale_value = float(HEAD) ** (-0.5)

    def visit(query_grad, block_index):
        block_start = block_index * KEYBLK
        key_piece = lax.dynamic_slice_in_dim(key_rows, block_start, KEYBLK, 0)
        allowed = allowed_fn(block_start)[None]
        key_heads = head_split(key_piece[:, :D])
        value_heads = head_split(key_piece[:, D:])
        weights = jnp.where(
            allowed, jnp.exp(block_scores(query_heads, key_heads) - log_totals[:, :, None]), 0.0
        )
        value_grad = jnp.einsum(
            "hlk,lhd->khd",
            weights.astype(jnp.bfloat16),
            grad_heads,
            preferred_element_type=jnp.float32,
        )
        weight_grad = jnp.einsum(
            "lhd,khd->hlk", grad_heads, value_heads, preferred_element_type=jnp.float32
        )
        score_grad = (weights * (weight_grad - offsets[:, :, None]) * scale_value).astype(
            jnp.bfloat16
        )
        query_grad = query_grad + jnp.einsum(
            "hlk,khd->lhd", score_grad, key_heads, preferred_element_type=jnp.float32
        )
        key_grad = jnp.einsum(
            "hlk,lhd->khd", score_grad, query_heads, preferred_element_type=jnp.float32
        )
        return (
            query_grad,
            jnp.concatenate((key_grad.reshape(KEYBLK, D), value_grad.reshape(KEYBLK, D)), axis=1),
        )

    query_grad, grad_pieces = lax.scan(
        visit, jnp.zeros(query_heads.shape, jnp.float32), jnp.arange(key_rows.shape[0] // KEYBLK)
    )
    return (query_grad.reshape(queries.shape[0], D), grad_pieces.reshape(key_rows.shape[0], 2 * D))


def normalize(values, gain_row, shift_row):
    row_mean = jnp.mean(values, axis=1, keepdims=True)
    centred = values - row_mean
    scale_inv = lax.rsqrt(jnp.mean(centred * centred, axis=1, keepdims=True) + layer_eps)
    normed = centred * scale_inv
    return (normed * gain_row + shift_row, normed, scale_inv)


def normalize_back(grad_out, normed, scale_inv, gain_row):
    gain_term = jnp.sum(grad_out * normed, axis=0)
    shift_term = jnp.sum(grad_out, axis=0)
    scaled = grad_out * gain_row
    grad_in = scale_inv * (
        scaled
        - jnp.mean(scaled, axis=1, keepdims=True)
        - normed * jnp.mean(scaled * normed, axis=1, keepdims=True)
    )
    return (grad_in, gain_term, shift_term)


def matmul(left, right):
    return jnp.dot(left, right, preferred_element_type=jnp.float32)


def general_shards(
    hidden,
    stream,
    encoder,
    lengths,
    order,
    ranks,
    thresholds,
    self_query,
    self_key_value,
    self_output,
    cross_query,
    cross_key_value,
    cross_output,
    ffn_in,
    ffn_out,
    norm_gain,
    norm_shift,
    cotangent,
):
    (
        full_query,
        full_pair,
        full_output,
        full_cross_query,
        full_cross_pair,
        full_cross_output,
        full_in,
        full_out,
        gain_rows,
        shift_rows,
    ) = (
        lax.all_gather(self_query, "wa", axis=0, tiled=True),
        lax.all_gather(self_key_value, "wa", axis=0, tiled=True),
        lax.all_gather(self_output, "wa", axis=0, tiled=True),
        lax.all_gather(cross_query, "wa", axis=0, tiled=True),
        lax.all_gather(cross_key_value, "wa", axis=0, tiled=True),
        lax.all_gather(cross_output, "wa", axis=0, tiled=True),
        lax.all_gather(ffn_in, "wa", axis=0, tiled=True),
        lax.all_gather(ffn_out, "wa", axis=0, tiled=True),
        lax.all_gather(norm_gain, "wa", axis=1, tiled=True),
        lax.all_gather(norm_shift, "wa", axis=1, tiled=True),
    )
    gains = gain_rows.astype(jnp.float32)
    shifts = shift_rows.astype(jnp.float32)
    local_rows = hidden.shape[1]
    total_rows = order.shape[1]
    row_start = lax.axis_index("ctx") * local_rows
    seq_ends = jnp.cumsum(lengths[0])
    token_seq = sequence_ids(order[0], seq_ends)
    source_seq = sequence_ids(jnp.arange(total_rows, dtype=jnp.int32), seq_ends)
    query_seq = lax.dynamic_slice_in_dim(token_seq, row_start, local_rows)
    query_rows = row_start + jnp.arange(local_rows, dtype=jnp.int32)
    all_limits = thresholds[0]
    limits = lax.dynamic_slice_in_dim(all_limits, row_start, local_rows)
    key_ranks = ranks[0]

    def self_allowed(block_start):
        block_seq = lax.dynamic_slice_in_dim(token_seq, block_start, KEYBLK)
        block_rank = lax.dynamic_slice_in_dim(key_ranks, block_start, KEYBLK)
        block_rows = block_start + jnp.arange(KEYBLK, dtype=jnp.int32)
        return (query_seq[:, None] == block_seq[None, :]) & (
            (block_rank[None, :] < limits[:, None]) | (query_rows[:, None] == block_rows[None, :])
        )

    def cross_allowed(block_start):
        return (
            query_seq[:, None] == lax.dynamic_slice_in_dim(source_seq, block_start, KEYBLK)[None, :]
        )

    inputs = hidden[0]
    stream_rows = stream[0]
    source_rows = encoder[0]
    queries = matmul(inputs, full_query).astype(jnp.bfloat16)
    self_local = matmul(stream_rows, full_pair).astype(jnp.bfloat16)
    cross_local = matmul(source_rows, full_cross_pair).astype(jnp.bfloat16)
    self_keys, cross_keys = (
        lax.all_gather(self_local, "ctx", axis=0, tiled=True),
        lax.all_gather(cross_local, "ctx", axis=0, tiled=True),
    )
    self_totals = softmax_totals(queries, self_keys, self_allowed)
    self_mixed = attend_values(queries, self_keys, self_totals, self_allowed)
    self_low = self_mixed.astype(jnp.bfloat16)
    first, first_normed, first_scale = normalize(
        inputs.astype(jnp.float32) + matmul(self_low, full_output), gains[0], shifts[0]
    )
    first_low = first.astype(jnp.bfloat16)
    cross_queries = matmul(first_low, full_cross_query).astype(jnp.bfloat16)
    cross_totals = softmax_totals(cross_queries, cross_keys, cross_allowed)
    cross_mixed = attend_values(cross_queries, cross_keys, cross_totals, cross_allowed)
    cross_low = cross_mixed.astype(jnp.bfloat16)
    second, second_normed, second_scale = normalize(
        first + matmul(cross_low, full_cross_output), gains[1], shifts[1]
    )
    second_low = second.astype(jnp.bfloat16)
    hidden_pre = matmul(second_low, full_in)
    sigmoid_pre = jax.nn.sigmoid(hidden_pre)
    activated = (hidden_pre * sigmoid_pre).astype(jnp.bfloat16)
    result, third_normed, third_scale = normalize(
        second + matmul(activated, full_out), gains[2], shifts[2]
    )
    third_grad, gain_grad_c, shift_grad_c = normalize_back(
        cotangent[0].astype(jnp.float32), third_normed, third_scale, gains[2]
    )
    branch_grad = third_grad.astype(jnp.bfloat16)
    grad_ffn_out = matmul(activated.T, branch_grad)
    slope = sigmoid_pre * (1.0 + hidden_pre * (1.0 - sigmoid_pre))
    pre_grad = (matmul(branch_grad, full_out.T) * slope).astype(jnp.bfloat16)
    grad_ffn_in = matmul(second_low.T, pre_grad)
    second_total = third_grad + matmul(pre_grad, full_in.T)
    second_grad, gain_grad_b, shift_grad_b = normalize_back(
        second_total, second_normed, second_scale, gains[1]
    )
    cross_branch = second_grad.astype(jnp.bfloat16)
    grad_cross_output = matmul(cross_low.T, cross_branch)
    cross_mixed_grad = matmul(cross_branch, full_cross_output.T).astype(jnp.bfloat16)
    cross_query_term, cross_terms = attend_back(
        cross_queries, cross_keys, cross_totals, cross_mixed, cross_mixed_grad, cross_allowed
    )
    cross_query_low = cross_query_term.astype(jnp.bfloat16)
    grad_cross_query = matmul(first_low.T, cross_query_low)
    first_total = second_grad + matmul(cross_query_low, full_cross_query.T)
    first_grad, gain_grad_a, shift_grad_a = normalize_back(
        first_total, first_normed, first_scale, gains[0]
    )
    self_branch = first_grad.astype(jnp.bfloat16)
    grad_self_output = matmul(self_low.T, self_branch)
    self_mixed_grad = matmul(self_branch, full_output.T).astype(jnp.bfloat16)
    self_query_term, self_terms = attend_back(
        queries, self_keys, self_totals, self_mixed, self_mixed_grad, self_allowed
    )
    self_sum, cross_sum = (
        lax.psum_scatter(self_terms, "ctx", scatter_dimension=0, tiled=True),
        lax.psum_scatter(cross_terms, "ctx", scatter_dimension=0, tiled=True),
    )
    self_query_low = self_query_term.astype(jnp.bfloat16)
    grad_self_query = matmul(inputs.T, self_query_low)
    input_grad = first_grad + matmul(self_query_low, full_query.T)
    self_sum_low = self_sum.astype(jnp.bfloat16)
    grad_self_pair = matmul(stream_rows.T, self_sum_low)
    stream_grad = matmul(self_sum_low, full_pair.T)
    cross_sum_low = cross_sum.astype(jnp.bfloat16)
    grad_cross_pair = matmul(source_rows.T, cross_sum_low)
    source_grad = matmul(cross_sum_low, full_cross_pair.T)
    gain_grads = jnp.stack((gain_grad_a, gain_grad_b, gain_grad_c))
    shift_grads = jnp.stack((shift_grad_a, shift_grad_b, shift_grad_c))
    (
        share_query,
        share_pair,
        share_output,
        share_cross_query,
        share_cross_pair,
        share_cross_output,
        share_in,
        share_out,
        share_gain,
        share_shift,
    ) = (
        lax.psum_scatter(
            grad_self_query.astype(jnp.bfloat16), "wa", scatter_dimension=0, tiled=True
        ).astype(jnp.float32),
        lax.psum_scatter(
            grad_self_pair.astype(jnp.bfloat16), "wa", scatter_dimension=0, tiled=True
        ).astype(jnp.float32),
        lax.psum_scatter(
            grad_self_output.astype(jnp.bfloat16), "wa", scatter_dimension=0, tiled=True
        ).astype(jnp.float32),
        lax.psum_scatter(
            grad_cross_query.astype(jnp.bfloat16), "wa", scatter_dimension=0, tiled=True
        ).astype(jnp.float32),
        lax.psum_scatter(
            grad_cross_pair.astype(jnp.bfloat16), "wa", scatter_dimension=0, tiled=True
        ).astype(jnp.float32),
        lax.psum_scatter(
            grad_cross_output.astype(jnp.bfloat16), "wa", scatter_dimension=0, tiled=True
        ).astype(jnp.float32),
        lax.psum_scatter(
            grad_ffn_in.astype(jnp.bfloat16), "wa", scatter_dimension=0, tiled=True
        ).astype(jnp.float32),
        lax.psum_scatter(
            grad_ffn_out.astype(jnp.bfloat16), "wa", scatter_dimension=0, tiled=True
        ).astype(jnp.float32),
        lax.psum_scatter(
            gain_grads.astype(jnp.bfloat16), "wa", scatter_dimension=1, tiled=True
        ).astype(jnp.float32),
        lax.psum_scatter(
            shift_grads.astype(jnp.bfloat16), "wa", scatter_dimension=1, tiled=True
        ).astype(jnp.float32),
    )
    (
        total_query,
        total_pair,
        total_output,
        total_cross_query,
        total_cross_pair,
        total_cross_output,
        total_in,
        total_out,
        total_gain,
        total_shift,
    ) = lax.psum(
        (
            share_query,
            share_pair,
            share_output,
            share_cross_query,
            share_cross_pair,
            share_cross_output,
            share_in,
            share_out,
            share_gain,
            share_shift,
        ),
        "ctx",
    )
    return (
        result.astype(jnp.bfloat16)[None],
        input_grad[None],
        stream_grad[None],
        source_grad[None],
        total_query,
        total_pair,
        total_output,
        total_cross_query,
        total_cross_pair,
        total_cross_output,
        total_in,
        total_out,
        total_gain,
        total_shift,
    )


PAIR = 2 * HEAD
PAIRS = HEADS // 2
FF = 2048
low_t = jnp.bfloat16
wide_t = jnp.float32
vmem_spec = pl.BlockSpec(memory_space=pltpu.VMEM)
smem_spec = pl.BlockSpec(memory_space=pltpu.SMEM)


def run(body, outs, ids, args, scratch=(), us=2, vmem=56):
    outs = [jax.ShapeDtypeStruct(shape, kind) for shape, kind in outs]
    arrays = [arg[0] if isinstance(arg, tuple) else arg for arg in args]
    parts = [n for n, arg in enumerate(args) if isinstance(arg, tuple)]
    total = len(args) + len(outs) + len(scratch)

    def kernel(ids, *refs):
        refs, buffers, sems = list(refs[:total]), refs[total:-1], refs[-1]
        copies = []
        for m, n in enumerate(parts):
            start = args[n][1] * D
            copies.append(
                pltpu.make_async_copy(refs[n].at[:, :, start : start + D], buffers[m], sems.at[m])
            )
            copies[m].start()
            refs[n] = buffers[m]
        for copy in copies:
            copy.wait()
        body(ids, *refs)

    buffers = [pltpu.VMEM(args[n][0].shape[:2] + (D,), args[n][0].dtype) for n in parts]
    specs = [pl.BlockSpec(memory_space=pl.ANY) if n in parts else vmem_spec for n in range(len(args))]
    moved = sum(a.size * a.dtype.itemsize for a in arrays + outs)
    return pl.pallas_call(
        kernel,
        name=getattr(body, "func", body).__name__,
        out_shape=outs,
        in_specs=[smem_spec] + specs,
        out_specs=[vmem_spec] * len(outs),
        scratch_shapes=[pltpu.VMEM(shape, kind) for shape, kind in scratch]
        + buffers
        + [pltpu.SemaphoreType.DMA((max(1, len(parts)),))],
        compiler_params=pltpu.CompilerParams(vmem_limit_bytes=vmem * 1024 * 1024),
        cost_estimate=pl.CostEstimate(flops=us * 1_000_000_000, bytes_accessed=moved, transcendentals=0),
    )(ids, *arrays)


def dot_nn(a, b):
    return lax.dot_general(a, b, (((1,), (0,)), ((), ())), preferred_element_type=wide_t)


def dot_nt(a, b):
    return lax.dot_general(a, b, (((1,), (1,)), ((), ())), preferred_element_type=wide_t)


def dot_tn(a, b):
    return lax.dot_general(a, b, (((0,), (0,)), ((), ())), preferred_element_type=wide_t)


def at16(start, size=16):
    return pl.ds(pl.multiple_of(start, 16), size)


def at128(start, size=128):
    return pl.ds(pl.multiple_of(start, 128), size)


def half_mask(shape, axis, core):
    return (lax.broadcasted_iota(jnp.int32, shape, axis) // HEAD) == core


def attend_rows(q_ref, k_ref, vt_ref, bias_ref, s_ref, ot_ref, lse_ref):
    keys, rows = bias_ref.shape
    tile = min(1024, keys)
    spans = [slice(start, start + tile) for start in range(0, keys, tile)]
    lowest = jnp.full((8, rows), neg_fill, wide_t)

    def scores(head, here, top):
        pair = slice(head // 2 * PAIR, (head // 2 + 1) * PAIR)
        q = q_ref[:, pair]
        own_q = jnp.where(half_mask((rows, PAIR), 1, head % 2), q, jnp.zeros_like(q))
        s = dot_nt(k_ref[here, pair], own_q) + bias_ref[here, :]
        s_ref[head % 2, here, :] = s
        return jnp.maximum(top, jnp.max(s.reshape(tile // 8, 8, rows), axis=0))

    top = lowest
    for here in spans:
        top = scores(0, here, top)
    for head in range(HEADS):
        features = slice(head * HEAD, (head + 1) * HEAD)
        highest = jnp.max(top, axis=0, keepdims=True)
        total = jnp.zeros((8, rows), wide_t)
        mixed = jnp.zeros((HEAD, rows), wide_t)
        top = lowest
        for here in spans:
            if head + 1 < HEADS:
                top = scores(head + 1, here, top)
            w = jnp.exp(s_ref[head % 2, here, :] - highest)
            total = total + jnp.sum(w.reshape(tile // 8, 8, rows), axis=0)
            mixed = mixed + dot_nn(vt_ref[features, here], w.astype(low_t))
        total = jnp.sum(total, axis=0, keepdims=True)
        ot_ref[features, :] = mixed / total
        lse_ref[head : head + 1, :] = highest + jnp.log(total)


def finish_rows(ot_ref, low_out, mixed_out):
    mixed = ot_ref[...].T
    low_out[...] = mixed.astype(low_t)
    mixed_out[...] = mixed


def three_parts(value):
    high = value.astype(low_t).astype(wide_t)
    rest = value - high
    middle = rest.astype(low_t).astype(wide_t)
    return high, middle, rest - middle


def side_rows(lse, grad_low, mixed, row_data):
    product = grad_low.astype(wide_t) * mixed[...]
    lane = lax.broadcasted_iota(jnp.int32, (grad_low.shape[0], PAIR), 1)
    sums = jnp.zeros((grad_low.shape[0], PAIR), wide_t)
    for p in range(PAIRS):
        piece = product[:, p * PAIR : (p + 1) * PAIR]
        for h in range(2):
            mine = half_mask(piece.shape, 1, h)
            offset = jnp.sum(jnp.where(mine, piece, 0.0), axis=1, keepdims=True)
            sums = jnp.where(lane == p * 2 + h, offset, sums)
    offsets = sums.T
    seq = row_data[16:17, :]
    onehot = [(seq == float(n)).astype(wide_t) for n in range(4)]
    sides = []
    for p in range(PAIRS):
        pieces = []
        for h in range(2):
            head = p * 2 + h
            pieces += three_parts(-lse[head : head + 1, :])
            pieces += three_parts(-offsets[head : head + 1, :])
        sides.append(jnp.concatenate(pieces + onehot, axis=0).astype(low_t))
    return sides


def side_lanes(side, core):
    side = side.astype(wide_t)
    head = jnp.where(core == 0, side[0:6], side[6:12])
    gap = jnp.zeros((5, side.shape[1]), wide_t)
    rest = jnp.zeros((HEAD - 20, side.shape[1]), wide_t)
    half = jnp.concatenate((head[0:3], gap, head[3:6], gap, side[12:16], rest), axis=0)
    return jnp.concatenate((half, half), axis=0).T.astype(low_t)


def assemble(ids, parts, column, outs):
    for chip, other, block in parts:
        own = chip * 2 + (ids[1] ^ other)
        for e in range(4):
            rows = at16((ids[2] ^ e) * 128 + own * 16)
            start = column
            for out in outs:
                width = out.shape[1]
                out[rows, :] = block[e * 16 : (e + 1) * 16, start : start + width]
                start += width


def project_pairs(parts, w_pair, k_ref, vt_ref, wvt_ref):
    wvt_ref[...] = w_pair[:, D:].astype(wide_t).T.astype(low_t)
    for n, part in enumerate(parts):
        for k in range(PAIRS):
            rows = part.shape[1]
            start = (n * 4 + k) * rows
            k_ref[start : start + rows, :] = dot_nn(part[k], w_pair[:, :D]).astype(low_t)
            vt_ref[:, start : start + rows] = dot_nt(wvt_ref[...], part[k]).astype(low_t)


def self_forward(ids, hidden, own, other, *refs):
    slices, (cols, row_data), refs = refs[:8], refs[8:10], refs[10:]
    out, mixed, lse, wq, wkv, q_ref, k_ref, vt_ref, wvt_ref, bias_ref, s_ref, ot_ref = refs
    rows = hidden.shape[0]
    parts = [(ids[0] ^ k, n, slices[n * 4 + k]) for n in range(2) for k in range(4)]
    assemble(ids, parts, 0, (wq, wkv))
    q_ref[...] = (dot_nn(hidden[...], wq[...]).astype(low_t) * 0.125).astype(low_t)
    project_pairs((own, other), wkv, k_ref, vt_ref, wvt_ref)
    seq, limit = row_data[16:17, :], row_data[17:18, :]
    for b in range(8):
        seen = (cols[:, b : b + 1] == seq) & (cols[:, 8 + b : 9 + b] < limit)
        bias_ref[b * rows : (b + 1) * rows, :] = jnp.where(seen, 0.0, neg_fill)
    mine = lax.broadcasted_iota(jnp.int32, (rows, rows), 0) == lax.broadcasted_iota(
        jnp.int32, (rows, rows), 1
    )
    block = at128(ids[0] * rows, rows)
    bias_ref[block, :] = jnp.where(mine, 0.0, bias_ref[block, :])
    attend_rows(q_ref, k_ref, vt_ref, bias_ref, s_ref, ot_ref, lse)
    finish_rows(ot_ref, out, mixed)


def layer_norm(values, gain_row, shift_row):
    mean = jnp.mean(values, axis=1, keepdims=True)
    centred = values - mean
    scale = lax.rsqrt(jnp.mean(centred * centred, axis=1, keepdims=True) + layer_eps)
    normed = centred * scale
    return normed * gain_row + shift_row, normed, scale


def layer_norm_back(grad, normed, scale, gain_row):
    gain_term = jnp.sum(grad * normed, axis=0, keepdims=True)
    shift_term = jnp.sum(grad, axis=0, keepdims=True)
    scaled = grad * gain_row
    grad_in = scale * (
        scaled
        - jnp.mean(scaled, axis=1, keepdims=True)
        - normed * jnp.mean(scaled * normed, axis=1, keepdims=True)
    )
    return grad_in, gain_term, shift_term


def cross_forward(ids, hidden, self_low, own, other, *refs):
    slices, (cols, row_data) = refs[:2], refs[2:4]
    first, normed, scale_out, first_low, cross_low, mixed, lse, cross_q = refs[4:12]
    wo, wcq, wckv, wco, gs, q_ref, k_ref, vt_ref, wvt_ref, bias_ref, s_ref, ot_ref = refs[12:]
    for n in range(2):
        for e in range(4):
            rows = at16(e * 128 + (ids[1] ^ n) * 64, 64)
            start = 0
            for out in (wo, wcq, wckv, wco):
                width = out.shape[1]
                out[rows, :] = slices[n][e, :, start : start + width]
                start += width
    for e in range(4):
        gs[:, e * 128 : (e + 1) * 128] = slices[0][e, :16, 5 * D :]
    gain, shift = gs[0:1, :].astype(wide_t), gs[3:4, :].astype(wide_t)
    value, n0, s0 = layer_norm(
        hidden[...].astype(wide_t) + dot_nn(self_low[...], wo[...]), gain, shift
    )
    first[...] = value
    normed[...] = n0
    scale_out[...] = jnp.broadcast_to(s0, scale_out.shape)
    low = value.astype(low_t)
    first_low[...] = low
    q = dot_nn(low, wcq[...]).astype(low_t)
    cross_q[...] = q
    q_ref[...] = (q * 0.125).astype(low_t)
    rows = hidden.shape[0]
    project_pairs((own, other), wckv, k_ref, vt_ref, wvt_ref)
    for b in range(8):
        seen = cols[:, 16 + b : 17 + b] == row_data[16:17, :]
        bias_ref[b * rows : (b + 1) * rows, :] = jnp.where(seen, 0.0, neg_fill)
    attend_rows(q_ref, k_ref, vt_ref, bias_ref, s_ref, ot_ref, lse)
    finish_rows(ot_ref, cross_low, mixed)


def feed_forward(ids, first, cross_low, cross_mixed, lse, row_data, cross_q, wco, gs, cotangent, *refs):
    slices = refs[0:8]
    result, dealt, second_grad, keep, send, sums, slope, wins, wouts = refs[8:]
    half_ff = FF // 2
    for n in range(2):
        for k in range(4):
            chip, core, part = ids[0] ^ k, ids[1] ^ n, slices[n * 4 + k]
            for e in range(4):
                w, here = ids[2] ^ e, slice(e * 16, (e + 1) * 16)
                rows = at16(w * 128 + (chip * 2 + core) * 16)
                for g in range(4):
                    row = w * 256 + ((chip % 2) * 2 + core) * 64 + g * 16
                    wouts[(chip // 2) ^ ids[1], at16(row), :] = part[here, FF + g * D : FF + (g + 1) * D]
                    for h in range(2):
                        column = g * 512 + h * 256
                        wins[h ^ ids[1], rows, g * 256 : (g + 1) * 256] = part[here, column : column + 256]
    gains, shifts = gs[0:3, :].astype(wide_t), gs[3:6, :].astype(wide_t)
    second, n1, s1 = layer_norm(
        first[...] + dot_nn(cross_low[...], wco[...]), gains[1:2], shifts[1:2]
    )
    low = second.astype(low_t)
    for out in (keep, send):
        out[:, 2 * half_ff : 2 * half_ff + D] = low
        out[:, 2 * half_ff + 2 * D : 2 * half_ff + 3 * D] = cross_low[...]
    width = 512
    chunks = [(n, c) for n in range(2) for c in range(FF // 2 // width)]
    total = second
    for n, c in chunks:
        here = slice(c * width, (c + 1) * width)
        wide = slice(n * half_ff + c * width, n * half_ff + (c + 1) * width)
        pre = dot_nn(low, wins[n, :, here])
        sig = 1.0 / (1.0 + jnp.exp(-pre))
        act = (pre * sig).astype(low_t)
        (keep, send)[n][:, half_ff + c * width : half_ff + (c + 1) * width] = act
        slope[:, wide] = sig * (1.0 + pre * (1.0 - sig))
        total = total + dot_nn(act, wouts[n, here, :])
    value, n2, s2 = layer_norm(total, gains[2:3], shifts[2:3])
    result[...] = value.astype(low_t)
    third, gain_c, shift_c = layer_norm_back(cotangent[...].astype(wide_t), n2, s2, gains[2:3])
    third_low = third.astype(low_t)
    for out in (keep, send):
        out[:, 2 * half_ff + D : 2 * half_ff + 2 * D] = third_low
    total = third
    for n, c in chunks:
        here = slice(c * width, (c + 1) * width)
        wide = slice(n * half_ff + c * width, n * half_ff + (c + 1) * width)
        back = (dot_nt(third_low, wouts[n, here, :]) * slope[:, wide]).astype(low_t)
        (keep, send)[n][:, here] = back
        total = total + dot_nt(back, wins[n, :, here])
    grad, gain_b, shift_b = layer_norm_back(total, n1, s1, gains[1:2])
    second_grad[...] = grad
    grad_low = grad.astype(low_t)
    for out, core in ((keep, ids[1]), (send, 1 - ids[1])):
        half = grad_low[:, : D // 2]
        out[:, 2 * half_ff + 3 * D :] = jnp.where(core == 0, half, grad_low[:, D // 2 :])
    mixed = dot_nt(grad_low, wco[...]).astype(low_t)
    rows = grad_low.shape[0]
    sides = side_rows(lse, mixed, cross_mixed, row_data)
    for p in range(PAIRS):
        dealt[p, :rows, :PAIR] = cross_q[:, p * PAIR : (p + 1) * PAIR]
        dealt[p, :rows, PAIR:] = mixed[:, p * PAIR : (p + 1) * PAIR]
        dealt[p, rows:, :] = sides[p]
    zero = jnp.zeros_like(gain_b)
    sums[...] = jnp.concatenate((zero, gain_b, gain_c, zero, shift_b, shift_c, zero, zero), axis=0)


def grads_a(ids, keep, received, out, g_in, g_out, g_cross):
    half = FF // 2

    def both(left, right):
        return (dot_tn(keep[:, left], keep[:, right]) + dot_tn(received[:, left], received[:, right])).astype(low_t)

    at = [0, half] + [2 * half + n * D for n in range(4)]
    pre, act = slice(at[0], at[1]), slice(at[1], at[2])
    second, branch, low = (slice(at[n], at[n] + D) for n in (2, 3, 4))
    g_in[...] = both(second, pre)
    g_out[...] = both(act, branch)
    g_cross[...] = both(low, slice(at[5], at[5] + D // 2))
    for chip in range(4):
        for e in range(4):
            w, here = ids[2] ^ e, slice(e * 32, (e + 1) * 32)
            rows = at16(w * 128 + chip * 32, 32)
            out[chip, here, :half] = g_in[rows, :]
            for g in range(2):
                out[chip, here, half + g * D : half + (g + 1) * D] = g_out[
                    at16(w * 256 + chip * 64 + g * 32, 32), :
                ]
            out[chip, here, half + 2 * D :] = g_cross[rows, :]


def grads_b(ids, first_low, cross_dq, self_low, branch, sums, dkv, out, g_query, g_output):
    g_query[...] = dot_tn(first_low[...], cross_dq[...]).astype(low_t)
    g_output[...] = dot_tn(self_low[...], branch[...]).astype(low_t)
    row = jnp.concatenate((sums[...], jnp.zeros_like(sums[...])), axis=0).astype(low_t)
    rows = dkv.shape[2]
    for e in range(4):
        w, here = ids[2] ^ e, slice(e * 16, (e + 1) * 16)
        piece = row[:, :128]
        for k in range(1, 4):
            piece = jnp.where(w == k, row[:, k * 128 : (k + 1) * 128], piece)
        for device in range(8):
            own = at16(w * 128 + device * 16)
            out[device, here, :D] = g_query[own, :]
            out[device, here, D : 2 * D] = g_output[own, :]
            out[device, here, 2 * D : 2 * D + 128] = piece
    for device in range(8):
        for n in range(2):
            start = 2 * D + 128 + n * rows
            out[device, :, start : start + rows] = dkv[device, n * HEAD : (n + 1) * HEAD, :]


def pair_setup(is_self, ids, own, other, w_pair, cols, *refs):
    k_all, v_all, kt, turn = refs
    chip, core = ids[0], ids[1]
    rows = own.shape[1]
    mine = half_mask((rows, PAIR), 1, core)
    features = pl.ds(pl.multiple_of(core * HEAD, HEAD), HEAD)
    lane = lax.broadcasted_iota(jnp.int32, (rows, PAIR), 1) % HEAD
    ones_v = jnp.where((lane >= 8) & (lane < 11), 1.0, 0.0).astype(low_t)
    pair = at128(chip * PAIR)
    wk, wv = w_pair[:, pair], w_pair[:, at128(D + chip * PAIR)]
    for n, part in enumerate((own, other)):
        for k in range(4):
            b = n * 4 + k
            here = slice(b * rows, (b + 1) * rows)
            column = b if is_self else 16 + b
            seq = cols[:, column : column + 1].astype(jnp.int32)
            other_seq = (lane >= 16) & (lane < 20) & (lane != seq + 16)
            ones_k = jnp.where(other_seq, neg_fill, jnp.where(lane < 3, 1.0, 0.0)).astype(low_t)
            key = dot_nn(part[k], wk)
            turn[...] = key.T
            kt[:, here] = turn[features, :].astype(low_t)
            k_all[here, :] = jnp.where(mine, key.astype(low_t), ones_k)
            v_all[here, :] = jnp.where(mine, dot_nn(part[k], wv).astype(low_t), ones_v)


def pair_queries(ids, own, other, w_query, q_all):
    wq = w_query[:, at128(ids[0] * PAIR)]
    for n, part in enumerate((own, other)):
        for k in range(4):
            q_all[n * 4 + k] = dot_nn(part[k], wq).astype(low_t)


def pair_back(is_self, ids, *refs):
    if is_self:
        q_parts, do_own, do_other, k_all, v_all, kt, cols, row_data, back = refs[:9]
        do_parts = (do_own, do_other)
    else:
        both_own, both_other, k_all, v_all, kt, dq_keep, dq_send, dkv = refs[:8]
        both_parts = (both_own, both_other)
    q_all, do_all, dq_t, dk, dv, rank, turn = refs[-7:]
    core = ids[1]
    rows = q_all.shape[1]
    keys = 8 * rows
    mine = half_mask((rows, PAIR), 1, core)
    features = pl.ds(pl.multiple_of(core * HEAD, HEAD), HEAD)
    for n in range(2):
        for k in range(4):
            b = n * 4 + k
            if is_self:
                here = slice(b * rows, (b + 1) * rows)
                rank[here, :] = jnp.broadcast_to(cols[:, 8 + b : 9 + b], (rows, 128))
                q, do = q_parts[b], do_parts[n][k, :rows, :]
                side = jnp.concatenate(
                    (do_parts[n][k, rows : rows + 16, :], do_parts[n][k, rows + 16 :, :]), axis=1
                )
            else:
                q, do = both_parts[n][k, :rows, :PAIR], both_parts[n][k, :rows, PAIR:]
                side = both_parts[n][k, rows:, :]
            side = side_lanes(side, core)
            q_all[b] = jnp.where(mine, (q * 0.125).astype(low_t), side)
            do_all[b] = jnp.where(mine, do, side)
    dk[...] = jnp.zeros_like(dk)
    dv[...] = jnp.zeros_like(dv)
    tile = min(1024, keys)
    blocks = 1 if is_self else 2

    def step(step, carry):
        b, wide = step * blocks, blocks * rows
        q, do = (ref[pl.ds(b, blocks)].reshape(wide, PAIR) for ref in (q_all, do_all))
        dqt = jnp.zeros((HEAD, wide), wide_t)
        for t in range(keys // tile):
            here = slice(t * tile, (t + 1) * tile)
            w = jnp.exp(dot_nt(k_all[here, :], q))
            if is_self:
                ranks = jnp.concatenate((rank[here, :],) * (wide // 128), axis=1)
                index = lax.broadcasted_iota(jnp.int32, (tile, wide), 0)
                own = lax.broadcasted_iota(jnp.int32, (tile, wide), 1) + (b * rows - t * tile)
                w = jnp.where((ranks < row_data[pl.ds(8 + b, 1), :]) | (index == own), w, 0.0)
            ds = (w * dot_nt(v_all[here, :], do)).astype(low_t)
            dv[here, :] += dot_nn(w.astype(low_t), do)
            dk[here, :] += dot_nn(ds, q)
            dqt = dqt + dot_nn(kt[:, here], ds)
        dqt = (dqt * 0.125).astype(low_t)
        for n in range(blocks):
            dq_t[b + n] = dqt[:, n * rows : (n + 1) * rows]
        return carry

    lax.fori_loop(0, 8 // blocks, step, 0)
    for n in range(2):
        for k in range(4):
            b = n * 4 + k
            device = k * 2 + (core ^ n)
            here = slice(b * rows, (b + 1) * rows)
            if is_self:
                back[device, :HEAD, :] = dq_t[b]
            else:
                (dq_keep, dq_send)[n][k] = dq_t[b]
            out, start = (back, HEAD) if is_self else (dkv, 0)
            for value in (dk, dv):
                turn[...] = value[here, :].T
                out[device, start : start + HEAD, :] = turn[features, :].astype(low_t)
                start += HEAD


def pair_grads(is_self, ids, grads, own, other, *refs):
    dw = refs[-1]
    first = HEAD if is_self else 0
    total = jnp.zeros((2 * HEAD, D), wide_t)
    total_q = jnp.zeros((HEAD, D), wide_t)
    for n, part in enumerate((own, other)):
        for k in range(4):
            device = k * 2 + (ids[1] ^ n)
            total += dot_nn(grads[device, first:, :], part[k])
            if is_self:
                total_q += dot_nn(grads[device, :HEAD, :], refs[n][k])
    for w in range(4):
        columns = slice(w * 128, (w + 1) * 128)
        dw[w, first:, :] = total[:, columns].astype(low_t)
        if is_self:
            dw[w, :HEAD, :] = total_q[:, columns].astype(low_t)


def turned(value):
    return value.astype(wide_t).T.astype(low_t)


def pair_up(ids, keep, received, *outs):
    for k in range(4):
        p = ids[0] ^ k
        outs[k][at16(ids[1] * HEAD, HEAD), :] = keep[p]
        outs[k][at16((1 - ids[1]) * HEAD, HEAD), :] = received[p]


def first_back(ids, *refs):
    parts = refs[:4]
    second_grad, normed, scale, self_mixed, lse, row_data, gs, wcq, wo, sums_in = refs[4:14]
    first_grad, branch, dealt, dq, sums, all_t = refs[14:]
    for k in range(4):
        all_t[at128((ids[0] ^ k) * PAIR), :] = parts[k][...]
    dq[...] = turned(all_t[...])
    total = second_grad[...] + dot_nt(dq[...], wcq[...])
    grad, gain_a, shift_a = layer_norm_back(
        total, normed[...], scale[:, 0:1], gs[0:1, :].astype(wide_t)
    )
    first_grad[...] = grad
    low = grad.astype(low_t)
    branch[...] = low
    mixed = dot_nt(low, wo[...]).astype(low_t)
    rows = low.shape[0]
    sides = side_rows(lse, mixed, self_mixed, row_data)
    for p in range(PAIRS):
        dealt[p, :rows, :] = mixed[:, p * PAIR : (p + 1) * PAIR]
        dealt[p, rows : rows + 16, :] = sides[p][:, :PAIR]
        dealt[p, rows + 16 :, :] = sides[p][:, PAIR:]
    zero = jnp.zeros_like(gain_a)
    sums[...] = sums_in[...] + jnp.concatenate(
        (gain_a, zero, zero, shift_a, zero, zero, zero, zero), axis=0
    )


def source_back(ids, parts, wckv, out, dkv):
    rows = out.shape[0]
    for device in range(8):
        for n in range(2):
            start = 2 * D + 128 + n * rows
            dkv[n * D + device * HEAD : n * D + (device + 1) * HEAD, :] = parts[
                device, :, start : start + rows
            ]
    out[...] = dot_nt(turned(dkv[...]), wckv[...])


def hidden_back(ids, back, first_grad, wq, wkv, hidden_grad, stream_grad, all_t):
    for device in range(8):
        for n in range(3):
            all_t[n * D + device * HEAD : n * D + (device + 1) * HEAD, :] = back[
                device, n * HEAD : (n + 1) * HEAD, :
            ]
    hidden_grad[...] = first_grad[...] + dot_nt(turned(all_t[:D, :]), wq[...])
    stream_grad[...] = dot_nt(turned(all_t[D:, :]), wkv[...])


def add_parts(parts, rows, columns):
    total = parts[0, rows, columns].astype(wide_t)
    for n in range(1, parts.shape[0]):
        total = total + parts[n, rows, columns].astype(wide_t)
    return total.astype(low_t)


def add_chips(ids, parts, dw, *outs):
    width = parts.shape[2]
    for e in range(4):
        outs[e][:, :width] = add_parts(parts, slice(e * 32, (e + 1) * 32), slice(None))
        piece = dw[ids[2] ^ e]
        for g in range(4):
            outs[e][:, width + g * 128 : width + (g + 1) * 128] = piece[g * 32 : (g + 1) * 32, :]


def end_sums(ids, parts, dw, *outs):
    width = 2 * D + 128
    for e in range(4):
        outs[e][:, :width] = add_parts(parts, slice(e * 16, (e + 1) * 16), slice(0, width))
        outs[e][:, width : width + 128] = jnp.zeros((16, 128), low_t)
        piece = dw[ids[2] ^ e]
        for g in range(12):
            start = width + 128 + g * 128
            outs[e][:, start : start + 128] = piece[g * 16 : (g + 1) * 16, :]


def add_shards(ids, *refs):
    out = refs[8]

    def total(parts):
        value = parts[0][...].astype(wide_t)
        for part in parts[1:]:
            value = value + part[...].astype(wide_t)
        return value.astype(low_t)

    first, last = total(refs[:4]), total(refs[4:8])
    width, half = first.shape[1], last.shape[1] // 2
    for k in range(4):
        out[k, :, :width] = first
        out[k, :16, width:] = last[:, :half]
        out[k, 16:, width:] = last[:, half:]


def place_all(ids, own, other, *refs):
    g_in, g_out, g_cross, g_cross_pair, g_cross_query, g_output, gains, shifts, g_query, g_pair = refs[:10]
    pair_t, all_t = refs[10:]
    half = FF // 2
    start_cross = half + 2 * D
    start_pair = start_cross + D // 2
    start_end = start_pair + 4 * 128
    half_end = own.shape[2] - start_end
    for n, part in enumerate((own, other)):
        core = ids[1] ^ n
        for chip in range(4):
            rows = slice(chip * 32, (chip + 1) * 32)
            device = chip * 2 + core
            for k in range(4):
                g_in[rows, at128(k * 512 + core * 256, 256)] = part[
                    chip, :, k * 256 : (k + 1) * 256
                ].astype(wide_t)
            for g in range(2):
                g_out[at16(core * 256 + chip * 64 + g * 32, 32), :] = part[
                    chip, :, half + g * D : half + (g + 1) * D
                ].astype(wide_t)
            g_cross[rows, at128(core * 256, 256)] = part[chip, :, start_cross:start_pair].astype(wide_t)
            for g in range(4):
                column = start_pair + g * 128
                row = (g // 2) * D + device * HEAD + (g % 2) * 32
                pair_t[at16(row, 32), :] = part[chip, :, column : column + 128].astype(wide_t)

            def piece(column, width):
                row, at = (0, column) if column < half_end else (16, column - half_end)
                return part[chip, row : row + 16, start_end + at : start_end + at + width].astype(wide_t)

            own_rows = at16(device * 16)
            for column in range(0, D, 128):
                g_cross_query[own_rows, column : column + 128] = piece(column, 128)
                g_output[own_rows, column : column + 128] = piece(D + column, 128)
            if n == 0 and chip == 0:
                norms = piece(2 * D, 128)
                gains[...], shifts[...] = norms[0:3], norms[3:6]
            for g in range(12):
                row = (g // 4) * D + device * HEAD + (g % 4) * 16
                all_t[at16(row), :] = piece(2 * D + 256 + g * 128, 128)
    g_cross_pair[...] = pair_t[...].T
    g_query[...] = all_t[:D, :].T
    g_pair[...] = all_t[D:, :].T


def pack_start(ids, stream, source, wq, wkv, ffn_in, ffn_out, many, pack):
    own = ids[0] * 2 + ids[1]
    for k in range(4):
        many[k, :, :D] = stream[...]
        many[k, :, D:] = source[...]
        start = 3 * D + FF + k * D
        pack[:, start : start + D] = ffn_out[at16(own * 64 + k * 16), :]
    pack[:, :D] = wq[at16(own * 16), :]
    pack[:, D : 3 * D] = wkv[at16(own * 16), :]
    pack[:, 3 * D : 3 * D + FF] = ffn_in[at16(own * 16), :]


def pack_more(ids, *refs):
    weights, gain, shift, rows_in, pack, many = refs[:4], *refs[4:]
    rows = at16(ids[1] * 64, 64)
    norms = (gain[...].astype(wide_t), shift[...].astype(wide_t), jnp.zeros((58, 128), wide_t))
    norms = jnp.concatenate(norms, axis=0).astype(low_t)
    for k in range(4):
        start = 0
        for w in weights:
            pack[k, :, start : start + w.shape[1]] = w[rows, :]
            start += w.shape[1]
        pack[k, :, start:] = norms
        many[k] = rows_in[...]


def mask_data(ids, order, ranks, limits, cols, row_data, all_rows):
    rows = cols.shape[0]
    ends = [ids[3]]
    for n in range(1, 4):
        ends.append(ends[-1] + ids[3 + n])

    def sequence(position):
        return sum((position >= end).astype(wide_t) for end in ends)

    for n in range(2):
        for k in range(4):
            b = n * 4 + k
            device = k * 2 + (ids[1] ^ n)
            here = at128(device * rows, rows)
            index = lax.broadcasted_iota(jnp.int32, (1, rows), 1) + device * rows
            all_rows[b : b + 1, :] = sequence(order[:, here])
            all_rows[8 + b : 9 + b, :] = ranks[:, here].astype(wide_t)
            all_rows[16 + b : 17 + b, :] = sequence(index)
            row_data[8 + b : 9 + b, :] = limits[:, here].astype(wide_t)
    row_data[0:8, :] = all_rows[0:8, :]
    all_rows[24:32, :] = jnp.zeros((8, rows), wide_t)
    all_rows[24:25, :] = all_rows[pl.ds(ids[0], 1), :]
    row_data[16:24, :] = jnp.zeros((8, rows), wide_t)
    row_data[16:17, :] = all_rows[pl.ds(ids[0], 1), :]
    row_data[17:18, :] = row_data[pl.ds(8 + ids[0], 1), :]
    cols[:, :32] = all_rows[...].T


def pack_first(ids, *refs):
    parts, (one, two) = refs[:4], refs[4:]
    width = one.shape[1]
    for e in range(4):
        here = slice(e * 16, (e + 1) * 16)
        one[here, :] = parts[e][:, :width]
        two[here, :] = parts[e][:, width:]


def core_swap(value):
    return lax.ppermute(value, "core", [(0, 1), (1, 0)])


def chip_swaps(parts):
    moves = [[(i, i ^ k) for i in range(4)] for k in range(4)]
    return [parts[0]] + [lax.ppermute(parts[k], "chip", moves[k]) for k in range(1, 4)]


def shard_swaps(parts):
    moves = [[(i, i ^ k) for i in range(4)] for k in range(4)]
    return [parts[0]] + [lax.ppermute(parts[k], "wa", moves[k]) for k in range(1, 4)]


def deal(value):
    return lax.all_to_all(value, "chip", 0, 0, tiled=True)


def deal_all(value):
    return lax.all_to_all(value, ("chip", "core"), 0, 0, tiled=True)


def deal_both(value):
    own = deal(value)
    return own, core_swap(own)


def after(value, *others):
    return lax.optimization_barrier((value,) + others)[0]


def fast_shards(
    hidden,
    stream,
    encoder,
    lengths,
    order,
    ranks,
    thresholds,
    self_query,
    self_key_value,
    self_output,
    cross_query,
    cross_key_value,
    cross_output,
    ffn_in,
    ffn_out,
    norm_gain,
    norm_shift,
    cotangent,
):
    rows, keys = hidden.shape[1], order.shape[1]
    chip, core, mw = lax.axis_index("chip"), lax.axis_index("core"), lax.axis_index("wa")
    ids = jnp.stack((chip, core, mw)).astype(jnp.int32)
    inputs = hidden[0]

    many, pack1 = run(
        pack_start,
        [((4, rows, 2 * D), low_t), ((16, 3 * D + 2 * FF), low_t)],
        ids,
        [stream[0], encoder[0], self_query, self_key_value, ffn_in, ffn_out],
    )
    x_own = deal(many)
    shards1 = shard_swaps([pack1] * 4)
    copies2, hidden_copies = run(
        pack_more,
        [((4, 64, 5 * D + 128), low_t), ((4, rows, D), low_t)],
        ids,
        [after(self_output, pack1), cross_query, cross_key_value, cross_output, norm_gain, norm_shift]
        + [inputs],
    )
    cols, row_data = run(
        mask_data,
        [((rows, 32), wide_t), ((24, rows), wide_t)],
        jnp.concatenate((after(ids, pack1), lengths[0])),
        [order, ranks, thresholds],
        [((32, rows), wide_t)],
    )
    part1, part3 = run(
        pack_first,
        [((64, 3 * D), low_t), ((64, 2 * FF), low_t)],
        ids,
        [after(shards1[0], x_own, cols, copies2)] + shards1[1:],
    )
    slices1 = chip_swaps([part1] * 4)
    slices1 = slices1 + [core_swap(part) for part in slices1]
    shards2 = lax.all_to_all(after(copies2, x_own), "wa", 0, 0, tiled=True)
    x_other = core_swap(after(x_own, part1))
    slices3 = chip_swaps([after(part3, slices1[1])] * 4)
    stream_own, stream_other = (x_own, 0), (x_other, 0)
    source_own, source_other = (x_own, 1), (x_other, 1)

    attend_scratch = [
        ((rows, D), low_t),
        ((keys, D), low_t),
        ((D, keys), low_t),
        ((D, D), low_t),
        ((keys, rows), wide_t),
        ((2, keys, rows), wide_t),
        ((D, rows), wide_t),
    ]
    self_low, self_mixed, self_lse, wq, wkv = run(
        self_forward,
        [((rows, D), low_t), ((rows, D), wide_t), ((HEADS, rows), wide_t)]
        + [((D, D), low_t), ((D, 2 * D), low_t)],
        ids,
        [inputs, stream_own, stream_other, *slices1, cols, row_data],
        attend_scratch,
        us=15,
    )
    head_shapes = [((keys, PAIR), low_t)] * 2 + [((HEAD, keys), low_t)]
    self_head = run(
        functools.partial(pair_setup, True),
        head_shapes,
        ids,
        [stream_own, stream_other, wkv, after(cols, self_low)],
        [((PAIR, rows), wide_t)],
        us=4,
    )
    slices3 = slices3 + [core_swap(after(part, self_head[0])) for part in slices3]
    shards2_other = core_swap(after(shards2, self_head[0], *slices3[:4]))
    hidden_own = deal(after(hidden_copies, shards2, self_head[0], *slices3[:4]))
    (
        first,
        normed,
        scale,
        first_low,
        cross_low,
        cross_mixed,
        cross_lse,
        cross_q,
        wo,
        wcq,
        wckv,
        wco,
        gs,
    ) = run(
        cross_forward,
        [((rows, D), wide_t)] * 2
        + [((rows, 128), wide_t)]
        + [((rows, D), low_t)] * 2
        + [((rows, D), wide_t), ((HEADS, rows), wide_t), ((rows, D), low_t)]
        + [((D, D), low_t), ((D, D), low_t), ((D, 2 * D), low_t), ((D, D), low_t), ((16, D), low_t)],
        ids,
        [inputs, after(self_low, self_head[0]), source_own, source_other, shards2, shards2_other]
        + [cols, row_data],
        attend_scratch,
        us=15,
    )
    hidden_other = core_swap(after(hidden_own, cross_low))
    width_s = 2 * FF // 2 + 3 * D + D // 2
    result, cross_dealt, second_grad, keep_a, send_a, sums = run(
        feed_forward,
        [
            ((rows, D), low_t),
            ((PAIRS, rows + 16, 2 * PAIR), low_t),
            ((rows, D), wide_t),
            ((rows, width_s), low_t),
            ((rows, width_s), low_t),
            ((8, D), wide_t),
        ],
        ids,
        [after(first, hidden_own), cross_low, cross_mixed, cross_lse, row_data, cross_q, wco, gs]
        + [cotangent[0], *slices3],
        [((rows, FF), wide_t), ((2, D, FF // 2), low_t), ((2, FF // 2, D), low_t)],
        us=8,
    )
    cross_head = run(
        functools.partial(pair_setup, False),
        head_shapes,
        ids,
        [source_own, source_other, wckv, after(cols, cross_dealt)],
        [((PAIR, rows), wide_t)],
        us=4,
    )
    both_own = deal(cross_dealt)
    width_a = FF // 2 + 2 * D + D // 2
    (dealt_a,) = run(
        grads_a,
        [((4, 128, width_a), low_t)],
        ids,
        [keep_a, core_swap(send_a)],
        [((D, FF // 2), low_t), ((FF // 2, D), low_t), ((D, D // 2), low_t)],
        us=6,
    )
    rows_a = deal(after(dealt_a, both_own))
    both_other = core_swap(after(both_own, cross_head[0], dealt_a))

    back_scratch = (
        [((8, rows, PAIR), low_t)] * 2
        + [((8, HEAD, rows), low_t)]
        + [((keys, PAIR), wide_t)] * 3
        + [((PAIR, rows), wide_t)]
    )
    cq_keep, cq_send, cross_dkv = run(
        functools.partial(pair_back, False),
        [((4, HEAD, rows), low_t)] * 2 + [((8, 2 * HEAD, rows), low_t)],
        ids,
        [after(both_own, dealt_a), both_other, *cross_head],
        back_scratch,
        us=16,
    )
    pairs = run(pair_up, [((PAIR, rows), low_t)] * 4, ids, [cq_keep, core_swap(cq_send)])
    cross_back = chip_swaps(pairs)
    (self_queries,) = run(
        pair_queries,
        [((8, rows, PAIR), low_t)],
        ids,
        [hidden_own, hidden_other, after(wq, pairs[0])],
    )
    (cross_dw,) = run(
        functools.partial(pair_grads, False),
        [((4, 2 * HEAD, 128), low_t)],
        ids,
        [after(cross_dkv, pairs[0]), source_own, source_other],
    )
    first_grad, self_branch, self_dealt, cross_dq, sums = run(
        first_back,
        [
            ((rows, D), wide_t),
            ((rows, D), low_t),
            ((PAIRS, rows + 32, PAIR), low_t),
            ((rows, D), low_t),
            ((8, D), wide_t),
        ],
        ids,
        [after(cross_back[0], cross_dw, self_queries), *cross_back[1:], second_grad, normed, scale, self_mixed, self_lse, row_data, gs, wcq, wo, sums],
        [((D, rows), low_t)],
        us=4,
    )
    do_own = deal(after(self_dealt, rows_a))
    shards_a = run(
        add_chips,
        [((32, width_a + 512), low_t)] * 4,
        ids,
        [after(rows_a, first_grad), cross_dw],
    )
    moved_a = shard_swaps([after(part, do_own) for part in shards_a])
    (dealt_b,) = run(
        grads_b,
        [((8, 64, 2 * D + 128 + 2 * rows), low_t)],
        ids,
        [first_low, cross_dq, self_low, self_branch, sums, cross_dkv],
        [((D, D), low_t)] * 2,
        us=3,
    )
    rows_b = deal_all(after(dealt_b, do_own))
    do_other = core_swap(after(do_own, dealt_b, *shards_a))
    (self_back_t,) = run(
        functools.partial(pair_back, True),
        [((8, 3 * HEAD, rows), low_t)],
        ids,
        [self_queries, after(do_own, dealt_b, *shards_a), do_other, *self_head, cols, row_data],
        back_scratch,
        us=16,
    )
    (self_dw,) = run(
        functools.partial(pair_grads, True),
        [((4, 3 * HEAD, 128), low_t)],
        ids,
        [self_back_t, stream_own, stream_other, hidden_own, hidden_other],
    )
    end_width = 2 * D + 2 * 128 + 12 * 128
    end_parts = run(end_sums, [((16, end_width), low_t)] * 4, ids, [rows_b, self_dw])
    moved_end = shard_swaps(end_parts)
    self_back = deal_all(after(self_back_t, end_parts[0], *moved_a))
    (source_grad,) = run(
        source_back,
        [((rows, D), wide_t)],
        ids,
        [rows_b, after(wckv, end_parts[0])],
        [((2 * D, rows), low_t)],
        us=3,
    )
    (copies_end,) = run(
        add_shards,
        [((4, 32, width_a + 512 + end_width // 2), low_t)],
        ids,
        [*moved_a, after(moved_end[0], source_grad), *moved_end[1:]],
    )
    all_own = deal(after(copies_end, self_back))
    hidden_grad, stream_grad = run(
        hidden_back,
        [((rows, D), wide_t)] * 2,
        ids,
        [self_back, first_grad, wq, wkv],
        [((3 * D, rows), low_t)],
        us=3,
    )
    all_other = core_swap(after(all_own, hidden_grad))
    (
        grad_in,
        grad_out,
        grad_cross_output,
        grad_cross_pair,
        grad_cross_query,
        grad_output,
        gain_grads,
        shift_grads,
        grad_query,
        grad_pair,
    ) = run(
        place_all,
        [((128, FF), wide_t), ((D, D), wide_t), ((128, D), wide_t), ((128, 2 * D), wide_t)]
        + [((128, D), wide_t)] * 2
        + [((3, 128), wide_t)] * 2
        + [((128, D), wide_t), ((128, 2 * D), wide_t)],
        ids,
        [all_own, all_other],
        [((2 * D, 128), wide_t), ((3 * D, 128), wide_t)],
    )
    return (
        result[None],
        hidden_grad[None],
        stream_grad[None],
        source_grad[None],
        grad_query,
        grad_pair,
        grad_output,
        grad_cross_query,
        grad_cross_pair,
        grad_cross_output,
        grad_in,
        grad_out,
        gain_grads,
        shift_grads,
    )


def solution(mesh):
    in_specs = (
        P("wa", "ctx", None),
        P("wa", "ctx", None),
        P("wa", "ctx", None),
        P("wa", None),
        P("wa", None),
        P("wa", None),
        P("wa", None),
        P("wa", None),
        P("wa", None),
        P("wa", None),
        P("wa", None),
        P("wa", None),
        P("wa", None),
        P("wa", None),
        P("wa", None),
        P(None, "wa"),
        P(None, "wa"),
        P("wa", "ctx", None),
    )
    out_specs = (
        P("wa", "ctx", None),
        P("wa", "ctx", None),
        P("wa", "ctx", None),
        P("wa", "ctx", None),
        P("wa", None),
        P("wa", None),
        P("wa", None),
        P("wa", None),
        P("wa", None),
        P("wa", None),
        P("wa", None),
        P("wa", None),
        P(None, "wa"),
        P(None, "wa"),
    )
    if mesh.axis_names != ("ctx", "wa") or mesh.shape["ctx"] != HEADS or mesh.shape["wa"] != 4:
        return jax.shard_map(
            general_shards, mesh=mesh, in_specs=in_specs, out_specs=out_specs, check_vma=False
        )

    def finer(spec):
        return P(*(("chip", "core") if axis == "ctx" else axis for axis in spec))

    return jax.shard_map(
        fast_shards,
        mesh=Mesh(mesh.devices.reshape(4, 2, 4), ("chip", "core", "wa")),
        in_specs=tuple(finer(spec) for spec in in_specs),
        out_specs=tuple(finer(spec) for spec in out_specs),
        check_vma=False,
    )
```

```python
import functools

import jax
import jax.numpy as jnp
from jax import lax
from jax.experimental import pallas as pl
from jax.experimental.pallas import tpu as pltpu
from jax.sharding import Mesh
from jax.sharding import PartitionSpec as P

D = 512
HEADS = 8
HEAD = 64
KEYBLK = 1024


layer_eps = 1e-05
neg_fill = -1e30


def sequence_ids(positions, seq_ends):
    return jnp.sum((positions[:, None] >= seq_ends[None, :]).astype(jnp.int32), axis=1)


def head_split(matrix):
    return matrix.reshape(matrix.shape[0], HEADS, HEAD)


def block_scores(query_heads, key_heads):
    raw_scores = jnp.einsum(
        "lhd,khd->hlk", query_heads, key_heads, preferred_element_type=jnp.float32
    )
    return raw_scores * float(HEAD) ** (-0.5)


def softmax_totals(queries, key_rows, allowed_fn):
    query_heads = head_split(queries)
    count_rows = queries.shape[0]

    def visit(state_pair, block_index):
        running_top, running_sum = state_pair
        block_start = block_index * KEYBLK
        key_piece = lax.dynamic_slice_in_dim(key_rows, block_start, KEYBLK, 0)
        allowed = allowed_fn(block_start)[None]
        scores = jnp.where(
            allowed, block_scores(query_heads, head_split(key_piece[:, :D])), neg_fill
        )
        new_top = jnp.maximum(running_top, jnp.max(scores, axis=2))
        weights = jnp.where(allowed, jnp.exp(scores - new_top[:, :, None]), 0.0)
        running_sum = running_sum * jnp.exp(running_top - new_top) + jnp.sum(weights, axis=2)
        return ((new_top, running_sum), None)

    initial = (
        jnp.full((HEADS, count_rows), neg_fill, jnp.float32),
        jnp.zeros((HEADS, count_rows), jnp.float32),
    )
    (final_top, final_sum), unused = lax.scan(
        visit, initial, jnp.arange(key_rows.shape[0] // KEYBLK)
    )
    return final_top + jnp.log(final_sum)


def attend_values(queries, key_rows, log_totals, allowed_fn):
    query_heads = head_split(queries)

    def visit(running, block_index):
        block_start = block_index * KEYBLK
        key_piece = lax.dynamic_slice_in_dim(key_rows, block_start, KEYBLK, 0)
        allowed = allowed_fn(block_start)[None]
        scores = block_scores(query_heads, head_split(key_piece[:, :D]))
        weights = jnp.where(allowed, jnp.exp(scores - log_totals[:, :, None]), 0.0)
        value_heads = head_split(key_piece[:, D:])
        return (
            running
            + jnp.einsum(
                "hlk,khd->lhd",
                weights.astype(jnp.bfloat16),
                value_heads,
                preferred_element_type=jnp.float32,
            ),
            None,
        )

    mixed, unused = lax.scan(
        visit, jnp.zeros(query_heads.shape, jnp.float32), jnp.arange(key_rows.shape[0] // KEYBLK)
    )
    return mixed.reshape(queries.shape[0], D)


def head_offsets(grad_low, attended):
    return jnp.sum(head_split(grad_low.astype(jnp.float32) * attended), axis=2).T


def attend_back(queries, key_rows, log_totals, attended, grad_low, allowed_fn):
    query_heads = head_split(queries)
    grad_heads = head_split(grad_low)
    offsets = head_offsets(grad_low, attended)
    scale_value = float(HEAD) ** (-0.5)

    def visit(query_grad, block_index):
        block_start = block_index * KEYBLK
        key_piece = lax.dynamic_slice_in_dim(key_rows, block_start, KEYBLK, 0)
        allowed = allowed_fn(block_start)[None]
        key_heads = head_split(key_piece[:, :D])
        value_heads = head_split(key_piece[:, D:])
        weights = jnp.where(
            allowed, jnp.exp(block_scores(query_heads, key_heads) - log_totals[:, :, None]), 0.0
        )
        value_grad = jnp.einsum(
            "hlk,lhd->khd",
            weights.astype(jnp.bfloat16),
            grad_heads,
            preferred_element_type=jnp.float32,
        )
        weight_grad = jnp.einsum(
            "lhd,khd->hlk", grad_heads, value_heads, preferred_element_type=jnp.float32
        )
        score_grad = (weights * (weight_grad - offsets[:, :, None]) * scale_value).astype(
            jnp.bfloat16
        )
        query_grad = query_grad + jnp.einsum(
            "hlk,khd->lhd", score_grad, key_heads, preferred_element_type=jnp.float32
        )
        key_grad = jnp.einsum(
            "hlk,lhd->khd", score_grad, query_heads, preferred_element_type=jnp.float32
        )
        return (
            query_grad,
            jnp.concatenate((key_grad.reshape(KEYBLK, D), value_grad.reshape(KEYBLK, D)), axis=1),
        )

    query_grad, grad_pieces = lax.scan(
        visit, jnp.zeros(query_heads.shape, jnp.float32), jnp.arange(key_rows.shape[0] // KEYBLK)
    )
    return (query_grad.reshape(queries.shape[0], D), grad_pieces.reshape(key_rows.shape[0], 2 * D))


def normalize(values, gain_row, shift_row):
    row_mean = jnp.mean(values, axis=1, keepdims=True)
    centred = values - row_mean
    scale_inv = lax.rsqrt(jnp.mean(centred * centred, axis=1, keepdims=True) + layer_eps)
    normed = centred * scale_inv
    return (normed * gain_row + shift_row, normed, scale_inv)


def normalize_back(grad_out, normed, scale_inv, gain_row):
    gain_term = jnp.sum(grad_out * normed, axis=0)
    shift_term = jnp.sum(grad_out, axis=0)
    scaled = grad_out * gain_row
    grad_in = scale_inv * (
        scaled
        - jnp.mean(scaled, axis=1, keepdims=True)
        - normed * jnp.mean(scaled * normed, axis=1, keepdims=True)
    )
    return (grad_in, gain_term, shift_term)


def matmul(left, right):
    return jnp.dot(left, right, preferred_element_type=jnp.float32)


def general_shards(
    hidden,
    stream,
    encoder,
    lengths,
    order,
    ranks,
    thresholds,
    self_query,
    self_key_value,
    self_output,
    cross_query,
    cross_key_value,
    cross_output,
    ffn_in,
    ffn_out,
    norm_gain,
    norm_shift,
    cotangent,
):
    (
        full_query,
        full_pair,
        full_output,
        full_cross_query,
        full_cross_pair,
        full_cross_output,
        full_in,
        full_out,
        gain_rows,
        shift_rows,
    ) = (
        lax.all_gather(self_query, "wa", axis=0, tiled=True),
        lax.all_gather(self_key_value, "wa", axis=0, tiled=True),
        lax.all_gather(self_output, "wa", axis=0, tiled=True),
        lax.all_gather(cross_query, "wa", axis=0, tiled=True),
        lax.all_gather(cross_key_value, "wa", axis=0, tiled=True),
        lax.all_gather(cross_output, "wa", axis=0, tiled=True),
        lax.all_gather(ffn_in, "wa", axis=0, tiled=True),
        lax.all_gather(ffn_out, "wa", axis=0, tiled=True),
        lax.all_gather(norm_gain, "wa", axis=1, tiled=True),
        lax.all_gather(norm_shift, "wa", axis=1, tiled=True),
    )
    gains = gain_rows.astype(jnp.float32)
    shifts = shift_rows.astype(jnp.float32)
    local_rows = hidden.shape[1]
    total_rows = order.shape[1]
    row_start = lax.axis_index("ctx") * local_rows
    seq_ends = jnp.cumsum(lengths[0])
    token_seq = sequence_ids(order[0], seq_ends)
    source_seq = sequence_ids(jnp.arange(total_rows, dtype=jnp.int32), seq_ends)
    query_seq = lax.dynamic_slice_in_dim(token_seq, row_start, local_rows)
    query_rows = row_start + jnp.arange(local_rows, dtype=jnp.int32)
    all_limits = thresholds[0]
    limits = lax.dynamic_slice_in_dim(all_limits, row_start, local_rows)
    key_ranks = ranks[0]

    def self_allowed(block_start):
        block_seq = lax.dynamic_slice_in_dim(token_seq, block_start, KEYBLK)
        block_rank = lax.dynamic_slice_in_dim(key_ranks, block_start, KEYBLK)
        block_rows = block_start + jnp.arange(KEYBLK, dtype=jnp.int32)
        return (query_seq[:, None] == block_seq[None, :]) & (
            (block_rank[None, :] < limits[:, None]) | (query_rows[:, None] == block_rows[None, :])
        )

    def cross_allowed(block_start):
        return (
            query_seq[:, None] == lax.dynamic_slice_in_dim(source_seq, block_start, KEYBLK)[None, :]
        )

    inputs = hidden[0]
    stream_rows = stream[0]
    source_rows = encoder[0]
    queries = matmul(inputs, full_query).astype(jnp.bfloat16)
    self_local = matmul(stream_rows, full_pair).astype(jnp.bfloat16)
    cross_local = matmul(source_rows, full_cross_pair).astype(jnp.bfloat16)
    self_keys, cross_keys = (
        lax.all_gather(self_local, "ctx", axis=0, tiled=True),
        lax.all_gather(cross_local, "ctx", axis=0, tiled=True),
    )
    self_totals = softmax_totals(queries, self_keys, self_allowed)
    self_mixed = attend_values(queries, self_keys, self_totals, self_allowed)
    self_low = self_mixed.astype(jnp.bfloat16)
    first, first_normed, first_scale = normalize(
        inputs.astype(jnp.float32) + matmul(self_low, full_output), gains[0], shifts[0]
    )
    first_low = first.astype(jnp.bfloat16)
    cross_queries = matmul(first_low, full_cross_query).astype(jnp.bfloat16)
    cross_totals = softmax_totals(cross_queries, cross_keys, cross_allowed)
    cross_mixed = attend_values(cross_queries, cross_keys, cross_totals, cross_allowed)
    cross_low = cross_mixed.astype(jnp.bfloat16)
    second, second_normed, second_scale = normalize(
        first + matmul(cross_low, full_cross_output), gains[1], shifts[1]
    )
    second_low = second.astype(jnp.bfloat16)
    hidden_pre = matmul(second_low, full_in)
    sigmoid_pre = jax.nn.sigmoid(hidden_pre)
    activated = (hidden_pre * sigmoid_pre).astype(jnp.bfloat16)
    result, third_normed, third_scale = normalize(
        second + matmul(activated, full_out), gains[2], shifts[2]
    )
    third_grad, gain_grad_c, shift_grad_c = normalize_back(
        cotangent[0].astype(jnp.float32), third_normed, third_scale, gains[2]
    )
    branch_grad = third_grad.astype(jnp.bfloat16)
    grad_ffn_out = matmul(activated.T, branch_grad)
    slope = sigmoid_pre * (1.0 + hidden_pre * (1.0 - sigmoid_pre))
    pre_grad = (matmul(branch_grad, full_out.T) * slope).astype(jnp.bfloat16)
    grad_ffn_in = matmul(second_low.T, pre_grad)
    second_total = third_grad + matmul(pre_grad, full_in.T)
    second_grad, gain_grad_b, shift_grad_b = normalize_back(
        second_total, second_normed, second_scale, gains[1]
    )
    cross_branch = second_grad.astype(jnp.bfloat16)
    grad_cross_output = matmul(cross_low.T, cross_branch)
    cross_mixed_grad = matmul(cross_branch, full_cross_output.T).astype(jnp.bfloat16)
    cross_query_term, cross_terms = attend_back(
        cross_queries, cross_keys, cross_totals, cross_mixed, cross_mixed_grad, cross_allowed
    )
    cross_query_low = cross_query_term.astype(jnp.bfloat16)
    grad_cross_query = matmul(first_low.T, cross_query_low)
    first_total = second_grad + matmul(cross_query_low, full_cross_query.T)
    first_grad, gain_grad_a, shift_grad_a = normalize_back(
        first_total, first_normed, first_scale, gains[0]
    )
    self_branch = first_grad.astype(jnp.bfloat16)
    grad_self_output = matmul(self_low.T, self_branch)
    self_mixed_grad = matmul(self_branch, full_output.T).astype(jnp.bfloat16)
    self_query_term, self_terms = attend_back(
        queries, self_keys, self_totals, self_mixed, self_mixed_grad, self_allowed
    )
    self_sum, cross_sum = (
        lax.psum_scatter(self_terms, "ctx", scatter_dimension=0, tiled=True),
        lax.psum_scatter(cross_terms, "ctx", scatter_dimension=0, tiled=True),
    )
    self_query_low = self_query_term.astype(jnp.bfloat16)
    grad_self_query = matmul(inputs.T, self_query_low)
    input_grad = first_grad + matmul(self_query_low, full_query.T)
    self_sum_low = self_sum.astype(jnp.bfloat16)
    grad_self_pair = matmul(stream_rows.T, self_sum_low)
    stream_grad = matmul(self_sum_low, full_pair.T)
    cross_sum_low = cross_sum.astype(jnp.bfloat16)
    grad_cross_pair = matmul(source_rows.T, cross_sum_low)
    source_grad = matmul(cross_sum_low, full_cross_pair.T)
    gain_grads = jnp.stack((gain_grad_a, gain_grad_b, gain_grad_c))
    shift_grads = jnp.stack((shift_grad_a, shift_grad_b, shift_grad_c))
    (
        share_query,
        share_pair,
        share_output,
        share_cross_query,
        share_cross_pair,
        share_cross_output,
        share_in,
        share_out,
        share_gain,
        share_shift,
    ) = (
        lax.psum_scatter(
            grad_self_query.astype(jnp.bfloat16), "wa", scatter_dimension=0, tiled=True
        ).astype(jnp.float32),
        lax.psum_scatter(
            grad_self_pair.astype(jnp.bfloat16), "wa", scatter_dimension=0, tiled=True
        ).astype(jnp.float32),
        lax.psum_scatter(
            grad_self_output.astype(jnp.bfloat16), "wa", scatter_dimension=0, tiled=True
        ).astype(jnp.float32),
        lax.psum_scatter(
            grad_cross_query.astype(jnp.bfloat16), "wa", scatter_dimension=0, tiled=True
        ).astype(jnp.float32),
        lax.psum_scatter(
            grad_cross_pair.astype(jnp.bfloat16), "wa", scatter_dimension=0, tiled=True
        ).astype(jnp.float32),
        lax.psum_scatter(
            grad_cross_output.astype(jnp.bfloat16), "wa", scatter_dimension=0, tiled=True
        ).astype(jnp.float32),
        lax.psum_scatter(
            grad_ffn_in.astype(jnp.bfloat16), "wa", scatter_dimension=0, tiled=True
        ).astype(jnp.float32),
        lax.psum_scatter(
            grad_ffn_out.astype(jnp.bfloat16), "wa", scatter_dimension=0, tiled=True
        ).astype(jnp.float32),
        lax.psum_scatter(
            gain_grads.astype(jnp.bfloat16), "wa", scatter_dimension=1, tiled=True
        ).astype(jnp.float32),
        lax.psum_scatter(
            shift_grads.astype(jnp.bfloat16), "wa", scatter_dimension=1, tiled=True
        ).astype(jnp.float32),
    )
    (
        total_query,
        total_pair,
        total_output,
        total_cross_query,
        total_cross_pair,
        total_cross_output,
        total_in,
        total_out,
        total_gain,
        total_shift,
    ) = lax.psum(
        (
            share_query,
            share_pair,
            share_output,
            share_cross_query,
            share_cross_pair,
            share_cross_output,
            share_in,
            share_out,
            share_gain,
            share_shift,
        ),
        "ctx",
    )
    return (
        result.astype(jnp.bfloat16)[None],
        input_grad[None],
        stream_grad[None],
        source_grad[None],
        total_query,
        total_pair,
        total_output,
        total_cross_query,
        total_cross_pair,
        total_cross_output,
        total_in,
        total_out,
        total_gain,
        total_shift,
    )


PAIR = 2 * HEAD
PAIRS = HEADS // 2
FF = 2048
low_t = jnp.bfloat16
wide_t = jnp.float32
vmem_spec = pl.BlockSpec(memory_space=pltpu.VMEM)
smem_spec = pl.BlockSpec(memory_space=pltpu.SMEM)


def run(body, outs, ids, args, scratch=(), us=2, vmem=56):
    outs = [jax.ShapeDtypeStruct(shape, kind) for shape, kind in outs]
    arrays = [arg[0] if isinstance(arg, tuple) else arg for arg in args]
    parts = [n for n, arg in enumerate(args) if isinstance(arg, tuple)]
    total = len(args) + len(outs) + len(scratch)

    def kernel(ids, *refs):
        refs, buffers, sems = list(refs[:total]), refs[total:-1], refs[-1]
        copies = []
        for m, n in enumerate(parts):
            start = args[n][1] * D
            copies.append(
                pltpu.make_async_copy(refs[n].at[:, :, start : start + D], buffers[m], sems.at[m])
            )
            copies[m].start()
            refs[n] = buffers[m]
        for copy in copies:
            copy.wait()
        body(ids, *refs)

    buffers = [pltpu.VMEM(args[n][0].shape[:2] + (D,), args[n][0].dtype) for n in parts]
    specs = [pl.BlockSpec(memory_space=pl.ANY) if n in parts else vmem_spec for n in range(len(args))]
    moved = sum(a.size * a.dtype.itemsize for a in arrays + outs)
    return pl.pallas_call(
        kernel,
        name=getattr(body, "func", body).__name__,
        out_shape=outs,
        in_specs=[smem_spec] + specs,
        out_specs=[vmem_spec] * len(outs),
        scratch_shapes=[pltpu.VMEM(shape, kind) for shape, kind in scratch]
        + buffers
        + [pltpu.SemaphoreType.DMA((max(1, len(parts)),))],
        compiler_params=pltpu.CompilerParams(vmem_limit_bytes=vmem * 1024 * 1024),
        cost_estimate=pl.CostEstimate(flops=us * 1_000_000_000, bytes_accessed=moved, transcendentals=0),
    )(ids, *arrays)


def dot_nn(a, b):
    return lax.dot_general(a, b, (((1,), (0,)), ((), ())), preferred_element_type=wide_t)


def dot_nt(a, b):
    return lax.dot_general(a, b, (((1,), (1,)), ((), ())), preferred_element_type=wide_t)


def dot_tn(a, b):
    return lax.dot_general(a, b, (((0,), (0,)), ((), ())), preferred_element_type=wide_t)


def at16(start, size=16):
    return pl.ds(pl.multiple_of(start, 16), size)


def at128(start, size=128):
    return pl.ds(pl.multiple_of(start, 128), size)


def half_mask(shape, axis, core):
    return (lax.broadcasted_iota(jnp.int32, shape, axis) // HEAD) == core


def attend_rows(q_ref, k_ref, vt_ref, bias_ref, s_ref, ot_ref, lse_ref):
    keys, rows = bias_ref.shape
    tile = min(1024, keys)
    spans = [slice(start, start + tile) for start in range(0, keys, tile)]
    lowest = jnp.full((8, rows), neg_fill, wide_t)

    def scores(head, here, top):
        pair = slice(head // 2 * PAIR, (head // 2 + 1) * PAIR)
        q = q_ref[:, pair]
        own_q = jnp.where(half_mask((rows, PAIR), 1, head % 2), q, jnp.zeros_like(q))
        s = dot_nt(k_ref[here, pair], own_q) + bias_ref[here, :]
        s_ref[head % 2, here, :] = s
        return jnp.maximum(top, jnp.max(s.reshape(tile // 8, 8, rows), axis=0))

    top = lowest
    for here in spans:
        top = scores(0, here, top)
    for head in range(HEADS):
        features = slice(head * HEAD, (head + 1) * HEAD)
        highest = jnp.max(top, axis=0, keepdims=True)
        total = jnp.zeros((8, rows), wide_t)
        mixed = jnp.zeros((HEAD, rows), wide_t)
        top = lowest
        for here in spans:
            if head + 1 < HEADS:
                top = scores(head + 1, here, top)
            w = jnp.exp(s_ref[head % 2, here, :] - highest)
            total = total + jnp.sum(w.reshape(tile // 8, 8, rows), axis=0)
            mixed = mixed + dot_nn(vt_ref[features, here], w.astype(low_t))
        total = jnp.sum(total, axis=0, keepdims=True)
        ot_ref[features, :] = mixed / total
        lse_ref[head : head + 1, :] = highest + jnp.log(total)


def finish_rows(ot_ref, low_out, mixed_out):
    mixed = ot_ref[...].T
    low_out[...] = mixed.astype(low_t)
    mixed_out[...] = mixed


def three_parts(value):
    high = value.astype(low_t).astype(wide_t)
    rest = value - high
    middle = rest.astype(low_t).astype(wide_t)
    return high, middle, rest - middle


def side_rows(lse, grad_low, mixed, row_data):
    product = grad_low.astype(wide_t) * mixed[...]
    lane = lax.broadcasted_iota(jnp.int32, (grad_low.shape[0], PAIR), 1)
    sums = jnp.zeros((grad_low.shape[0], PAIR), wide_t)
    for p in range(PAIRS):
        piece = product[:, p * PAIR : (p + 1) * PAIR]
        for h in range(2):
            mine = half_mask(piece.shape, 1, h)
            offset = jnp.sum(jnp.where(mine, piece, 0.0), axis=1, keepdims=True)
            sums = jnp.where(lane == p * 2 + h, offset, sums)
    offsets = sums.T
    seq = row_data[16:17, :]
    onehot = [(seq == float(n)).astype(wide_t) for n in range(4)]
    sides = []
    for p in range(PAIRS):
        pieces = []
        for h in range(2):
            head = p * 2 + h
            pieces += three_parts(-lse[head : head + 1, :])
            pieces += three_parts(-offsets[head : head + 1, :])
        sides.append(jnp.concatenate(pieces + onehot, axis=0).astype(low_t))
    return sides


def side_lanes(side, core):
    side = side.astype(wide_t)
    head = jnp.where(core == 0, side[0:6], side[6:12])
    gap = jnp.zeros((5, side.shape[1]), wide_t)
    rest = jnp.zeros((HEAD - 20, side.shape[1]), wide_t)
    half = jnp.concatenate((head[0:3], gap, head[3:6], gap, side[12:16], rest), axis=0)
    return jnp.concatenate((half, half), axis=0).T.astype(low_t)


def assemble(ids, parts, column, outs):
    for chip, other, block in parts:
        own = chip * 2 + (ids[1] ^ other)
        for e in range(4):
            rows = at16((ids[2] ^ e) * 128 + own * 16)
            start = column
            for out in outs:
                width = out.shape[1]
                out[rows, :] = block[e * 16 : (e + 1) * 16, start : start + width]
                start += width


def project_pairs(parts, w_pair, k_ref, vt_ref, wvt_ref):
    wvt_ref[...] = w_pair[:, D:].astype(wide_t).T.astype(low_t)
    for n, part in enumerate(parts):
        for k in range(PAIRS):
            rows = part.shape[1]
            start = (n * 4 + k) * rows
            k_ref[start : start + rows, :] = dot_nn(part[k], w_pair[:, :D]).astype(low_t)
            vt_ref[:, start : start + rows] = dot_nt(wvt_ref[...], part[k]).astype(low_t)


def self_forward(ids, hidden, own, other, *refs):
    slices, (cols, row_data), refs = refs[:8], refs[8:10], refs[10:]
    out, mixed, lse, wq, wkv, q_ref, k_ref, vt_ref, wvt_ref, bias_ref, s_ref, ot_ref = refs
    rows = hidden.shape[0]
    parts = [(ids[0] ^ k, n, slices[n * 4 + k]) for n in range(2) for k in range(4)]
    assemble(ids, parts, 0, (wq, wkv))
    q_ref[...] = (dot_nn(hidden[...], wq[...]).astype(low_t) * 0.125).astype(low_t)
    project_pairs((own, other), wkv, k_ref, vt_ref, wvt_ref)
    seq, limit = row_data[16:17, :], row_data[17:18, :]
    for b in range(8):
        seen = (cols[:, b : b + 1] == seq) & (cols[:, 8 + b : 9 + b] < limit)
        bias_ref[b * rows : (b + 1) * rows, :] = jnp.where(seen, 0.0, neg_fill)
    mine = lax.broadcasted_iota(jnp.int32, (rows, rows), 0) == lax.broadcasted_iota(
        jnp.int32, (rows, rows), 1
    )
    block = at128(ids[0] * rows, rows)
    bias_ref[block, :] = jnp.where(mine, 0.0, bias_ref[block, :])
    attend_rows(q_ref, k_ref, vt_ref, bias_ref, s_ref, ot_ref, lse)
    finish_rows(ot_ref, out, mixed)


def layer_norm(values, gain_row, shift_row):
    mean = jnp.mean(values, axis=1, keepdims=True)
    centred = values - mean
    scale = lax.rsqrt(jnp.mean(centred * centred, axis=1, keepdims=True) + layer_eps)
    normed = centred * scale
    return normed * gain_row + shift_row, normed, scale


def layer_norm_back(grad, normed, scale, gain_row):
    gain_term = jnp.sum(grad * normed, axis=0, keepdims=True)
    shift_term = jnp.sum(grad, axis=0, keepdims=True)
    scaled = grad * gain_row
    grad_in = scale * (
        scaled
        - jnp.mean(scaled, axis=1, keepdims=True)
        - normed * jnp.mean(scaled * normed, axis=1, keepdims=True)
    )
    return grad_in, gain_term, shift_term


def head_arrays(ids, k_ref, vt_ref, cols, column, k_all, v_all, kt, turn):
    rows = turn.shape[1]
    core = ids[1]
    mine = half_mask((rows, PAIR), 1, core)
    features = pl.ds(pl.multiple_of(core * HEAD, HEAD), HEAD)
    lane = lax.broadcasted_iota(jnp.int32, (rows, PAIR), 1) % HEAD
    ones_v = jnp.where((lane >= 8) & (lane < 11), 1.0, 0.0).astype(low_t)
    pair = at128(ids[0] * PAIR)
    for b in range(8):
        here = slice(b * rows, (b + 1) * rows)
        seq = cols[:, column + b : column + b + 1].astype(jnp.int32)
        other_seq = (lane >= 16) & (lane < 20) & (lane != seq + 16)
        ones_k = jnp.where(other_seq, neg_fill, jnp.where(lane < 3, 1.0, 0.0)).astype(low_t)
        key = k_ref[here, pair]
        k_all[here, :] = jnp.where(mine, key, ones_k)
        turn[...] = key.astype(wide_t).T
        kt[:, here] = turn[features, :].astype(low_t)
        v_all[here, :] = jnp.where(mine, turned(vt_ref[pair, here]), ones_v)


def cross_forward(ids, hidden, self_low, own, other, *refs):
    slices, (cols, row_data) = refs[:2], refs[2:4]
    first, normed, scale_out, first_low, cross_low, mixed, lse, cross_q = refs[4:12]
    wo, wcq, wckv, wco, gs, k_all, v_all, kt = refs[12:20]
    q_ref, k_ref, vt_ref, wvt_ref, bias_ref, s_ref, ot_ref, turn = refs[20:]
    for n in range(2):
        for e in range(4):
            rows = at16(e * 128 + (ids[1] ^ n) * 64, 64)
            start = 0
            for out in (wo, wcq, wckv, wco):
                width = out.shape[1]
                out[rows, :] = slices[n][e, :, start : start + width]
                start += width
    for e in range(4):
        gs[:, e * 128 : (e + 1) * 128] = slices[0][e, :16, 5 * D :]
    gain, shift = gs[0:1, :].astype(wide_t), gs[3:4, :].astype(wide_t)
    value, n0, s0 = layer_norm(
        hidden[...].astype(wide_t) + dot_nn(self_low[...], wo[...]), gain, shift
    )
    first[...] = value
    normed[...] = n0
    scale_out[...] = jnp.broadcast_to(s0, scale_out.shape)
    low = value.astype(low_t)
    first_low[...] = low
    q = dot_nn(low, wcq[...]).astype(low_t)
    cross_q[...] = q
    q_ref[...] = (q * 0.125).astype(low_t)
    rows = hidden.shape[0]
    project_pairs((own, other), wckv, k_ref, vt_ref, wvt_ref)
    for b in range(8):
        seen = cols[:, 16 + b : 17 + b] == row_data[16:17, :]
        bias_ref[b * rows : (b + 1) * rows, :] = jnp.where(seen, 0.0, neg_fill)
    attend_rows(q_ref, k_ref, vt_ref, bias_ref, s_ref, ot_ref, lse)
    finish_rows(ot_ref, cross_low, mixed)
    head_arrays(ids, k_ref, vt_ref, cols, 16, k_all, v_all, kt, turn)


def feed_forward(ids, first, cross_low, cross_mixed, lse, row_data, cross_q, wco, gs, cotangent, *refs):
    slices = refs[0:8]
    result, dealt, second_grad, keep, send, sums, slope, wins, wouts = refs[8:]
    half_ff = FF // 2
    for n in range(2):
        for k in range(4):
            chip, core, part = ids[0] ^ k, ids[1] ^ n, slices[n * 4 + k]
            for e in range(4):
                w, here = ids[2] ^ e, slice(e * 16, (e + 1) * 16)
                rows = at16(w * 128 + (chip * 2 + core) * 16)
                for g in range(4):
                    row = w * 256 + ((chip % 2) * 2 + core) * 64 + g * 16
                    wouts[(chip // 2) ^ ids[1], at16(row), :] = part[here, FF + g * D : FF + (g + 1) * D]
                    for h in range(2):
                        column = g * 512 + h * 256
                        wins[h ^ ids[1], rows, g * 256 : (g + 1) * 256] = part[here, column : column + 256]
    gains, shifts = gs[0:3, :].astype(wide_t), gs[3:6, :].astype(wide_t)
    second, n1, s1 = layer_norm(
        first[...] + dot_nn(cross_low[...], wco[...]), gains[1:2], shifts[1:2]
    )
    low = second.astype(low_t)
    for out in (keep, send):
        out[:, 2 * half_ff : 2 * half_ff + D] = low
        out[:, 2 * half_ff + 2 * D : 2 * half_ff + 3 * D] = cross_low[...]
    width = 512
    chunks = [(n, c) for n in range(2) for c in range(FF // 2 // width)]
    total = second
    for n, c in chunks:
        here = slice(c * width, (c + 1) * width)
        wide = slice(n * half_ff + c * width, n * half_ff + (c + 1) * width)
        pre = dot_nn(low, wins[n, :, here])
        sig = 1.0 / (1.0 + jnp.exp(-pre))
        act = (pre * sig).astype(low_t)
        (keep, send)[n][:, half_ff + c * width : half_ff + (c + 1) * width] = act
        slope[:, wide] = sig * (1.0 + pre * (1.0 - sig))
        total = total + dot_nn(act, wouts[n, here, :])
    value, n2, s2 = layer_norm(total, gains[2:3], shifts[2:3])
    result[...] = value.astype(low_t)
    third, gain_c, shift_c = layer_norm_back(cotangent[...].astype(wide_t), n2, s2, gains[2:3])
    third_low = third.astype(low_t)
    for out in (keep, send):
        out[:, 2 * half_ff + D : 2 * half_ff + 2 * D] = third_low
    total = third
    for n, c in chunks:
        here = slice(c * width, (c + 1) * width)
        wide = slice(n * half_ff + c * width, n * half_ff + (c + 1) * width)
        back = (dot_nt(third_low, wouts[n, here, :]) * slope[:, wide]).astype(low_t)
        (keep, send)[n][:, here] = back
        total = total + dot_nt(back, wins[n, :, here])
    grad, gain_b, shift_b = layer_norm_back(total, n1, s1, gains[1:2])
    second_grad[...] = grad
    grad_low = grad.astype(low_t)
    for out, core in ((keep, ids[1]), (send, 1 - ids[1])):
        half = grad_low[:, : D // 2]
        out[:, 2 * half_ff + 3 * D :] = jnp.where(core == 0, half, grad_low[:, D // 2 :])
    mixed = dot_nt(grad_low, wco[...]).astype(low_t)
    rows = grad_low.shape[0]
    sides = side_rows(lse, mixed, cross_mixed, row_data)
    for p in range(PAIRS):
        dealt[p, :rows, :PAIR] = cross_q[:, p * PAIR : (p + 1) * PAIR]
        dealt[p, :rows, PAIR:] = mixed[:, p * PAIR : (p + 1) * PAIR]
        dealt[p, rows:, :] = sides[p]
    zero = jnp.zeros_like(gain_b)
    sums[...] = jnp.concatenate((zero, gain_b, gain_c, zero, shift_b, shift_c, zero, zero), axis=0)


def grads_a(ids, keep, received, out, g_in, g_out, g_cross):
    half = FF // 2

    def both(left, right):
        return (dot_tn(keep[:, left], keep[:, right]) + dot_tn(received[:, left], received[:, right])).astype(low_t)

    at = [0, half] + [2 * half + n * D for n in range(4)]
    pre, act = slice(at[0], at[1]), slice(at[1], at[2])
    second, branch, low = (slice(at[n], at[n] + D) for n in (2, 3, 4))
    g_in[...] = both(second, pre)
    g_out[...] = both(act, branch)
    g_cross[...] = both(low, slice(at[5], at[5] + D // 2))
    for chip in range(4):
        for e in range(4):
            w, here = ids[2] ^ e, slice(e * 32, (e + 1) * 32)
            rows = at16(w * 128 + chip * 32, 32)
            out[chip, here, :half] = g_in[rows, :]
            for g in range(2):
                out[chip, here, half + g * D : half + (g + 1) * D] = g_out[
                    at16(w * 256 + chip * 64 + g * 32, 32), :
                ]
            out[chip, here, half + 2 * D :] = g_cross[rows, :]


def grads_b(ids, first_low, cross_dq, self_low, branch, sums, dkv, out, g_query, g_output):
    g_query[...] = dot_tn(first_low[...], cross_dq[...]).astype(low_t)
    g_output[...] = dot_tn(self_low[...], branch[...]).astype(low_t)
    row = jnp.concatenate((sums[...], jnp.zeros_like(sums[...])), axis=0).astype(low_t)
    rows = dkv.shape[2]
    for e in range(4):
        w, here = ids[2] ^ e, slice(e * 16, (e + 1) * 16)
        piece = row[:, :128]
        for k in range(1, 4):
            piece = jnp.where(w == k, row[:, k * 128 : (k + 1) * 128], piece)
        for device in range(8):
            own = at16(w * 128 + device * 16)
            out[device, here, :D] = g_query[own, :]
            out[device, here, D : 2 * D] = g_output[own, :]
            out[device, here, 2 * D : 2 * D + 128] = piece
    for device in range(8):
        for n in range(2):
            start = 2 * D + 128 + n * rows
            out[device, :, start : start + rows] = dkv[device, n * HEAD : (n + 1) * HEAD, :]


def pair_setup(is_self, ids, own, other, w_pair, cols, *refs):
    k_all, v_all, kt, turn = refs
    chip, core = ids[0], ids[1]
    rows = own.shape[1]
    mine = half_mask((rows, PAIR), 1, core)
    features = pl.ds(pl.multiple_of(core * HEAD, HEAD), HEAD)
    lane = lax.broadcasted_iota(jnp.int32, (rows, PAIR), 1) % HEAD
    ones_v = jnp.where((lane >= 8) & (lane < 11), 1.0, 0.0).astype(low_t)
    pair = at128(chip * PAIR)
    wk, wv = w_pair[:, pair], w_pair[:, at128(D + chip * PAIR)]
    for n, part in enumerate((own, other)):
        for k in range(4):
            b = n * 4 + k
            here = slice(b * rows, (b + 1) * rows)
            column = b if is_self else 16 + b
            seq = cols[:, column : column + 1].astype(jnp.int32)
            other_seq = (lane >= 16) & (lane < 20) & (lane != seq + 16)
            ones_k = jnp.where(other_seq, neg_fill, jnp.where(lane < 3, 1.0, 0.0)).astype(low_t)
            key = dot_nn(part[k], wk)
            turn[...] = key.T
            kt[:, here] = turn[features, :].astype(low_t)
            k_all[here, :] = jnp.where(mine, key.astype(low_t), ones_k)
            v_all[here, :] = jnp.where(mine, dot_nn(part[k], wv).astype(low_t), ones_v)


def pair_queries(ids, own, other, w_query, q_all):
    wq = w_query[:, at128(ids[0] * PAIR)]
    for n, part in enumerate((own, other)):
        for k in range(4):
            q_all[n * 4 + k] = dot_nn(part[k], wq).astype(low_t)


def pair_back(is_self, ids, *refs):
    if is_self:
        q_parts, do_own, do_other, k_all, v_all, kt, cols, row_data, back = refs[:9]
        do_parts = (do_own, do_other)
    else:
        both_own, both_other, k_all, v_all, kt, dq_keep, dq_send, dkv = refs[:8]
        both_parts = (both_own, both_other)
    q_all, do_all, dq_t, dk, dv, rank, turn = refs[-7:]
    core = ids[1]
    rows = q_all.shape[1]
    keys = 8 * rows
    mine = half_mask((rows, PAIR), 1, core)
    features = pl.ds(pl.multiple_of(core * HEAD, HEAD), HEAD)
    for n in range(2):
        for k in range(4):
            b = n * 4 + k
            if is_self:
                here = slice(b * rows, (b + 1) * rows)
                rank[here, :] = jnp.broadcast_to(cols[:, 8 + b : 9 + b], (rows, 128))
                q, do = q_parts[b], do_parts[n][k, :rows, :]
                side = jnp.concatenate(
                    (do_parts[n][k, rows : rows + 16, :], do_parts[n][k, rows + 16 :, :]), axis=1
                )
            else:
                q, do = both_parts[n][k, :rows, :PAIR], both_parts[n][k, :rows, PAIR:]
                side = both_parts[n][k, rows:, :]
            side = side_lanes(side, core)
            q_all[b] = jnp.where(mine, (q * 0.125).astype(low_t), side)
            do_all[b] = jnp.where(mine, do, side)
    dk[...] = jnp.zeros_like(dk)
    dv[...] = jnp.zeros_like(dv)
    tile = min(1024, keys)
    blocks = 1 if is_self else 2

    def step(step, carry):
        b, wide = step * blocks, blocks * rows
        q, do = (ref[pl.ds(b, blocks)].reshape(wide, PAIR) for ref in (q_all, do_all))
        dqt = jnp.zeros((HEAD, wide), wide_t)
        for t in range(keys // tile):
            here = slice(t * tile, (t + 1) * tile)
            w = jnp.exp(dot_nt(k_all[here, :], q))
            if is_self:
                ranks = jnp.concatenate((rank[here, :],) * (wide // 128), axis=1)
                index = lax.broadcasted_iota(jnp.int32, (tile, wide), 0)
                own = lax.broadcasted_iota(jnp.int32, (tile, wide), 1) + (b * rows - t * tile)
                w = jnp.where((ranks < row_data[pl.ds(8 + b, 1), :]) | (index == own), w, 0.0)
            ds = (w * dot_nt(v_all[here, :], do)).astype(low_t)
            dv[here, :] += dot_nn(w.astype(low_t), do)
            dk[here, :] += dot_nn(ds, q)
            dqt = dqt + dot_nn(kt[:, here], ds)
        dqt = (dqt * 0.125).astype(low_t)
        for n in range(blocks):
            dq_t[b + n] = dqt[:, n * rows : (n + 1) * rows]
        return carry

    lax.fori_loop(0, 8 // blocks, step, 0)
    for n in range(2):
        for k in range(4):
            b = n * 4 + k
            device = k * 2 + (core ^ n)
            here = slice(b * rows, (b + 1) * rows)
            if is_self:
                back[device, :HEAD, :] = dq_t[b]
            else:
                (dq_keep, dq_send)[n][k] = dq_t[b]
            out, start = (back, HEAD) if is_self else (dkv, 0)
            for value in (dk, dv):
                turn[...] = value[here, :].T
                out[device, start : start + HEAD, :] = turn[features, :].astype(low_t)
                start += HEAD


def head_grads(grads, own, other, core, hidden=None):
    first = HEAD if hidden else 0
    total = jnp.zeros((2 * HEAD, D), wide_t)
    total_q = jnp.zeros((HEAD, D), wide_t)
    for n, part in enumerate((own, other)):
        for k in range(4):
            device = k * 2 + (core ^ n)
            total += dot_nn(grads[device, first:, :], part[k])
            if hidden:
                total_q += dot_nn(grads[device, :HEAD, :], hidden[n][k])
    return total, total_q


def pair_grads(ids, grads, own, other, dw):
    total, unused = head_grads(grads, own, other, ids[1])
    for w in range(4):
        dw[w] = total[:, w * 128 : (w + 1) * 128].astype(low_t)


def turned(value):
    return value.astype(wide_t).T.astype(low_t)


def pair_up(ids, keep, received, *outs):
    for k in range(4):
        p = ids[0] ^ k
        outs[k][at16(ids[1] * HEAD, HEAD), :] = keep[p]
        outs[k][at16((1 - ids[1]) * HEAD, HEAD), :] = received[p]


def first_back(ids, *refs):
    parts = refs[:4]
    second_grad, normed, scale, self_mixed, lse, row_data, gs, wcq, wo, sums_in = refs[4:14]
    first_grad, branch, dealt, dq, sums, all_t = refs[14:]
    for k in range(4):
        all_t[at128((ids[0] ^ k) * PAIR), :] = parts[k][...]
    dq[...] = turned(all_t[...])
    total = second_grad[...] + dot_nt(dq[...], wcq[...])
    grad, gain_a, shift_a = layer_norm_back(
        total, normed[...], scale[:, 0:1], gs[0:1, :].astype(wide_t)
    )
    first_grad[...] = grad
    low = grad.astype(low_t)
    branch[...] = low
    mixed = dot_nt(low, wo[...]).astype(low_t)
    rows = low.shape[0]
    sides = side_rows(lse, mixed, self_mixed, row_data)
    for p in range(PAIRS):
        dealt[p, :rows, :] = mixed[:, p * PAIR : (p + 1) * PAIR]
        dealt[p, rows : rows + 16, :] = sides[p][:, :PAIR]
        dealt[p, rows + 16 :, :] = sides[p][:, PAIR:]
    zero = jnp.zeros_like(gain_a)
    sums[...] = sums_in[...] + jnp.concatenate(
        (gain_a, zero, zero, shift_a, zero, zero, zero, zero), axis=0
    )


def source_back(ids, parts, wckv, out, dkv):
    rows = out.shape[0]
    for device in range(8):
        for n in range(2):
            start = 2 * D + 128 + n * rows
            dkv[n * D + device * HEAD : n * D + (device + 1) * HEAD, :] = parts[
                device, :, start : start + rows
            ]
    out[...] = dot_nt(turned(dkv[...]), wckv[...])


def hidden_back(ids, back, first_grad, wq, wkv, hidden_grad, stream_grad, all_t):
    for device in range(8):
        for n in range(3):
            all_t[n * D + device * HEAD : n * D + (device + 1) * HEAD, :] = back[
                device, n * HEAD : (n + 1) * HEAD, :
            ]
    hidden_grad[...] = first_grad[...] + dot_nt(turned(all_t[:D, :]), wq[...])
    stream_grad[...] = dot_nt(turned(all_t[D:, :]), wkv[...])


def add_parts(parts, rows, columns):
    total = parts[0, rows, columns].astype(wide_t)
    for n in range(1, parts.shape[0]):
        total = total + parts[n, rows, columns].astype(wide_t)
    return total.astype(low_t)


def add_chips(ids, parts, dw, *outs):
    width = parts.shape[2]
    for e in range(4):
        outs[e][:, :width] = add_parts(parts, slice(e * 32, (e + 1) * 32), slice(None))
        piece = dw[ids[2] ^ e]
        for g in range(4):
            outs[e][:, width + g * 128 : width + (g + 1) * 128] = piece[g * 32 : (g + 1) * 32, :]


def self_grads(ids, grads, own, other, hidden_own, hidden_other, dw):
    total, total_q = head_grads(grads, own, other, ids[1], (hidden_own, hidden_other))
    for w in range(4):
        columns = slice(w * 128, (w + 1) * 128)
        dw[w, :HEAD, :] = total_q[:, columns].astype(low_t)
        dw[w, HEAD:, :] = total[:, columns].astype(low_t)


def end_sums(ids, parts, dw, *outs):
    width = 2 * D + 128
    for e in range(4):
        outs[e][:, :width] = add_parts(parts, slice(e * 16, (e + 1) * 16), slice(0, width))
        outs[e][:, width : width + 128] = jnp.zeros((16, 128), low_t)
        piece = dw[ids[2] ^ e]
        for g in range(12):
            start = width + 128 + g * 128
            outs[e][:, start : start + 128] = piece[g * 16 : (g + 1) * 16, :]


def add_shards(ids, *refs):
    out = refs[8]

    def total(parts):
        value = parts[0][...].astype(wide_t)
        for part in parts[1:]:
            value = value + part[...].astype(wide_t)
        return value.astype(low_t)

    first, last = total(refs[:4]), total(refs[4:8])
    width, half = first.shape[1], last.shape[1] // 2
    out[:, :width] = first
    out[:16, width:] = last[:, :half]
    out[16:, width:] = last[:, half:]


def place_all(ids, *refs):
    parts, refs = refs[:8], refs[8:]
    g_in, g_out, g_cross, g_cross_pair, g_cross_query, g_output, gains, shifts, g_query, g_pair = refs[:10]
    pair_t, all_t = refs[10:]
    half = FF // 2
    start_cross = half + 2 * D
    start_pair = start_cross + D // 2
    start_end = start_pair + 4 * 128
    half_end = parts[0].shape[1] - start_end
    for n in range(2):
        core = ids[1] ^ n
        for step in range(4):
            chip, part = ids[0] ^ step, parts[n * 4 + step]
            rows = at16(chip * 32, 32)
            device = chip * 2 + core
            for k in range(4):
                g_in[rows, at128(k * 512 + core * 256, 256)] = part[
                    :, k * 256 : (k + 1) * 256
                ].astype(wide_t)
            for g in range(2):
                g_out[at16(core * 256 + chip * 64 + g * 32, 32), :] = part[
                    :, half + g * D : half + (g + 1) * D
                ].astype(wide_t)
            g_cross[rows, at128(core * 256, 256)] = part[:, start_cross:start_pair].astype(wide_t)
            for g in range(4):
                column = start_pair + g * 128
                row = (g // 2) * D + device * HEAD + (g % 2) * 32
                pair_t[at16(row, 32), :] = part[:, column : column + 128].astype(wide_t)

            def piece(column, width):
                row, at = (0, column) if column < half_end else (16, column - half_end)
                return part[row : row + 16, start_end + at : start_end + at + width].astype(wide_t)

            own_rows = at16(device * 16)
            for column in range(0, D, 128):
                g_cross_query[own_rows, column : column + 128] = piece(column, 128)
                g_output[own_rows, column : column + 128] = piece(D + column, 128)
            if n == 0 and step == 0:
                norms = piece(2 * D, 128)
                gains[...], shifts[...] = norms[0:3], norms[3:6]
            for g in range(12):
                row = (g // 4) * D + device * HEAD + (g % 4) * 16
                all_t[at16(row), :] = piece(2 * D + 256 + g * 128, 128)
    g_cross_pair[...] = pair_t[...].T
    g_query[...] = all_t[:D, :].T
    g_pair[...] = all_t[D:, :].T


def pack_rows(ids, stream, source, many):
    for k in range(4):
        many[k, :, :D] = stream[...]
        many[k, :, D:] = source[...]


def pack_start(ids, wq, wkv, ffn_in, ffn_out, pack):
    own = ids[0] * 2 + ids[1]
    for k in range(4):
        start = 3 * D + FF + k * D
        pack[:, start : start + D] = ffn_out[at16(own * 64 + k * 16), :]
    pack[:, :D] = wq[at16(own * 16), :]
    pack[:, D : 3 * D] = wkv[at16(own * 16), :]
    pack[:, 3 * D : 3 * D + FF] = ffn_in[at16(own * 16), :]


def pack_more(ids, *refs):
    weights, gain, shift, rows_in, pack, many = refs[:4], *refs[4:]
    rows = at16(ids[1] * 64, 64)
    norms = (gain[...].astype(wide_t), shift[...].astype(wide_t), jnp.zeros((58, 128), wide_t))
    norms = jnp.concatenate(norms, axis=0).astype(low_t)
    for k in range(4):
        start = 0
        for w in weights:
            pack[k, :, start : start + w.shape[1]] = w[rows, :]
            start += w.shape[1]
        pack[k, :, start:] = norms
        many[k] = rows_in[...]


def mask_data(ids, order, ranks, limits, cols, row_data, all_rows):
    rows = cols.shape[0]
    ends = [ids[3]]
    for n in range(1, 4):
        ends.append(ends[-1] + ids[3 + n])

    def sequence(position):
        return sum((position >= end).astype(wide_t) for end in ends)

    for n in range(2):
        for k in range(4):
            b = n * 4 + k
            device = k * 2 + (ids[1] ^ n)
            here = at128(device * rows, rows)
            index = lax.broadcasted_iota(jnp.int32, (1, rows), 1) + device * rows
            all_rows[b : b + 1, :] = sequence(order[:, here])
            all_rows[8 + b : 9 + b, :] = ranks[:, here].astype(wide_t)
            all_rows[16 + b : 17 + b, :] = sequence(index)
            row_data[8 + b : 9 + b, :] = limits[:, here].astype(wide_t)
    row_data[0:8, :] = all_rows[0:8, :]
    all_rows[24:32, :] = jnp.zeros((8, rows), wide_t)
    all_rows[24:25, :] = all_rows[pl.ds(ids[0], 1), :]
    row_data[16:24, :] = jnp.zeros((8, rows), wide_t)
    row_data[16:17, :] = all_rows[pl.ds(ids[0], 1), :]
    row_data[17:18, :] = row_data[pl.ds(8 + ids[0], 1), :]
    cols[:, :32] = all_rows[...].T


def pack_first(ids, *refs):
    parts, (one, two) = refs[:4], refs[4:]
    width = one.shape[1]
    for e in range(4):
        here = slice(e * 16, (e + 1) * 16)
        one[here, :] = parts[e][:, :width]
        two[here, :] = parts[e][:, width:]


def core_swap(value):
    return lax.ppermute(value, "core", [(0, 1), (1, 0)])


def chip_swaps(parts):
    moves = [[(i, i ^ k) for i in range(4)] for k in range(4)]
    return [parts[0]] + [lax.ppermute(parts[k], "chip", moves[k]) for k in range(1, 4)]


def shard_swaps(parts):
    moves = [[(i, i ^ k) for i in range(4)] for k in range(4)]
    return [parts[0]] + [lax.ppermute(parts[k], "wa", moves[k]) for k in range(1, 4)]


def deal(value):
    return lax.all_to_all(value, "chip", 0, 0, tiled=True)


def deal_all(value):
    return lax.all_to_all(value, ("chip", "core"), 0, 0, tiled=True)


def deal_both(value):
    own = deal(value)
    return own, core_swap(own)


def after(value, *others):
    return lax.optimization_barrier((value,) + others)[0]


def fast_shards(
    hidden,
    stream,
    encoder,
    lengths,
    order,
    ranks,
    thresholds,
    self_query,
    self_key_value,
    self_output,
    cross_query,
    cross_key_value,
    cross_output,
    ffn_in,
    ffn_out,
    norm_gain,
    norm_shift,
    cotangent,
):
    rows, keys = hidden.shape[1], order.shape[1]
    chip, core, mw = lax.axis_index("chip"), lax.axis_index("core"), lax.axis_index("wa")
    ids = jnp.stack((chip, core, mw)).astype(jnp.int32)
    inputs = hidden[0]

    (many,) = run(pack_rows, [((4, rows, 2 * D), low_t)], ids, [stream[0], encoder[0]])
    (pack1,) = run(
        pack_start,
        [((16, 3 * D + 2 * FF), low_t)],
        ids,
        [after(self_query, many), self_key_value, ffn_in, ffn_out],
    )
    x_own = deal(many)
    shards1 = shard_swaps([pack1] * 4)
    copies2, hidden_copies = run(
        pack_more,
        [((4, 64, 5 * D + 128), low_t), ((4, rows, D), low_t)],
        ids,
        [after(self_output, pack1), cross_query, cross_key_value, cross_output, norm_gain, norm_shift]
        + [inputs],
    )
    cols, row_data = run(
        mask_data,
        [((rows, 32), wide_t), ((24, rows), wide_t)],
        jnp.concatenate((after(ids, pack1), lengths[0])),
        [order, ranks, thresholds],
        [((32, rows), wide_t)],
    )
    part1, part3 = run(
        pack_first,
        [((64, 3 * D), low_t), ((64, 2 * FF), low_t)],
        ids,
        [after(shards1[0], x_own, cols, copies2)] + shards1[1:],
    )
    slices1 = chip_swaps([part1] * 4)
    slices1 = slices1 + [core_swap(part) for part in slices1]
    shards2 = lax.all_to_all(after(copies2, x_own), "wa", 0, 0, tiled=True)
    x_other = core_swap(after(x_own, part1))
    slices3 = chip_swaps([after(part3, slices1[1])] * 4)
    stream_own, stream_other = (x_own, 0), (x_other, 0)
    source_own, source_other = (x_own, 1), (x_other, 1)

    attend_scratch = [
        ((rows, D), low_t),
        ((keys, D), low_t),
        ((D, keys), low_t),
        ((D, D), low_t),
        ((keys, rows), wide_t),
        ((2, keys, rows), wide_t),
        ((D, rows), wide_t),
    ]
    self_low, self_mixed, self_lse, wq, wkv = run(
        self_forward,
        [((rows, D), low_t), ((rows, D), wide_t), ((HEADS, rows), wide_t)]
        + [((D, D), low_t), ((D, 2 * D), low_t)],
        ids,
        [inputs, stream_own, stream_other, *slices1, cols, row_data],
        attend_scratch,
        us=15,
    )
    head_shapes = [((keys, PAIR), low_t)] * 2 + [((HEAD, keys), low_t)]
    self_head = run(
        functools.partial(pair_setup, True),
        head_shapes,
        ids,
        [stream_own, stream_other, wkv, after(cols, self_low)],
        [((PAIR, rows), wide_t)],
        us=4,
    )
    slices3 = slices3 + [core_swap(after(part, self_head[0])) for part in slices3]
    shards2_other = core_swap(after(shards2, self_head[0], *slices3[:4]))
    hidden_own = deal(after(hidden_copies, shards2, self_head[0], *slices3[:4]))
    (
        first,
        normed,
        scale,
        first_low,
        cross_low,
        cross_mixed,
        cross_lse,
        cross_q,
        wo,
        wcq,
        wckv,
        wco,
        gs,
        *cross_head,
    ) = run(
        cross_forward,
        [((rows, D), wide_t)] * 2
        + [((rows, 128), wide_t)]
        + [((rows, D), low_t)] * 2
        + [((rows, D), wide_t), ((HEADS, rows), wide_t), ((rows, D), low_t)]
        + [((D, D), low_t), ((D, D), low_t), ((D, 2 * D), low_t), ((D, D), low_t), ((16, D), low_t)]
        + head_shapes,
        ids,
        [inputs, after(self_low, self_head[0]), source_own, source_other, shards2, shards2_other]
        + [cols, row_data],
        attend_scratch + [((PAIR, rows), wide_t)],
        us=15,
    )
    hidden_other = core_swap(after(hidden_own, cross_low))
    width_s = 2 * FF // 2 + 3 * D + D // 2
    result, cross_dealt, second_grad, keep_a, send_a, sums = run(
        feed_forward,
        [
            ((rows, D), low_t),
            ((PAIRS, rows + 16, 2 * PAIR), low_t),
            ((rows, D), wide_t),
            ((rows, width_s), low_t),
            ((rows, width_s), low_t),
            ((8, D), wide_t),
        ],
        ids,
        [after(first, hidden_own), cross_low, cross_mixed, cross_lse, row_data, cross_q, wco, gs]
        + [cotangent[0], *slices3],
        [((rows, FF), wide_t), ((2, D, FF // 2), low_t), ((2, FF // 2, D), low_t)],
        us=8,
    )
    both_own = deal(cross_dealt)
    width_a = FF // 2 + 2 * D + D // 2
    (dealt_a,) = run(
        grads_a,
        [((4, 128, width_a), low_t)],
        ids,
        [keep_a, core_swap(send_a)],
        [((D, FF // 2), low_t), ((FF // 2, D), low_t), ((D, D // 2), low_t)],
        us=6,
    )
    rows_a = deal(after(dealt_a, both_own))
    both_other = core_swap(after(both_own, dealt_a))

    back_scratch = (
        [((8, rows, PAIR), low_t)] * 2
        + [((8, HEAD, rows), low_t)]
        + [((keys, PAIR), wide_t)] * 3
        + [((PAIR, rows), wide_t)]
    )
    cq_keep, cq_send, cross_dkv = run(
        functools.partial(pair_back, False),
        [((4, HEAD, rows), low_t)] * 2 + [((8, 2 * HEAD, rows), low_t)],
        ids,
        [after(both_own, dealt_a), both_other, *cross_head],
        back_scratch,
        us=16,
    )
    pairs = run(pair_up, [((PAIR, rows), low_t)] * 4, ids, [cq_keep, core_swap(cq_send)])
    cross_back = chip_swaps(pairs)
    (self_queries,) = run(
        pair_queries,
        [((8, rows, PAIR), low_t)],
        ids,
        [hidden_own, hidden_other, after(wq, pairs[0])],
    )
    (cross_dw,) = run(
        pair_grads,
        [((4, 2 * HEAD, 128), low_t)],
        ids,
        [after(cross_dkv, pairs[0]), source_own, source_other],
    )
    first_grad, self_branch, self_dealt, cross_dq, sums = run(
        first_back,
        [
            ((rows, D), wide_t),
            ((rows, D), low_t),
            ((PAIRS, rows + 32, PAIR), low_t),
            ((rows, D), low_t),
            ((8, D), wide_t),
        ],
        ids,
        [after(cross_back[0], cross_dw, self_queries), *cross_back[1:], second_grad, normed, scale, self_mixed, self_lse, row_data, gs, wcq, wo, sums],
        [((D, rows), low_t)],
        us=4,
    )
    do_own = deal(after(self_dealt, rows_a))
    shards_a = run(
        add_chips,
        [((32, width_a + 512), low_t)] * 4,
        ids,
        [after(rows_a, first_grad), cross_dw],
    )
    moved_a = shard_swaps([after(part, do_own) for part in shards_a])
    (dealt_b,) = run(
        grads_b,
        [((8, 64, 2 * D + 128 + 2 * rows), low_t)],
        ids,
        [first_low, cross_dq, self_low, self_branch, sums, cross_dkv],
        [((D, D), low_t)] * 2,
        us=3,
    )
    rows_b = deal_all(after(dealt_b, do_own))
    do_other = core_swap(after(do_own, dealt_b, *shards_a))
    (self_back_t,) = run(
        functools.partial(pair_back, True),
        [((8, 3 * HEAD, rows), low_t)],
        ids,
        [self_queries, after(do_own, dealt_b, *shards_a), do_other, *self_head, cols, row_data],
        back_scratch,
        us=16,
    )
    end_width = 2 * D + 2 * 128 + 12 * 128
    (self_dw,) = run(
        self_grads,
        [((4, 3 * HEAD, 128), low_t)],
        ids,
        [self_back_t, stream_own, stream_other, hidden_own, hidden_other],
    )
    end_parts = run(
        end_sums, [((16, end_width), low_t)] * 4, ids, [after(rows_b, self_dw), self_dw]
    )
    moved_end = shard_swaps(end_parts)
    self_back = deal_all(after(self_back_t, end_parts[0], *moved_a))
    (source_grad,) = run(
        source_back,
        [((rows, D), wide_t)],
        ids,
        [rows_b, after(wckv, end_parts[0])],
        [((2 * D, rows), low_t)],
        us=3,
    )
    (sums_end,) = run(
        add_shards,
        [((32, width_a + 512 + end_width // 2), low_t)],
        ids,
        [*moved_a, after(moved_end[0], source_grad), *moved_end[1:]],
    )
    all_parts = chip_swaps([sums_end] * 4)
    hidden_grad, stream_grad = run(
        hidden_back,
        [((rows, D), wide_t)] * 2,
        ids,
        [self_back, first_grad, wq, wkv],
        [((3 * D, rows), low_t)],
        us=3,
    )
    all_parts = all_parts + [core_swap(after(part, hidden_grad)) for part in all_parts]
    (
        grad_in,
        grad_out,
        grad_cross_output,
        grad_cross_pair,
        grad_cross_query,
        grad_output,
        gain_grads,
        shift_grads,
        grad_query,
        grad_pair,
    ) = run(
        place_all,
        [((128, FF), wide_t), ((D, D), wide_t), ((128, D), wide_t), ((128, 2 * D), wide_t)]
        + [((128, D), wide_t)] * 2
        + [((3, 128), wide_t)] * 2
        + [((128, D), wide_t), ((128, 2 * D), wide_t)],
        ids,
        all_parts,
        [((2 * D, 128), wide_t), ((3 * D, 128), wide_t)],
    )
    return (
        result[None],
        hidden_grad[None],
        stream_grad[None],
        source_grad[None],
        grad_query,
        grad_pair,
        grad_output,
        grad_cross_query,
        grad_cross_pair,
        grad_cross_output,
        grad_in,
        grad_out,
        gain_grads,
        shift_grads,
    )


def solution(mesh):
    in_specs = (
        P("wa", "ctx", None),
        P("wa", "ctx", None),
        P("wa", "ctx", None),
        P("wa", None),
        P("wa", None),
        P("wa", None),
        P("wa", None),
        P("wa", None),
        P("wa", None),
        P("wa", None),
        P("wa", None),
        P("wa", None),
        P("wa", None),
        P("wa", None),
        P("wa", None),
        P(None, "wa"),
        P(None, "wa"),
        P("wa", "ctx", None),
    )
    out_specs = (
        P("wa", "ctx", None),
        P("wa", "ctx", None),
        P("wa", "ctx", None),
        P("wa", "ctx", None),
        P("wa", None),
        P("wa", None),
        P("wa", None),
        P("wa", None),
        P("wa", None),
        P("wa", None),
        P("wa", None),
        P("wa", None),
        P(None, "wa"),
        P(None, "wa"),
    )
    if mesh.axis_names != ("ctx", "wa") or mesh.shape["ctx"] != HEADS or mesh.shape["wa"] != 4:
        return jax.shard_map(
            general_shards, mesh=mesh, in_specs=in_specs, out_specs=out_specs, check_vma=False
        )

    def finer(spec):
        return P(*(("chip", "core") if axis == "ctx" else axis for axis in spec))

    return jax.shard_map(
        fast_shards,
        mesh=Mesh(mesh.devices.reshape(4, 2, 4), ("chip", "core", "wa")),
        in_specs=tuple(finer(spec) for spec in in_specs),
        out_specs=tuple(finer(spec) for spec in out_specs),
        check_vma=False,
    )
```

```python
import functools

import jax
import jax.numpy as jnp
from jax import lax
from jax.experimental import pallas as pl
from jax.experimental.pallas import tpu as pltpu
from jax.sharding import Mesh
from jax.sharding import PartitionSpec as P

D = 512
HEADS = 8
HEAD = 64
KEYBLK = 1024


layer_eps = 1e-05
neg_fill = -1e30


def sequence_ids(positions, seq_ends):
    return jnp.sum((positions[:, None] >= seq_ends[None, :]).astype(jnp.int32), axis=1)


def head_split(matrix):
    return matrix.reshape(matrix.shape[0], HEADS, HEAD)


def block_scores(query_heads, key_heads):
    raw_scores = jnp.einsum(
        "lhd,khd->hlk", query_heads, key_heads, preferred_element_type=jnp.float32
    )
    return raw_scores * float(HEAD) ** (-0.5)


def softmax_totals(queries, key_rows, allowed_fn):
    query_heads = head_split(queries)
    count_rows = queries.shape[0]

    def visit(state_pair, block_index):
        running_top, running_sum = state_pair
        block_start = block_index * KEYBLK
        key_piece = lax.dynamic_slice_in_dim(key_rows, block_start, KEYBLK, 0)
        allowed = allowed_fn(block_start)[None]
        scores = jnp.where(
            allowed, block_scores(query_heads, head_split(key_piece[:, :D])), neg_fill
        )
        new_top = jnp.maximum(running_top, jnp.max(scores, axis=2))
        weights = jnp.where(allowed, jnp.exp(scores - new_top[:, :, None]), 0.0)
        running_sum = running_sum * jnp.exp(running_top - new_top) + jnp.sum(weights, axis=2)
        return ((new_top, running_sum), None)

    initial = (
        jnp.full((HEADS, count_rows), neg_fill, jnp.float32),
        jnp.zeros((HEADS, count_rows), jnp.float32),
    )
    (final_top, final_sum), unused = lax.scan(
        visit, initial, jnp.arange(key_rows.shape[0] // KEYBLK)
    )
    return final_top + jnp.log(final_sum)


def attend_values(queries, key_rows, log_totals, allowed_fn):
    query_heads = head_split(queries)

    def visit(running, block_index):
        block_start = block_index * KEYBLK
        key_piece = lax.dynamic_slice_in_dim(key_rows, block_start, KEYBLK, 0)
        allowed = allowed_fn(block_start)[None]
        scores = block_scores(query_heads, head_split(key_piece[:, :D]))
        weights = jnp.where(allowed, jnp.exp(scores - log_totals[:, :, None]), 0.0)
        value_heads = head_split(key_piece[:, D:])
        return (
            running
            + jnp.einsum(
                "hlk,khd->lhd",
                weights.astype(jnp.bfloat16),
                value_heads,
                preferred_element_type=jnp.float32,
            ),
            None,
        )

    mixed, unused = lax.scan(
        visit, jnp.zeros(query_heads.shape, jnp.float32), jnp.arange(key_rows.shape[0] // KEYBLK)
    )
    return mixed.reshape(queries.shape[0], D)


def head_offsets(grad_low, attended):
    return jnp.sum(head_split(grad_low.astype(jnp.float32) * attended), axis=2).T


def attend_back(queries, key_rows, log_totals, attended, grad_low, allowed_fn):
    query_heads = head_split(queries)
    grad_heads = head_split(grad_low)
    offsets = head_offsets(grad_low, attended)
    scale_value = float(HEAD) ** (-0.5)

    def visit(query_grad, block_index):
        block_start = block_index * KEYBLK
        key_piece = lax.dynamic_slice_in_dim(key_rows, block_start, KEYBLK, 0)
        allowed = allowed_fn(block_start)[None]
        key_heads = head_split(key_piece[:, :D])
        value_heads = head_split(key_piece[:, D:])
        weights = jnp.where(
            allowed, jnp.exp(block_scores(query_heads, key_heads) - log_totals[:, :, None]), 0.0
        )
        value_grad = jnp.einsum(
            "hlk,lhd->khd",
            weights.astype(jnp.bfloat16),
            grad_heads,
            preferred_element_type=jnp.float32,
        )
        weight_grad = jnp.einsum(
            "lhd,khd->hlk", grad_heads, value_heads, preferred_element_type=jnp.float32
        )
        score_grad = (weights * (weight_grad - offsets[:, :, None]) * scale_value).astype(
            jnp.bfloat16
        )
        query_grad = query_grad + jnp.einsum(
            "hlk,khd->lhd", score_grad, key_heads, preferred_element_type=jnp.float32
        )
        key_grad = jnp.einsum(
            "hlk,lhd->khd", score_grad, query_heads, preferred_element_type=jnp.float32
        )
        return (
            query_grad,
            jnp.concatenate((key_grad.reshape(KEYBLK, D), value_grad.reshape(KEYBLK, D)), axis=1),
        )

    query_grad, grad_pieces = lax.scan(
        visit, jnp.zeros(query_heads.shape, jnp.float32), jnp.arange(key_rows.shape[0] // KEYBLK)
    )
    return (query_grad.reshape(queries.shape[0], D), grad_pieces.reshape(key_rows.shape[0], 2 * D))


def normalize(values, gain_row, shift_row):
    row_mean = jnp.mean(values, axis=1, keepdims=True)
    centred = values - row_mean
    scale_inv = lax.rsqrt(jnp.mean(centred * centred, axis=1, keepdims=True) + layer_eps)
    normed = centred * scale_inv
    return (normed * gain_row + shift_row, normed, scale_inv)


def normalize_back(grad_out, normed, scale_inv, gain_row):
    gain_term = jnp.sum(grad_out * normed, axis=0)
    shift_term = jnp.sum(grad_out, axis=0)
    scaled = grad_out * gain_row
    grad_in = scale_inv * (
        scaled
        - jnp.mean(scaled, axis=1, keepdims=True)
        - normed * jnp.mean(scaled * normed, axis=1, keepdims=True)
    )
    return (grad_in, gain_term, shift_term)


def matmul(left, right):
    return jnp.dot(left, right, preferred_element_type=jnp.float32)


def general_shards(
    hidden,
    stream,
    encoder,
    lengths,
    order,
    ranks,
    thresholds,
    self_query,
    self_key_value,
    self_output,
    cross_query,
    cross_key_value,
    cross_output,
    ffn_in,
    ffn_out,
    norm_gain,
    norm_shift,
    cotangent,
):
    (
        full_query,
        full_pair,
        full_output,
        full_cross_query,
        full_cross_pair,
        full_cross_output,
        full_in,
        full_out,
        gain_rows,
        shift_rows,
    ) = (
        lax.all_gather(self_query, "wa", axis=0, tiled=True),
        lax.all_gather(self_key_value, "wa", axis=0, tiled=True),
        lax.all_gather(self_output, "wa", axis=0, tiled=True),
        lax.all_gather(cross_query, "wa", axis=0, tiled=True),
        lax.all_gather(cross_key_value, "wa", axis=0, tiled=True),
        lax.all_gather(cross_output, "wa", axis=0, tiled=True),
        lax.all_gather(ffn_in, "wa", axis=0, tiled=True),
        lax.all_gather(ffn_out, "wa", axis=0, tiled=True),
        lax.all_gather(norm_gain, "wa", axis=1, tiled=True),
        lax.all_gather(norm_shift, "wa", axis=1, tiled=True),
    )
    gains = gain_rows.astype(jnp.float32)
    shifts = shift_rows.astype(jnp.float32)
    local_rows = hidden.shape[1]
    total_rows = order.shape[1]
    row_start = lax.axis_index("ctx") * local_rows
    seq_ends = jnp.cumsum(lengths[0])
    token_seq = sequence_ids(order[0], seq_ends)
    source_seq = sequence_ids(jnp.arange(total_rows, dtype=jnp.int32), seq_ends)
    query_seq = lax.dynamic_slice_in_dim(token_seq, row_start, local_rows)
    query_rows = row_start + jnp.arange(local_rows, dtype=jnp.int32)
    all_limits = thresholds[0]
    limits = lax.dynamic_slice_in_dim(all_limits, row_start, local_rows)
    key_ranks = ranks[0]

    def self_allowed(block_start):
        block_seq = lax.dynamic_slice_in_dim(token_seq, block_start, KEYBLK)
        block_rank = lax.dynamic_slice_in_dim(key_ranks, block_start, KEYBLK)
        block_rows = block_start + jnp.arange(KEYBLK, dtype=jnp.int32)
        return (query_seq[:, None] == block_seq[None, :]) & (
            (block_rank[None, :] < limits[:, None]) | (query_rows[:, None] == block_rows[None, :])
        )

    def cross_allowed(block_start):
        return (
            query_seq[:, None] == lax.dynamic_slice_in_dim(source_seq, block_start, KEYBLK)[None, :]
        )

    inputs = hidden[0]
    stream_rows = stream[0]
    source_rows = encoder[0]
    queries = matmul(inputs, full_query).astype(jnp.bfloat16)
    self_local = matmul(stream_rows, full_pair).astype(jnp.bfloat16)
    cross_local = matmul(source_rows, full_cross_pair).astype(jnp.bfloat16)
    self_keys, cross_keys = (
        lax.all_gather(self_local, "ctx", axis=0, tiled=True),
        lax.all_gather(cross_local, "ctx", axis=0, tiled=True),
    )
    self_totals = softmax_totals(queries, self_keys, self_allowed)
    self_mixed = attend_values(queries, self_keys, self_totals, self_allowed)
    self_low = self_mixed.astype(jnp.bfloat16)
    first, first_normed, first_scale = normalize(
        inputs.astype(jnp.float32) + matmul(self_low, full_output), gains[0], shifts[0]
    )
    first_low = first.astype(jnp.bfloat16)
    cross_queries = matmul(first_low, full_cross_query).astype(jnp.bfloat16)
    cross_totals = softmax_totals(cross_queries, cross_keys, cross_allowed)
    cross_mixed = attend_values(cross_queries, cross_keys, cross_totals, cross_allowed)
    cross_low = cross_mixed.astype(jnp.bfloat16)
    second, second_normed, second_scale = normalize(
        first + matmul(cross_low, full_cross_output), gains[1], shifts[1]
    )
    second_low = second.astype(jnp.bfloat16)
    hidden_pre = matmul(second_low, full_in)
    sigmoid_pre = jax.nn.sigmoid(hidden_pre)
    activated = (hidden_pre * sigmoid_pre).astype(jnp.bfloat16)
    result, third_normed, third_scale = normalize(
        second + matmul(activated, full_out), gains[2], shifts[2]
    )
    third_grad, gain_grad_c, shift_grad_c = normalize_back(
        cotangent[0].astype(jnp.float32), third_normed, third_scale, gains[2]
    )
    branch_grad = third_grad.astype(jnp.bfloat16)
    grad_ffn_out = matmul(activated.T, branch_grad)
    slope = sigmoid_pre * (1.0 + hidden_pre * (1.0 - sigmoid_pre))
    pre_grad = (matmul(branch_grad, full_out.T) * slope).astype(jnp.bfloat16)
    grad_ffn_in = matmul(second_low.T, pre_grad)
    second_total = third_grad + matmul(pre_grad, full_in.T)
    second_grad, gain_grad_b, shift_grad_b = normalize_back(
        second_total, second_normed, second_scale, gains[1]
    )
    cross_branch = second_grad.astype(jnp.bfloat16)
    grad_cross_output = matmul(cross_low.T, cross_branch)
    cross_mixed_grad = matmul(cross_branch, full_cross_output.T).astype(jnp.bfloat16)
    cross_query_term, cross_terms = attend_back(
        cross_queries, cross_keys, cross_totals, cross_mixed, cross_mixed_grad, cross_allowed
    )
    cross_query_low = cross_query_term.astype(jnp.bfloat16)
    grad_cross_query = matmul(first_low.T, cross_query_low)
    first_total = second_grad + matmul(cross_query_low, full_cross_query.T)
    first_grad, gain_grad_a, shift_grad_a = normalize_back(
        first_total, first_normed, first_scale, gains[0]
    )
    self_branch = first_grad.astype(jnp.bfloat16)
    grad_self_output = matmul(self_low.T, self_branch)
    self_mixed_grad = matmul(self_branch, full_output.T).astype(jnp.bfloat16)
    self_query_term, self_terms = attend_back(
        queries, self_keys, self_totals, self_mixed, self_mixed_grad, self_allowed
    )
    self_sum, cross_sum = (
        lax.psum_scatter(self_terms, "ctx", scatter_dimension=0, tiled=True),
        lax.psum_scatter(cross_terms, "ctx", scatter_dimension=0, tiled=True),
    )
    self_query_low = self_query_term.astype(jnp.bfloat16)
    grad_self_query = matmul(inputs.T, self_query_low)
    input_grad = first_grad + matmul(self_query_low, full_query.T)
    self_sum_low = self_sum.astype(jnp.bfloat16)
    grad_self_pair = matmul(stream_rows.T, self_sum_low)
    stream_grad = matmul(self_sum_low, full_pair.T)
    cross_sum_low = cross_sum.astype(jnp.bfloat16)
    grad_cross_pair = matmul(source_rows.T, cross_sum_low)
    source_grad = matmul(cross_sum_low, full_cross_pair.T)
    gain_grads = jnp.stack((gain_grad_a, gain_grad_b, gain_grad_c))
    shift_grads = jnp.stack((shift_grad_a, shift_grad_b, shift_grad_c))
    (
        share_query,
        share_pair,
        share_output,
        share_cross_query,
        share_cross_pair,
        share_cross_output,
        share_in,
        share_out,
        share_gain,
        share_shift,
    ) = (
        lax.psum_scatter(
            grad_self_query.astype(jnp.bfloat16), "wa", scatter_dimension=0, tiled=True
        ).astype(jnp.float32),
        lax.psum_scatter(
            grad_self_pair.astype(jnp.bfloat16), "wa", scatter_dimension=0, tiled=True
        ).astype(jnp.float32),
        lax.psum_scatter(
            grad_self_output.astype(jnp.bfloat16), "wa", scatter_dimension=0, tiled=True
        ).astype(jnp.float32),
        lax.psum_scatter(
            grad_cross_query.astype(jnp.bfloat16), "wa", scatter_dimension=0, tiled=True
        ).astype(jnp.float32),
        lax.psum_scatter(
            grad_cross_pair.astype(jnp.bfloat16), "wa", scatter_dimension=0, tiled=True
        ).astype(jnp.float32),
        lax.psum_scatter(
            grad_cross_output.astype(jnp.bfloat16), "wa", scatter_dimension=0, tiled=True
        ).astype(jnp.float32),
        lax.psum_scatter(
            grad_ffn_in.astype(jnp.bfloat16), "wa", scatter_dimension=0, tiled=True
        ).astype(jnp.float32),
        lax.psum_scatter(
            grad_ffn_out.astype(jnp.bfloat16), "wa", scatter_dimension=0, tiled=True
        ).astype(jnp.float32),
        lax.psum_scatter(
            gain_grads.astype(jnp.bfloat16), "wa", scatter_dimension=1, tiled=True
        ).astype(jnp.float32),
        lax.psum_scatter(
            shift_grads.astype(jnp.bfloat16), "wa", scatter_dimension=1, tiled=True
        ).astype(jnp.float32),
    )
    (
        total_query,
        total_pair,
        total_output,
        total_cross_query,
        total_cross_pair,
        total_cross_output,
        total_in,
        total_out,
        total_gain,
        total_shift,
    ) = lax.psum(
        (
            share_query,
            share_pair,
            share_output,
            share_cross_query,
            share_cross_pair,
            share_cross_output,
            share_in,
            share_out,
            share_gain,
            share_shift,
        ),
        "ctx",
    )
    return (
        result.astype(jnp.bfloat16)[None],
        input_grad[None],
        stream_grad[None],
        source_grad[None],
        total_query,
        total_pair,
        total_output,
        total_cross_query,
        total_cross_pair,
        total_cross_output,
        total_in,
        total_out,
        total_gain,
        total_shift,
    )


PAIR = 2 * HEAD
PAIRS = HEADS // 2
FF = 2048
low_t = jnp.bfloat16
wide_t = jnp.float32
vmem_spec = pl.BlockSpec(memory_space=pltpu.VMEM)
smem_spec = pl.BlockSpec(memory_space=pltpu.SMEM)


def run(body, outs, ids, args, scratch=(), us=2, vmem=56):
    outs = [jax.ShapeDtypeStruct(shape, kind) for shape, kind in outs]
    arrays = [arg[0] if isinstance(arg, tuple) else arg for arg in args]
    parts = [n for n, arg in enumerate(args) if isinstance(arg, tuple)]
    total = len(args) + len(outs) + len(scratch)

    def kernel(ids, *refs):
        refs, buffers, sems = list(refs[:total]), refs[total:-1], refs[-1]
        copies = []
        for m, n in enumerate(parts):
            start = args[n][1] * D
            copies.append(
                pltpu.make_async_copy(refs[n].at[:, :, start : start + D], buffers[m], sems.at[m])
            )
            copies[m].start()
            refs[n] = buffers[m]
        for copy in copies:
            copy.wait()
        body(ids, *refs)

    buffers = [pltpu.VMEM(args[n][0].shape[:2] + (D,), args[n][0].dtype) for n in parts]
    specs = [pl.BlockSpec(memory_space=pl.ANY) if n in parts else vmem_spec for n in range(len(args))]
    moved = sum(a.size * a.dtype.itemsize for a in arrays + outs)
    return pl.pallas_call(
        kernel,
        name=getattr(body, "func", body).__name__,
        out_shape=outs,
        in_specs=[smem_spec] + specs,
        out_specs=[vmem_spec] * len(outs),
        scratch_shapes=[pltpu.VMEM(shape, kind) for shape, kind in scratch]
        + buffers
        + [pltpu.SemaphoreType.DMA((max(1, len(parts)),))],
        compiler_params=pltpu.CompilerParams(vmem_limit_bytes=vmem * 1024 * 1024),
        cost_estimate=pl.CostEstimate(flops=us * 1_000_000_000, bytes_accessed=moved, transcendentals=0),
    )(ids, *arrays)


def dot_nn(a, b):
    return lax.dot_general(a, b, (((1,), (0,)), ((), ())), preferred_element_type=wide_t)


def dot_nt(a, b):
    return lax.dot_general(a, b, (((1,), (1,)), ((), ())), preferred_element_type=wide_t)


def dot_tn(a, b):
    return lax.dot_general(a, b, (((0,), (0,)), ((), ())), preferred_element_type=wide_t)


def at16(start, size=16):
    return pl.ds(pl.multiple_of(start, 16), size)


def at128(start, size=128):
    return pl.ds(pl.multiple_of(start, 128), size)


def half_mask(shape, axis, core):
    return (lax.broadcasted_iota(jnp.int32, shape, axis) // HEAD) == core


def attend_rows(q_ref, k_ref, vt_ref, bias_ref, s_ref, ot_ref, lse_ref):
    keys, rows = bias_ref.shape
    tile = min(1024, keys)
    spans = [slice(start, start + tile) for start in range(0, keys, tile)]
    lowest = jnp.full((8, rows), neg_fill, wide_t)
    group = 4

    def step(p, carry):
        def scores(head, here, top):
            pair = at128((p * (group // 2) + head // 2) * PAIR)
            q = q_ref[:, pair]
            own_q = jnp.where(half_mask((rows, PAIR), 1, head % 2), q, jnp.zeros_like(q))
            s = dot_nt(k_ref[here, pair], own_q) + bias_ref[here, :]
            s_ref[head % 2, here, :] = s
            return jnp.maximum(top, jnp.max(s.reshape(tile // 8, 8, rows), axis=0))

        top = lowest
        for here in spans:
            top = scores(0, here, top)
        for head in range(group):
            features = pl.ds(pl.multiple_of((p * group + head) * HEAD, HEAD), HEAD)
            highest = jnp.max(top, axis=0, keepdims=True)
            total = jnp.zeros((8, rows), wide_t)
            mixed = jnp.zeros((HEAD, rows), wide_t)
            top = lowest
            for here in spans:
                if head + 1 < group:
                    top = scores(head + 1, here, top)
                w = jnp.exp(s_ref[head % 2, here, :] - highest)
                total = total + jnp.sum(w.reshape(tile // 8, 8, rows), axis=0)
                mixed = mixed + dot_nn(vt_ref[features, here], w.astype(low_t))
            total = jnp.sum(total, axis=0, keepdims=True)
            ot_ref[features, :] = mixed / total
            lse_ref[pl.ds(p * group + head, 1), :] = highest + jnp.log(total)
        return carry

    lax.fori_loop(0, HEADS // group, step, 0)


def finish_rows(ot_ref, low_out, mixed_out):
    mixed = ot_ref[...].T
    low_out[...] = mixed.astype(low_t)
    mixed_out[...] = mixed


def three_parts(value):
    high = value.astype(low_t).astype(wide_t)
    rest = value - high
    middle = rest.astype(low_t).astype(wide_t)
    return high, middle, rest - middle


def side_rows(lse, grad_low, mixed, row_data):
    product = grad_low.astype(wide_t) * mixed[...]
    lane = lax.broadcasted_iota(jnp.int32, (grad_low.shape[0], PAIR), 1)
    sums = jnp.zeros((grad_low.shape[0], PAIR), wide_t)
    for p in range(PAIRS):
        piece = product[:, p * PAIR : (p + 1) * PAIR]
        for h in range(2):
            mine = half_mask(piece.shape, 1, h)
            offset = jnp.sum(jnp.where(mine, piece, 0.0), axis=1, keepdims=True)
            sums = jnp.where(lane == p * 2 + h, offset, sums)
    offsets = sums.T
    seq = row_data[16:17, :]
    onehot = [(seq == float(n)).astype(wide_t) for n in range(4)]
    sides = []
    for p in range(PAIRS):
        pieces = []
        for h in range(2):
            head = p * 2 + h
            pieces += three_parts(-lse[head : head + 1, :])
            pieces += three_parts(-offsets[head : head + 1, :])
        sides.append(jnp.concatenate(pieces + onehot, axis=0).astype(low_t))
    return sides


def side_lanes(side, core):
    side = side.astype(wide_t)
    head = jnp.where(core == 0, side[0:6], side[6:12])
    gap = jnp.zeros((5, side.shape[1]), wide_t)
    rest = jnp.zeros((HEAD - 20, side.shape[1]), wide_t)
    half = jnp.concatenate((head[0:3], gap, head[3:6], gap, side[12:16], rest), axis=0)
    return jnp.concatenate((half, half), axis=0).T.astype(low_t)


def assemble(ids, parts, column, outs):
    for chip, other, block in parts:
        own = chip * 2 + (ids[1] ^ other)
        for e in range(4):
            rows = at16((ids[2] ^ e) * 128 + own * 16)
            start = column
            for out in outs:
                width = out.shape[1]
                out[rows, :] = block[e * 16 : (e + 1) * 16, start : start + width]
                start += width


def project_pairs(parts, w_pair, k_ref, vt_ref, wvt_ref):
    wvt_ref[...] = w_pair[:, D:].astype(wide_t).T.astype(low_t)
    for n, part in enumerate(parts):
        for k in range(PAIRS):
            rows = part.shape[1]
            start = (n * 4 + k) * rows
            k_ref[start : start + rows, :] = dot_nn(part[k], w_pair[:, :D]).astype(low_t)
            vt_ref[:, start : start + rows] = dot_nt(wvt_ref[...], part[k]).astype(low_t)


def self_forward(ids, hidden, own, other, *refs):
    slices, (cols, row_data), refs = refs[:8], refs[8:10], refs[10:]
    out, mixed, lse, wq, wkv, q_ref, k_ref, vt_ref, wvt_ref, bias_ref, s_ref, ot_ref = refs
    rows = hidden.shape[0]
    parts = [(ids[0] ^ k, n, slices[n * 4 + k]) for n in range(2) for k in range(4)]
    assemble(ids, parts, 0, (wq, wkv))
    q_ref[...] = (dot_nn(hidden[...], wq[...]).astype(low_t) * 0.125).astype(low_t)
    project_pairs((own, other), wkv, k_ref, vt_ref, wvt_ref)
    seq, limit = row_data[16:17, :], row_data[17:18, :]
    for b in range(8):
        seen = (cols[:, b : b + 1] == seq) & (cols[:, 8 + b : 9 + b] < limit)
        bias_ref[b * rows : (b + 1) * rows, :] = jnp.where(seen, 0.0, neg_fill)
    mine = lax.broadcasted_iota(jnp.int32, (rows, rows), 0) == lax.broadcasted_iota(
        jnp.int32, (rows, rows), 1
    )
    block = at128(ids[0] * rows, rows)
    bias_ref[block, :] = jnp.where(mine, 0.0, bias_ref[block, :])
    attend_rows(q_ref, k_ref, vt_ref, bias_ref, s_ref, ot_ref, lse)
    finish_rows(ot_ref, out, mixed)


def layer_norm(values, gain_row, shift_row):
    mean = jnp.mean(values, axis=1, keepdims=True)
    centred = values - mean
    scale = lax.rsqrt(jnp.mean(centred * centred, axis=1, keepdims=True) + layer_eps)
    normed = centred * scale
    return normed * gain_row + shift_row, normed, scale


def layer_norm_back(grad, normed, scale, gain_row):
    gain_term = jnp.sum(grad * normed, axis=0, keepdims=True)
    shift_term = jnp.sum(grad, axis=0, keepdims=True)
    scaled = grad * gain_row
    grad_in = scale * (
        scaled
        - jnp.mean(scaled, axis=1, keepdims=True)
        - normed * jnp.mean(scaled * normed, axis=1, keepdims=True)
    )
    return grad_in, gain_term, shift_term


def head_arrays(ids, k_ref, vt_ref, cols, column, k_all, v_all, kt, turn):
    rows = turn.shape[1]
    core = ids[1]
    mine = half_mask((rows, PAIR), 1, core)
    features = pl.ds(pl.multiple_of(core * HEAD, HEAD), HEAD)
    lane = lax.broadcasted_iota(jnp.int32, (rows, PAIR), 1) % HEAD
    ones_v = jnp.where((lane >= 8) & (lane < 11), 1.0, 0.0).astype(low_t)
    pair = at128(ids[0] * PAIR)
    for b in range(8):
        here = slice(b * rows, (b + 1) * rows)
        seq = cols[:, column + b : column + b + 1].astype(jnp.int32)
        other_seq = (lane >= 16) & (lane < 20) & (lane != seq + 16)
        ones_k = jnp.where(other_seq, neg_fill, jnp.where(lane < 3, 1.0, 0.0)).astype(low_t)
        key = k_ref[here, pair]
        k_all[here, :] = jnp.where(mine, key, ones_k)
        turn[...] = key.astype(wide_t).T
        kt[:, here] = turn[features, :].astype(low_t)
        v_all[here, :] = jnp.where(mine, turned(vt_ref[pair, here]), ones_v)


def cross_forward(ids, hidden, self_low, own, other, *refs):
    slices, (cols, row_data) = refs[:2], refs[2:4]
    first, normed, scale_out, first_low, cross_low, mixed, lse, cross_q = refs[4:12]
    wo, wcq, wckv, wco, gs, k_all, v_all, kt = refs[12:20]
    q_ref, k_ref, vt_ref, wvt_ref, bias_ref, s_ref, ot_ref, turn = refs[20:]
    for n in range(2):
        for e in range(4):
            rows = at16(e * 128 + (ids[1] ^ n) * 64, 64)
            start = 0
            for out in (wo, wcq, wckv, wco):
                width = out.shape[1]
                out[rows, :] = slices[n][e, :, start : start + width]
                start += width
    for e in range(4):
        gs[:, e * 128 : (e + 1) * 128] = slices[0][e, :16, 5 * D :]
    gain, shift = gs[0:1, :].astype(wide_t), gs[3:4, :].astype(wide_t)
    value, n0, s0 = layer_norm(
        hidden[...].astype(wide_t) + dot_nn(self_low[...], wo[...]), gain, shift
    )
    first[...] = value
    normed[...] = n0
    scale_out[...] = jnp.broadcast_to(s0, scale_out.shape)
    low = value.astype(low_t)
    first_low[...] = low
    q = dot_nn(low, wcq[...]).astype(low_t)
    cross_q[...] = q
    q_ref[...] = (q * 0.125).astype(low_t)
    rows = hidden.shape[0]
    project_pairs((own, other), wckv, k_ref, vt_ref, wvt_ref)
    for b in range(8):
        seen = cols[:, 16 + b : 17 + b] == row_data[16:17, :]
        bias_ref[b * rows : (b + 1) * rows, :] = jnp.where(seen, 0.0, neg_fill)
    attend_rows(q_ref, k_ref, vt_ref, bias_ref, s_ref, ot_ref, lse)
    finish_rows(ot_ref, cross_low, mixed)
    head_arrays(ids, k_ref, vt_ref, cols, 16, k_all, v_all, kt, turn)


def feed_forward(ids, first, cross_low, cross_mixed, lse, row_data, cross_q, wco, gs, cotangent, *refs):
    slices = refs[0:8]
    result, dealt, second_grad, keep, send, sums, slope, wins, wouts = refs[8:]
    half_ff = FF // 2
    for n in range(2):
        for k in range(4):
            chip, core, part = ids[0] ^ k, ids[1] ^ n, slices[n * 4 + k]
            for e in range(4):
                w, here = ids[2] ^ e, slice(e * 16, (e + 1) * 16)
                rows = at16(w * 128 + (chip * 2 + core) * 16)
                for g in range(4):
                    row = w * 256 + ((chip % 2) * 2 + core) * 64 + g * 16
                    wouts[(chip // 2) ^ ids[1], at16(row), :] = part[here, FF + g * D : FF + (g + 1) * D]
                    for h in range(2):
                        column = g * 512 + h * 256
                        wins[h ^ ids[1], rows, g * 256 : (g + 1) * 256] = part[here, column : column + 256]
    gains, shifts = gs[0:3, :].astype(wide_t), gs[3:6, :].astype(wide_t)
    second, n1, s1 = layer_norm(
        first[...] + dot_nn(cross_low[...], wco[...]), gains[1:2], shifts[1:2]
    )
    low = second.astype(low_t)
    for out in (keep, send):
        out[:, 2 * half_ff : 2 * half_ff + D] = low
        out[:, 2 * half_ff + 2 * D : 2 * half_ff + 3 * D] = cross_low[...]
    width = 512
    chunks = [(n, c) for n in range(2) for c in range(FF // 2 // width)]
    total = second
    for n, c in chunks:
        here = slice(c * width, (c + 1) * width)
        wide = slice(n * half_ff + c * width, n * half_ff + (c + 1) * width)
        pre = dot_nn(low, wins[n, :, here])
        sig = 1.0 / (1.0 + jnp.exp(-pre))
        act = (pre * sig).astype(low_t)
        (keep, send)[n][:, half_ff + c * width : half_ff + (c + 1) * width] = act
        slope[:, wide] = sig * (1.0 + pre * (1.0 - sig))
        total = total + dot_nn(act, wouts[n, here, :])
    value, n2, s2 = layer_norm(total, gains[2:3], shifts[2:3])
    result[...] = value.astype(low_t)
    third, gain_c, shift_c = layer_norm_back(cotangent[...].astype(wide_t), n2, s2, gains[2:3])
    third_low = third.astype(low_t)
    for out in (keep, send):
        out[:, 2 * half_ff + D : 2 * half_ff + 2 * D] = third_low
    total = third
    for n, c in chunks:
        here = slice(c * width, (c + 1) * width)
        wide = slice(n * half_ff + c * width, n * half_ff + (c + 1) * width)
        back = (dot_nt(third_low, wouts[n, here, :]) * slope[:, wide]).astype(low_t)
        (keep, send)[n][:, here] = back
        total = total + dot_nt(back, wins[n, :, here])
    grad, gain_b, shift_b = layer_norm_back(total, n1, s1, gains[1:2])
    second_grad[...] = grad
    grad_low = grad.astype(low_t)
    for out, core in ((keep, ids[1]), (send, 1 - ids[1])):
        half = grad_low[:, : D // 2]
        out[:, 2 * half_ff + 3 * D :] = jnp.where(core == 0, half, grad_low[:, D // 2 :])
    mixed = dot_nt(grad_low, wco[...]).astype(low_t)
    rows = grad_low.shape[0]
    sides = side_rows(lse, mixed, cross_mixed, row_data)
    for p in range(PAIRS):
        dealt[p, :rows, :PAIR] = cross_q[:, p * PAIR : (p + 1) * PAIR]
        dealt[p, :rows, PAIR:] = mixed[:, p * PAIR : (p + 1) * PAIR]
        dealt[p, rows:, :] = sides[p]
    zero = jnp.zeros_like(gain_b)
    sums[...] = jnp.concatenate((zero, gain_b, gain_c, zero, shift_b, shift_c, zero, zero), axis=0)


def grads_a(ids, keep, received, out, g_in, g_out, g_cross):
    half = FF // 2

    def both(left, right):
        return (dot_tn(keep[:, left], keep[:, right]) + dot_tn(received[:, left], received[:, right])).astype(low_t)

    at = [0, half] + [2 * half + n * D for n in range(4)]
    pre, act = slice(at[0], at[1]), slice(at[1], at[2])
    second, branch, low = (slice(at[n], at[n] + D) for n in (2, 3, 4))
    g_in[...] = both(second, pre)
    g_out[...] = both(act, branch)
    g_cross[...] = both(low, slice(at[5], at[5] + D // 2))
    for chip in range(4):
        for e in range(4):
            w, here = ids[2] ^ e, slice(e * 32, (e + 1) * 32)
            rows = at16(w * 128 + chip * 32, 32)
            out[chip, here, :half] = g_in[rows, :]
            for g in range(2):
                out[chip, here, half + g * D : half + (g + 1) * D] = g_out[
                    at16(w * 256 + chip * 64 + g * 32, 32), :
                ]
            out[chip, here, half + 2 * D :] = g_cross[rows, :]


def grads_b(ids, first_low, cross_dq, self_low, branch, sums, dkv, out, g_query, g_output):
    g_query[...] = dot_tn(first_low[...], cross_dq[...]).astype(low_t)
    g_output[...] = dot_tn(self_low[...], branch[...]).astype(low_t)
    row = jnp.concatenate((sums[...], jnp.zeros_like(sums[...])), axis=0).astype(low_t)
    rows = dkv.shape[2]
    for e in range(4):
        w, here = ids[2] ^ e, slice(e * 16, (e + 1) * 16)
        piece = row[:, :128]
        for k in range(1, 4):
            piece = jnp.where(w == k, row[:, k * 128 : (k + 1) * 128], piece)
        for device in range(8):
            own = at16(w * 128 + device * 16)
            out[device, here, :D] = g_query[own, :]
            out[device, here, D : 2 * D] = g_output[own, :]
            out[device, here, 2 * D : 2 * D + 128] = piece
    for device in range(8):
        for n in range(2):
            start = 2 * D + 128 + n * rows
            out[device, :, start : start + rows] = dkv[device, n * HEAD : (n + 1) * HEAD, :]


def pair_setup(is_self, ids, own, other, w_pair, cols, *refs):
    k_all, v_all, kt, turn = refs
    chip, core = ids[0], ids[1]
    rows = own.shape[1]
    mine = half_mask((rows, PAIR), 1, core)
    features = pl.ds(pl.multiple_of(core * HEAD, HEAD), HEAD)
    lane = lax.broadcasted_iota(jnp.int32, (rows, PAIR), 1) % HEAD
    ones_v = jnp.where((lane >= 8) & (lane < 11), 1.0, 0.0).astype(low_t)
    pair = at128(chip * PAIR)
    wk, wv = w_pair[:, pair], w_pair[:, at128(D + chip * PAIR)]
    for n, part in enumerate((own, other)):
        for k in range(4):
            b = n * 4 + k
            here = slice(b * rows, (b + 1) * rows)
            column = b if is_self else 16 + b
            seq = cols[:, column : column + 1].astype(jnp.int32)
            other_seq = (lane >= 16) & (lane < 20) & (lane != seq + 16)
            ones_k = jnp.where(other_seq, neg_fill, jnp.where(lane < 3, 1.0, 0.0)).astype(low_t)
            key = dot_nn(part[k], wk)
            turn[...] = key.T
            kt[:, here] = turn[features, :].astype(low_t)
            k_all[here, :] = jnp.where(mine, key.astype(low_t), ones_k)
            v_all[here, :] = jnp.where(mine, dot_nn(part[k], wv).astype(low_t), ones_v)


def pair_queries(ids, own, other, w_query, q_all):
    wq = w_query[:, at128(ids[0] * PAIR)]
    for n, part in enumerate((own, other)):
        for k in range(4):
            q_all[n * 4 + k] = dot_nn(part[k], wq).astype(low_t)


def pair_back(is_self, ids, *refs):
    if is_self:
        q_parts, do_own, do_other, k_all, v_all, kt, cols, row_data, back = refs[:9]
        do_parts = (do_own, do_other)
    else:
        both_own, both_other, k_all, v_all, kt, dq_keep, dq_send, dkv = refs[:8]
        both_parts = (both_own, both_other)
    q_all, do_all, dq_t, dk, dv, rank, turn = refs[-7:]
    core = ids[1]
    rows = q_all.shape[1]
    keys = 8 * rows
    mine = half_mask((rows, PAIR), 1, core)
    features = pl.ds(pl.multiple_of(core * HEAD, HEAD), HEAD)
    for n in range(2):
        for k in range(4):
            b = n * 4 + k
            if is_self:
                here = slice(b * rows, (b + 1) * rows)
                rank[here, :] = jnp.broadcast_to(cols[:, 8 + b : 9 + b], (rows, 128))
                q, do = q_parts[b], do_parts[n][k, :rows, :]
                side = jnp.concatenate(
                    (do_parts[n][k, rows : rows + 16, :], do_parts[n][k, rows + 16 :, :]), axis=1
                )
            else:
                q, do = both_parts[n][k, :rows, :PAIR], both_parts[n][k, :rows, PAIR:]
                side = both_parts[n][k, rows:, :]
            side = side_lanes(side, core)
            q_all[b] = jnp.where(mine, (q * 0.125).astype(low_t), side)
            do_all[b] = jnp.where(mine, do, side)
    dk[...] = jnp.zeros_like(dk)
    dv[...] = jnp.zeros_like(dv)
    tile = min(1024, keys)
    blocks = 1 if is_self else 2

    def step(step, carry):
        b, wide = step * blocks, blocks * rows
        q, do = (ref[pl.ds(b, blocks)].reshape(wide, PAIR) for ref in (q_all, do_all))
        dqt = jnp.zeros((HEAD, wide), wide_t)
        for t in range(keys // tile):
            here = slice(t * tile, (t + 1) * tile)
            w = jnp.exp(dot_nt(k_all[here, :], q))
            if is_self:
                ranks = jnp.concatenate((rank[here, :],) * (wide // 128), axis=1)
                index = lax.broadcasted_iota(jnp.int32, (tile, wide), 0)
                own = lax.broadcasted_iota(jnp.int32, (tile, wide), 1) + (b * rows - t * tile)
                w = jnp.where((ranks < row_data[pl.ds(8 + b, 1), :]) | (index == own), w, 0.0)
            ds = (w * dot_nt(v_all[here, :], do)).astype(low_t)
            dv[here, :] += dot_nn(w.astype(low_t), do)
            dk[here, :] += dot_nn(ds, q)
            dqt = dqt + dot_nn(kt[:, here], ds)
        dqt = (dqt * 0.125).astype(low_t)
        for n in range(blocks):
            dq_t[b + n] = dqt[:, n * rows : (n + 1) * rows]
        return carry

    lax.fori_loop(0, 8 // blocks, step, 0)
    for n in range(2):
        for k in range(4):
            b = n * 4 + k
            device = k * 2 + (core ^ n)
            here = slice(b * rows, (b + 1) * rows)
            if is_self:
                back[device, :HEAD, :] = dq_t[b]
            else:
                (dq_keep, dq_send)[n][k] = dq_t[b]
            out, start = (back, HEAD) if is_self else (dkv, 0)
            for value in (dk, dv):
                turn[...] = value[here, :].T
                out[device, start : start + HEAD, :] = turn[features, :].astype(low_t)
                start += HEAD


def head_grads(grads, own, other, core, hidden=None):
    first = HEAD if hidden else 0
    total = jnp.zeros((2 * HEAD, D), wide_t)
    total_q = jnp.zeros((HEAD, D), wide_t)
    for n, part in enumerate((own, other)):
        for k in range(4):
            device = k * 2 + (core ^ n)
            total += dot_nn(grads[device, first:, :], part[k])
            if hidden:
                total_q += dot_nn(grads[device, :HEAD, :], hidden[n][k])
    return total, total_q


def pair_grads(ids, grads, own, other, dw):
    total, unused = head_grads(grads, own, other, ids[1])
    for w in range(4):
        dw[w] = total[:, w * 128 : (w + 1) * 128].astype(low_t)


def turned(value):
    return value.astype(wide_t).T.astype(low_t)


def pair_up(ids, keep, received, *outs):
    for k in range(4):
        p = ids[0] ^ k
        outs[k][at16(ids[1] * HEAD, HEAD), :] = keep[p]
        outs[k][at16((1 - ids[1]) * HEAD, HEAD), :] = received[p]


def first_back(ids, *refs):
    parts = refs[:4]
    second_grad, normed, scale, self_mixed, lse, row_data, gs, wcq, wo, sums_in = refs[4:14]
    first_grad, branch, dealt, dq, sums, all_t = refs[14:]
    for k in range(4):
        all_t[at128((ids[0] ^ k) * PAIR), :] = parts[k][...]
    dq[...] = turned(all_t[...])
    total = second_grad[...] + dot_nt(dq[...], wcq[...])
    grad, gain_a, shift_a = layer_norm_back(
        total, normed[...], scale[:, 0:1], gs[0:1, :].astype(wide_t)
    )
    first_grad[...] = grad
    low = grad.astype(low_t)
    branch[...] = low
    mixed = dot_nt(low, wo[...]).astype(low_t)
    rows = low.shape[0]
    sides = side_rows(lse, mixed, self_mixed, row_data)
    for p in range(PAIRS):
        dealt[p, :rows, :] = mixed[:, p * PAIR : (p + 1) * PAIR]
        dealt[p, rows : rows + 16, :] = sides[p][:, :PAIR]
        dealt[p, rows + 16 :, :] = sides[p][:, PAIR:]
    zero = jnp.zeros_like(gain_a)
    sums[...] = sums_in[...] + jnp.concatenate(
        (gain_a, zero, zero, shift_a, zero, zero, zero, zero), axis=0
    )


def source_back(ids, parts, wckv, out, dkv):
    rows = out.shape[0]
    for device in range(8):
        for n in range(2):
            start = 2 * D + 128 + n * rows
            dkv[n * D + device * HEAD : n * D + (device + 1) * HEAD, :] = parts[
                device, :, start : start + rows
            ]
    out[...] = dot_nt(turned(dkv[...]), wckv[...])


def hidden_back(ids, back, first_grad, wq, wkv, hidden_grad, stream_grad, all_t):
    for device in range(8):
        for n in range(3):
            all_t[n * D + device * HEAD : n * D + (device + 1) * HEAD, :] = back[
                device, n * HEAD : (n + 1) * HEAD, :
            ]
    hidden_grad[...] = first_grad[...] + dot_nt(turned(all_t[:D, :]), wq[...])
    stream_grad[...] = dot_nt(turned(all_t[D:, :]), wkv[...])


def add_parts(parts, rows, columns):
    total = parts[0, rows, columns].astype(wide_t)
    for n in range(1, parts.shape[0]):
        total = total + parts[n, rows, columns].astype(wide_t)
    return total.astype(low_t)


def add_chips(ids, parts, dw, *outs):
    width = parts.shape[2]
    for e in range(4):
        outs[e][:, :width] = add_parts(parts, slice(e * 32, (e + 1) * 32), slice(None))
        piece = dw[ids[2] ^ e]
        for g in range(4):
            outs[e][:, width + g * 128 : width + (g + 1) * 128] = piece[g * 32 : (g + 1) * 32, :]


def self_grads(ids, grads, own, other, hidden_own, hidden_other, dw):
    total, total_q = head_grads(grads, own, other, ids[1], (hidden_own, hidden_other))
    for w in range(4):
        columns = slice(w * 128, (w + 1) * 128)
        dw[w, :HEAD, :] = total_q[:, columns].astype(low_t)
        dw[w, HEAD:, :] = total[:, columns].astype(low_t)


def end_sums(ids, parts, dw, *outs):
    width = 2 * D + 128
    for e in range(4):
        outs[e][:, :width] = add_parts(parts, slice(e * 16, (e + 1) * 16), slice(0, width))
        outs[e][:, width : width + 128] = jnp.zeros((16, 128), low_t)
        piece = dw[ids[2] ^ e]
        for g in range(12):
            start = width + 128 + g * 128
            outs[e][:, start : start + 128] = piece[g * 16 : (g + 1) * 16, :]


def add_shards(ids, *refs):
    out = refs[8]

    def total(parts):
        value = parts[0][...].astype(wide_t)
        for part in parts[1:]:
            value = value + part[...].astype(wide_t)
        return value.astype(low_t)

    first, last = total(refs[:4]), total(refs[4:8])
    width, half = first.shape[1], last.shape[1] // 2
    out[:, :width] = first
    out[:16, width:] = last[:, :half]
    out[16:, width:] = last[:, half:]


def place_all(ids, *refs):
    parts, refs = refs[:8], refs[8:]
    g_in, g_out, g_cross, g_cross_pair, g_cross_query, g_output, gains, shifts, g_query, g_pair = refs[:10]
    pair_t, all_t = refs[10:]
    half = FF // 2
    start_cross = half + 2 * D
    start_pair = start_cross + D // 2
    start_end = start_pair + 4 * 128
    half_end = parts[0].shape[1] - start_end
    for n in range(2):
        core = ids[1] ^ n
        for step in range(4):
            chip, part = ids[0] ^ step, parts[n * 4 + step]
            rows = at16(chip * 32, 32)
            device = chip * 2 + core
            for k in range(4):
                g_in[rows, at128(k * 512 + core * 256, 256)] = part[
                    :, k * 256 : (k + 1) * 256
                ].astype(wide_t)
            for g in range(2):
                g_out[at16(core * 256 + chip * 64 + g * 32, 32), :] = part[
                    :, half + g * D : half + (g + 1) * D
                ].astype(wide_t)
            g_cross[rows, at128(core * 256, 256)] = part[:, start_cross:start_pair].astype(wide_t)
            for g in range(4):
                column = start_pair + g * 128
                row = (g // 2) * D + device * HEAD + (g % 2) * 32
                pair_t[at16(row, 32), :] = part[:, column : column + 128].astype(wide_t)

            def piece(column, width):
                row, at = (0, column) if column < half_end else (16, column - half_end)
                return part[row : row + 16, start_end + at : start_end + at + width].astype(wide_t)

            own_rows = at16(device * 16)
            for column in range(0, D, 128):
                g_cross_query[own_rows, column : column + 128] = piece(column, 128)
                g_output[own_rows, column : column + 128] = piece(D + column, 128)
            if n == 0 and step == 0:
                norms = piece(2 * D, 128)
                gains[...], shifts[...] = norms[0:3], norms[3:6]
            for g in range(12):
                row = (g // 4) * D + device * HEAD + (g % 4) * 16
                all_t[at16(row), :] = piece(2 * D + 256 + g * 128, 128)
    g_cross_pair[...] = pair_t[...].T
    g_query[...] = all_t[:D, :].T
    g_pair[...] = all_t[D:, :].T


def pack_rows(ids, stream, source, many):
    for k in range(4):
        many[k, :, :D] = stream[...]
        many[k, :, D:] = source[...]


def pack_start(ids, wq, wkv, ffn_in, ffn_out, pack):
    own = ids[0] * 2 + ids[1]
    for k in range(4):
        start = 3 * D + FF + k * D
        pack[:, start : start + D] = ffn_out[at16(own * 64 + k * 16), :]
    pack[:, :D] = wq[at16(own * 16), :]
    pack[:, D : 3 * D] = wkv[at16(own * 16), :]
    pack[:, 3 * D : 3 * D + FF] = ffn_in[at16(own * 16), :]


def pack_more(ids, *refs):
    weights, gain, shift, rows_in, pack, many = refs[:4], *refs[4:]
    rows = at16(ids[1] * 64, 64)
    norms = (gain[...].astype(wide_t), shift[...].astype(wide_t), jnp.zeros((58, 128), wide_t))
    norms = jnp.concatenate(norms, axis=0).astype(low_t)
    for k in range(4):
        start = 0
        for w in weights:
            pack[k, :, start : start + w.shape[1]] = w[rows, :]
            start += w.shape[1]
        pack[k, :, start:] = norms
        many[k] = rows_in[...]


def mask_data(ids, order, ranks, limits, cols, row_data, all_rows):
    rows = cols.shape[0]
    ends = [ids[3]]
    for n in range(1, 4):
        ends.append(ends[-1] + ids[3 + n])

    def sequence(position):
        return sum((position >= end).astype(wide_t) for end in ends)

    for n in range(2):
        for k in range(4):
            b = n * 4 + k
            device = k * 2 + (ids[1] ^ n)
            here = at128(device * rows, rows)
            index = lax.broadcasted_iota(jnp.int32, (1, rows), 1) + device * rows
            all_rows[b : b + 1, :] = sequence(order[:, here])
            all_rows[8 + b : 9 + b, :] = ranks[:, here].astype(wide_t)
            all_rows[16 + b : 17 + b, :] = sequence(index)
            row_data[8 + b : 9 + b, :] = limits[:, here].astype(wide_t)
    row_data[0:8, :] = all_rows[0:8, :]
    all_rows[24:32, :] = jnp.zeros((8, rows), wide_t)
    all_rows[24:25, :] = all_rows[pl.ds(ids[0], 1), :]
    row_data[16:24, :] = jnp.zeros((8, rows), wide_t)
    row_data[16:17, :] = all_rows[pl.ds(ids[0], 1), :]
    row_data[17:18, :] = row_data[pl.ds(8 + ids[0], 1), :]
    cols[:, :32] = all_rows[...].T


def pack_first(ids, *refs):
    parts, (one, two) = refs[:4], refs[4:]
    width = one.shape[1]
    for e in range(4):
        here = slice(e * 16, (e + 1) * 16)
        one[here, :] = parts[e][:, :width]
        two[here, :] = parts[e][:, width:]


def core_swap(value):
    return lax.ppermute(value, "core", [(0, 1), (1, 0)])


def chip_swaps(parts):
    moves = [[(i, i ^ k) for i in range(4)] for k in range(4)]
    return [parts[0]] + [lax.ppermute(parts[k], "chip", moves[k]) for k in range(1, 4)]


def shard_swaps(parts):
    moves = [[(i, i ^ k) for i in range(4)] for k in range(4)]
    return [parts[0]] + [lax.ppermute(parts[k], "wa", moves[k]) for k in range(1, 4)]


def deal(value):
    return lax.all_to_all(value, "chip", 0, 0, tiled=True)


def deal_all(value):
    return lax.all_to_all(value, ("chip", "core"), 0, 0, tiled=True)


def deal_both(value):
    own = deal(value)
    return own, core_swap(own)


def after(value, *others):
    return lax.optimization_barrier((value,) + others)[0]


def fast_shards(
    hidden,
    stream,
    encoder,
    lengths,
    order,
    ranks,
    thresholds,
    self_query,
    self_key_value,
    self_output,
    cross_query,
    cross_key_value,
    cross_output,
    ffn_in,
    ffn_out,
    norm_gain,
    norm_shift,
    cotangent,
):
    rows, keys = hidden.shape[1], order.shape[1]
    chip, core, mw = lax.axis_index("chip"), lax.axis_index("core"), lax.axis_index("wa")
    ids = jnp.stack((chip, core, mw)).astype(jnp.int32)
    inputs = hidden[0]

    (many,) = run(pack_rows, [((4, rows, 2 * D), low_t)], ids, [stream[0], encoder[0]])
    (pack1,) = run(
        pack_start,
        [((16, 3 * D + 2 * FF), low_t)],
        ids,
        [after(self_query, many), self_key_value, ffn_in, ffn_out],
    )
    x_own = deal(many)
    shards1 = shard_swaps([pack1] * 4)
    copies2, hidden_copies = run(
        pack_more,
        [((4, 64, 5 * D + 128), low_t), ((4, rows, D), low_t)],
        ids,
        [after(self_output, pack1), cross_query, cross_key_value, cross_output, norm_gain, norm_shift]
        + [inputs],
    )
    cols, row_data = run(
        mask_data,
        [((rows, 32), wide_t), ((24, rows), wide_t)],
        jnp.concatenate((after(ids, pack1), lengths[0])),
        [order, ranks, thresholds],
        [((32, rows), wide_t)],
    )
    part1, part3 = run(
        pack_first,
        [((64, 3 * D), low_t), ((64, 2 * FF), low_t)],
        ids,
        [after(shards1[0], x_own, cols, copies2)] + shards1[1:],
    )
    slices1 = chip_swaps([part1] * 4)
    slices1 = slices1 + [core_swap(part) for part in slices1]
    shards2 = lax.all_to_all(after(copies2, x_own), "wa", 0, 0, tiled=True)
    x_other = core_swap(after(x_own, part1))
    slices3 = chip_swaps([after(part3, slices1[1])] * 4)
    stream_own, stream_other = (x_own, 0), (x_other, 0)
    source_own, source_other = (x_own, 1), (x_other, 1)

    attend_scratch = [
        ((rows, D), low_t),
        ((keys, D), low_t),
        ((D, keys), low_t),
        ((D, D), low_t),
        ((keys, rows), wide_t),
        ((2, keys, rows), wide_t),
        ((D, rows), wide_t),
    ]
    self_low, self_mixed, self_lse, wq, wkv = run(
        self_forward,
        [((rows, D), low_t), ((rows, D), wide_t), ((HEADS, rows), wide_t)]
        + [((D, D), low_t), ((D, 2 * D), low_t)],
        ids,
        [inputs, stream_own, stream_other, *slices1, cols, row_data],
        attend_scratch,
        us=15,
    )
    head_shapes = [((keys, PAIR), low_t)] * 2 + [((HEAD, keys), low_t)]
    self_head = run(
        functools.partial(pair_setup, True),
        head_shapes,
        ids,
        [stream_own, stream_other, wkv, after(cols, self_low)],
        [((PAIR, rows), wide_t)],
        us=4,
    )
    slices3 = slices3 + [core_swap(after(part, self_head[0])) for part in slices3]
    shards2_other = core_swap(after(shards2, self_head[0], *slices3[:4]))
    hidden_own = deal(after(hidden_copies, shards2, self_head[0], *slices3[:4]))
    (
        first,
        normed,
        scale,
        first_low,
        cross_low,
        cross_mixed,
        cross_lse,
        cross_q,
        wo,
        wcq,
        wckv,
        wco,
        gs,
        *cross_head,
    ) = run(
        cross_forward,
        [((rows, D), wide_t)] * 2
        + [((rows, 128), wide_t)]
        + [((rows, D), low_t)] * 2
        + [((rows, D), wide_t), ((HEADS, rows), wide_t), ((rows, D), low_t)]
        + [((D, D), low_t), ((D, D), low_t), ((D, 2 * D), low_t), ((D, D), low_t), ((16, D), low_t)]
        + head_shapes,
        ids,
        [inputs, after(self_low, self_head[0]), source_own, source_other, shards2, shards2_other]
        + [cols, row_data],
        attend_scratch + [((PAIR, rows), wide_t)],
        us=15,
    )
    hidden_other = core_swap(after(hidden_own, cross_low))
    width_s = 2 * FF // 2 + 3 * D + D // 2
    result, cross_dealt, second_grad, keep_a, send_a, sums = run(
        feed_forward,
        [
            ((rows, D), low_t),
            ((PAIRS, rows + 16, 2 * PAIR), low_t),
            ((rows, D), wide_t),
            ((rows, width_s), low_t),
            ((rows, width_s), low_t),
            ((8, D), wide_t),
        ],
        ids,
        [after(first, hidden_own), cross_low, cross_mixed, cross_lse, row_data, cross_q, wco, gs]
        + [cotangent[0], *slices3],
        [((rows, FF), wide_t), ((2, D, FF // 2), low_t), ((2, FF // 2, D), low_t)],
        us=8,
    )
    both_own = deal(cross_dealt)
    width_a = FF // 2 + 2 * D + D // 2
    (dealt_a,) = run(
        grads_a,
        [((4, 128, width_a), low_t)],
        ids,
        [keep_a, core_swap(send_a)],
        [((D, FF // 2), low_t), ((FF // 2, D), low_t), ((D, D // 2), low_t)],
        us=6,
    )
    rows_a = deal(after(dealt_a, both_own))
    both_other = core_swap(after(both_own, dealt_a))

    back_scratch = (
        [((8, rows, PAIR), low_t)] * 2
        + [((8, HEAD, rows), low_t)]
        + [((keys, PAIR), wide_t)] * 3
        + [((PAIR, rows), wide_t)]
    )
    cq_keep, cq_send, cross_dkv = run(
        functools.partial(pair_back, False),
        [((4, HEAD, rows), low_t)] * 2 + [((8, 2 * HEAD, rows), low_t)],
        ids,
        [after(both_own, dealt_a), both_other, *cross_head],
        back_scratch,
        us=16,
    )
    pairs = run(pair_up, [((PAIR, rows), low_t)] * 4, ids, [cq_keep, core_swap(cq_send)])
    cross_back = chip_swaps(pairs)
    (self_queries,) = run(
        pair_queries,
        [((8, rows, PAIR), low_t)],
        ids,
        [hidden_own, hidden_other, after(wq, pairs[0])],
    )
    (cross_dw,) = run(
        pair_grads,
        [((4, 2 * HEAD, 128), low_t)],
        ids,
        [after(cross_dkv, pairs[0]), source_own, source_other],
    )
    first_grad, self_branch, self_dealt, cross_dq, sums = run(
        first_back,
        [
            ((rows, D), wide_t),
            ((rows, D), low_t),
            ((PAIRS, rows + 32, PAIR), low_t),
            ((rows, D), low_t),
            ((8, D), wide_t),
        ],
        ids,
        [after(cross_back[0], cross_dw, self_queries), *cross_back[1:], second_grad, normed, scale, self_mixed, self_lse, row_data, gs, wcq, wo, sums],
        [((D, rows), low_t)],
        us=4,
    )
    do_own = deal(after(self_dealt, rows_a))
    shards_a = run(
        add_chips,
        [((32, width_a + 512), low_t)] * 4,
        ids,
        [after(rows_a, first_grad), cross_dw],
    )
    moved_a = shard_swaps([after(part, do_own) for part in shards_a])
    (dealt_b,) = run(
        grads_b,
        [((8, 64, 2 * D + 128 + 2 * rows), low_t)],
        ids,
        [first_low, cross_dq, self_low, self_branch, sums, cross_dkv],
        [((D, D), low_t)] * 2,
        us=3,
    )
    rows_b = deal_all(after(dealt_b, do_own))
    do_other = core_swap(after(do_own, dealt_b, *shards_a))
    (self_back_t,) = run(
        functools.partial(pair_back, True),
        [((8, 3 * HEAD, rows), low_t)],
        ids,
        [self_queries, after(do_own, dealt_b, *shards_a), do_other, *self_head, cols, row_data],
        back_scratch,
        us=16,
    )
    end_width = 2 * D + 2 * 128 + 12 * 128
    (self_dw,) = run(
        self_grads,
        [((4, 3 * HEAD, 128), low_t)],
        ids,
        [self_back_t, stream_own, stream_other, hidden_own, hidden_other],
    )
    end_parts = run(
        end_sums, [((16, end_width), low_t)] * 4, ids, [after(rows_b, self_dw), self_dw]
    )
    moved_end = shard_swaps(end_parts)
    self_back = deal_all(after(self_back_t, end_parts[0], *moved_a))
    (source_grad,) = run(
        source_back,
        [((rows, D), wide_t)],
        ids,
        [rows_b, after(wckv, end_parts[0])],
        [((2 * D, rows), low_t)],
        us=3,
    )
    (sums_end,) = run(
        add_shards,
        [((32, width_a + 512 + end_width // 2), low_t)],
        ids,
        [*moved_a, after(moved_end[0], source_grad), *moved_end[1:]],
    )
    all_parts = chip_swaps([sums_end] * 4)
    hidden_grad, stream_grad = run(
        hidden_back,
        [((rows, D), wide_t)] * 2,
        ids,
        [self_back, first_grad, wq, wkv],
        [((3 * D, rows), low_t)],
        us=3,
    )
    all_parts = all_parts + [core_swap(after(part, hidden_grad)) for part in all_parts]
    (
        grad_in,
        grad_out,
        grad_cross_output,
        grad_cross_pair,
        grad_cross_query,
        grad_output,
        gain_grads,
        shift_grads,
        grad_query,
        grad_pair,
    ) = run(
        place_all,
        [((128, FF), wide_t), ((D, D), wide_t), ((128, D), wide_t), ((128, 2 * D), wide_t)]
        + [((128, D), wide_t)] * 2
        + [((3, 128), wide_t)] * 2
        + [((128, D), wide_t), ((128, 2 * D), wide_t)],
        ids,
        all_parts,
        [((2 * D, 128), wide_t), ((3 * D, 128), wide_t)],
    )
    return (
        result[None],
        hidden_grad[None],
        stream_grad[None],
        source_grad[None],
        grad_query,
        grad_pair,
        grad_output,
        grad_cross_query,
        grad_cross_pair,
        grad_cross_output,
        grad_in,
        grad_out,
        gain_grads,
        shift_grads,
    )


def solution(mesh):
    in_specs = (
        P("wa", "ctx", None),
        P("wa", "ctx", None),
        P("wa", "ctx", None),
        P("wa", None),
        P("wa", None),
        P("wa", None),
        P("wa", None),
        P("wa", None),
        P("wa", None),
        P("wa", None),
        P("wa", None),
        P("wa", None),
        P("wa", None),
        P("wa", None),
        P("wa", None),
        P(None, "wa"),
        P(None, "wa"),
        P("wa", "ctx", None),
    )
    out_specs = (
        P("wa", "ctx", None),
        P("wa", "ctx", None),
        P("wa", "ctx", None),
        P("wa", "ctx", None),
        P("wa", None),
        P("wa", None),
        P("wa", None),
        P("wa", None),
        P("wa", None),
        P("wa", None),
        P("wa", None),
        P("wa", None),
        P(None, "wa"),
        P(None, "wa"),
    )
    if mesh.axis_names != ("ctx", "wa") or mesh.shape["ctx"] != HEADS or mesh.shape["wa"] != 4:
        return jax.shard_map(
            general_shards, mesh=mesh, in_specs=in_specs, out_specs=out_specs, check_vma=False
        )

    def finer(spec):
        return P(*(("chip", "core") if axis == "ctx" else axis for axis in spec))

    return jax.shard_map(
        fast_shards,
        mesh=Mesh(mesh.devices.reshape(4, 2, 4), ("chip", "core", "wa")),
        in_specs=tuple(finer(spec) for spec in in_specs),
        out_specs=tuple(finer(spec) for spec in out_specs),
        check_vma=False,
    )
```

```python
import functools

import jax
import jax.numpy as jnp
from jax import lax
from jax.experimental import pallas as pl
from jax.experimental.pallas import tpu as pltpu
from jax.sharding import Mesh
from jax.sharding import PartitionSpec as P

D = 512
HEADS = 8
HEAD = 64
KEYBLK = 1024


layer_eps = 1e-05
neg_fill = -1e30


def sequence_ids(positions, seq_ends):
    return jnp.sum((positions[:, None] >= seq_ends[None, :]).astype(jnp.int32), axis=1)


def head_split(matrix):
    return matrix.reshape(matrix.shape[0], HEADS, HEAD)


def block_scores(query_heads, key_heads):
    raw_scores = jnp.einsum(
        "lhd,khd->hlk", query_heads, key_heads, preferred_element_type=jnp.float32
    )
    return raw_scores * float(HEAD) ** (-0.5)


def softmax_totals(queries, key_rows, allowed_fn):
    query_heads = head_split(queries)
    count_rows = queries.shape[0]

    def visit(state_pair, block_index):
        running_top, running_sum = state_pair
        block_start = block_index * KEYBLK
        key_piece = lax.dynamic_slice_in_dim(key_rows, block_start, KEYBLK, 0)
        allowed = allowed_fn(block_start)[None]
        scores = jnp.where(
            allowed, block_scores(query_heads, head_split(key_piece[:, :D])), neg_fill
        )
        new_top = jnp.maximum(running_top, jnp.max(scores, axis=2))
        weights = jnp.where(allowed, jnp.exp(scores - new_top[:, :, None]), 0.0)
        running_sum = running_sum * jnp.exp(running_top - new_top) + jnp.sum(weights, axis=2)
        return ((new_top, running_sum), None)

    initial = (
        jnp.full((HEADS, count_rows), neg_fill, jnp.float32),
        jnp.zeros((HEADS, count_rows), jnp.float32),
    )
    (final_top, final_sum), unused = lax.scan(
        visit, initial, jnp.arange(key_rows.shape[0] // KEYBLK)
    )
    return final_top + jnp.log(final_sum)


def attend_values(queries, key_rows, log_totals, allowed_fn):
    query_heads = head_split(queries)

    def visit(running, block_index):
        block_start = block_index * KEYBLK
        key_piece = lax.dynamic_slice_in_dim(key_rows, block_start, KEYBLK, 0)
        allowed = allowed_fn(block_start)[None]
        scores = block_scores(query_heads, head_split(key_piece[:, :D]))
        weights = jnp.where(allowed, jnp.exp(scores - log_totals[:, :, None]), 0.0)
        value_heads = head_split(key_piece[:, D:])
        return (
            running
            + jnp.einsum(
                "hlk,khd->lhd",
                weights.astype(jnp.bfloat16),
                value_heads,
                preferred_element_type=jnp.float32,
            ),
            None,
        )

    mixed, unused = lax.scan(
        visit, jnp.zeros(query_heads.shape, jnp.float32), jnp.arange(key_rows.shape[0] // KEYBLK)
    )
    return mixed.reshape(queries.shape[0], D)


def head_offsets(grad_low, attended):
    return jnp.sum(head_split(grad_low.astype(jnp.float32) * attended), axis=2).T


def attend_back(queries, key_rows, log_totals, attended, grad_low, allowed_fn):
    query_heads = head_split(queries)
    grad_heads = head_split(grad_low)
    offsets = head_offsets(grad_low, attended)
    scale_value = float(HEAD) ** (-0.5)

    def visit(query_grad, block_index):
        block_start = block_index * KEYBLK
        key_piece = lax.dynamic_slice_in_dim(key_rows, block_start, KEYBLK, 0)
        allowed = allowed_fn(block_start)[None]
        key_heads = head_split(key_piece[:, :D])
        value_heads = head_split(key_piece[:, D:])
        weights = jnp.where(
            allowed, jnp.exp(block_scores(query_heads, key_heads) - log_totals[:, :, None]), 0.0
        )
        value_grad = jnp.einsum(
            "hlk,lhd->khd",
            weights.astype(jnp.bfloat16),
            grad_heads,
            preferred_element_type=jnp.float32,
        )
        weight_grad = jnp.einsum(
            "lhd,khd->hlk", grad_heads, value_heads, preferred_element_type=jnp.float32
        )
        score_grad = (weights * (weight_grad - offsets[:, :, None]) * scale_value).astype(
            jnp.bfloat16
        )
        query_grad = query_grad + jnp.einsum(
            "hlk,khd->lhd", score_grad, key_heads, preferred_element_type=jnp.float32
        )
        key_grad = jnp.einsum(
            "hlk,lhd->khd", score_grad, query_heads, preferred_element_type=jnp.float32
        )
        return (
            query_grad,
            jnp.concatenate((key_grad.reshape(KEYBLK, D), value_grad.reshape(KEYBLK, D)), axis=1),
        )

    query_grad, grad_pieces = lax.scan(
        visit, jnp.zeros(query_heads.shape, jnp.float32), jnp.arange(key_rows.shape[0] // KEYBLK)
    )
    return (query_grad.reshape(queries.shape[0], D), grad_pieces.reshape(key_rows.shape[0], 2 * D))


def normalize(values, gain_row, shift_row):
    row_mean = jnp.mean(values, axis=1, keepdims=True)
    centred = values - row_mean
    scale_inv = lax.rsqrt(jnp.mean(centred * centred, axis=1, keepdims=True) + layer_eps)
    normed = centred * scale_inv
    return (normed * gain_row + shift_row, normed, scale_inv)


def normalize_back(grad_out, normed, scale_inv, gain_row):
    gain_term = jnp.sum(grad_out * normed, axis=0)
    shift_term = jnp.sum(grad_out, axis=0)
    scaled = grad_out * gain_row
    grad_in = scale_inv * (
        scaled
        - jnp.mean(scaled, axis=1, keepdims=True)
        - normed * jnp.mean(scaled * normed, axis=1, keepdims=True)
    )
    return (grad_in, gain_term, shift_term)


def matmul(left, right):
    return jnp.dot(left, right, preferred_element_type=jnp.float32)


def general_shards(
    hidden,
    stream,
    encoder,
    lengths,
    order,
    ranks,
    thresholds,
    self_query,
    self_key_value,
    self_output,
    cross_query,
    cross_key_value,
    cross_output,
    ffn_in,
    ffn_out,
    norm_gain,
    norm_shift,
    cotangent,
):
    (
        full_query,
        full_pair,
        full_output,
        full_cross_query,
        full_cross_pair,
        full_cross_output,
        full_in,
        full_out,
        gain_rows,
        shift_rows,
    ) = (
        lax.all_gather(self_query, "wa", axis=0, tiled=True),
        lax.all_gather(self_key_value, "wa", axis=0, tiled=True),
        lax.all_gather(self_output, "wa", axis=0, tiled=True),
        lax.all_gather(cross_query, "wa", axis=0, tiled=True),
        lax.all_gather(cross_key_value, "wa", axis=0, tiled=True),
        lax.all_gather(cross_output, "wa", axis=0, tiled=True),
        lax.all_gather(ffn_in, "wa", axis=0, tiled=True),
        lax.all_gather(ffn_out, "wa", axis=0, tiled=True),
        lax.all_gather(norm_gain, "wa", axis=1, tiled=True),
        lax.all_gather(norm_shift, "wa", axis=1, tiled=True),
    )
    gains = gain_rows.astype(jnp.float32)
    shifts = shift_rows.astype(jnp.float32)
    local_rows = hidden.shape[1]
    total_rows = order.shape[1]
    row_start = lax.axis_index("ctx") * local_rows
    seq_ends = jnp.cumsum(lengths[0])
    token_seq = sequence_ids(order[0], seq_ends)
    source_seq = sequence_ids(jnp.arange(total_rows, dtype=jnp.int32), seq_ends)
    query_seq = lax.dynamic_slice_in_dim(token_seq, row_start, local_rows)
    query_rows = row_start + jnp.arange(local_rows, dtype=jnp.int32)
    all_limits = thresholds[0]
    limits = lax.dynamic_slice_in_dim(all_limits, row_start, local_rows)
    key_ranks = ranks[0]

    def self_allowed(block_start):
        block_seq = lax.dynamic_slice_in_dim(token_seq, block_start, KEYBLK)
        block_rank = lax.dynamic_slice_in_dim(key_ranks, block_start, KEYBLK)
        block_rows = block_start + jnp.arange(KEYBLK, dtype=jnp.int32)
        return (query_seq[:, None] == block_seq[None, :]) & (
            (block_rank[None, :] < limits[:, None]) | (query_rows[:, None] == block_rows[None, :])
        )

    def cross_allowed(block_start):
        return (
            query_seq[:, None] == lax.dynamic_slice_in_dim(source_seq, block_start, KEYBLK)[None, :]
        )

    inputs = hidden[0]
    stream_rows = stream[0]
    source_rows = encoder[0]
    queries = matmul(inputs, full_query).astype(jnp.bfloat16)
    self_local = matmul(stream_rows, full_pair).astype(jnp.bfloat16)
    cross_local = matmul(source_rows, full_cross_pair).astype(jnp.bfloat16)
    self_keys, cross_keys = (
        lax.all_gather(self_local, "ctx", axis=0, tiled=True),
        lax.all_gather(cross_local, "ctx", axis=0, tiled=True),
    )
    self_totals = softmax_totals(queries, self_keys, self_allowed)
    self_mixed = attend_values(queries, self_keys, self_totals, self_allowed)
    self_low = self_mixed.astype(jnp.bfloat16)
    first, first_normed, first_scale = normalize(
        inputs.astype(jnp.float32) + matmul(self_low, full_output), gains[0], shifts[0]
    )
    first_low = first.astype(jnp.bfloat16)
    cross_queries = matmul(first_low, full_cross_query).astype(jnp.bfloat16)
    cross_totals = softmax_totals(cross_queries, cross_keys, cross_allowed)
    cross_mixed = attend_values(cross_queries, cross_keys, cross_totals, cross_allowed)
    cross_low = cross_mixed.astype(jnp.bfloat16)
    second, second_normed, second_scale = normalize(
        first + matmul(cross_low, full_cross_output), gains[1], shifts[1]
    )
    second_low = second.astype(jnp.bfloat16)
    hidden_pre = matmul(second_low, full_in)
    sigmoid_pre = jax.nn.sigmoid(hidden_pre)
    activated = (hidden_pre * sigmoid_pre).astype(jnp.bfloat16)
    result, third_normed, third_scale = normalize(
        second + matmul(activated, full_out), gains[2], shifts[2]
    )
    third_grad, gain_grad_c, shift_grad_c = normalize_back(
        cotangent[0].astype(jnp.float32), third_normed, third_scale, gains[2]
    )
    branch_grad = third_grad.astype(jnp.bfloat16)
    grad_ffn_out = matmul(activated.T, branch_grad)
    slope = sigmoid_pre * (1.0 + hidden_pre * (1.0 - sigmoid_pre))
    pre_grad = (matmul(branch_grad, full_out.T) * slope).astype(jnp.bfloat16)
    grad_ffn_in = matmul(second_low.T, pre_grad)
    second_total = third_grad + matmul(pre_grad, full_in.T)
    second_grad, gain_grad_b, shift_grad_b = normalize_back(
        second_total, second_normed, second_scale, gains[1]
    )
    cross_branch = second_grad.astype(jnp.bfloat16)
    grad_cross_output = matmul(cross_low.T, cross_branch)
    cross_mixed_grad = matmul(cross_branch, full_cross_output.T).astype(jnp.bfloat16)
    cross_query_term, cross_terms = attend_back(
        cross_queries, cross_keys, cross_totals, cross_mixed, cross_mixed_grad, cross_allowed
    )
    cross_query_low = cross_query_term.astype(jnp.bfloat16)
    grad_cross_query = matmul(first_low.T, cross_query_low)
    first_total = second_grad + matmul(cross_query_low, full_cross_query.T)
    first_grad, gain_grad_a, shift_grad_a = normalize_back(
        first_total, first_normed, first_scale, gains[0]
    )
    self_branch = first_grad.astype(jnp.bfloat16)
    grad_self_output = matmul(self_low.T, self_branch)
    self_mixed_grad = matmul(self_branch, full_output.T).astype(jnp.bfloat16)
    self_query_term, self_terms = attend_back(
        queries, self_keys, self_totals, self_mixed, self_mixed_grad, self_allowed
    )
    self_sum, cross_sum = (
        lax.psum_scatter(self_terms, "ctx", scatter_dimension=0, tiled=True),
        lax.psum_scatter(cross_terms, "ctx", scatter_dimension=0, tiled=True),
    )
    self_query_low = self_query_term.astype(jnp.bfloat16)
    grad_self_query = matmul(inputs.T, self_query_low)
    input_grad = first_grad + matmul(self_query_low, full_query.T)
    self_sum_low = self_sum.astype(jnp.bfloat16)
    grad_self_pair = matmul(stream_rows.T, self_sum_low)
    stream_grad = matmul(self_sum_low, full_pair.T)
    cross_sum_low = cross_sum.astype(jnp.bfloat16)
    grad_cross_pair = matmul(source_rows.T, cross_sum_low)
    source_grad = matmul(cross_sum_low, full_cross_pair.T)
    gain_grads = jnp.stack((gain_grad_a, gain_grad_b, gain_grad_c))
    shift_grads = jnp.stack((shift_grad_a, shift_grad_b, shift_grad_c))
    (
        share_query,
        share_pair,
        share_output,
        share_cross_query,
        share_cross_pair,
        share_cross_output,
        share_in,
        share_out,
        share_gain,
        share_shift,
    ) = (
        lax.psum_scatter(
            grad_self_query.astype(jnp.bfloat16), "wa", scatter_dimension=0, tiled=True
        ).astype(jnp.float32),
        lax.psum_scatter(
            grad_self_pair.astype(jnp.bfloat16), "wa", scatter_dimension=0, tiled=True
        ).astype(jnp.float32),
        lax.psum_scatter(
            grad_self_output.astype(jnp.bfloat16), "wa", scatter_dimension=0, tiled=True
        ).astype(jnp.float32),
        lax.psum_scatter(
            grad_cross_query.astype(jnp.bfloat16), "wa", scatter_dimension=0, tiled=True
        ).astype(jnp.float32),
        lax.psum_scatter(
            grad_cross_pair.astype(jnp.bfloat16), "wa", scatter_dimension=0, tiled=True
        ).astype(jnp.float32),
        lax.psum_scatter(
            grad_cross_output.astype(jnp.bfloat16), "wa", scatter_dimension=0, tiled=True
        ).astype(jnp.float32),
        lax.psum_scatter(
            grad_ffn_in.astype(jnp.bfloat16), "wa", scatter_dimension=0, tiled=True
        ).astype(jnp.float32),
        lax.psum_scatter(
            grad_ffn_out.astype(jnp.bfloat16), "wa", scatter_dimension=0, tiled=True
        ).astype(jnp.float32),
        lax.psum_scatter(
            gain_grads.astype(jnp.bfloat16), "wa", scatter_dimension=1, tiled=True
        ).astype(jnp.float32),
        lax.psum_scatter(
            shift_grads.astype(jnp.bfloat16), "wa", scatter_dimension=1, tiled=True
        ).astype(jnp.float32),
    )
    (
        total_query,
        total_pair,
        total_output,
        total_cross_query,
        total_cross_pair,
        total_cross_output,
        total_in,
        total_out,
        total_gain,
        total_shift,
    ) = lax.psum(
        (
            share_query,
            share_pair,
            share_output,
            share_cross_query,
            share_cross_pair,
            share_cross_output,
            share_in,
            share_out,
            share_gain,
            share_shift,
        ),
        "ctx",
    )
    return (
        result.astype(jnp.bfloat16)[None],
        input_grad[None],
        stream_grad[None],
        source_grad[None],
        total_query,
        total_pair,
        total_output,
        total_cross_query,
        total_cross_pair,
        total_cross_output,
        total_in,
        total_out,
        total_gain,
        total_shift,
    )


PAIR = 2 * HEAD
PAIRS = HEADS // 2
FF = 2048
low_t = jnp.bfloat16
wide_t = jnp.float32
vmem_spec = pl.BlockSpec(memory_space=pltpu.VMEM)
smem_spec = pl.BlockSpec(memory_space=pltpu.SMEM)


def run(body, outs, ids, args, scratch=(), us=2, vmem=56):
    outs = [jax.ShapeDtypeStruct(shape, kind) for shape, kind in outs]
    arrays = [arg[0] if isinstance(arg, tuple) else arg for arg in args]
    parts = [n for n, arg in enumerate(args) if isinstance(arg, tuple)]
    total = len(args) + len(outs) + len(scratch)

    def kernel(ids, *refs):
        refs, buffers, sems = list(refs[:total]), refs[total:-1], refs[-1]
        copies = []
        for m, n in enumerate(parts):
            start = args[n][1] * D
            copies.append(
                pltpu.make_async_copy(refs[n].at[:, :, start : start + D], buffers[m], sems.at[m])
            )
            copies[m].start()
            refs[n] = buffers[m]
        for copy in copies:
            copy.wait()
        body(ids, *refs)

    buffers = [pltpu.VMEM(args[n][0].shape[:2] + (D,), args[n][0].dtype) for n in parts]
    specs = [pl.BlockSpec(memory_space=pl.ANY) if n in parts else vmem_spec for n in range(len(args))]
    moved = sum(a.size * a.dtype.itemsize for a in arrays + outs)
    return pl.pallas_call(
        kernel,
        name=getattr(body, "func", body).__name__,
        out_shape=outs,
        in_specs=[smem_spec] + specs,
        out_specs=[vmem_spec] * len(outs),
        scratch_shapes=[pltpu.VMEM(shape, kind) for shape, kind in scratch]
        + buffers
        + [pltpu.SemaphoreType.DMA((max(1, len(parts)),))],
        compiler_params=pltpu.CompilerParams(vmem_limit_bytes=vmem * 1024 * 1024),
        cost_estimate=pl.CostEstimate(flops=us * 1_000_000_000, bytes_accessed=moved, transcendentals=0),
    )(ids, *arrays)


def dot_nn(a, b):
    return lax.dot_general(a, b, (((1,), (0,)), ((), ())), preferred_element_type=wide_t)


def dot_nt(a, b):
    return lax.dot_general(a, b, (((1,), (1,)), ((), ())), preferred_element_type=wide_t)


def dot_tn(a, b):
    return lax.dot_general(a, b, (((0,), (0,)), ((), ())), preferred_element_type=wide_t)


def at16(start, size=16):
    return pl.ds(pl.multiple_of(start, 16), size)


def at128(start, size=128):
    return pl.ds(pl.multiple_of(start, 128), size)


def half_mask(shape, axis, core):
    return (lax.broadcasted_iota(jnp.int32, shape, axis) // HEAD) == core


def attend_rows(q_ref, k_ref, vt_ref, bias_ref, s_ref, ot_ref, lse_ref):
    keys, rows = bias_ref.shape
    tile = min(1024, keys)
    spans = [slice(start, start + tile) for start in range(0, keys, tile)]
    lowest = jnp.full((8, rows), neg_fill, wide_t)
    group = 4

    def step(p, carry):
        def scores(head, here, top):
            pair = at128((p * (group // 2) + head // 2) * PAIR)
            q = q_ref[:, pair]
            own_q = jnp.where(half_mask((rows, PAIR), 1, head % 2), q, jnp.zeros_like(q))
            s = dot_nt(k_ref[here, pair], own_q) + bias_ref[here, :]
            s_ref[head % 2, here, :] = s
            return jnp.maximum(top, jnp.max(s.reshape(tile // 8, 8, rows), axis=0))

        top = lowest
        for here in spans:
            top = scores(0, here, top)
        for head in range(group):
            features = pl.ds(pl.multiple_of((p * group + head) * HEAD, HEAD), HEAD)
            highest = jnp.max(top, axis=0, keepdims=True)
            total = jnp.zeros((8, rows), wide_t)
            mixed = jnp.zeros((HEAD, rows), wide_t)
            top = lowest
            for here in spans:
                if head + 1 < group:
                    top = scores(head + 1, here, top)
                w = jnp.exp(s_ref[head % 2, here, :] - highest)
                total = total + jnp.sum(w.reshape(tile // 8, 8, rows), axis=0)
                mixed = mixed + dot_nn(vt_ref[features, here], w.astype(low_t))
            total = jnp.sum(total, axis=0, keepdims=True)
            ot_ref[features, :] = mixed / total
            lse_ref[pl.ds(p * group + head, 1), :] = highest + jnp.log(total)
        return carry

    lax.fori_loop(0, HEADS // group, step, 0)


def finish_rows(ot_ref, low_out, mixed_out):
    mixed = ot_ref[...].T
    low_out[...] = mixed.astype(low_t)
    mixed_out[...] = mixed


def three_parts(value):
    high = value.astype(low_t).astype(wide_t)
    rest = value - high
    middle = rest.astype(low_t).astype(wide_t)
    return high, middle, rest - middle


def side_rows(lse, grad_low, mixed, row_data):
    product = grad_low.astype(wide_t) * mixed[...]
    lane = lax.broadcasted_iota(jnp.int32, (grad_low.shape[0], PAIR), 1)
    sums = jnp.zeros((grad_low.shape[0], PAIR), wide_t)
    for p in range(PAIRS):
        piece = product[:, p * PAIR : (p + 1) * PAIR]
        for h in range(2):
            mine = half_mask(piece.shape, 1, h)
            offset = jnp.sum(jnp.where(mine, piece, 0.0), axis=1, keepdims=True)
            sums = jnp.where(lane == p * 2 + h, offset, sums)
    offsets = sums.T
    seq = row_data[16:17, :]
    onehot = [(seq == float(n)).astype(wide_t) for n in range(4)]
    sides = []
    for p in range(PAIRS):
        pieces = []
        for h in range(2):
            head = p * 2 + h
            pieces += three_parts(-lse[head : head + 1, :])
            pieces += three_parts(-offsets[head : head + 1, :])
        sides.append(jnp.concatenate(pieces + onehot, axis=0).astype(low_t))
    return sides


def side_lanes(side, core):
    side = side.astype(wide_t)
    head = jnp.where(core == 0, side[0:6], side[6:12])
    gap = jnp.zeros((5, side.shape[1]), wide_t)
    rest = jnp.zeros((HEAD - 20, side.shape[1]), wide_t)
    half = jnp.concatenate((head[0:3], gap, head[3:6], gap, side[12:16], rest), axis=0)
    return jnp.concatenate((half, half), axis=0).T.astype(low_t)


def assemble(ids, parts, column, outs):
    for chip, other, block in parts:
        own = chip * 2 + (ids[1] ^ other)
        for e in range(4):
            rows = at16((ids[2] ^ e) * 128 + own * 16)
            start = column
            for out in outs:
                width = out.shape[1]
                out[rows, :] = block[e * 16 : (e + 1) * 16, start : start + width]
                start += width


def project_pairs(parts, w_pair, k_ref, vt_ref, wvt_ref):
    wvt_ref[...] = w_pair[:, D:].astype(wide_t).T.astype(low_t)
    for n, part in enumerate(parts):
        for k in range(PAIRS):
            rows = part.shape[1]
            start = (n * 4 + k) * rows
            k_ref[start : start + rows, :] = dot_nn(part[k], w_pair[:, :D]).astype(low_t)
            vt_ref[:, start : start + rows] = dot_nt(wvt_ref[...], part[k]).astype(low_t)


def self_forward(ids, hidden, own, other, *refs):
    slices, (cols, row_data), refs = refs[:8], refs[8:10], refs[10:]
    out, mixed, lse, wq, wkv, q_ref, k_ref, vt_ref, wvt_ref, bias_ref, s_ref, ot_ref = refs
    rows = hidden.shape[0]
    parts = [(ids[0] ^ k, n, slices[n * 4 + k]) for n in range(2) for k in range(4)]
    assemble(ids, parts, 0, (wq, wkv))
    q_ref[...] = (dot_nn(hidden[...], wq[...]).astype(low_t) * 0.125).astype(low_t)
    project_pairs((own, other), wkv, k_ref, vt_ref, wvt_ref)
    seq, limit = row_data[16:17, :], row_data[17:18, :]
    for b in range(8):
        seen = (cols[:, b : b + 1] == seq) & (cols[:, 8 + b : 9 + b] < limit)
        bias_ref[b * rows : (b + 1) * rows, :] = jnp.where(seen, 0.0, neg_fill)
    mine = lax.broadcasted_iota(jnp.int32, (rows, rows), 0) == lax.broadcasted_iota(
        jnp.int32, (rows, rows), 1
    )
    block = at128(ids[0] * rows, rows)
    bias_ref[block, :] = jnp.where(mine, 0.0, bias_ref[block, :])
    attend_rows(q_ref, k_ref, vt_ref, bias_ref, s_ref, ot_ref, lse)
    finish_rows(ot_ref, out, mixed)


def layer_norm(values, gain_row, shift_row):
    mean = jnp.mean(values, axis=1, keepdims=True)
    centred = values - mean
    scale = lax.rsqrt(jnp.mean(centred * centred, axis=1, keepdims=True) + layer_eps)
    normed = centred * scale
    return normed * gain_row + shift_row, normed, scale


def layer_norm_back(grad, normed, scale, gain_row):
    gain_term = jnp.sum(grad * normed, axis=0, keepdims=True)
    shift_term = jnp.sum(grad, axis=0, keepdims=True)
    scaled = grad * gain_row
    grad_in = scale * (
        scaled
        - jnp.mean(scaled, axis=1, keepdims=True)
        - normed * jnp.mean(scaled * normed, axis=1, keepdims=True)
    )
    return grad_in, gain_term, shift_term


def head_arrays(ids, k_ref, vt_ref, cols, column, k_all, v_all, kt, turn):
    rows = turn.shape[1]
    core = ids[1]
    mine = half_mask((rows, PAIR), 1, core)
    features = pl.ds(pl.multiple_of(core * HEAD, HEAD), HEAD)
    lane = lax.broadcasted_iota(jnp.int32, (rows, PAIR), 1) % HEAD
    ones_v = jnp.where((lane >= 8) & (lane < 11), 1.0, 0.0).astype(low_t)
    pair = at128(ids[0] * PAIR)
    for b in range(8):
        here = slice(b * rows, (b + 1) * rows)
        seq = cols[:, column + b : column + b + 1].astype(jnp.int32)
        other_seq = (lane >= 16) & (lane < 20) & (lane != seq + 16)
        ones_k = jnp.where(other_seq, neg_fill, jnp.where(lane < 3, 1.0, 0.0)).astype(low_t)
        key = k_ref[here, pair]
        k_all[here, :] = jnp.where(mine, key, ones_k)
        turn[...] = key.astype(wide_t).T
        kt[:, here] = turn[features, :].astype(low_t)
        v_all[here, :] = jnp.where(mine, turned(vt_ref[pair, here]), ones_v)


def cross_forward(ids, hidden, self_low, own, other, *refs):
    slices, (cols, row_data) = refs[:2], refs[2:4]
    first, normed, scale_out, first_low, cross_low, mixed, lse, cross_q = refs[4:12]
    wo, wcq, wckv, wco, gs, k_all, v_all, kt = refs[12:20]
    q_ref, k_ref, vt_ref, wvt_ref, bias_ref, s_ref, ot_ref, turn = refs[20:]
    for n in range(2):
        for e in range(4):
            rows = at16(e * 128 + (ids[1] ^ n) * 64, 64)
            start = 0
            for out in (wo, wcq, wckv, wco):
                width = out.shape[1]
                out[rows, :] = slices[n][e, :, start : start + width]
                start += width
    for e in range(4):
        gs[:, e * 128 : (e + 1) * 128] = slices[0][e, :16, 5 * D :]
    gain, shift = gs[0:1, :].astype(wide_t), gs[3:4, :].astype(wide_t)
    value, n0, s0 = layer_norm(
        hidden[...].astype(wide_t) + dot_nn(self_low[...], wo[...]), gain, shift
    )
    first[...] = value
    normed[...] = n0
    scale_out[...] = jnp.broadcast_to(s0, scale_out.shape)
    low = value.astype(low_t)
    first_low[...] = low
    q = dot_nn(low, wcq[...]).astype(low_t)
    cross_q[...] = q
    q_ref[...] = (q * 0.125).astype(low_t)
    rows = hidden.shape[0]
    project_pairs((own, other), wckv, k_ref, vt_ref, wvt_ref)
    for b in range(8):
        seen = cols[:, 16 + b : 17 + b] == row_data[16:17, :]
        bias_ref[b * rows : (b + 1) * rows, :] = jnp.where(seen, 0.0, neg_fill)
    attend_rows(q_ref, k_ref, vt_ref, bias_ref, s_ref, ot_ref, lse)
    finish_rows(ot_ref, cross_low, mixed)
    head_arrays(ids, k_ref, vt_ref, cols, 16, k_all, v_all, kt, turn)


def feed_forward(ids, first, cross_low, cross_mixed, lse, row_data, cross_q, wco, gs, cotangent, *refs):
    slices = refs[0:8]
    result, dealt, second_grad, keep, send, sums, slope, wins, wouts = refs[8:]
    half_ff = FF // 2
    for n in range(2):
        for k in range(4):
            chip, core, part = ids[0] ^ k, ids[1] ^ n, slices[n * 4 + k]
            for e in range(4):
                w, here = ids[2] ^ e, slice(e * 16, (e + 1) * 16)
                rows = at16(w * 128 + (chip * 2 + core) * 16)
                for g in range(4):
                    row = w * 256 + ((chip % 2) * 2 + core) * 64 + g * 16
                    wouts[(chip // 2) ^ ids[1], at16(row), :] = part[here, FF + g * D : FF + (g + 1) * D]
                    for h in range(2):
                        column = g * 512 + h * 256
                        wins[h ^ ids[1], rows, g * 256 : (g + 1) * 256] = part[here, column : column + 256]
    gains, shifts = gs[0:3, :].astype(wide_t), gs[3:6, :].astype(wide_t)
    second, n1, s1 = layer_norm(
        first[...] + dot_nn(cross_low[...], wco[...]), gains[1:2], shifts[1:2]
    )
    low = second.astype(low_t)
    for out in (keep, send):
        out[:, 2 * half_ff : 2 * half_ff + D] = low
        out[:, 2 * half_ff + 2 * D : 2 * half_ff + 3 * D] = cross_low[...]
    width = 512
    chunks = [(n, c) for n in range(2) for c in range(FF // 2 // width)]
    total = second
    for n, c in chunks:
        here = slice(c * width, (c + 1) * width)
        wide = slice(n * half_ff + c * width, n * half_ff + (c + 1) * width)
        pre = dot_nn(low, wins[n, :, here])
        sig = 1.0 / (1.0 + jnp.exp(-pre))
        act = (pre * sig).astype(low_t)
        (keep, send)[n][:, half_ff + c * width : half_ff + (c + 1) * width] = act
        slope[:, wide] = sig * (1.0 + pre * (1.0 - sig))
        total = total + dot_nn(act, wouts[n, here, :])
    value, n2, s2 = layer_norm(total, gains[2:3], shifts[2:3])
    result[...] = value.astype(low_t)
    third, gain_c, shift_c = layer_norm_back(cotangent[...].astype(wide_t), n2, s2, gains[2:3])
    third_low = third.astype(low_t)
    for out in (keep, send):
        out[:, 2 * half_ff + D : 2 * half_ff + 2 * D] = third_low
    total = third
    for n, c in chunks:
        here = slice(c * width, (c + 1) * width)
        wide = slice(n * half_ff + c * width, n * half_ff + (c + 1) * width)
        back = (dot_nt(third_low, wouts[n, here, :]) * slope[:, wide]).astype(low_t)
        (keep, send)[n][:, here] = back
        total = total + dot_nt(back, wins[n, :, here])
    grad, gain_b, shift_b = layer_norm_back(total, n1, s1, gains[1:2])
    second_grad[...] = grad
    grad_low = grad.astype(low_t)
    for out, core in ((keep, ids[1]), (send, 1 - ids[1])):
        half = grad_low[:, : D // 2]
        out[:, 2 * half_ff + 3 * D :] = jnp.where(core == 0, half, grad_low[:, D // 2 :])
    mixed = dot_nt(grad_low, wco[...]).astype(low_t)
    rows = grad_low.shape[0]
    sides = side_rows(lse, mixed, cross_mixed, row_data)
    for p in range(PAIRS):
        dealt[p, :rows, :PAIR] = cross_q[:, p * PAIR : (p + 1) * PAIR]
        dealt[p, :rows, PAIR:] = mixed[:, p * PAIR : (p + 1) * PAIR]
        dealt[p, rows:, :] = sides[p]
    zero = jnp.zeros_like(gain_b)
    sums[...] = jnp.concatenate((zero, gain_b, gain_c, zero, shift_b, shift_c, zero, zero), axis=0)


def grads_a(ids, keep, received, out, g_in, g_out, g_cross):
    half = FF // 2

    def both(left, right):
        return (dot_tn(keep[:, left], keep[:, right]) + dot_tn(received[:, left], received[:, right])).astype(low_t)

    at = [0, half] + [2 * half + n * D for n in range(4)]
    pre, act = slice(at[0], at[1]), slice(at[1], at[2])
    second, branch, low = (slice(at[n], at[n] + D) for n in (2, 3, 4))
    g_in[...] = both(second, pre)
    g_out[...] = both(act, branch)
    g_cross[...] = both(low, slice(at[5], at[5] + D // 2))
    for chip in range(4):
        for e in range(4):
            w, here = ids[2] ^ e, slice(e * 32, (e + 1) * 32)
            rows = at16(w * 128 + chip * 32, 32)
            out[chip, here, :half] = g_in[rows, :]
            for g in range(2):
                out[chip, here, half + g * D : half + (g + 1) * D] = g_out[
                    at16(w * 256 + chip * 64 + g * 32, 32), :
                ]
            out[chip, here, half + 2 * D :] = g_cross[rows, :]


def grads_b(ids, first_low, cross_dq, self_low, branch, sums, dkv, out, g_query, g_output):
    g_query[...] = dot_tn(first_low[...], cross_dq[...]).astype(low_t)
    g_output[...] = dot_tn(self_low[...], branch[...]).astype(low_t)
    row = jnp.concatenate((sums[...], jnp.zeros_like(sums[...])), axis=0).astype(low_t)
    rows = dkv.shape[2]
    for e in range(4):
        w, here = ids[2] ^ e, slice(e * 16, (e + 1) * 16)
        piece = row[:, :128]
        for k in range(1, 4):
            piece = jnp.where(w == k, row[:, k * 128 : (k + 1) * 128], piece)
        for device in range(8):
            own = at16(w * 128 + device * 16)
            out[device, here, :D] = g_query[own, :]
            out[device, here, D : 2 * D] = g_output[own, :]
            out[device, here, 2 * D : 2 * D + 128] = piece
    for device in range(8):
        for n in range(2):
            start = 2 * D + 128 + n * rows
            out[device, :, start : start + rows] = dkv[device, n * HEAD : (n + 1) * HEAD, :]


def pair_setup(is_self, ids, own, other, w_pair, cols, *refs):
    k_all, v_all, kt, turn = refs
    chip, core = ids[0], ids[1]
    rows = own.shape[1]
    mine = half_mask((rows, PAIR), 1, core)
    features = pl.ds(pl.multiple_of(core * HEAD, HEAD), HEAD)
    lane = lax.broadcasted_iota(jnp.int32, (rows, PAIR), 1) % HEAD
    ones_v = jnp.where((lane >= 8) & (lane < 11), 1.0, 0.0).astype(low_t)
    pair = at128(chip * PAIR)
    wk, wv = w_pair[:, pair], w_pair[:, at128(D + chip * PAIR)]
    for n, part in enumerate((own, other)):
        for k in range(4):
            b = n * 4 + k
            here = slice(b * rows, (b + 1) * rows)
            column = b if is_self else 16 + b
            seq = cols[:, column : column + 1].astype(jnp.int32)
            other_seq = (lane >= 16) & (lane < 20) & (lane != seq + 16)
            ones_k = jnp.where(other_seq, neg_fill, jnp.where(lane < 3, 1.0, 0.0)).astype(low_t)
            key = dot_nn(part[k], wk)
            turn[...] = key.T
            kt[:, here] = turn[features, :].astype(low_t)
            k_all[here, :] = jnp.where(mine, key.astype(low_t), ones_k)
            v_all[here, :] = jnp.where(mine, dot_nn(part[k], wv).astype(low_t), ones_v)


def pair_queries(ids, own, other, w_query, q_all):
    wq = w_query[:, at128(ids[0] * PAIR)]
    for n, part in enumerate((own, other)):
        for k in range(4):
            q_all[n * 4 + k] = dot_nn(part[k], wq).astype(low_t)


def pair_back(is_self, ids, *refs):
    if is_self:
        q_parts, do_own, do_other, k_all, v_all, kt, cols, row_data, back = refs[:9]
        do_parts = (do_own, do_other)
    else:
        both_own, both_other, k_all, v_all, kt, dq_keep, dq_send, dkv = refs[:8]
        both_parts = (both_own, both_other)
    q_all, do_all, dq_t, dk, dv, rank, turn = refs[-7:]
    core = ids[1]
    rows = q_all.shape[1]
    keys = 8 * rows
    mine = half_mask((rows, PAIR), 1, core)
    features = pl.ds(pl.multiple_of(core * HEAD, HEAD), HEAD)
    for n in range(2):
        for k in range(4):
            b = n * 4 + k
            if is_self:
                here = slice(b * rows, (b + 1) * rows)
                rank[here, :] = jnp.broadcast_to(cols[:, 8 + b : 9 + b], (rows, 128))
                q, do = q_parts[b], do_parts[n][k, :rows, :]
                side = jnp.concatenate(
                    (do_parts[n][k, rows : rows + 16, :], do_parts[n][k, rows + 16 :, :]), axis=1
                )
            else:
                q, do = both_parts[n][k, :rows, :PAIR], both_parts[n][k, :rows, PAIR:]
                side = both_parts[n][k, rows:, :]
            side = side_lanes(side, core)
            q_all[b] = jnp.where(mine, (q * 0.125).astype(low_t), side)
            do_all[b] = jnp.where(mine, do, side)
    dk[...] = jnp.zeros_like(dk)
    dv[...] = jnp.zeros_like(dv)
    tile = min(512 if is_self else 1024, keys)
    blocks = 1 if is_self else 2

    def step(step, carry):
        b, wide = step * blocks, blocks * rows
        q, do = (ref[pl.ds(b, blocks)].reshape(wide, PAIR) for ref in (q_all, do_all))
        dqt = jnp.zeros((HEAD, wide), wide_t)
        for t in range(keys // tile):
            here = slice(t * tile, (t + 1) * tile)
            if is_self:
                start = (b * rows // tile + t) % (keys // tile) * tile
                here = at128(start, tile)
            w = jnp.exp(dot_nt(k_all[here, :], q))
            if is_self:
                ranks = jnp.concatenate((rank[here, :],) * (wide // 128), axis=1)
                seen = ranks < row_data[pl.ds(8 + b, 1), :]
                if t == 0:
                    index = lax.broadcasted_iota(jnp.int32, (tile, wide), 0)
                    own = lax.broadcasted_iota(jnp.int32, (tile, wide), 1) + (b * rows - start)
                    seen = seen | (index == own)
                w = jnp.where(seen, w, 0.0)
            ds = (w * dot_nt(v_all[here, :], do)).astype(low_t)
            dv[here, :] += dot_nn(w.astype(low_t), do)
            dk[here, :] += dot_nn(ds, q)
            dqt = dqt + dot_nn(kt[:, here], ds)
        dqt = (dqt * 0.125).astype(low_t)
        for n in range(blocks):
            dq_t[b + n] = dqt[:, n * rows : (n + 1) * rows]
        return carry

    lax.fori_loop(0, 8 // blocks, step, 0)
    for n in range(2):
        for k in range(4):
            b = n * 4 + k
            device = k * 2 + (core ^ n)
            here = slice(b * rows, (b + 1) * rows)
            if is_self:
                back[device, :HEAD, :] = dq_t[b]
            else:
                (dq_keep, dq_send)[n][k] = dq_t[b]
            out, start = (back, HEAD) if is_self else (dkv, 0)
            for value in (dk, dv):
                turn[...] = value[here, :].T
                out[device, start : start + HEAD, :] = turn[features, :].astype(low_t)
                start += HEAD


def head_grads(grads, own, other, core, hidden=None):
    first = HEAD if hidden else 0
    total = jnp.zeros((2 * HEAD, D), wide_t)
    total_q = jnp.zeros((HEAD, D), wide_t)
    for n, part in enumerate((own, other)):
        for k in range(4):
            device = k * 2 + (core ^ n)
            total += dot_nn(grads[device, first:, :], part[k])
            if hidden:
                total_q += dot_nn(grads[device, :HEAD, :], hidden[n][k])
    return total, total_q


def pair_grads(ids, grads, own, other, dw):
    total, unused = head_grads(grads, own, other, ids[1])
    for w in range(4):
        dw[w] = total[:, w * 128 : (w + 1) * 128].astype(low_t)


def turned(value):
    return value.astype(wide_t).T.astype(low_t)


def pair_up(ids, keep, received, *outs):
    for k in range(4):
        p = ids[0] ^ k
        outs[k][at16(ids[1] * HEAD, HEAD), :] = keep[p]
        outs[k][at16((1 - ids[1]) * HEAD, HEAD), :] = received[p]


def first_back(ids, *refs):
    parts = refs[:4]
    second_grad, normed, scale, self_mixed, lse, row_data, gs, wcq, wo, sums_in = refs[4:14]
    first_grad, branch, dealt, dq, sums, all_t = refs[14:]
    for k in range(4):
        all_t[at128((ids[0] ^ k) * PAIR), :] = parts[k][...]
    dq[...] = turned(all_t[...])
    total = second_grad[...] + dot_nt(dq[...], wcq[...])
    grad, gain_a, shift_a = layer_norm_back(
        total, normed[...], scale[:, 0:1], gs[0:1, :].astype(wide_t)
    )
    first_grad[...] = grad
    low = grad.astype(low_t)
    branch[...] = low
    mixed = dot_nt(low, wo[...]).astype(low_t)
    rows = low.shape[0]
    sides = side_rows(lse, mixed, self_mixed, row_data)
    for p in range(PAIRS):
        dealt[p, :rows, :] = mixed[:, p * PAIR : (p + 1) * PAIR]
        dealt[p, rows : rows + 16, :] = sides[p][:, :PAIR]
        dealt[p, rows + 16 :, :] = sides[p][:, PAIR:]
    zero = jnp.zeros_like(gain_a)
    sums[...] = sums_in[...] + jnp.concatenate(
        (gain_a, zero, zero, shift_a, zero, zero, zero, zero), axis=0
    )


def source_back(ids, parts, wckv, out, dkv):
    rows = out.shape[0]
    for device in range(8):
        for n in range(2):
            start = 2 * D + 128 + n * rows
            dkv[n * D + device * HEAD : n * D + (device + 1) * HEAD, :] = parts[
                device, :, start : start + rows
            ]
    out[...] = dot_nt(turned(dkv[...]), wckv[...])


def hidden_back(ids, back, first_grad, wq, wkv, hidden_grad, stream_grad, all_t):
    for device in range(8):
        for n in range(3):
            all_t[n * D + device * HEAD : n * D + (device + 1) * HEAD, :] = back[
                device, n * HEAD : (n + 1) * HEAD, :
            ]
    hidden_grad[...] = first_grad[...] + dot_nt(turned(all_t[:D, :]), wq[...])
    stream_grad[...] = dot_nt(turned(all_t[D:, :]), wkv[...])


def add_parts(parts, rows, columns):
    total = parts[0, rows, columns].astype(wide_t)
    for n in range(1, parts.shape[0]):
        total = total + parts[n, rows, columns].astype(wide_t)
    return total.astype(low_t)


def add_chips(ids, parts, dw, *outs):
    width = parts.shape[2]
    for e in range(4):
        outs[e][:, :width] = add_parts(parts, slice(e * 32, (e + 1) * 32), slice(None))
        piece = dw[ids[2] ^ e]
        for g in range(4):
            outs[e][:, width + g * 128 : width + (g + 1) * 128] = piece[g * 32 : (g + 1) * 32, :]


def self_grads(ids, grads, own, other, hidden_own, hidden_other, dw):
    total, total_q = head_grads(grads, own, other, ids[1], (hidden_own, hidden_other))
    for w in range(4):
        columns = slice(w * 128, (w + 1) * 128)
        dw[w, :HEAD, :] = total_q[:, columns].astype(low_t)
        dw[w, HEAD:, :] = total[:, columns].astype(low_t)


def end_sums(ids, parts, dw, *outs):
    width = 2 * D + 128
    for e in range(4):
        outs[e][:, :width] = add_parts(parts, slice(e * 16, (e + 1) * 16), slice(0, width))
        outs[e][:, width : width + 128] = jnp.zeros((16, 128), low_t)
        piece = dw[ids[2] ^ e]
        for g in range(12):
            start = width + 128 + g * 128
            outs[e][:, start : start + 128] = piece[g * 16 : (g + 1) * 16, :]


def add_shards(ids, *refs):
    out = refs[8]

    def total(parts):
        value = parts[0][...].astype(wide_t)
        for part in parts[1:]:
            value = value + part[...].astype(wide_t)
        return value.astype(low_t)

    first, last = total(refs[:4]), total(refs[4:8])
    width, half = first.shape[1], last.shape[1] // 2
    out[:, :width] = first
    out[:16, width:] = last[:, :half]
    out[16:, width:] = last[:, half:]


def place_all(ids, *refs):
    parts, refs = refs[:8], refs[8:]
    g_in, g_out, g_cross, g_cross_pair, g_cross_query, g_output, gains, shifts, g_query, g_pair = refs[:10]
    pair_t, all_t = refs[10:]
    half = FF // 2
    start_cross = half + 2 * D
    start_pair = start_cross + D // 2
    start_end = start_pair + 4 * 128
    half_end = parts[0].shape[1] - start_end
    for n in range(2):
        core = ids[1] ^ n
        for step in range(4):
            chip, part = ids[0] ^ step, parts[n * 4 + step]
            rows = at16(chip * 32, 32)
            device = chip * 2 + core
            for k in range(4):
                g_in[rows, at128(k * 512 + core * 256, 256)] = part[
                    :, k * 256 : (k + 1) * 256
                ].astype(wide_t)
            for g in range(2):
                g_out[at16(core * 256 + chip * 64 + g * 32, 32), :] = part[
                    :, half + g * D : half + (g + 1) * D
                ].astype(wide_t)
            g_cross[rows, at128(core * 256, 256)] = part[:, start_cross:start_pair].astype(wide_t)
            for g in range(4):
                column = start_pair + g * 128
                row = (g // 2) * D + device * HEAD + (g % 2) * 32
                pair_t[at16(row, 32), :] = part[:, column : column + 128].astype(wide_t)

            def piece(column, width):
                row, at = (0, column) if column < half_end else (16, column - half_end)
                return part[row : row + 16, start_end + at : start_end + at + width].astype(wide_t)

            own_rows = at16(device * 16)
            for column in range(0, D, 128):
                g_cross_query[own_rows, column : column + 128] = piece(column, 128)
                g_output[own_rows, column : column + 128] = piece(D + column, 128)
            if n == 0 and step == 0:
                norms = piece(2 * D, 128)
                gains[...], shifts[...] = norms[0:3], norms[3:6]
            for g in range(12):
                row = (g // 4) * D + device * HEAD + (g % 4) * 16
                all_t[at16(row), :] = piece(2 * D + 256 + g * 128, 128)
    g_cross_pair[...] = pair_t[...].T
    g_query[...] = all_t[:D, :].T
    g_pair[...] = all_t[D:, :].T


def pack_rows(ids, stream, source, many):
    for k in range(4):
        many[k, :, :D] = stream[...]
        many[k, :, D:] = source[...]


def pack_start(ids, wq, wkv, ffn_in, ffn_out, pack):
    own = ids[0] * 2 + ids[1]
    for k in range(4):
        start = 3 * D + FF + k * D
        pack[:, start : start + D] = ffn_out[at16(own * 64 + k * 16), :]
    pack[:, :D] = wq[at16(own * 16), :]
    pack[:, D : 3 * D] = wkv[at16(own * 16), :]
    pack[:, 3 * D : 3 * D + FF] = ffn_in[at16(own * 16), :]


def pack_more(ids, *refs):
    weights, gain, shift, rows_in, pack, many = refs[:4], *refs[4:]
    rows = at16(ids[1] * 64, 64)
    norms = (gain[...].astype(wide_t), shift[...].astype(wide_t), jnp.zeros((58, 128), wide_t))
    norms = jnp.concatenate(norms, axis=0).astype(low_t)
    for k in range(4):
        start = 0
        for w in weights:
            pack[k, :, start : start + w.shape[1]] = w[rows, :]
            start += w.shape[1]
        pack[k, :, start:] = norms
        many[k] = rows_in[...]


def mask_data(ids, order, ranks, limits, cols, row_data, all_rows):
    rows = cols.shape[0]
    ends = [ids[3]]
    for n in range(1, 4):
        ends.append(ends[-1] + ids[3 + n])

    def sequence(position):
        return sum((position >= end).astype(wide_t) for end in ends)

    for n in range(2):
        for k in range(4):
            b = n * 4 + k
            device = k * 2 + (ids[1] ^ n)
            here = at128(device * rows, rows)
            index = lax.broadcasted_iota(jnp.int32, (1, rows), 1) + device * rows
            all_rows[b : b + 1, :] = sequence(order[:, here])
            all_rows[8 + b : 9 + b, :] = ranks[:, here].astype(wide_t)
            all_rows[16 + b : 17 + b, :] = sequence(index)
            row_data[8 + b : 9 + b, :] = limits[:, here].astype(wide_t)
    row_data[0:8, :] = all_rows[0:8, :]
    all_rows[24:32, :] = jnp.zeros((8, rows), wide_t)
    all_rows[24:25, :] = all_rows[pl.ds(ids[0], 1), :]
    row_data[16:24, :] = jnp.zeros((8, rows), wide_t)
    row_data[16:17, :] = all_rows[pl.ds(ids[0], 1), :]
    row_data[17:18, :] = row_data[pl.ds(8 + ids[0], 1), :]
    cols[:, :32] = all_rows[...].T


def pack_first(ids, *refs):
    parts, (one, two) = refs[:4], refs[4:]
    width = one.shape[1]
    for e in range(4):
        here = slice(e * 16, (e + 1) * 16)
        one[here, :] = parts[e][:, :width]
        two[here, :] = parts[e][:, width:]


def core_swap(value):
    return lax.ppermute(value, "core", [(0, 1), (1, 0)])


def chip_swaps(parts):
    moves = [[(i, i ^ k) for i in range(4)] for k in range(4)]
    return [parts[0]] + [lax.ppermute(parts[k], "chip", moves[k]) for k in range(1, 4)]


def shard_swaps(parts):
    moves = [[(i, i ^ k) for i in range(4)] for k in range(4)]
    return [parts[0]] + [lax.ppermute(parts[k], "wa", moves[k]) for k in range(1, 4)]


def deal(value):
    return lax.all_to_all(value, "chip", 0, 0, tiled=True)


def deal_all(value):
    return lax.all_to_all(value, ("chip", "core"), 0, 0, tiled=True)


def deal_both(value):
    own = deal(value)
    return own, core_swap(own)


def after(value, *others):
    return lax.optimization_barrier((value,) + others)[0]


def fast_shards(
    hidden,
    stream,
    encoder,
    lengths,
    order,
    ranks,
    thresholds,
    self_query,
    self_key_value,
    self_output,
    cross_query,
    cross_key_value,
    cross_output,
    ffn_in,
    ffn_out,
    norm_gain,
    norm_shift,
    cotangent,
):
    rows, keys = hidden.shape[1], order.shape[1]
    chip, core, mw = lax.axis_index("chip"), lax.axis_index("core"), lax.axis_index("wa")
    ids = jnp.stack((chip, core, mw)).astype(jnp.int32)
    inputs = hidden[0]

    (many,) = run(pack_rows, [((4, rows, 2 * D), low_t)], ids, [stream[0], encoder[0]])
    (pack1,) = run(
        pack_start,
        [((16, 3 * D + 2 * FF), low_t)],
        ids,
        [after(self_query, many), self_key_value, ffn_in, ffn_out],
    )
    x_own = deal(many)
    shards1 = shard_swaps([pack1] * 4)
    copies2, hidden_copies = run(
        pack_more,
        [((4, 64, 5 * D + 128), low_t), ((4, rows, D), low_t)],
        ids,
        [after(self_output, pack1), cross_query, cross_key_value, cross_output, norm_gain, norm_shift]
        + [inputs],
    )
    cols, row_data = run(
        mask_data,
        [((rows, 32), wide_t), ((24, rows), wide_t)],
        jnp.concatenate((after(ids, pack1), lengths[0])),
        [order, ranks, thresholds],
        [((32, rows), wide_t)],
    )
    part1, part3 = run(
        pack_first,
        [((64, 3 * D), low_t), ((64, 2 * FF), low_t)],
        ids,
        [after(shards1[0], x_own, cols, copies2)] + shards1[1:],
    )
    slices1 = chip_swaps([part1] * 4)
    slices1 = slices1 + [core_swap(part) for part in slices1]
    shards2 = lax.all_to_all(after(copies2, x_own), "wa", 0, 0, tiled=True)
    x_other = core_swap(after(x_own, part1))
    slices3 = chip_swaps([after(part3, slices1[1])] * 4)
    stream_own, stream_other = (x_own, 0), (x_other, 0)
    source_own, source_other = (x_own, 1), (x_other, 1)

    attend_scratch = [
        ((rows, D), low_t),
        ((keys, D), low_t),
        ((D, keys), low_t),
        ((D, D), low_t),
        ((keys, rows), wide_t),
        ((2, keys, rows), wide_t),
        ((D, rows), wide_t),
    ]
    self_low, self_mixed, self_lse, wq, wkv = run(
        self_forward,
        [((rows, D), low_t), ((rows, D), wide_t), ((HEADS, rows), wide_t)]
        + [((D, D), low_t), ((D, 2 * D), low_t)],
        ids,
        [inputs, stream_own, stream_other, *slices1, cols, row_data],
        attend_scratch,
        us=15,
    )
    head_shapes = [((keys, PAIR), low_t)] * 2 + [((HEAD, keys), low_t)]
    self_head = run(
        functools.partial(pair_setup, True),
        head_shapes,
        ids,
        [stream_own, stream_other, wkv, after(cols, self_low)],
        [((PAIR, rows), wide_t)],
        us=4,
    )
    slices3 = slices3 + [core_swap(after(part, self_head[0])) for part in slices3]
    shards2_other = core_swap(after(shards2, self_head[0], *slices3[:4]))
    hidden_own = deal(after(hidden_copies, shards2, self_head[0], *slices3[:4]))
    (
        first,
        normed,
        scale,
        first_low,
        cross_low,
        cross_mixed,
        cross_lse,
        cross_q,
        wo,
        wcq,
        wckv,
        wco,
        gs,
        *cross_head,
    ) = run(
        cross_forward,
        [((rows, D), wide_t)] * 2
        + [((rows, 128), wide_t)]
        + [((rows, D), low_t)] * 2
        + [((rows, D), wide_t), ((HEADS, rows), wide_t), ((rows, D), low_t)]
        + [((D, D), low_t), ((D, D), low_t), ((D, 2 * D), low_t), ((D, D), low_t), ((16, D), low_t)]
        + head_shapes,
        ids,
        [inputs, after(self_low, self_head[0]), source_own, source_other, shards2, shards2_other]
        + [cols, row_data],
        attend_scratch + [((PAIR, rows), wide_t)],
        us=15,
    )
    hidden_other = core_swap(after(hidden_own, cross_low))
    width_s = 2 * FF // 2 + 3 * D + D // 2
    result, cross_dealt, second_grad, keep_a, send_a, sums = run(
        feed_forward,
        [
            ((rows, D), low_t),
            ((PAIRS, rows + 16, 2 * PAIR), low_t),
            ((rows, D), wide_t),
            ((rows, width_s), low_t),
            ((rows, width_s), low_t),
            ((8, D), wide_t),
        ],
        ids,
        [after(first, hidden_own), cross_low, cross_mixed, cross_lse, row_data, cross_q, wco, gs]
        + [cotangent[0], *slices3],
        [((rows, FF), wide_t), ((2, D, FF // 2), low_t), ((2, FF // 2, D), low_t)],
        us=8,
    )
    both_own = deal(cross_dealt)
    width_a = FF // 2 + 2 * D + D // 2
    (dealt_a,) = run(
        grads_a,
        [((4, 128, width_a), low_t)],
        ids,
        [keep_a, core_swap(send_a)],
        [((D, FF // 2), low_t), ((FF // 2, D), low_t), ((D, D // 2), low_t)],
        us=6,
    )
    rows_a = deal(after(dealt_a, both_own))
    both_other = core_swap(after(both_own, dealt_a))

    back_scratch = (
        [((8, rows, PAIR), low_t)] * 2
        + [((8, HEAD, rows), low_t)]
        + [((keys, PAIR), wide_t)] * 3
        + [((PAIR, rows), wide_t)]
    )
    cq_keep, cq_send, cross_dkv = run(
        functools.partial(pair_back, False),
        [((4, HEAD, rows), low_t)] * 2 + [((8, 2 * HEAD, rows), low_t)],
        ids,
        [after(both_own, dealt_a), both_other, *cross_head],
        back_scratch,
        us=16,
    )
    pairs = run(pair_up, [((PAIR, rows), low_t)] * 4, ids, [cq_keep, core_swap(cq_send)])
    cross_back = chip_swaps(pairs)
    (self_queries,) = run(
        pair_queries,
        [((8, rows, PAIR), low_t)],
        ids,
        [hidden_own, hidden_other, after(wq, pairs[0])],
    )
    (cross_dw,) = run(
        pair_grads,
        [((4, 2 * HEAD, 128), low_t)],
        ids,
        [after(cross_dkv, pairs[0]), source_own, source_other],
    )
    first_grad, self_branch, self_dealt, cross_dq, sums = run(
        first_back,
        [
            ((rows, D), wide_t),
            ((rows, D), low_t),
            ((PAIRS, rows + 32, PAIR), low_t),
            ((rows, D), low_t),
            ((8, D), wide_t),
        ],
        ids,
        [after(cross_back[0], cross_dw, self_queries), *cross_back[1:], second_grad, normed, scale, self_mixed, self_lse, row_data, gs, wcq, wo, sums],
        [((D, rows), low_t)],
        us=4,
    )
    do_own = deal(after(self_dealt, rows_a))
    shards_a = run(
        add_chips,
        [((32, width_a + 512), low_t)] * 4,
        ids,
        [after(rows_a, first_grad), cross_dw],
    )
    moved_a = shard_swaps([after(part, do_own) for part in shards_a])
    (dealt_b,) = run(
        grads_b,
        [((8, 64, 2 * D + 128 + 2 * rows), low_t)],
        ids,
        [first_low, cross_dq, self_low, self_branch, sums, cross_dkv],
        [((D, D), low_t)] * 2,
        us=3,
    )
    rows_b = deal_all(after(dealt_b, do_own))
    do_other = core_swap(after(do_own, dealt_b, *shards_a))
    (self_back_t,) = run(
        functools.partial(pair_back, True),
        [((8, 3 * HEAD, rows), low_t)],
        ids,
        [self_queries, after(do_own, dealt_b, *shards_a), do_other, *self_head, cols, row_data],
        back_scratch,
        us=16,
    )
    end_width = 2 * D + 2 * 128 + 12 * 128
    (self_dw,) = run(
        self_grads,
        [((4, 3 * HEAD, 128), low_t)],
        ids,
        [self_back_t, stream_own, stream_other, hidden_own, hidden_other],
    )
    end_parts = run(
        end_sums, [((16, end_width), low_t)] * 4, ids, [after(rows_b, self_dw), self_dw]
    )
    moved_end = shard_swaps(end_parts)
    self_back = deal_all(after(self_back_t, end_parts[0], *moved_a))
    (source_grad,) = run(
        source_back,
        [((rows, D), wide_t)],
        ids,
        [rows_b, after(wckv, end_parts[0])],
        [((2 * D, rows), low_t)],
        us=3,
    )
    (sums_end,) = run(
        add_shards,
        [((32, width_a + 512 + end_width // 2), low_t)],
        ids,
        [*moved_a, after(moved_end[0], source_grad), *moved_end[1:]],
    )
    all_parts = chip_swaps([sums_end] * 4)
    hidden_grad, stream_grad = run(
        hidden_back,
        [((rows, D), wide_t)] * 2,
        ids,
        [self_back, first_grad, wq, wkv],
        [((3 * D, rows), low_t)],
        us=3,
    )
    all_parts = all_parts + [core_swap(after(part, hidden_grad)) for part in all_parts]
    (
        grad_in,
        grad_out,
        grad_cross_output,
        grad_cross_pair,
        grad_cross_query,
        grad_output,
        gain_grads,
        shift_grads,
        grad_query,
        grad_pair,
    ) = run(
        place_all,
        [((128, FF), wide_t), ((D, D), wide_t), ((128, D), wide_t), ((128, 2 * D), wide_t)]
        + [((128, D), wide_t)] * 2
        + [((3, 128), wide_t)] * 2
        + [((128, D), wide_t), ((128, 2 * D), wide_t)],
        ids,
        all_parts,
        [((2 * D, 128), wide_t), ((3 * D, 128), wide_t)],
    )
    return (
        result[None],
        hidden_grad[None],
        stream_grad[None],
        source_grad[None],
        grad_query,
        grad_pair,
        grad_output,
        grad_cross_query,
        grad_cross_pair,
        grad_cross_output,
        grad_in,
        grad_out,
        gain_grads,
        shift_grads,
    )


def solution(mesh):
    in_specs = (
        P("wa", "ctx", None),
        P("wa", "ctx", None),
        P("wa", "ctx", None),
        P("wa", None),
        P("wa", None),
        P("wa", None),
        P("wa", None),
        P("wa", None),
        P("wa", None),
        P("wa", None),
        P("wa", None),
        P("wa", None),
        P("wa", None),
        P("wa", None),
        P("wa", None),
        P(None, "wa"),
        P(None, "wa"),
        P("wa", "ctx", None),
    )
    out_specs = (
        P("wa", "ctx", None),
        P("wa", "ctx", None),
        P("wa", "ctx", None),
        P("wa", "ctx", None),
        P("wa", None),
        P("wa", None),
        P("wa", None),
        P("wa", None),
        P("wa", None),
        P("wa", None),
        P("wa", None),
        P("wa", None),
        P(None, "wa"),
        P(None, "wa"),
    )
    if mesh.axis_names != ("ctx", "wa") or mesh.shape["ctx"] != HEADS or mesh.shape["wa"] != 4:
        return jax.shard_map(
            general_shards, mesh=mesh, in_specs=in_specs, out_specs=out_specs, check_vma=False
        )

    def finer(spec):
        return P(*(("chip", "core") if axis == "ctx" else axis for axis in spec))

    return jax.shard_map(
        fast_shards,
        mesh=Mesh(mesh.devices.reshape(4, 2, 4), ("chip", "core", "wa")),
        in_specs=tuple(finer(spec) for spec in in_specs),
        out_specs=tuple(finer(spec) for spec in out_specs),
        check_vma=False,
    )
```

```python
import functools

import jax
import jax.numpy as jnp
from jax import lax
from jax.experimental import pallas as pl
from jax.experimental.pallas import tpu as pltpu
from jax.sharding import Mesh
from jax.sharding import PartitionSpec as P

D = 512
HEADS = 8
HEAD = 64
KEYBLK = 1024


layer_eps = 1e-05
neg_fill = -1e30


def sequence_ids(positions, seq_ends):
    return jnp.sum((positions[:, None] >= seq_ends[None, :]).astype(jnp.int32), axis=1)


def head_split(matrix):
    return matrix.reshape(matrix.shape[0], HEADS, HEAD)


def block_scores(query_heads, key_heads):
    raw_scores = jnp.einsum(
        "lhd,khd->hlk", query_heads, key_heads, preferred_element_type=jnp.float32
    )
    return raw_scores * float(HEAD) ** (-0.5)


def softmax_totals(queries, key_rows, allowed_fn):
    query_heads = head_split(queries)
    count_rows = queries.shape[0]

    def visit(state_pair, block_index):
        running_top, running_sum = state_pair
        block_start = block_index * KEYBLK
        key_piece = lax.dynamic_slice_in_dim(key_rows, block_start, KEYBLK, 0)
        allowed = allowed_fn(block_start)[None]
        scores = jnp.where(
            allowed, block_scores(query_heads, head_split(key_piece[:, :D])), neg_fill
        )
        new_top = jnp.maximum(running_top, jnp.max(scores, axis=2))
        weights = jnp.where(allowed, jnp.exp(scores - new_top[:, :, None]), 0.0)
        running_sum = running_sum * jnp.exp(running_top - new_top) + jnp.sum(weights, axis=2)
        return ((new_top, running_sum), None)

    initial = (
        jnp.full((HEADS, count_rows), neg_fill, jnp.float32),
        jnp.zeros((HEADS, count_rows), jnp.float32),
    )
    (final_top, final_sum), unused = lax.scan(
        visit, initial, jnp.arange(key_rows.shape[0] // KEYBLK)
    )
    return final_top + jnp.log(final_sum)


def attend_values(queries, key_rows, log_totals, allowed_fn):
    query_heads = head_split(queries)

    def visit(running, block_index):
        block_start = block_index * KEYBLK
        key_piece = lax.dynamic_slice_in_dim(key_rows, block_start, KEYBLK, 0)
        allowed = allowed_fn(block_start)[None]
        scores = block_scores(query_heads, head_split(key_piece[:, :D]))
        weights = jnp.where(allowed, jnp.exp(scores - log_totals[:, :, None]), 0.0)
        value_heads = head_split(key_piece[:, D:])
        return (
            running
            + jnp.einsum(
                "hlk,khd->lhd",
                weights.astype(jnp.bfloat16),
                value_heads,
                preferred_element_type=jnp.float32,
            ),
            None,
        )

    mixed, unused = lax.scan(
        visit, jnp.zeros(query_heads.shape, jnp.float32), jnp.arange(key_rows.shape[0] // KEYBLK)
    )
    return mixed.reshape(queries.shape[0], D)


def head_offsets(grad_low, attended):
    return jnp.sum(head_split(grad_low.astype(jnp.float32) * attended), axis=2).T


def attend_back(queries, key_rows, log_totals, attended, grad_low, allowed_fn):
    query_heads = head_split(queries)
    grad_heads = head_split(grad_low)
    offsets = head_offsets(grad_low, attended)
    scale_value = float(HEAD) ** (-0.5)

    def visit(query_grad, block_index):
        block_start = block_index * KEYBLK
        key_piece = lax.dynamic_slice_in_dim(key_rows, block_start, KEYBLK, 0)
        allowed = allowed_fn(block_start)[None]
        key_heads = head_split(key_piece[:, :D])
        value_heads = head_split(key_piece[:, D:])
        weights = jnp.where(
            allowed, jnp.exp(block_scores(query_heads, key_heads) - log_totals[:, :, None]), 0.0
        )
        value_grad = jnp.einsum(
            "hlk,lhd->khd",
            weights.astype(jnp.bfloat16),
            grad_heads,
            preferred_element_type=jnp.float32,
        )
        weight_grad = jnp.einsum(
            "lhd,khd->hlk", grad_heads, value_heads, preferred_element_type=jnp.float32
        )
        score_grad = (weights * (weight_grad - offsets[:, :, None]) * scale_value).astype(
            jnp.bfloat16
        )
        query_grad = query_grad + jnp.einsum(
            "hlk,khd->lhd", score_grad, key_heads, preferred_element_type=jnp.float32
        )
        key_grad = jnp.einsum(
            "hlk,lhd->khd", score_grad, query_heads, preferred_element_type=jnp.float32
        )
        return (
            query_grad,
            jnp.concatenate((key_grad.reshape(KEYBLK, D), value_grad.reshape(KEYBLK, D)), axis=1),
        )

    query_grad, grad_pieces = lax.scan(
        visit, jnp.zeros(query_heads.shape, jnp.float32), jnp.arange(key_rows.shape[0] // KEYBLK)
    )
    return (query_grad.reshape(queries.shape[0], D), grad_pieces.reshape(key_rows.shape[0], 2 * D))


def normalize(values, gain_row, shift_row):
    row_mean = jnp.mean(values, axis=1, keepdims=True)
    centred = values - row_mean
    scale_inv = lax.rsqrt(jnp.mean(centred * centred, axis=1, keepdims=True) + layer_eps)
    normed = centred * scale_inv
    return (normed * gain_row + shift_row, normed, scale_inv)


def normalize_back(grad_out, normed, scale_inv, gain_row):
    gain_term = jnp.sum(grad_out * normed, axis=0)
    shift_term = jnp.sum(grad_out, axis=0)
    scaled = grad_out * gain_row
    grad_in = scale_inv * (
        scaled
        - jnp.mean(scaled, axis=1, keepdims=True)
        - normed * jnp.mean(scaled * normed, axis=1, keepdims=True)
    )
    return (grad_in, gain_term, shift_term)


def matmul(left, right):
    return jnp.dot(left, right, preferred_element_type=jnp.float32)


def general_shards(
    hidden,
    stream,
    encoder,
    lengths,
    order,
    ranks,
    thresholds,
    self_query,
    self_key_value,
    self_output,
    cross_query,
    cross_key_value,
    cross_output,
    ffn_in,
    ffn_out,
    norm_gain,
    norm_shift,
    cotangent,
):
    (
        full_query,
        full_pair,
        full_output,
        full_cross_query,
        full_cross_pair,
        full_cross_output,
        full_in,
        full_out,
        gain_rows,
        shift_rows,
    ) = (
        lax.all_gather(self_query, "wa", axis=0, tiled=True),
        lax.all_gather(self_key_value, "wa", axis=0, tiled=True),
        lax.all_gather(self_output, "wa", axis=0, tiled=True),
        lax.all_gather(cross_query, "wa", axis=0, tiled=True),
        lax.all_gather(cross_key_value, "wa", axis=0, tiled=True),
        lax.all_gather(cross_output, "wa", axis=0, tiled=True),
        lax.all_gather(ffn_in, "wa", axis=0, tiled=True),
        lax.all_gather(ffn_out, "wa", axis=0, tiled=True),
        lax.all_gather(norm_gain, "wa", axis=1, tiled=True),
        lax.all_gather(norm_shift, "wa", axis=1, tiled=True),
    )
    gains = gain_rows.astype(jnp.float32)
    shifts = shift_rows.astype(jnp.float32)
    local_rows = hidden.shape[1]
    total_rows = order.shape[1]
    row_start = lax.axis_index("ctx") * local_rows
    seq_ends = jnp.cumsum(lengths[0])
    token_seq = sequence_ids(order[0], seq_ends)
    source_seq = sequence_ids(jnp.arange(total_rows, dtype=jnp.int32), seq_ends)
    query_seq = lax.dynamic_slice_in_dim(token_seq, row_start, local_rows)
    query_rows = row_start + jnp.arange(local_rows, dtype=jnp.int32)
    all_limits = thresholds[0]
    limits = lax.dynamic_slice_in_dim(all_limits, row_start, local_rows)
    key_ranks = ranks[0]

    def self_allowed(block_start):
        block_seq = lax.dynamic_slice_in_dim(token_seq, block_start, KEYBLK)
        block_rank = lax.dynamic_slice_in_dim(key_ranks, block_start, KEYBLK)
        block_rows = block_start + jnp.arange(KEYBLK, dtype=jnp.int32)
        return (query_seq[:, None] == block_seq[None, :]) & (
            (block_rank[None, :] < limits[:, None]) | (query_rows[:, None] == block_rows[None, :])
        )

    def cross_allowed(block_start):
        return (
            query_seq[:, None] == lax.dynamic_slice_in_dim(source_seq, block_start, KEYBLK)[None, :]
        )

    inputs = hidden[0]
    stream_rows = stream[0]
    source_rows = encoder[0]
    queries = matmul(inputs, full_query).astype(jnp.bfloat16)
    self_local = matmul(stream_rows, full_pair).astype(jnp.bfloat16)
    cross_local = matmul(source_rows, full_cross_pair).astype(jnp.bfloat16)
    self_keys, cross_keys = (
        lax.all_gather(self_local, "ctx", axis=0, tiled=True),
        lax.all_gather(cross_local, "ctx", axis=0, tiled=True),
    )
    self_totals = softmax_totals(queries, self_keys, self_allowed)
    self_mixed = attend_values(queries, self_keys, self_totals, self_allowed)
    self_low = self_mixed.astype(jnp.bfloat16)
    first, first_normed, first_scale = normalize(
        inputs.astype(jnp.float32) + matmul(self_low, full_output), gains[0], shifts[0]
    )
    first_low = first.astype(jnp.bfloat16)
    cross_queries = matmul(first_low, full_cross_query).astype(jnp.bfloat16)
    cross_totals = softmax_totals(cross_queries, cross_keys, cross_allowed)
    cross_mixed = attend_values(cross_queries, cross_keys, cross_totals, cross_allowed)
    cross_low = cross_mixed.astype(jnp.bfloat16)
    second, second_normed, second_scale = normalize(
        first + matmul(cross_low, full_cross_output), gains[1], shifts[1]
    )
    second_low = second.astype(jnp.bfloat16)
    hidden_pre = matmul(second_low, full_in)
    sigmoid_pre = jax.nn.sigmoid(hidden_pre)
    activated = (hidden_pre * sigmoid_pre).astype(jnp.bfloat16)
    result, third_normed, third_scale = normalize(
        second + matmul(activated, full_out), gains[2], shifts[2]
    )
    third_grad, gain_grad_c, shift_grad_c = normalize_back(
        cotangent[0].astype(jnp.float32), third_normed, third_scale, gains[2]
    )
    branch_grad = third_grad.astype(jnp.bfloat16)
    grad_ffn_out = matmul(activated.T, branch_grad)
    slope = sigmoid_pre * (1.0 + hidden_pre * (1.0 - sigmoid_pre))
    pre_grad = (matmul(branch_grad, full_out.T) * slope).astype(jnp.bfloat16)
    grad_ffn_in = matmul(second_low.T, pre_grad)
    second_total = third_grad + matmul(pre_grad, full_in.T)
    second_grad, gain_grad_b, shift_grad_b = normalize_back(
        second_total, second_normed, second_scale, gains[1]
    )
    cross_branch = second_grad.astype(jnp.bfloat16)
    grad_cross_output = matmul(cross_low.T, cross_branch)
    cross_mixed_grad = matmul(cross_branch, full_cross_output.T).astype(jnp.bfloat16)
    cross_query_term, cross_terms = attend_back(
        cross_queries, cross_keys, cross_totals, cross_mixed, cross_mixed_grad, cross_allowed
    )
    cross_query_low = cross_query_term.astype(jnp.bfloat16)
    grad_cross_query = matmul(first_low.T, cross_query_low)
    first_total = second_grad + matmul(cross_query_low, full_cross_query.T)
    first_grad, gain_grad_a, shift_grad_a = normalize_back(
        first_total, first_normed, first_scale, gains[0]
    )
    self_branch = first_grad.astype(jnp.bfloat16)
    grad_self_output = matmul(self_low.T, self_branch)
    self_mixed_grad = matmul(self_branch, full_output.T).astype(jnp.bfloat16)
    self_query_term, self_terms = attend_back(
        queries, self_keys, self_totals, self_mixed, self_mixed_grad, self_allowed
    )
    self_sum, cross_sum = (
        lax.psum_scatter(self_terms, "ctx", scatter_dimension=0, tiled=True),
        lax.psum_scatter(cross_terms, "ctx", scatter_dimension=0, tiled=True),
    )
    self_query_low = self_query_term.astype(jnp.bfloat16)
    grad_self_query = matmul(inputs.T, self_query_low)
    input_grad = first_grad + matmul(self_query_low, full_query.T)
    self_sum_low = self_sum.astype(jnp.bfloat16)
    grad_self_pair = matmul(stream_rows.T, self_sum_low)
    stream_grad = matmul(self_sum_low, full_pair.T)
    cross_sum_low = cross_sum.astype(jnp.bfloat16)
    grad_cross_pair = matmul(source_rows.T, cross_sum_low)
    source_grad = matmul(cross_sum_low, full_cross_pair.T)
    gain_grads = jnp.stack((gain_grad_a, gain_grad_b, gain_grad_c))
    shift_grads = jnp.stack((shift_grad_a, shift_grad_b, shift_grad_c))
    (
        share_query,
        share_pair,
        share_output,
        share_cross_query,
        share_cross_pair,
        share_cross_output,
        share_in,
        share_out,
        share_gain,
        share_shift,
    ) = (
        lax.psum_scatter(
            grad_self_query.astype(jnp.bfloat16), "wa", scatter_dimension=0, tiled=True
        ).astype(jnp.float32),
        lax.psum_scatter(
            grad_self_pair.astype(jnp.bfloat16), "wa", scatter_dimension=0, tiled=True
        ).astype(jnp.float32),
        lax.psum_scatter(
            grad_self_output.astype(jnp.bfloat16), "wa", scatter_dimension=0, tiled=True
        ).astype(jnp.float32),
        lax.psum_scatter(
            grad_cross_query.astype(jnp.bfloat16), "wa", scatter_dimension=0, tiled=True
        ).astype(jnp.float32),
        lax.psum_scatter(
            grad_cross_pair.astype(jnp.bfloat16), "wa", scatter_dimension=0, tiled=True
        ).astype(jnp.float32),
        lax.psum_scatter(
            grad_cross_output.astype(jnp.bfloat16), "wa", scatter_dimension=0, tiled=True
        ).astype(jnp.float32),
        lax.psum_scatter(
            grad_ffn_in.astype(jnp.bfloat16), "wa", scatter_dimension=0, tiled=True
        ).astype(jnp.float32),
        lax.psum_scatter(
            grad_ffn_out.astype(jnp.bfloat16), "wa", scatter_dimension=0, tiled=True
        ).astype(jnp.float32),
        lax.psum_scatter(
            gain_grads.astype(jnp.bfloat16), "wa", scatter_dimension=1, tiled=True
        ).astype(jnp.float32),
        lax.psum_scatter(
            shift_grads.astype(jnp.bfloat16), "wa", scatter_dimension=1, tiled=True
        ).astype(jnp.float32),
    )
    (
        total_query,
        total_pair,
        total_output,
        total_cross_query,
        total_cross_pair,
        total_cross_output,
        total_in,
        total_out,
        total_gain,
        total_shift,
    ) = lax.psum(
        (
            share_query,
            share_pair,
            share_output,
            share_cross_query,
            share_cross_pair,
            share_cross_output,
            share_in,
            share_out,
            share_gain,
            share_shift,
        ),
        "ctx",
    )
    return (
        result.astype(jnp.bfloat16)[None],
        input_grad[None],
        stream_grad[None],
        source_grad[None],
        total_query,
        total_pair,
        total_output,
        total_cross_query,
        total_cross_pair,
        total_cross_output,
        total_in,
        total_out,
        total_gain,
        total_shift,
    )


PAIR = 2 * HEAD
PAIRS = HEADS // 2
FF = 2048
low_t = jnp.bfloat16
wide_t = jnp.float32
vmem_spec = pl.BlockSpec(memory_space=pltpu.VMEM)
smem_spec = pl.BlockSpec(memory_space=pltpu.SMEM)


def run(body, outs, ids, args, scratch=(), us=2, vmem=56):
    outs = [jax.ShapeDtypeStruct(shape, kind) for shape, kind in outs]
    arrays = [arg[0] if isinstance(arg, tuple) else arg for arg in args]
    parts = [n for n, arg in enumerate(args) if isinstance(arg, tuple)]
    total = len(args) + len(outs) + len(scratch)

    def kernel(ids, *refs):
        refs, buffers, sems = list(refs[:total]), refs[total:-1], refs[-1]
        copies = []
        for m, n in enumerate(parts):
            start = args[n][1] * D
            copies.append(
                pltpu.make_async_copy(refs[n].at[:, :, start : start + D], buffers[m], sems.at[m])
            )
            copies[m].start()
            refs[n] = buffers[m]
        for copy in copies:
            copy.wait()
        body(ids, *refs)

    buffers = [pltpu.VMEM(args[n][0].shape[:2] + (D,), args[n][0].dtype) for n in parts]
    specs = [pl.BlockSpec(memory_space=pl.ANY) if n in parts else vmem_spec for n in range(len(args))]
    moved = sum(a.size * a.dtype.itemsize for a in arrays + outs)
    return pl.pallas_call(
        kernel,
        name=getattr(body, "func", body).__name__,
        out_shape=outs,
        in_specs=[smem_spec] + specs,
        out_specs=[vmem_spec] * len(outs),
        scratch_shapes=[pltpu.VMEM(shape, kind) for shape, kind in scratch]
        + buffers
        + [pltpu.SemaphoreType.DMA((max(1, len(parts)),))],
        compiler_params=pltpu.CompilerParams(vmem_limit_bytes=vmem * 1024 * 1024),
        cost_estimate=pl.CostEstimate(flops=us * 1_000_000_000, bytes_accessed=moved, transcendentals=0),
    )(ids, *arrays)


def dot_nn(a, b):
    return lax.dot_general(a, b, (((1,), (0,)), ((), ())), preferred_element_type=wide_t)


def dot_nt(a, b):
    return lax.dot_general(a, b, (((1,), (1,)), ((), ())), preferred_element_type=wide_t)


def dot_tn(a, b):
    return lax.dot_general(a, b, (((0,), (0,)), ((), ())), preferred_element_type=wide_t)


def at16(start, size=16):
    return pl.ds(pl.multiple_of(start, 16), size)


def at128(start, size=128):
    return pl.ds(pl.multiple_of(start, 128), size)


def half_mask(shape, axis, core):
    return (lax.broadcasted_iota(jnp.int32, shape, axis) // HEAD) == core


def attend_rows(q_ref, k_ref, vt_ref, bias_ref, s_ref, ot_ref, lse_ref):
    keys, rows = bias_ref.shape
    tile = min(1024, keys)
    spans = [slice(start, start + tile) for start in range(0, keys, tile)]
    lowest = jnp.full((8, rows), neg_fill, wide_t)
    group = 4

    def step(p, carry):
        def scores(head, here, top):
            pair = at128((p * (group // 2) + head // 2) * PAIR)
            q = q_ref[:, pair]
            own_q = jnp.where(half_mask((rows, PAIR), 1, head % 2), q, jnp.zeros_like(q))
            s = dot_nt(k_ref[here, pair], own_q) + bias_ref[here, :]
            s_ref[head % 2, here, :] = s
            return jnp.maximum(top, jnp.max(s.reshape(tile // 8, 8, rows), axis=0))

        top = lowest
        for here in spans:
            top = scores(0, here, top)
        for head in range(group):
            features = pl.ds(pl.multiple_of((p * group + head) * HEAD, HEAD), HEAD)
            highest = jnp.max(top, axis=0, keepdims=True)
            total = jnp.zeros((8, rows), wide_t)
            mixed = jnp.zeros((HEAD, rows), wide_t)
            top = lowest
            for here in spans:
                if head + 1 < group:
                    top = scores(head + 1, here, top)
                w = jnp.exp(s_ref[head % 2, here, :] - highest)
                total = total + jnp.sum(w.reshape(tile // 8, 8, rows), axis=0)
                mixed = mixed + dot_nn(vt_ref[features, here], w.astype(low_t))
            total = jnp.sum(total, axis=0, keepdims=True)
            ot_ref[features, :] = mixed / total
            lse_ref[pl.ds(p * group + head, 1), :] = highest + jnp.log(total)
        return carry

    lax.fori_loop(0, HEADS // group, step, 0)


def finish_rows(ot_ref, low_out, mixed_out):
    mixed = ot_ref[...].T
    low_out[...] = mixed.astype(low_t)
    mixed_out[...] = mixed


def three_parts(value):
    high = value.astype(low_t).astype(wide_t)
    rest = value - high
    middle = rest.astype(low_t).astype(wide_t)
    return high, middle, rest - middle


def side_rows(lse, grad_low, mixed, row_data):
    product = grad_low.astype(wide_t) * mixed[...]
    lane = lax.broadcasted_iota(jnp.int32, (grad_low.shape[0], PAIR), 1)
    sums = jnp.zeros((grad_low.shape[0], PAIR), wide_t)
    for p in range(PAIRS):
        piece = product[:, p * PAIR : (p + 1) * PAIR]
        for h in range(2):
            mine = half_mask(piece.shape, 1, h)
            offset = jnp.sum(jnp.where(mine, piece, 0.0), axis=1, keepdims=True)
            sums = jnp.where(lane == p * 2 + h, offset, sums)
    offsets = sums.T
    seq = row_data[16:17, :]
    onehot = [(seq == float(n)).astype(wide_t) for n in range(4)]
    sides = []
    for p in range(PAIRS):
        pieces = []
        for h in range(2):
            head = p * 2 + h
            pieces += three_parts(-lse[head : head + 1, :])
            pieces += three_parts(-offsets[head : head + 1, :])
        sides.append(jnp.concatenate(pieces + onehot, axis=0).astype(low_t))
    return sides


def side_lanes(side, core):
    side = side.astype(wide_t)
    head = jnp.where(core == 0, side[0:6], side[6:12])
    gap = jnp.zeros((5, side.shape[1]), wide_t)
    rest = jnp.zeros((HEAD - 20, side.shape[1]), wide_t)
    half = jnp.concatenate((head[0:3], gap, head[3:6], gap, side[12:16], rest), axis=0)
    return jnp.concatenate((half, half), axis=0).T.astype(low_t)


def assemble(ids, parts, column, outs):
    for chip, other, block in parts:
        own = chip * 2 + (ids[1] ^ other)
        for e in range(4):
            rows = at16((ids[2] ^ e) * 128 + own * 16)
            start = column
            for out in outs:
                width = out.shape[1]
                out[rows, :] = block[e * 16 : (e + 1) * 16, start : start + width]
                start += width


def project_pairs(parts, w_pair, k_ref, vt_ref, wvt_ref):
    wvt_ref[...] = w_pair[:, D:].astype(wide_t).T.astype(low_t)
    for n, part in enumerate(parts):
        for k in range(PAIRS):
            rows = part.shape[1]
            start = (n * 4 + k) * rows
            k_ref[start : start + rows, :] = dot_nn(part[k], w_pair[:, :D]).astype(low_t)
            vt_ref[:, start : start + rows] = dot_nt(wvt_ref[...], part[k]).astype(low_t)


def self_forward(ids, hidden, own, other, *refs):
    slices, (cols, row_data), refs = refs[:8], refs[8:10], refs[10:]
    out, mixed, lse, wq, wkv, q_ref, k_ref, vt_ref, wvt_ref, bias_ref, s_ref, ot_ref = refs
    rows = hidden.shape[0]
    parts = [(ids[0] ^ k, n, slices[n * 4 + k]) for n in range(2) for k in range(4)]
    assemble(ids, parts, 0, (wq, wkv))
    q_ref[...] = (dot_nn(hidden[...], wq[...]).astype(low_t) * 0.125).astype(low_t)
    project_pairs((own, other), wkv, k_ref, vt_ref, wvt_ref)
    seq, limit = row_data[16:17, :], row_data[17:18, :]
    for b in range(8):
        seen = (cols[:, b : b + 1] == seq) & (cols[:, 8 + b : 9 + b] < limit)
        bias_ref[b * rows : (b + 1) * rows, :] = jnp.where(seen, 0.0, neg_fill)
    mine = lax.broadcasted_iota(jnp.int32, (rows, rows), 0) == lax.broadcasted_iota(
        jnp.int32, (rows, rows), 1
    )
    block = at128(ids[0] * rows, rows)
    bias_ref[block, :] = jnp.where(mine, 0.0, bias_ref[block, :])
    attend_rows(q_ref, k_ref, vt_ref, bias_ref, s_ref, ot_ref, lse)
    finish_rows(ot_ref, out, mixed)


def layer_norm(values, gain_row, shift_row):
    mean = jnp.mean(values, axis=1, keepdims=True)
    centred = values - mean
    scale = lax.rsqrt(jnp.mean(centred * centred, axis=1, keepdims=True) + layer_eps)
    normed = centred * scale
    return normed * gain_row + shift_row, normed, scale


def layer_norm_back(grad, normed, scale, gain_row):
    gain_term = jnp.sum(grad * normed, axis=0, keepdims=True)
    shift_term = jnp.sum(grad, axis=0, keepdims=True)
    scaled = grad * gain_row
    grad_in = scale * (
        scaled
        - jnp.mean(scaled, axis=1, keepdims=True)
        - normed * jnp.mean(scaled * normed, axis=1, keepdims=True)
    )
    return grad_in, gain_term, shift_term


def head_arrays(ids, k_ref, vt_ref, cols, column, k_all, v_all, kt, turn):
    rows = turn.shape[1]
    core = ids[1]
    mine = half_mask((rows, PAIR), 1, core)
    features = pl.ds(pl.multiple_of(core * HEAD, HEAD), HEAD)
    lane = lax.broadcasted_iota(jnp.int32, (rows, PAIR), 1) % HEAD
    ones_v = jnp.where((lane >= 8) & (lane < 11), 1.0, 0.0).astype(low_t)
    pair = at128(ids[0] * PAIR)
    for b in range(8):
        here = slice(b * rows, (b + 1) * rows)
        seq = cols[:, column + b : column + b + 1].astype(jnp.int32)
        other_seq = (lane >= 16) & (lane < 20) & (lane != seq + 16)
        ones_k = jnp.where(other_seq, neg_fill, jnp.where(lane < 3, 1.0, 0.0)).astype(low_t)
        key = k_ref[here, pair]
        k_all[here, :] = jnp.where(mine, key, ones_k)
        turn[...] = key.astype(wide_t).T
        kt[:, here] = turn[features, :].astype(low_t)
        v_all[here, :] = jnp.where(mine, turned(vt_ref[pair, here]), ones_v)


def cross_forward(ids, hidden, self_low, own, other, *refs):
    slices, (cols, row_data) = refs[:2], refs[2:4]
    first, normed, scale_out, first_low, cross_low, mixed, lse, cross_q = refs[4:12]
    wo, wcq, wckv, wco, gs, k_all, v_all, kt = refs[12:20]
    q_ref, k_ref, vt_ref, wvt_ref, bias_ref, s_ref, ot_ref, turn = refs[20:]
    for n in range(2):
        for e in range(4):
            rows = at16(e * 128 + (ids[1] ^ n) * 64, 64)
            start = 0
            for out in (wo, wcq, wckv, wco):
                width = out.shape[1]
                out[rows, :] = slices[n][e, :, start : start + width]
                start += width
    for e in range(4):
        gs[:, e * 128 : (e + 1) * 128] = slices[0][e, :16, 5 * D :]
    gain, shift = gs[0:1, :].astype(wide_t), gs[3:4, :].astype(wide_t)
    value, n0, s0 = layer_norm(
        hidden[...].astype(wide_t) + dot_nn(self_low[...], wo[...]), gain, shift
    )
    first[...] = value
    normed[...] = n0
    scale_out[...] = jnp.broadcast_to(s0, scale_out.shape)
    low = value.astype(low_t)
    first_low[...] = low
    q = dot_nn(low, wcq[...]).astype(low_t)
    cross_q[...] = q
    q_ref[...] = (q * 0.125).astype(low_t)
    rows = hidden.shape[0]
    project_pairs((own, other), wckv, k_ref, vt_ref, wvt_ref)
    for b in range(8):
        seen = cols[:, 16 + b : 17 + b] == row_data[16:17, :]
        bias_ref[b * rows : (b + 1) * rows, :] = jnp.where(seen, 0.0, neg_fill)
    attend_rows(q_ref, k_ref, vt_ref, bias_ref, s_ref, ot_ref, lse)
    finish_rows(ot_ref, cross_low, mixed)
    head_arrays(ids, k_ref, vt_ref, cols, 16, k_all, v_all, kt, turn)


def feed_forward(ids, first, cross_low, cross_mixed, lse, row_data, cross_q, wco, gs, cotangent, *refs):
    slices = refs[0:8]
    result, dealt, second_grad, keep, send, sums, slope, wins, wouts = refs[8:]
    half_ff = FF // 2
    for n in range(2):
        for k in range(4):
            chip, core, part = ids[0] ^ k, ids[1] ^ n, slices[n * 4 + k]
            for e in range(4):
                w, here = ids[2] ^ e, slice(e * 16, (e + 1) * 16)
                rows = at16(w * 128 + (chip * 2 + core) * 16)
                for g in range(4):
                    row = w * 256 + ((chip % 2) * 2 + core) * 64 + g * 16
                    wouts[(chip // 2) ^ ids[1], at16(row), :] = part[here, FF + g * D : FF + (g + 1) * D]
                    for h in range(2):
                        column = g * 512 + h * 256
                        wins[h ^ ids[1], rows, g * 256 : (g + 1) * 256] = part[here, column : column + 256]
    gains, shifts = gs[0:3, :].astype(wide_t), gs[3:6, :].astype(wide_t)
    second, n1, s1 = layer_norm(
        first[...] + dot_nn(cross_low[...], wco[...]), gains[1:2], shifts[1:2]
    )
    low = second.astype(low_t)
    for out in (keep, send):
        out[:, 2 * half_ff : 2 * half_ff + D] = low
        out[:, 2 * half_ff + 2 * D : 2 * half_ff + 3 * D] = cross_low[...]
    width = 1024
    chunks = [(n, c) for n in range(2) for c in range(FF // 2 // width)]
    total = second
    for n, c in chunks:
        here = slice(c * width, (c + 1) * width)
        wide = slice(n * half_ff + c * width, n * half_ff + (c + 1) * width)
        pre = dot_nn(low, wins[n, :, here])
        sig = 1.0 / (1.0 + jnp.exp(-pre))
        act = (pre * sig).astype(low_t)
        (keep, send)[n][:, half_ff + c * width : half_ff + (c + 1) * width] = act
        slope[:, wide] = sig * (1.0 + pre * (1.0 - sig))
        total = total + dot_nn(act, wouts[n, here, :])
    value, n2, s2 = layer_norm(total, gains[2:3], shifts[2:3])
    result[...] = value.astype(low_t)
    third, gain_c, shift_c = layer_norm_back(cotangent[...].astype(wide_t), n2, s2, gains[2:3])
    third_low = third.astype(low_t)
    for out in (keep, send):
        out[:, 2 * half_ff + D : 2 * half_ff + 2 * D] = third_low
    total = third
    for n, c in chunks:
        here = slice(c * width, (c + 1) * width)
        wide = slice(n * half_ff + c * width, n * half_ff + (c + 1) * width)
        back = (dot_nt(third_low, wouts[n, here, :]) * slope[:, wide]).astype(low_t)
        (keep, send)[n][:, here] = back
        total = total + dot_nt(back, wins[n, :, here])
    grad, gain_b, shift_b = layer_norm_back(total, n1, s1, gains[1:2])
    second_grad[...] = grad
    grad_low = grad.astype(low_t)
    for out, core in ((keep, ids[1]), (send, 1 - ids[1])):
        half = grad_low[:, : D // 2]
        out[:, 2 * half_ff + 3 * D :] = jnp.where(core == 0, half, grad_low[:, D // 2 :])
    mixed = dot_nt(grad_low, wco[...]).astype(low_t)
    rows = grad_low.shape[0]
    sides = side_rows(lse, mixed, cross_mixed, row_data)
    for p in range(PAIRS):
        dealt[p, :rows, :PAIR] = cross_q[:, p * PAIR : (p + 1) * PAIR]
        dealt[p, :rows, PAIR:] = mixed[:, p * PAIR : (p + 1) * PAIR]
        dealt[p, rows:, :] = sides[p]
    zero = jnp.zeros_like(gain_b)
    sums[...] = jnp.concatenate((zero, gain_b, gain_c, zero, shift_b, shift_c, zero, zero), axis=0)


def grads_a(ids, keep, received, out, g_in, g_out, g_cross):
    half = FF // 2

    def both(left, right):
        return (dot_tn(keep[:, left], keep[:, right]) + dot_tn(received[:, left], received[:, right])).astype(low_t)

    at = [0, half] + [2 * half + n * D for n in range(4)]
    pre, act = slice(at[0], at[1]), slice(at[1], at[2])
    second, branch, low = (slice(at[n], at[n] + D) for n in (2, 3, 4))
    g_in[...] = both(second, pre)
    g_out[...] = both(act, branch)
    g_cross[...] = both(low, slice(at[5], at[5] + D // 2))
    for chip in range(4):
        for e in range(4):
            w, here = ids[2] ^ e, slice(e * 32, (e + 1) * 32)
            rows = at16(w * 128 + chip * 32, 32)
            out[chip, here, :half] = g_in[rows, :]
            for g in range(2):
                out[chip, here, half + g * D : half + (g + 1) * D] = g_out[
                    at16(w * 256 + chip * 64 + g * 32, 32), :
                ]
            out[chip, here, half + 2 * D :] = g_cross[rows, :]


def grads_b(ids, first_low, cross_dq, self_low, branch, sums, dkv, out, g_query, g_output):
    g_query[...] = dot_tn(first_low[...], cross_dq[...]).astype(low_t)
    g_output[...] = dot_tn(self_low[...], branch[...]).astype(low_t)
    row = jnp.concatenate((sums[...], jnp.zeros_like(sums[...])), axis=0).astype(low_t)
    rows = dkv.shape[2]
    for e in range(4):
        w, here = ids[2] ^ e, slice(e * 16, (e + 1) * 16)
        piece = row[:, :128]
        for k in range(1, 4):
            piece = jnp.where(w == k, row[:, k * 128 : (k + 1) * 128], piece)
        for device in range(8):
            own = at16(w * 128 + device * 16)
            out[device, here, :D] = g_query[own, :]
            out[device, here, D : 2 * D] = g_output[own, :]
            out[device, here, 2 * D : 2 * D + 128] = piece
    for device in range(8):
        for n in range(2):
            start = 2 * D + 128 + n * rows
            out[device, :, start : start + rows] = dkv[device, n * HEAD : (n + 1) * HEAD, :]


def pair_setup(is_self, ids, own, other, w_pair, cols, *refs):
    k_all, v_all, kt, turn = refs
    chip, core = ids[0], ids[1]
    rows = own.shape[1]
    mine = half_mask((rows, PAIR), 1, core)
    features = pl.ds(pl.multiple_of(core * HEAD, HEAD), HEAD)
    lane = lax.broadcasted_iota(jnp.int32, (rows, PAIR), 1) % HEAD
    ones_v = jnp.where((lane >= 8) & (lane < 11), 1.0, 0.0).astype(low_t)
    pair = at128(chip * PAIR)
    wk, wv = w_pair[:, pair], w_pair[:, at128(D + chip * PAIR)]
    for n, part in enumerate((own, other)):
        for k in range(4):
            b = n * 4 + k
            here = slice(b * rows, (b + 1) * rows)
            column = b if is_self else 16 + b
            seq = cols[:, column : column + 1].astype(jnp.int32)
            other_seq = (lane >= 16) & (lane < 20) & (lane != seq + 16)
            ones_k = jnp.where(other_seq, neg_fill, jnp.where(lane < 3, 1.0, 0.0)).astype(low_t)
            key = dot_nn(part[k], wk)
            turn[...] = key.T
            kt[:, here] = turn[features, :].astype(low_t)
            k_all[here, :] = jnp.where(mine, key.astype(low_t), ones_k)
            v_all[here, :] = jnp.where(mine, dot_nn(part[k], wv).astype(low_t), ones_v)


def pair_queries(ids, own, other, w_query, q_all):
    wq = w_query[:, at128(ids[0] * PAIR)]
    for n, part in enumerate((own, other)):
        for k in range(4):
            q_all[n * 4 + k] = dot_nn(part[k], wq).astype(low_t)


def pair_back(is_self, ids, *refs):
    if is_self:
        q_parts, do_own, do_other, k_all, v_all, kt, cols, row_data, back = refs[:9]
        do_parts = (do_own, do_other)
    else:
        both_own, both_other, k_all, v_all, kt, dq_keep, dq_send, dkv = refs[:8]
        both_parts = (both_own, both_other)
    q_all, do_all, dq_t, dk, dv, rank, turn = refs[-7:]
    core = ids[1]
    rows = q_all.shape[1]
    keys = 8 * rows
    mine = half_mask((rows, PAIR), 1, core)
    features = pl.ds(pl.multiple_of(core * HEAD, HEAD), HEAD)
    for n in range(2):
        for k in range(4):
            b = n * 4 + k
            if is_self:
                here = slice(b * rows, (b + 1) * rows)
                rank[here, :] = jnp.broadcast_to(cols[:, 8 + b : 9 + b], (rows, 128))
                q, do = q_parts[b], do_parts[n][k, :rows, :]
                side = jnp.concatenate(
                    (do_parts[n][k, rows : rows + 16, :], do_parts[n][k, rows + 16 :, :]), axis=1
                )
            else:
                q, do = both_parts[n][k, :rows, :PAIR], both_parts[n][k, :rows, PAIR:]
                side = both_parts[n][k, rows:, :]
            side = side_lanes(side, core)
            q_all[b] = jnp.where(mine, (q * 0.125).astype(low_t), side)
            do_all[b] = jnp.where(mine, do, side)
    dk[...] = jnp.zeros_like(dk)
    dv[...] = jnp.zeros_like(dv)
    tile = min(512 if is_self else 1024, keys)
    blocks = 1 if is_self else 2

    def step(step, carry):
        b, wide = step * blocks, blocks * rows
        q, do = (ref[pl.ds(b, blocks)].reshape(wide, PAIR) for ref in (q_all, do_all))
        dqt = jnp.zeros((HEAD, wide), wide_t)
        for t in range(keys // tile):
            here = slice(t * tile, (t + 1) * tile)
            if is_self:
                start = (b * rows // tile + t) % (keys // tile) * tile
                here = at128(start, tile)
            w = jnp.exp(dot_nt(k_all[here, :], q))
            if is_self:
                ranks = jnp.concatenate((rank[here, :],) * (wide // 128), axis=1)
                seen = ranks < row_data[pl.ds(8 + b, 1), :]
                if t == 0:
                    index = lax.broadcasted_iota(jnp.int32, (tile, wide), 0)
                    own = lax.broadcasted_iota(jnp.int32, (tile, wide), 1) + (b * rows - start)
                    seen = seen | (index == own)
                w = jnp.where(seen, w, 0.0)
            ds = (w * dot_nt(v_all[here, :], do)).astype(low_t)
            dv[here, :] += dot_nn(w.astype(low_t), do)
            dk[here, :] += dot_nn(ds, q)
            dqt = dqt + dot_nn(kt[:, here], ds)
        dqt = (dqt * 0.125).astype(low_t)
        for n in range(blocks):
            dq_t[b + n] = dqt[:, n * rows : (n + 1) * rows]
        return carry

    lax.fori_loop(0, 8 // blocks, step, 0)
    for n in range(2):
        for k in range(4):
            b = n * 4 + k
            device = k * 2 + (core ^ n)
            here = slice(b * rows, (b + 1) * rows)
            if is_self:
                back[device, :HEAD, :] = dq_t[b]
            else:
                (dq_keep, dq_send)[n][k] = dq_t[b]
            out, start = (back, HEAD) if is_self else (dkv, 0)
            for value in (dk, dv):
                turn[...] = value[here, :].T
                out[device, start : start + HEAD, :] = turn[features, :].astype(low_t)
                start += HEAD


def head_grads(grads, own, other, core, hidden=None):
    first = HEAD if hidden else 0
    total = jnp.zeros((2 * HEAD, D), wide_t)
    total_q = jnp.zeros((HEAD, D), wide_t)
    for n, part in enumerate((own, other)):
        for k in range(4):
            device = k * 2 + (core ^ n)
            total += dot_nn(grads[device, first:, :], part[k])
            if hidden:
                total_q += dot_nn(grads[device, :HEAD, :], hidden[n][k])
    return total, total_q


def pair_grads(ids, grads, own, other, dw):
    total, unused = head_grads(grads, own, other, ids[1])
    for w in range(4):
        dw[w] = total[:, w * 128 : (w + 1) * 128].astype(low_t)


def turned(value):
    return value.astype(wide_t).T.astype(low_t)


def pair_up(ids, keep, received, *outs):
    for k in range(4):
        p = ids[0] ^ k
        outs[k][at16(ids[1] * HEAD, HEAD), :] = keep[p]
        outs[k][at16((1 - ids[1]) * HEAD, HEAD), :] = received[p]


def first_back(ids, *refs):
    parts = refs[:4]
    second_grad, normed, scale, self_mixed, lse, row_data, gs, wcq, wo, sums_in = refs[4:14]
    first_grad, branch, dealt, dq, sums, all_t = refs[14:]
    for k in range(4):
        all_t[at128((ids[0] ^ k) * PAIR), :] = parts[k][...]
    dq[...] = turned(all_t[...])
    total = second_grad[...] + dot_nt(dq[...], wcq[...])
    grad, gain_a, shift_a = layer_norm_back(
        total, normed[...], scale[:, 0:1], gs[0:1, :].astype(wide_t)
    )
    first_grad[...] = grad
    low = grad.astype(low_t)
    branch[...] = low
    mixed = dot_nt(low, wo[...]).astype(low_t)
    rows = low.shape[0]
    sides = side_rows(lse, mixed, self_mixed, row_data)
    for p in range(PAIRS):
        dealt[p, :rows, :] = mixed[:, p * PAIR : (p + 1) * PAIR]
        dealt[p, rows : rows + 16, :] = sides[p][:, :PAIR]
        dealt[p, rows + 16 :, :] = sides[p][:, PAIR:]
    zero = jnp.zeros_like(gain_a)
    sums[...] = sums_in[...] + jnp.concatenate(
        (gain_a, zero, zero, shift_a, zero, zero, zero, zero), axis=0
    )


def source_back(ids, parts, wckv, out, dkv):
    rows = out.shape[0]
    for device in range(8):
        for n in range(2):
            start = 2 * D + 128 + n * rows
            dkv[n * D + device * HEAD : n * D + (device + 1) * HEAD, :] = parts[
                device, :, start : start + rows
            ]
    out[...] = dot_nt(turned(dkv[...]), wckv[...])


def hidden_back(ids, back, first_grad, wq, wkv, hidden_grad, stream_grad, all_t):
    for device in range(8):
        for n in range(3):
            all_t[n * D + device * HEAD : n * D + (device + 1) * HEAD, :] = back[
                device, n * HEAD : (n + 1) * HEAD, :
            ]
    hidden_grad[...] = first_grad[...] + dot_nt(turned(all_t[:D, :]), wq[...])
    stream_grad[...] = dot_nt(turned(all_t[D:, :]), wkv[...])


def add_parts(parts, rows, columns):
    total = parts[0, rows, columns].astype(wide_t)
    for n in range(1, parts.shape[0]):
        total = total + parts[n, rows, columns].astype(wide_t)
    return total.astype(low_t)


def add_chips(ids, parts, dw, *outs):
    width = parts.shape[2]
    for e in range(4):
        outs[e][:, :width] = add_parts(parts, slice(e * 32, (e + 1) * 32), slice(None))
        piece = dw[ids[2] ^ e]
        for g in range(4):
            outs[e][:, width + g * 128 : width + (g + 1) * 128] = piece[g * 32 : (g + 1) * 32, :]


def self_grads(ids, grads, own, other, hidden_own, hidden_other, dw):
    total, total_q = head_grads(grads, own, other, ids[1], (hidden_own, hidden_other))
    for w in range(4):
        columns = slice(w * 128, (w + 1) * 128)
        dw[w, :HEAD, :] = total_q[:, columns].astype(low_t)
        dw[w, HEAD:, :] = total[:, columns].astype(low_t)


def end_sums(ids, parts, dw, *outs):
    width = 2 * D + 128
    for e in range(4):
        outs[e][:, :width] = add_parts(parts, slice(e * 16, (e + 1) * 16), slice(0, width))
        outs[e][:, width : width + 128] = jnp.zeros((16, 128), low_t)
        piece = dw[ids[2] ^ e]
        for g in range(12):
            start = width + 128 + g * 128
            outs[e][:, start : start + 128] = piece[g * 16 : (g + 1) * 16, :]


def add_shards(ids, *refs):
    out = refs[8]

    def total(parts):
        value = parts[0][...].astype(wide_t)
        for part in parts[1:]:
            value = value + part[...].astype(wide_t)
        return value.astype(low_t)

    first, last = total(refs[:4]), total(refs[4:8])
    width, half = first.shape[1], last.shape[1] // 2
    out[:, :width] = first
    out[:16, width:] = last[:, :half]
    out[16:, width:] = last[:, half:]


def place_all(ids, *refs):
    parts, refs = refs[:8], refs[8:]
    g_in, g_out, g_cross, g_cross_pair, g_cross_query, g_output, gains, shifts, g_query, g_pair = refs[:10]
    pair_t, all_t = refs[10:]
    half = FF // 2
    start_cross = half + 2 * D
    start_pair = start_cross + D // 2
    start_end = start_pair + 4 * 128
    half_end = parts[0].shape[1] - start_end
    for n in range(2):
        core = ids[1] ^ n
        for step in range(4):
            chip, part = ids[0] ^ step, parts[n * 4 + step]
            rows = at16(chip * 32, 32)
            device = chip * 2 + core
            for k in range(4):
                g_in[rows, at128(k * 512 + core * 256, 256)] = part[
                    :, k * 256 : (k + 1) * 256
                ].astype(wide_t)
            for g in range(2):
                g_out[at16(core * 256 + chip * 64 + g * 32, 32), :] = part[
                    :, half + g * D : half + (g + 1) * D
                ].astype(wide_t)
            g_cross[rows, at128(core * 256, 256)] = part[:, start_cross:start_pair].astype(wide_t)
            for g in range(4):
                column = start_pair + g * 128
                row = (g // 2) * D + device * HEAD + (g % 2) * 32
                pair_t[at16(row, 32), :] = part[:, column : column + 128].astype(wide_t)

            def piece(column, width):
                row, at = (0, column) if column < half_end else (16, column - half_end)
                return part[row : row + 16, start_end + at : start_end + at + width].astype(wide_t)

            own_rows = at16(device * 16)
            for column in range(0, D, 128):
                g_cross_query[own_rows, column : column + 128] = piece(column, 128)
                g_output[own_rows, column : column + 128] = piece(D + column, 128)
            if n == 0 and step == 0:
                norms = piece(2 * D, 128)
                gains[...], shifts[...] = norms[0:3], norms[3:6]
            for g in range(12):
                row = (g // 4) * D + device * HEAD + (g % 4) * 16
                all_t[at16(row), :] = piece(2 * D + 256 + g * 128, 128)
    g_cross_pair[...] = pair_t[...].T
    g_query[...] = all_t[:D, :].T
    g_pair[...] = all_t[D:, :].T


def pack_rows(ids, stream, source, many):
    for k in range(4):
        many[k, :, :D] = stream[...]
        many[k, :, D:] = source[...]


def pack_start(ids, wq, wkv, ffn_in, ffn_out, pack):
    own = ids[0] * 2 + ids[1]
    for k in range(4):
        start = 3 * D + FF + k * D
        pack[:, start : start + D] = ffn_out[at16(own * 64 + k * 16), :]
    pack[:, :D] = wq[at16(own * 16), :]
    pack[:, D : 3 * D] = wkv[at16(own * 16), :]
    pack[:, 3 * D : 3 * D + FF] = ffn_in[at16(own * 16), :]


def pack_more(ids, *refs):
    weights, gain, shift, rows_in, pack, many = refs[:4], *refs[4:]
    rows = at16(ids[1] * 64, 64)
    norms = (gain[...].astype(wide_t), shift[...].astype(wide_t), jnp.zeros((58, 128), wide_t))
    norms = jnp.concatenate(norms, axis=0).astype(low_t)
    for k in range(4):
        start = 0
        for w in weights:
            pack[k, :, start : start + w.shape[1]] = w[rows, :]
            start += w.shape[1]
        pack[k, :, start:] = norms
        many[k] = rows_in[...]


def mask_data(ids, order, ranks, limits, cols, row_data, all_rows):
    rows = cols.shape[0]
    ends = [ids[3]]
    for n in range(1, 4):
        ends.append(ends[-1] + ids[3 + n])

    def sequence(position):
        return sum((position >= end).astype(wide_t) for end in ends)

    for n in range(2):
        for k in range(4):
            b = n * 4 + k
            device = k * 2 + (ids[1] ^ n)
            here = at128(device * rows, rows)
            index = lax.broadcasted_iota(jnp.int32, (1, rows), 1) + device * rows
            all_rows[b : b + 1, :] = sequence(order[:, here])
            all_rows[8 + b : 9 + b, :] = ranks[:, here].astype(wide_t)
            all_rows[16 + b : 17 + b, :] = sequence(index)
            row_data[8 + b : 9 + b, :] = limits[:, here].astype(wide_t)
    row_data[0:8, :] = all_rows[0:8, :]
    all_rows[24:32, :] = jnp.zeros((8, rows), wide_t)
    all_rows[24:25, :] = all_rows[pl.ds(ids[0], 1), :]
    row_data[16:24, :] = jnp.zeros((8, rows), wide_t)
    row_data[16:17, :] = all_rows[pl.ds(ids[0], 1), :]
    row_data[17:18, :] = row_data[pl.ds(8 + ids[0], 1), :]
    cols[:, :32] = all_rows[...].T


def pack_first(ids, *refs):
    parts, (one, two) = refs[:4], refs[4:]
    width = one.shape[1]
    for e in range(4):
        here = slice(e * 16, (e + 1) * 16)
        one[here, :] = parts[e][:, :width]
        two[here, :] = parts[e][:, width:]


def core_swap(value):
    return lax.ppermute(value, "core", [(0, 1), (1, 0)])


def chip_swaps(parts):
    moves = [[(i, i ^ k) for i in range(4)] for k in range(4)]
    return [parts[0]] + [lax.ppermute(parts[k], "chip", moves[k]) for k in range(1, 4)]


def shard_swaps(parts):
    moves = [[(i, i ^ k) for i in range(4)] for k in range(4)]
    return [parts[0]] + [lax.ppermute(parts[k], "wa", moves[k]) for k in range(1, 4)]


def deal(value):
    return lax.all_to_all(value, "chip", 0, 0, tiled=True)


def deal_all(value):
    return lax.all_to_all(value, ("chip", "core"), 0, 0, tiled=True)


def deal_both(value):
    own = deal(value)
    return own, core_swap(own)


def after(value, *others):
    return lax.optimization_barrier((value,) + others)[0]


def fast_shards(
    hidden,
    stream,
    encoder,
    lengths,
    order,
    ranks,
    thresholds,
    self_query,
    self_key_value,
    self_output,
    cross_query,
    cross_key_value,
    cross_output,
    ffn_in,
    ffn_out,
    norm_gain,
    norm_shift,
    cotangent,
):
    rows, keys = hidden.shape[1], order.shape[1]
    chip, core, mw = lax.axis_index("chip"), lax.axis_index("core"), lax.axis_index("wa")
    ids = jnp.stack((chip, core, mw)).astype(jnp.int32)
    inputs = hidden[0]

    (many,) = run(pack_rows, [((4, rows, 2 * D), low_t)], ids, [stream[0], encoder[0]])
    (pack1,) = run(
        pack_start,
        [((16, 3 * D + 2 * FF), low_t)],
        ids,
        [after(self_query, many), self_key_value, ffn_in, ffn_out],
    )
    x_own = deal(many)
    shards1 = shard_swaps([pack1] * 4)
    copies2, hidden_copies = run(
        pack_more,
        [((4, 64, 5 * D + 128), low_t), ((4, rows, D), low_t)],
        ids,
        [after(self_output, pack1), cross_query, cross_key_value, cross_output, norm_gain, norm_shift]
        + [inputs],
    )
    cols, row_data = run(
        mask_data,
        [((rows, 32), wide_t), ((24, rows), wide_t)],
        jnp.concatenate((after(ids, pack1), lengths[0])),
        [order, ranks, thresholds],
        [((32, rows), wide_t)],
    )
    part1, part3 = run(
        pack_first,
        [((64, 3 * D), low_t), ((64, 2 * FF), low_t)],
        ids,
        [after(shards1[0], x_own, cols, copies2)] + shards1[1:],
    )
    slices1 = chip_swaps([part1] * 4)
    slices1 = slices1 + [core_swap(part) for part in slices1]
    shards2 = lax.all_to_all(after(copies2, x_own), "wa", 0, 0, tiled=True)
    x_other = core_swap(after(x_own, part1))
    slices3 = chip_swaps([after(part3, slices1[1])] * 4)
    stream_own, stream_other = (x_own, 0), (x_other, 0)
    source_own, source_other = (x_own, 1), (x_other, 1)

    attend_scratch = [
        ((rows, D), low_t),
        ((keys, D), low_t),
        ((D, keys), low_t),
        ((D, D), low_t),
        ((keys, rows), wide_t),
        ((2, keys, rows), wide_t),
        ((D, rows), wide_t),
    ]
    self_low, self_mixed, self_lse, wq, wkv = run(
        self_forward,
        [((rows, D), low_t), ((rows, D), wide_t), ((HEADS, rows), wide_t)]
        + [((D, D), low_t), ((D, 2 * D), low_t)],
        ids,
        [inputs, stream_own, stream_other, *slices1, cols, row_data],
        attend_scratch,
        us=15,
    )
    head_shapes = [((keys, PAIR), low_t)] * 2 + [((HEAD, keys), low_t)]
    self_head = run(
        functools.partial(pair_setup, True),
        head_shapes,
        ids,
        [stream_own, stream_other, wkv, after(cols, self_low)],
        [((PAIR, rows), wide_t)],
        us=4,
    )
    slices3 = slices3 + [core_swap(after(part, self_head[0])) for part in slices3]
    shards2_other = core_swap(after(shards2, self_head[0], *slices3[:4]))
    hidden_own = deal(after(hidden_copies, shards2, self_head[0], *slices3[:4]))
    (
        first,
        normed,
        scale,
        first_low,
        cross_low,
        cross_mixed,
        cross_lse,
        cross_q,
        wo,
        wcq,
        wckv,
        wco,
        gs,
        *cross_head,
    ) = run(
        cross_forward,
        [((rows, D), wide_t)] * 2
        + [((rows, 128), wide_t)]
        + [((rows, D), low_t)] * 2
        + [((rows, D), wide_t), ((HEADS, rows), wide_t), ((rows, D), low_t)]
        + [((D, D), low_t), ((D, D), low_t), ((D, 2 * D), low_t), ((D, D), low_t), ((16, D), low_t)]
        + head_shapes,
        ids,
        [inputs, after(self_low, self_head[0]), source_own, source_other, shards2, shards2_other]
        + [cols, row_data],
        attend_scratch + [((PAIR, rows), wide_t)],
        us=15,
    )
    hidden_other = core_swap(after(hidden_own, cross_low))
    width_s = 2 * FF // 2 + 3 * D + D // 2
    result, cross_dealt, second_grad, keep_a, send_a, sums = run(
        feed_forward,
        [
            ((rows, D), low_t),
            ((PAIRS, rows + 16, 2 * PAIR), low_t),
            ((rows, D), wide_t),
            ((rows, width_s), low_t),
            ((rows, width_s), low_t),
            ((8, D), wide_t),
        ],
        ids,
        [after(first, hidden_own), cross_low, cross_mixed, cross_lse, row_data, cross_q, wco, gs]
        + [cotangent[0], *slices3],
        [((rows, FF), wide_t), ((2, D, FF // 2), low_t), ((2, FF // 2, D), low_t)],
        us=8,
    )
    both_own = deal(cross_dealt)
    width_a = FF // 2 + 2 * D + D // 2
    (dealt_a,) = run(
        grads_a,
        [((4, 128, width_a), low_t)],
        ids,
        [keep_a, core_swap(send_a)],
        [((D, FF // 2), low_t), ((FF // 2, D), low_t), ((D, D // 2), low_t)],
        us=6,
    )
    rows_a = deal(after(dealt_a, both_own))
    both_other = core_swap(after(both_own, dealt_a))

    back_scratch = (
        [((8, rows, PAIR), low_t)] * 2
        + [((8, HEAD, rows), low_t)]
        + [((keys, PAIR), wide_t)] * 3
        + [((PAIR, rows), wide_t)]
    )
    cq_keep, cq_send, cross_dkv = run(
        functools.partial(pair_back, False),
        [((4, HEAD, rows), low_t)] * 2 + [((8, 2 * HEAD, rows), low_t)],
        ids,
        [after(both_own, dealt_a), both_other, *cross_head],
        back_scratch,
        us=16,
    )
    pairs = run(pair_up, [((PAIR, rows), low_t)] * 4, ids, [cq_keep, core_swap(cq_send)])
    cross_back = chip_swaps(pairs)
    (self_queries,) = run(
        pair_queries,
        [((8, rows, PAIR), low_t)],
        ids,
        [hidden_own, hidden_other, after(wq, pairs[0])],
    )
    (cross_dw,) = run(
        pair_grads,
        [((4, 2 * HEAD, 128), low_t)],
        ids,
        [after(cross_dkv, pairs[0]), source_own, source_other],
    )
    first_grad, self_branch, self_dealt, cross_dq, sums = run(
        first_back,
        [
            ((rows, D), wide_t),
            ((rows, D), low_t),
            ((PAIRS, rows + 32, PAIR), low_t),
            ((rows, D), low_t),
            ((8, D), wide_t),
        ],
        ids,
        [after(cross_back[0], cross_dw, self_queries), *cross_back[1:], second_grad, normed, scale, self_mixed, self_lse, row_data, gs, wcq, wo, sums],
        [((D, rows), low_t)],
        us=4,
    )
    do_own = deal(after(self_dealt, rows_a))
    shards_a = run(
        add_chips,
        [((32, width_a + 512), low_t)] * 4,
        ids,
        [after(rows_a, first_grad), cross_dw],
    )
    moved_a = shard_swaps([after(part, do_own) for part in shards_a])
    (dealt_b,) = run(
        grads_b,
        [((8, 64, 2 * D + 128 + 2 * rows), low_t)],
        ids,
        [first_low, cross_dq, self_low, self_branch, sums, cross_dkv],
        [((D, D), low_t)] * 2,
        us=3,
    )
    rows_b = deal_all(after(dealt_b, do_own))
    do_other = core_swap(after(do_own, dealt_b, *shards_a))
    (self_back_t,) = run(
        functools.partial(pair_back, True),
        [((8, 3 * HEAD, rows), low_t)],
        ids,
        [self_queries, after(do_own, dealt_b, *shards_a), do_other, *self_head, cols, row_data],
        back_scratch,
        us=16,
    )
    end_width = 2 * D + 2 * 128 + 12 * 128
    (self_dw,) = run(
        self_grads,
        [((4, 3 * HEAD, 128), low_t)],
        ids,
        [self_back_t, stream_own, stream_other, hidden_own, hidden_other],
    )
    end_parts = run(
        end_sums, [((16, end_width), low_t)] * 4, ids, [after(rows_b, self_dw), self_dw]
    )
    moved_end = shard_swaps(end_parts)
    self_back = deal_all(after(self_back_t, end_parts[0], *moved_a))
    (source_grad,) = run(
        source_back,
        [((rows, D), wide_t)],
        ids,
        [rows_b, after(wckv, end_parts[0])],
        [((2 * D, rows), low_t)],
        us=3,
    )
    (sums_end,) = run(
        add_shards,
        [((32, width_a + 512 + end_width // 2), low_t)],
        ids,
        [*moved_a, after(moved_end[0], source_grad), *moved_end[1:]],
    )
    all_parts = chip_swaps([sums_end] * 4)
    hidden_grad, stream_grad = run(
        hidden_back,
        [((rows, D), wide_t)] * 2,
        ids,
        [self_back, first_grad, wq, wkv],
        [((3 * D, rows), low_t)],
        us=3,
    )
    all_parts = all_parts + [core_swap(after(part, hidden_grad)) for part in all_parts]
    (
        grad_in,
        grad_out,
        grad_cross_output,
        grad_cross_pair,
        grad_cross_query,
        grad_output,
        gain_grads,
        shift_grads,
        grad_query,
        grad_pair,
    ) = run(
        place_all,
        [((128, FF), wide_t), ((D, D), wide_t), ((128, D), wide_t), ((128, 2 * D), wide_t)]
        + [((128, D), wide_t)] * 2
        + [((3, 128), wide_t)] * 2
        + [((128, D), wide_t), ((128, 2 * D), wide_t)],
        ids,
        all_parts,
        [((2 * D, 128), wide_t), ((3 * D, 128), wide_t)],
    )
    return (
        result[None],
        hidden_grad[None],
        stream_grad[None],
        source_grad[None],
        grad_query,
        grad_pair,
        grad_output,
        grad_cross_query,
        grad_cross_pair,
        grad_cross_output,
        grad_in,
        grad_out,
        gain_grads,
        shift_grads,
    )


def solution(mesh):
    in_specs = (
        P("wa", "ctx", None),
        P("wa", "ctx", None),
        P("wa", "ctx", None),
        P("wa", None),
        P("wa", None),
        P("wa", None),
        P("wa", None),
        P("wa", None),
        P("wa", None),
        P("wa", None),
        P("wa", None),
        P("wa", None),
        P("wa", None),
        P("wa", None),
        P("wa", None),
        P(None, "wa"),
        P(None, "wa"),
        P("wa", "ctx", None),
    )
    out_specs = (
        P("wa", "ctx", None),
        P("wa", "ctx", None),
        P("wa", "ctx", None),
        P("wa", "ctx", None),
        P("wa", None),
        P("wa", None),
        P("wa", None),
        P("wa", None),
        P("wa", None),
        P("wa", None),
        P("wa", None),
        P("wa", None),
        P(None, "wa"),
        P(None, "wa"),
    )
    if mesh.axis_names != ("ctx", "wa") or mesh.shape["ctx"] != HEADS or mesh.shape["wa"] != 4:
        return jax.shard_map(
            general_shards, mesh=mesh, in_specs=in_specs, out_specs=out_specs, check_vma=False
        )

    def finer(spec):
        return P(*(("chip", "core") if axis == "ctx" else axis for axis in spec))

    return jax.shard_map(
        fast_shards,
        mesh=Mesh(mesh.devices.reshape(4, 2, 4), ("chip", "core", "wa")),
        in_specs=tuple(finer(spec) for spec in in_specs),
        out_specs=tuple(finer(spec) for spec in out_specs),
        check_vma=False,
    )
```
